32 devices in a mesh: seq: 8 (over y, x, core), batch: 4 (over z).
Axes of the slice: x: 2, y: 2, z: 4, core: 2. Of those that a mesh axis runs over, the one named last changes fastest.
Arguments:
- tokens: float32 [8, 1024, 1024], P('batch', 'seq'), may hold values from -6 to 6
- lengths: int32 [8], P('batch'), may hold values from 102 to 1024, as said below
- out_grad: float32 [8, 1024, 1024], P('batch', 'seq'), may hold values from -6 to 6
- first_gain: float32 [1024], P('seq'), may hold values from 0.25 to 1.75
- smooth_alpha: float32 [1024, 16], P('seq'), may hold values from -9 to -2
- smooth_delta: float32 [1024, 16], P('seq'), may hold values from -3 to 2
- smooth_beta: float32 [1024, 16], P('seq'), may hold values from -4 to 4
- smooth_gamma: float32 [1024, 16], P('seq'), may hold values from -4 to 4
- smooth_omega: float32 [1024], P('seq'), may hold values from -4 to 4
- value_weight: float32 [1024, 2048], P('seq'), may hold values from -0.1875 to 0.1875
- mix_weight: float32 [1024, 4224], P('seq'), may hold values from -0.1875 to 0.1875
- query_affine: float32 [128, 3], P('seq'), may hold values from -10 to 10
- merge_weight: float32 [2048, 1024], P('seq'), may hold values from -0.75 to 0.75
- second_gain: float32 [1024], P('seq'), may hold values from 0.25 to 1.75
- widen_weight: float32 [1024, 4096], P('seq'), may hold values from -0.1875 to 0.1875
- narrow_weight: float32 [4096, 1024], P('seq'), may hold values from -0.09375 to 0.09375
Outputs:
- block_out: float32 [8, 1024, 1024], P('batch', 'seq')
- tokens_grad: float32 [8, 1024, 1024], P('batch', 'seq')
- first_gain_grad: float32 [1024], P('seq')
- smooth_alpha_grad: float32 [1024, 16], P('seq')
- smooth_delta_grad: float32 [1024, 16], P('seq')
- smooth_beta_grad: float32 [1024, 16], P('seq')
- smooth_gamma_grad: float32 [1024, 16], P('seq')
- smooth_omega_grad: float32 [1024], P('seq')
- value_weight_grad: float32 [1024, 2048], P('seq')
- mix_weight_grad: float32 [1024, 4224], P('seq')
- query_affine_grad: float32 [128, 3], P('seq')
- merge_weight_grad: float32 [2048, 1024], P('seq')
- second_gain_grad: float32 [1024], P('seq')
- widen_weight_grad: float32 [1024, 4096], P('seq')
- narrow_weight_grad: float32 [4096, 1024], P('seq')
The draws below stay inside these ranges and needn't reach their ends.
Inputs may be any that keep to these rules, and one draw needn't show every extreme that they name: `lengths`: in every group of 2 consecutive slots at least one sequence has length 1024.
All inputs are finite; a program needn't handle non-finite values.
Results may differ from the reference program's by a relative error of at most 0.0003.
Values sent between devices are 32-bit elements; how exact they have to be, the bound alone decides.
A program may use at most 512 MiB of HBM per device.

```python
import jax
import jax.numpy as jnp
from jax import lax

D = 1024
Z = 128
V = 2048
NDIM = 16
FF = 4096
SPAN = 128
SEQS = 2
SEQUENCES = 8
SEQ_LEN = 1024


def draw_lengths(key, part):
    first_key = jax.random.fold_in(key, 11)
    second_key = jax.random.fold_in(key, 12)
    drawn = jax.random.randint(first_key, (SEQUENCES,), SEQ_LEN // 10, SEQ_LEN + 1)
    picked = jax.random.randint(second_key, (SEQUENCES // SEQS,), 0, SEQS)
    chosen = jnp.repeat(picked, SEQS, total_repeat_length=SEQUENCES)
    position = jnp.arange(SEQUENCES) % SEQS
    return jnp.where(position == chosen, SEQ_LEN, drawn).astype(jnp.int32)


def shard_levels(own_key, extent, shards, low, high):
    def one(axis_at, parts):
        heights = jax.random.uniform(jax.random.fold_in(jax.random.fold_in(own_key, 6), axis_at), (parts,), jnp.float32, low / len(shards), high / len(shards))
        return jnp.repeat(jnp.exp(heights), extent[axis_at] // parts).reshape((-1,) + (1,) * (len(extent) - axis_at - 1))

    factor_of = one(*shards[0])
    for cut in shards[1:]:
        factor_of = factor_of * one(*cut)
    return factor_of


def scatter_about(own_key, shape, scale, most, split=(), kind=jnp.bfloat16):
    loudness = shard_levels(own_key, shape, split, -0.22, 0.18) if split else 1.0
    values = jax.random.normal(own_key, shape, jnp.float32) * scale * loudness
    return jnp.minimum(jnp.maximum(values, -most), most).astype(kind)


def setup_inputs(seed: int = 0) -> dict:
    key_of = jax.random.split(jax.random.key(seed), 17)
    return {
        "tokens": scatter_about(key_of[0], (SEQUENCES, SEQ_LEN, D), 1.0, 6.0, ((0, 4), (1, 8)), jnp.float32),
        "lengths": draw_lengths(jax.random.fold_in(key_of[16], 71), 0),
        "out_grad": scatter_about(key_of[2], (SEQUENCES, SEQ_LEN, D), 1.0, 6.0, ((0, 4), (1, 8)), jnp.float32),
        "first_gain": jnp.clip(1.0 + 0.15 * jax.random.normal(key_of[3], (D,), jnp.float32), 0.25, 1.75),
        "smooth_alpha": jnp.clip(-9.0 + 7.0 * jax.random.uniform(key_of[4], (D, NDIM), jnp.float32) ** shard_levels(key_of[4], (D, NDIM), ((0, 8),), -0.2, 0.2), -9.0, -2.0),
        "smooth_delta": jnp.clip(-3.0 + 5.0 * jax.random.uniform(key_of[5], (D, NDIM), jnp.float32) ** shard_levels(key_of[5], (D, NDIM), ((0, 8),), -0.2, 0.2), -3.0, 2.0),
        "smooth_beta": scatter_about(key_of[6], (D, NDIM), 1.0, 4.0, ((0, 8),), jnp.float32),
        "smooth_gamma": scatter_about(key_of[7], (D, NDIM), 1.0, 4.0, ((0, 8),), jnp.float32),
        "smooth_omega": scatter_about(key_of[8], (D,), 1.0, 4.0, ((0, 8),), jnp.float32),
        "value_weight": scatter_about(key_of[9], (D, V), D ** -0.5, 0.1875, ((0, 8),), jnp.float32),
        "mix_weight": scatter_about(key_of[10], (D, 2 * D + Z + V), D ** -0.5, 0.1875, ((0, 8),), jnp.float32),
        "query_affine": scatter_about(key_of[11], (Z, 3), 2.5, 10.0, ((0, 8),), jnp.float32),
        "merge_weight": scatter_about(key_of[12], (V, D), (V // 32) ** -0.5, 0.75, ((0, 8),), jnp.float32),
        "second_gain": jnp.clip(1.0 + 0.15 * jax.random.normal(key_of[13], (D,), jnp.float32), 0.25, 1.75),
        "widen_weight": scatter_about(key_of[14], (D, FF), D ** -0.5, 0.1875, ((0, 8),), jnp.float32),
        "narrow_weight": scatter_about(key_of[15], (FF, D), FF ** -0.5, 0.09375, ((0, 8),), jnp.float32),
    }


precise = lax.Precision.HIGHEST
norm_eps = 1e-05
masked_score = -1000000000.0

@jax.custom_vjp
def low(v):
    return lax.optimization_barrier(v.astype(jnp.bfloat16)).astype(jnp.float32)

@jax.custom_vjp
def low_back(v):
    return v

def low_keep(v):
    return (low(v), None)

def low_pass(kept, grad):
    return (grad,)

def back_keep(v):
    return (v, None)

def back_low(kept, grad):
    return (low(grad),)
low.defvjp(low_keep, low_pass)
low_back.defvjp(back_keep, back_low)

def layer_norm(signal, norm_gain):
    centre = lax.optimization_barrier(jnp.mean(signal, axis=-1, keepdims=True))
    shifted = signal - centre
    spread = lax.optimization_barrier(jnp.mean(shifted * shifted, axis=-1, keepdims=True))
    return shifted * lax.rsqrt(spread + norm_eps) * norm_gain

def smoothing_tables(alpha_logit, delta_logit, expand_gain, project_gain, block_len):
    alpha_rate = jax.nn.sigmoid(alpha_logit)
    damp_rate = jax.nn.sigmoid(delta_logit)
    log_decay = jnp.log1p(-alpha_rate * damp_rate)
    offsets = jnp.arange(block_len + 1, dtype=jnp.float32)
    powers = jnp.exp(offsets[:, None, None] * log_decay[None])
    rising = jnp.exp(-offsets[:block_len, None, None] * log_decay[None])
    input_gain = alpha_rate * expand_gain
    out_scale = project_gain.shape[1] ** (-0.5)
    weighted = powers[:block_len] * (input_gain * project_gain * out_scale)[None]
    toeplitz = jnp.einsum('tdn,sdn->dts', weighted, rising, precision=precise)
    causal = offsets[:block_len, None] >= offsets[None, :block_len]
    toeplitz = jnp.where(causal[None], toeplitz, 0.0)
    return (powers, input_gain, toeplitz)

def gated_mix(masked_in, normed, smoothed, skip_gain, value_weight, mix_weight, query_affine, merge_weight, valid_mask, block_len):
    model_width = masked_in.shape[-1]
    shared_dim = query_affine.shape[0]
    value_dim = value_weight.shape[1]
    values = jax.nn.silu(jnp.einsum('bld,dv->blv', normed, value_weight, precision=precise))
    mixed_in = jax.nn.silu(smoothed + skip_gain * normed)
    projected = jnp.einsum('bld,dk->blk', mixed_in, mix_weight, precision=precise)
    second_cut = model_width + shared_dim
    third_cut = second_cut + value_dim
    update = jax.nn.sigmoid(projected[..., :model_width])
    shared = jax.nn.silu(projected[..., model_width:second_cut])
    reset_gate = jax.nn.silu(projected[..., second_cut:third_cut])
    candidate_in = projected[..., third_cut:]
    queries = shared * query_affine[:, 0] + query_affine[:, 2]
    key_rows = shared * query_affine[:, 1]
    blocks = masked_in.shape[0] * masked_in.shape[1] // block_len
    scores = jnp.einsum('cqz,ckz->cqk', queries.reshape(blocks, block_len, shared_dim), key_rows.reshape(blocks, block_len, shared_dim), precision=precise) * shared_dim ** (-0.5)
    key_valid = valid_mask.reshape(blocks, 1, block_len)
    scores = jnp.where(key_valid > 0.5, scores, masked_score)
    soft_weights = jax.nn.softmax(scores, axis=-1)
    attended = jnp.einsum('cqk,ckv->cqv', soft_weights, values.reshape(blocks, block_len, value_dim), precision=precise).reshape(values.shape)
    candidate = jax.nn.silu(candidate_in + jnp.einsum('blv,vd->bld', attended * reset_gate, merge_weight, precision=precise))
    return masked_in + update * (candidate - masked_in)

def feed_forward(middle, norm_gain, widen_weight, narrow_weight, valid_mask):
    normed_two = layer_norm(middle, norm_gain)
    hidden = jax.nn.silu(jnp.einsum('bld,df->blf', normed_two, widen_weight, precision=precise))
    return (middle + jnp.einsum('blf,fd->bld', hidden, narrow_weight, precision=precise)) * valid_mask[:, :, None]

def block_forward(params, tokens, valid_mask):
    first_gain, smooth_alpha, smooth_delta, smooth_beta, smooth_gamma, smooth_omega, value_weight, mix_weight, query_affine, merge_weight, second_gain, widen_weight, narrow_weight = params
    masked_in = tokens * valid_mask[:, :, None]
    normed = layer_norm(masked_in, first_gain)
    seq_count, seq_len, model_width = tokens.shape
    powers, input_gain, toeplitz = smoothing_tables(smooth_alpha, smooth_delta, smooth_beta, smooth_gamma, SPAN)
    out_scale = smooth_gamma.shape[1] ** (-0.5)
    carry_table = powers[1:] * (smooth_gamma * out_scale)[None]
    reversed_powers = powers[:SPAN][::-1]
    ordered = normed.reshape(seq_count, seq_len // SPAN, SPAN, model_width).transpose(1, 0, 2, 3)

    def advance(carry_state, segment):
        local_sum = jnp.einsum('dts,bsd->btd', toeplitz, segment, precision=precise)
        carried = jnp.einsum('tdn,bdn->btd', carry_table, carry_state, precision=precise)
        end_state = input_gain[None] * jnp.einsum('sdn,bsd->bdn', reversed_powers, segment, precision=precise)
        return (powers[SPAN][None] * carry_state + end_state, local_sum + carried)
    initial = jnp.zeros((seq_count, model_width, smooth_gamma.shape[1]), jnp.float32)
    final_state, smoothed = lax.scan(jax.checkpoint(advance), initial, ordered)
    smoothed = smoothed.transpose(1, 0, 2, 3).reshape(seq_count, seq_len, model_width)
    middle = gated_mix(masked_in, normed, smoothed, smooth_omega, value_weight, mix_weight, query_affine, merge_weight, valid_mask, SPAN)
    return feed_forward(middle, second_gain, widen_weight, narrow_weight, valid_mask)

def reference(tokens, lengths, out_grad, first_gain, smooth_alpha, smooth_delta, smooth_beta, smooth_gamma, smooth_omega, value_weight, mix_weight, query_affine, merge_weight, second_gain, widen_weight, narrow_weight):
    params = (first_gain, smooth_alpha, smooth_delta, smooth_beta, smooth_gamma, smooth_omega, value_weight, mix_weight, query_affine, merge_weight, second_gain, widen_weight, narrow_weight)
    groups = SEQUENCES // SEQS
    offsets = jnp.arange(SEQ_LEN, dtype=jnp.int32)

    def one_group(totals, inputs):
        group_tokens, group_lengths, group_grad = inputs
        valid_mask = (offsets[None, :] < group_lengths[:, None]).astype(jnp.float32)

        def forward(weights, signal):
            return block_forward(weights, signal, valid_mask)
        result, pullback = jax.vjp(forward, params, group_tokens)
        weight_grads, token_grads = pullback(group_grad)
        return (jax.tree.map(jnp.add, totals, weight_grads), (result, token_grads))
    zero_sums = jax.tree.map(jnp.zeros_like, params)
    totals, (results, token_grads) = lax.scan(one_group, zero_sums, (tokens.reshape(groups, SEQS, SEQ_LEN, D), lengths.reshape(groups, SEQS), out_grad.reshape(groups, SEQS, SEQ_LEN, D)))
    return (results.reshape(SEQUENCES, SEQ_LEN, D), token_grads.reshape(SEQUENCES, SEQ_LEN, D), totals[0], totals[1], totals[2], totals[3], totals[4], totals[5], totals[6], totals[7], totals[8], totals[9], totals[10], totals[11], totals[12])
```

```python
import functools

import jax
import jax.numpy as jnp
from jax import lax
from jax.experimental import pallas as pl
from jax.experimental.pallas import tpu as pltpu
from jax.sharding import PartitionSpec as P

exact = lax.Precision.HIGHEST
triple = lax.Precision.HIGH
norm_eps = 1e-05
masked_score = -1000000000.0
lanes = 128


def swap(value, bit):
    count = lax.axis_size("seq")
    return lax.ppermute(value, "seq", [(i, i ^ bit) for i in range(count)])


def gather_rows(shard):
    count = lax.axis_size("seq")
    if count != 8:
        return lax.all_gather(shard, "seq", axis=0, tiled=True)
    me = lax.axis_index("seq")
    rows, columns = shard.shape
    half = rows // 2
    across_x = swap(shard, 2)
    across_y = swap(shard, 4)
    corner_top = swap(across_x[:half], 4)
    corner_low = swap(across_y[half:], 2)
    full = jnp.zeros((count, 2, half, columns), shard.dtype)
    pieces = (
        (shard.reshape(2, half, columns), 0, 0),
        (across_x.reshape(2, half, columns), 2, 0),
        (across_y.reshape(2, half, columns), 4, 0),
        (corner_top[None], 6, 0),
        (corner_low[None], 6, 1),
    )
    for piece, bit, part in pieces:
        full = lax.dynamic_update_slice(full, piece[None], (me ^ bit, part, 0, 0))
    for piece, bit, part in pieces:
        full = lax.dynamic_update_slice(full, swap(piece, 1)[None], (me ^ bit ^ 1, part, 0, 0))
    return full.reshape(count * rows, columns)


def product_grad(left, right):
    return lax.dot_general(left, right, (((0,), (0,)), ((), ())), precision=triple)


def split(value):
    high = lax.reduce_precision(value, 8, 7)
    return high.astype(jnp.bfloat16), (value - high).astype(jnp.bfloat16)


def slot_of(count):
    table, chunk, left, right = [], 0, 0, 0
    for lefts, rights in count:
        table.append((chunk, left, right, rights))
        chunk, left, right = chunk + lefts * rights, left + lefts, right + rights
    return table, chunk


def reduce_body(
    count, left_high, left_low, right_high, right_low, extra, out,
    away, keep, got, got_x, got_y, got_xy, got_yx, part, from_edge, from_inner, sent, came,
):
    table, chunks = slot_of(count)
    depth, delay = away.shape[0], 2
    me, place = lax.axis_index("seq"), lax.axis_index("batch")
    core, along_x, along_y = me % 2, (me // 2) % 2, me // 4
    is_edge = (place == 0) | (place == 3)
    partner = jnp.where(place < 2, 1 - place, 5 - place)
    sibling, across_x, across_y = (
        {"seq": me + bit * (1 - 2 * own)} for bit, own in ((1, core), (2, along_x), (4, along_y))
    )

    barrier = pltpu.get_barrier_semaphore()
    for target in (sibling, across_x, across_y, {"batch": partner}):
        pl.semaphore_signal(barrier, inc=1, device_id=target, device_id_type=pl.DeviceIdType.MESH)

    @pl.when(jnp.logical_not(is_edge))
    def _():
        pl.semaphore_signal(
            barrier, inc=1, device_id={"batch": 3 - place}, device_id_type=pl.DeviceIdType.MESH
        )
        pl.semaphore_wait(barrier, 5)

    @pl.when(is_edge)
    def _():
        pl.semaphore_wait(barrier, 4)

    def copy(kind, slot, source, target, device):
        return pltpu.make_async_remote_copy(
            src_ref=source, dst_ref=target, send_sem=sent.at[kind, slot], recv_sem=came.at[kind, slot],
            device_id=device, device_id_type=pl.DeviceIdType.MESH,
        )

    def link(kind, chunk):
        slot = chunk % depth
        pairs = (
            lambda: (away.at[slot], got.at[slot], sibling),
            lambda: (keep.at[slot, :, 1 - along_x, 0], got_x.at[slot], across_x),
            lambda: (keep.at[slot, 1 - along_y, :, 1], got_y.at[slot], across_y),
            lambda: (got_x.at[slot, 1 - along_y], got_xy.at[slot], across_y),
            lambda: (got_y.at[slot, 1 - along_x], got_yx.at[slot], across_x),
            lambda: (part.at[slot], from_edge.at[slot], {"batch": partner}),
            lambda: (part.at[slot], from_inner.at[slot], {"batch": 3 - place}),
            lambda: (out.at[chunk], out.at[chunk], {"batch": partner}),
        )
        return copy(kind, slot, *pairs[kind]())

    def start(chunk):
        slot = chunk % depth
        to_sibling = link(0, chunk)

        @pl.when(chunk < chunks)
        def _():
            left, right = chunk * 0, chunk * 0
            for first, first_left, first_right, rights in table:
                inside = chunk >= first
                left = jnp.where(inside, first_left + (chunk - first) // rights, left)
                right = jnp.where(inside, first_right + (chunk - first) % rights, right)

            def product(parity):
                high, low = left_high[left, parity], left_low[left, parity]
                other = right_high[right]
                dot = functools.partial(jnp.dot, preferred_element_type=jnp.float32)
                total = dot(high, other) + (dot(low, other) + dot(high, right_low[right]))
                return total.reshape(away.shape[1:])

            away[slot] = product(1 - core)
            to_sibling.start()
            keep[slot] = product(core)

        @pl.when(chunk == chunks)
        def _():
            away[slot] = extra[1 - core].reshape(away.shape[1:])
            to_sibling.start()
            keep[slot] = extra[core].reshape(away.shape[1:])

    def with_sibling(chunk):
        slot = chunk % depth
        to_sibling, first, second = (link(kind, chunk) for kind in (0, 1, 2))
        to_sibling.wait()
        keep[slot] = keep[slot] + got[slot]
        first.start()
        second.start()

    def with_neighbour(chunk):
        slot = chunk % depth
        first, second, third, fourth = (link(kind, chunk) for kind in (1, 2, 3, 4))
        first.wait()
        second.wait()
        got_x[slot] = got_x[slot] + keep[slot, :, along_x, 0]
        got_y[slot] = got_y[slot] + keep[slot, along_y, :, 1]
        third.start()
        fourth.start()

    def with_corner(chunk):
        slot = chunk % depth
        third, fourth, to_inner = (link(kind, chunk) for kind in (3, 4, 5))
        third.wait()
        fourth.wait()
        part[slot, 0] = got_x[slot, along_y] + got_xy[slot]
        part[slot, 1] = got_y[slot, along_x] + got_yx[slot]

        @pl.when(is_edge)
        def _():
            to_inner.start()

    def inner_sum(chunk):
        slot = chunk % depth
        to_inner, across = (link(kind, chunk) for kind in (5, 6))

        @pl.when(is_edge)
        def _():
            to_inner.wait_send()

        @pl.when(jnp.logical_not(is_edge))
        def _():
            to_inner.wait_recv()
            part[slot] = part[slot] + from_edge[slot]
            across.start()

    def total_sum(chunk):
        slot = chunk % depth
        across, to_edge = (link(kind, chunk) for kind in (6, 7))

        @pl.when(jnp.logical_not(is_edge))
        def _():
            across.wait()
            out[chunk] = (part[slot] + from_inner[slot]).reshape(out.shape[1:])
            to_edge.start()

    def finish(chunk):
        to_edge = link(7, chunk)

        @pl.when(is_edge)
        def _():
            to_edge.wait_recv()

        @pl.when(jnp.logical_not(is_edge))
        def _():
            to_edge.wait_send()

    phases = (start, with_sibling, with_neighbour, with_corner, inner_sum, total_sum, finish)

    def step(at, carry):
        for number in range(len(phases) - 1, -1, -1):
            chunk = at - number * delay

            @pl.when((chunk >= 0) & (chunk <= chunks))
            def _():
                phases[number](chunk)

        return carry

    lax.fori_loop(0, chunks + 1 + (len(phases) - 1) * delay, step, 0)


def reduce_grads(products, extra, width=256):
    rows = products[0][0].shape[0]
    lefts, rights, count = [], [], []
    for left, right in products:
        blocks = left.shape[1] // (8 * lanes)
        cut = left.reshape(rows, 4, 2, blocks, lanes).transpose(3, 2, 1, 4, 0)
        lefts.append(cut.reshape(blocks, 2, 4 * lanes, rows))
        wide = right.shape[1] // width
        rights.append(right.reshape(rows, wide, width).transpose(1, 0, 2))
        count.append((blocks, wide))
    left_high, left_low = split(jnp.concatenate(lefts, axis=0))
    right_high, right_low = split(jnp.concatenate(rights, axis=0))
    _, chunks = slot_of(count)
    pairs = extra.reshape(4, 2, lanes, width).transpose(1, 0, 2, 3).reshape(2, 4 * lanes, width)
    depth, half = 8, lanes // 2
    vmem = pl.BlockSpec(memory_space=pltpu.VMEM)
    out = pl.pallas_call(
        functools.partial(reduce_body, tuple(count)),
        out_shape=jax.ShapeDtypeStruct((chunks + 1, 2, half, width), jnp.float32),
        in_specs=[vmem] * 5,
        out_specs=vmem,
        scratch_shapes=[pltpu.VMEM((depth, 2, 2, 2, half, width), jnp.float32)] * 3
        + [pltpu.VMEM((depth, 2, half, width), jnp.float32)] * 2
        + [pltpu.VMEM((depth, half, width), jnp.float32)] * 2
        + [pltpu.VMEM((depth, 2, half, width), jnp.float32)] * 3
        + [pltpu.SemaphoreType.DMA((8, depth))] * 2,
        compiler_params=pltpu.CompilerParams(
            collective_id=1, has_side_effects=True, vmem_limit_bytes=60 * 1024 * 1024
        ),
    )(left_high, left_low, right_high, right_low, pairs)
    out = out.reshape(chunks + 1, lanes, width)
    grads = []
    for (blocks, wide), (first, _, _, _) in zip(count, slot_of(count)[0]):
        piece = out[first : first + blocks * wide].reshape(blocks, wide, lanes, width)
        grads.append(piece.transpose(0, 2, 1, 3).reshape(blocks * lanes, wide * width))
    return grads, out[chunks]


def all_grads(products, packed, single):
    count = lax.axis_size("seq")
    rows, features = packed.shape
    blocks = packed.reshape(rows, count, features // count).transpose(1, 0, 2)
    last = product_grad(*single)
    if count != 8 or lax.axis_size("batch") != 4:

        def total(whole, tiled):
            part = lax.psum_scatter(whole, "seq", scatter_dimension=0, tiled=tiled)
            return lax.psum(part, "batch")

        wholes = [total(product_grad(*pair), True) for pair in products]
        return wholes, total(blocks, False), total(last, True)
    blocks = jnp.pad(blocks, ((0, 0), (0, lanes - rows), (0, 0)))
    extra = jnp.concatenate([last.reshape(count, lanes, -1), blocks], axis=2)
    wholes, rest = reduce_grads(products, extra)
    return wholes, rest[:rows, lanes:], rest[:, :lanes]


def tree_sum(terms):
    while len(terms) > 1:
        terms = [a + b for a, b in zip(terms[::2], terms[1::2])] + (
            [terms[-1]] if len(terms) % 2 else []
        )
    return terms[0]


def filter_body(reverse, decay_ref, weight_ref, signal_ref, out_ref, end_ref):
    sequences, length = signal_ref.shape[:2]
    states = decay_ref.shape[0]
    for s in range(sequences):

        def step(t, held):
            at = length - 1 - t if reverse else t
            entry = signal_ref[s, at]
            held = tuple(decay_ref[n] * held[n] + entry for n in range(states))
            out_ref[s, at] = tree_sum([weight_ref[n] * held[n] for n in range(states)])
            return held

        zero = jnp.zeros(signal_ref.shape[2:], jnp.float32)
        held = lax.fori_loop(0, length, step, (zero,) * states, unroll=4)
        for n in range(states):
            end_ref[s, n] = held[n]


def carried_body(reverse, decay_ref, weight_ref, enter_ref, local_ref, out_ref):
    sequences, length = local_ref.shape[:2]
    states = decay_ref.shape[0]
    for s in range(sequences):

        def step(t, held):
            at = length - 1 - t if reverse else t
            held = tuple(decay_ref[n] * held[n] for n in range(states))
            out_ref[s, at] = local_ref[s, at] + tree_sum(list(held))
            return held

        start = tuple(weight_ref[n] * enter_ref[s, n] for n in range(states))
        lax.fori_loop(0, length, step, start, unroll=4)


def moments_body(decay_ref, enter_ref, signal_ref, grad_ref, direct_ref, slope_ref, last_ref):
    sequences, length = signal_ref.shape[:2]
    states = decay_ref.shape[0]
    group = min(8, states)
    zero = jnp.zeros(signal_ref.shape[2:], jnp.float32)
    for low in range(0, states, group):
        span = range(low, min(low + group, states))
        sums = ((zero,) * len(span), (zero,) * len(span))
        for s in range(sequences):

            def step(t, carry):
                held, slope, direct, sloped = carry
                entry, grad = signal_ref[s, t], grad_ref[s, t]
                slope = tuple(decay_ref[n] * d + h for n, d, h in zip(span, slope, held))
                held = tuple(decay_ref[n] * h + entry for n, h in zip(span, held))
                direct = tuple(q + grad * h for q, h in zip(direct, held))
                sloped = tuple(q + grad * d for q, d in zip(sloped, slope))
                return held, slope, direct, sloped

            start = (tuple(enter_ref[s, n] for n in span), (zero,) * len(span)) + sums
            _, slope, direct, sloped = lax.fori_loop(0, length, step, start, unroll=2)
            sums = (direct, sloped)
            for n, d in zip(span, slope):
                last_ref[s, n] = d
        for n, q, d in zip(span, *sums):
            direct_ref[n] = q
            slope_ref[n] = d


def call_kernel(body, shapes, *operands):
    return pl.pallas_call(
        body,
        out_shape=[jax.ShapeDtypeStruct(shape, jnp.float32) for shape in shapes],
        in_specs=[pl.BlockSpec(memory_space=pltpu.VMEM)] * len(operands),
        out_specs=[pl.BlockSpec(memory_space=pltpu.VMEM)] * len(shapes),
        compiler_params=pltpu.CompilerParams(vmem_limit_bytes=32 * 1024 * 1024),
    )(*operands)


def entering(ends, block_decay, backward):
    count, mine = lax.axis_size("seq"), lax.axis_index("seq")
    pieces = lax.all_gather(ends, "seq")
    if backward:
        mine = count - 1 - mine
    total = jnp.zeros_like(ends)
    for position in range(count - 1):
        piece = pieces[count - 1 - position if backward else position]
        total = jnp.where(position < mine, block_decay * total + piece, total)
    return total


def silu(value):
    return value * jax.nn.sigmoid(value)


def silu_slope(value):
    gate = jax.nn.sigmoid(value)
    return gate * (1.0 + value * (1.0 - gate))


def normalise(signal):
    centre = jnp.mean(signal, axis=-1, keepdims=True)
    shifted = signal - centre
    spread = jnp.mean(shifted * shifted, axis=-1, keepdims=True)
    scale = lax.rsqrt(spread + norm_eps)
    return shifted * scale, scale


def normalise_back(grad, gain, hat, scale):
    inner = grad * gain
    return (
        inner
        - jnp.mean(inner, axis=-1, keepdims=True)
        - hat * jnp.mean(inner * hat, axis=-1, keepdims=True)
    ) * scale


def times(left, right):
    return jnp.dot(left, right, precision=triple)


def times_back(left, right):
    return lax.dot_general(left, right, (((1,), (1,)), ((), ())), precision=triple)


def per_device(
    tokens,
    lengths,
    out_grad,
    first_gain,
    smooth_alpha,
    smooth_delta,
    smooth_beta,
    smooth_gamma,
    smooth_omega,
    value_weight,
    mix_weight,
    query_affine,
    merge_weight,
    second_gain,
    widen_weight,
    narrow_weight,
):
    sequences, block_len, width = tokens.shape
    count = lax.axis_size("seq")
    states = smooth_alpha.shape[1]
    own = first_gain.shape[0]
    own_shared = query_affine.shape[0]
    rows = sequences * block_len
    value_dim = value_weight.shape[1]
    shared_dim = own_shared * count

    affine_row = jnp.pad(query_affine.reshape(-1), (0, own - 3 * own_shared))
    packed = jnp.concatenate(
        [
            smooth_alpha.T,
            smooth_delta.T,
            smooth_beta.T,
            smooth_gamma.T,
            jnp.stack([first_gain, smooth_omega, second_gain, affine_row]),
        ],
        axis=0,
    )
    small = lax.all_gather(packed, "seq").transpose(1, 0, 2)
    value_full = gather_rows(value_weight)
    mix_full = gather_rows(mix_weight)
    merge_full = gather_rows(merge_weight)
    widen_full = gather_rows(widen_weight)
    narrow_full = gather_rows(narrow_weight)

    tiles = (width // lanes, lanes)
    alpha_rate = jax.nn.sigmoid(small[:states].reshape(states, *tiles))
    damp_rate = jax.nn.sigmoid(small[states : 2 * states].reshape(states, *tiles))
    beta = small[2 * states : 3 * states].reshape(states, *tiles)
    gamma = small[3 * states : 4 * states].reshape(states, *tiles)
    gain_one = small[4 * states].reshape(1, width)
    omega = small[4 * states + 1].reshape(1, width)
    gain_two = small[4 * states + 2].reshape(1, width)
    affine = small[4 * states + 3, :, : 3 * own_shared].reshape(shared_dim, 3)
    out_scale = states ** (-0.5)
    decay = 1.0 - alpha_rate * damp_rate
    block_decay = jnp.exp(block_len * jnp.log1p(-alpha_rate * damp_rate))
    weight = alpha_rate * beta * gamma * out_scale

    offsets = lax.axis_index("seq") * block_len + lax.iota(jnp.int32, block_len)
    valid = (offsets[None, :] < lengths[:, None]).astype(jnp.float32)
    row_valid = valid.reshape(rows, 1)
    key_valid = valid.reshape(sequences, 1, block_len) > 0.5

    masked_in = tokens.reshape(rows, width) * row_valid
    hat_one, scale_one = normalise(masked_in)
    normed = hat_one * gain_one
    tiled = (sequences, block_len) + tiles
    ending = (sequences, states) + tiles
    signal = normed.reshape(tiled)
    local, ends = call_kernel(
        functools.partial(filter_body, False), [tiled, ending], decay, weight, signal
    )
    enter = entering(ends, block_decay, False)
    (smoothed,) = call_kernel(
        functools.partial(carried_body, False), [tiled], decay, weight, enter, local
    )
    mix_pre = smoothed.reshape(rows, width) + omega * normed
    mixed = silu(mix_pre)
    value_pre = times(normed, value_full)
    values = silu(value_pre)
    projected = times(mixed, mix_full)
    second_cut = width + shared_dim
    third_cut = second_cut + value_dim
    update = jax.nn.sigmoid(projected[:, :width])
    shared_pre = projected[:, width:second_cut]
    reset_pre = projected[:, second_cut:third_cut]
    shared = silu(shared_pre)
    reset_gate = silu(reset_pre)
    queries = (shared * affine[:, 0] + affine[:, 2]).reshape(sequences, block_len, shared_dim)
    key_rows = (shared * affine[:, 1]).reshape(sequences, block_len, shared_dim)
    score_scale = shared_dim ** (-0.5)
    scores = jnp.einsum("cqz,ckz->cqk", queries, key_rows, precision=exact) * score_scale
    scores = jnp.where(key_valid, scores, masked_score)
    soft = jax.nn.softmax(scores, axis=-1)
    values_cut = values.reshape(sequences, block_len, value_dim)
    attended = jnp.einsum("cqk,ckv->cqv", soft, values_cut, precision=triple)
    attended = attended.reshape(rows, value_dim)
    gated = attended * reset_gate
    cand_pre = projected[:, third_cut:] + times(gated, merge_full)
    candidate = silu(cand_pre)
    middle = masked_in + update * (candidate - masked_in)
    hat_two, scale_two = normalise(middle)
    normed_two = hat_two * gain_two
    wide_pre = times(normed_two, widen_full)
    hidden = silu(wide_pre)

    g_out = out_grad.reshape(rows, width) * row_valid
    g_wide = times_back(g_out, narrow_full) * silu_slope(wide_pre)
    g_normed_two = times_back(g_wide, widen_full)
    second_gain_sum = jnp.sum(g_normed_two * hat_two, axis=0)
    g_middle = g_out + normalise_back(g_normed_two, gain_two, hat_two, scale_two)

    g_cand = g_middle * update * silu_slope(cand_pre)
    g_gated = times_back(g_cand, merge_full)
    g_attended = (g_gated * reset_gate).reshape(sequences, block_len, value_dim)
    g_reset = g_gated * attended
    g_soft = jnp.einsum("cqv,ckv->cqk", g_attended, values_cut, precision=triple)
    g_values = jnp.einsum("cqk,cqv->ckv", soft, g_attended, precision=triple)
    g_scores = soft * (g_soft - jnp.sum(g_soft * soft, axis=-1, keepdims=True))
    g_scores = jnp.where(key_valid, g_scores, 0.0) * score_scale
    g_queries = jnp.einsum("cqk,ckz->cqz", g_scores, key_rows, precision=exact)
    g_keys = jnp.einsum("cqk,cqz->ckz", g_scores, queries, precision=exact)
    g_queries = g_queries.reshape(rows, shared_dim)
    g_keys = g_keys.reshape(rows, shared_dim)
    affine_sum = jnp.stack(
        [
            jnp.sum(g_queries * shared, axis=0),
            jnp.sum(g_keys * shared, axis=0),
            jnp.sum(g_queries, axis=0),
        ],
        axis=1,
    )
    g_shared = (g_queries * affine[:, 0] + g_keys * affine[:, 1]) * silu_slope(shared_pre)
    g_update = g_middle * (candidate - masked_in) * update * (1.0 - update)
    g_reset_pre = g_reset * silu_slope(reset_pre)
    g_projected = jnp.concatenate([g_update, g_shared, g_reset_pre, g_cand], axis=1)
    g_smooth = times_back(g_projected, mix_full) * silu_slope(mix_pre)
    g_val = g_values.reshape(rows, value_dim) * silu_slope(value_pre)
    g_from_values = times_back(g_val, value_full)

    smooth_tiled = g_smooth.reshape(tiled)
    back_local, back_ends = call_kernel(
        functools.partial(filter_body, True), [tiled, ending], decay, weight, smooth_tiled
    )
    back_enter = entering(back_ends, block_decay, True)
    direct, slope, last = call_kernel(
        moments_body,
        [(states,) + tiles, (states,) + tiles, ending],
        decay,
        enter,
        signal,
        smooth_tiled,
    )
    (back_full,) = call_kernel(
        functools.partial(carried_body, True), [tiled], decay, weight, back_enter, back_local
    )
    slope = slope + decay * jnp.sum(back_enter * last, axis=0)
    decay_grad = weight * slope
    alpha_grad = (beta * gamma * out_scale * direct - damp_rate * decay_grad) * (
        alpha_rate * (1.0 - alpha_rate)
    )
    delta_grad = -alpha_rate * decay_grad * damp_rate * (1.0 - damp_rate)
    beta_grad = alpha_rate * gamma * out_scale * direct
    gamma_grad = alpha_rate * beta * out_scale * direct

    g_normed = g_from_values + g_smooth * omega + back_full.reshape(rows, width)
    tokens_grad = (
        g_middle * (1.0 - update) + normalise_back(g_normed, gain_one, hat_one, scale_one)
    ) * row_valid
    first_gain_sum = jnp.sum(g_normed * hat_one, axis=0)
    omega_sum = jnp.sum(g_smooth * normed, axis=0)
    affine_rows = jnp.pad(
        affine_sum.reshape(count, 3 * own_shared), ((0, 0), (0, own - 3 * own_shared))
    )
    small_rows = [
        alpha_grad.reshape(states, width),
        delta_grad.reshape(states, width),
        beta_grad.reshape(states, width),
        gamma_grad.reshape(states, width),
        jnp.stack([first_gain_sum, omega_sum, second_gain_sum, affine_rows.reshape(width)]),
    ]
    wholes, small_grad, shared_grad = all_grads(
        (
            (hidden, g_out),
            (normed_two, g_wide),
            (gated, g_cand),
            (mixed, jnp.concatenate([g_update, g_reset_pre, g_cand], axis=1)),
            (normed, g_val),
        ),
        jnp.concatenate(small_rows, axis=0),
        (mixed, g_shared),
    )
    narrow_grad, widen_grad, merge_grad, mix_rest, value_grad = wholes
    mix_grad = jnp.concatenate([mix_rest[:, :width], shared_grad, mix_rest[:, width:]], axis=1)

    block_out = (middle + times(hidden, narrow_full)) * row_valid

    return (
        block_out.reshape(tokens.shape),
        tokens_grad.reshape(tokens.shape),
        small_grad[4 * states],
        small_grad[:states].T,
        small_grad[states : 2 * states].T,
        small_grad[2 * states : 3 * states].T,
        small_grad[3 * states : 4 * states].T,
        small_grad[4 * states + 1],
        value_grad,
        mix_grad,
        small_grad[4 * states + 3, : 3 * own_shared].reshape(own_shared, 3),
        merge_grad,
        small_grad[4 * states + 2],
        widen_grad,
        narrow_grad,
    )


def solution(mesh):
    rows = P("batch", "seq", None)
    split = P("seq", None)
    in_specs = (
        (rows, P("batch"), rows, P("seq"))
        + (split,) * 4
        + (P("seq"),)
        + (split,) * 4
        + (P("seq"),)
        + (split,) * 2
    )
    out_specs = (
        (rows, rows, P("seq"))
        + (split,) * 4
        + (P("seq"),)
        + (split,) * 4
        + (P("seq"),)
        + (split,) * 2
    )
    return jax.shard_map(
        per_device, mesh=mesh, in_specs=in_specs, out_specs=out_specs, check_vma=False
    )
```

```python
import functools

import jax
import jax.numpy as jnp
from jax import lax
from jax.experimental import pallas as pl
from jax.experimental.pallas import tpu as pltpu
from jax.sharding import PartitionSpec as P

exact = lax.Precision.HIGHEST
triple = lax.Precision.HIGH
norm_eps = 1e-05
masked_score = -1000000000.0
lanes = 128


def gather_rows(shard):
    return lax.all_gather(shard, "seq", axis=0, tiled=True)


def product_grad(left, right):
    return lax.dot_general(left, right, (((0,), (0,)), ((), ())), precision=triple)


def split(value):
    high = lax.reduce_precision(value, 8, 7)
    return high.astype(jnp.bfloat16), (value - high).astype(jnp.bfloat16)


def halves(value):
    high = value.astype(jnp.bfloat16)
    return high, (value - high.astype(jnp.float32)).astype(jnp.bfloat16)


def contract(left, right, left_dim, right_dim, precision=None):
    return lax.dot_general(
        left, right, (((left_dim,), (right_dim,)), ((), ())),
        precision=precision, preferred_element_type=jnp.float32,
    )


def turned(left, right):
    return contract(left, right, 0, 0)


def three(left, right, left_dim, right_dim):
    (high, low), (other, rest) = left, right
    return contract(high, other, left_dim, right_dim) + (
        contract(low, other, left_dim, right_dim) + contract(high, rest, left_dim, right_dim)
    )


def place_of(device):
    return (device % 2) * 4 + device // 2


gather_shapes = ((1, 8), (1, 16), (2, 4), (1, 16), (4, 4))


def forward_body(
    value_ref, mix_ref, merge_ref, widen_ref, narrow_ref,
    normed_h, normed_l, mixed_h, mixed_l, shared_w, affine, key_valid, row_valid, masked, g_out, gain_two,
    w_high, w_low, value_pre, attended, projected, shared_pre, soft, cand_pre, middle, block_out,
    two_h, two_l, gated_h, gated_l, hidden_h, hidden_l, g_wide,
    buf, stage_h, stage_l, g_hidden, loaded, sent, came, stored,
):
    weights = (value_ref, mix_ref, merge_ref, widen_ref, narrow_ref)
    firsts, chunks = chunk_table(gather_shapes)
    depth, delay = buf.shape[0], 2
    width = buf.shape[-1]
    half = lanes * 4
    me, level = lax.axis_index("seq"), lax.axis_index("batch")
    core, along_x, along_y = me % 2, (me // 2) % 2, me // 4
    id_sibling = me + 1 - 2 * core
    id_x, id_y = me + 2 - 4 * along_x, me + 4 - 8 * along_y
    id_corner = id_x + 4 - 8 * along_y
    mine, at_x, at_y, at_corner = (place_of(device) for device in (me, id_x, id_y, id_corner))
    above, below = (level + 1) % 4, (level + 3) % 4
    quarter, eighth = lanes // 4, lanes // 8

    barrier = pltpu.get_barrier_semaphore()
    for target in (
        {"seq": id_sibling}, {"seq": id_x}, {"seq": id_y}, {"batch": above}, {"batch": below}
    ):
        pl.semaphore_signal(barrier, inc=1, **on_other(**target))
    pl.semaphore_wait(barrier, 5)

    def link(kind, chunk):
        slot = chunk % depth

        def rows(place, start, count):
            return buf.at[slot, place, pl.ds(pl.multiple_of(start, 8), count)]

        piece, target = (
            lambda: (buf.at[slot, mine], {"seq": id_x}),
            lambda: (buf.at[slot, mine], {"seq": id_y}),
            lambda: (buf.at[slot, mine], {"seq": id_sibling}),
            lambda: (rows(at_x, level * quarter, eighth), {"seq": id_y}),
            lambda: (rows(at_y, level * quarter + eighth, eighth), {"seq": id_x}),
            lambda: (buf.at[slot, at_x], {"seq": id_sibling}),
            lambda: (buf.at[slot, at_y], {"seq": id_sibling}),
            lambda: (rows(at_corner, level * quarter, quarter), {"batch": above}),
            lambda: (rows(at_corner, ((level + 3) % 4) * quarter, quarter), {"batch": above}),
            lambda: (rows(at_corner, ((level + 2) % 4) * quarter, quarter), {"batch": above}),
            lambda: (buf.at[slot, at_corner], {"seq": id_sibling}),
        )[kind]()
        return pltpu.make_async_remote_copy(
            src_ref=piece, dst_ref=piece, send_sem=sent.at[kind, slot], recv_sem=came.at[kind, slot],
            **on_other(**target),
        )

    def load(chunk):
        slot = chunk % depth
        for number, ((blocks, wide), first, weight) in enumerate(
            zip(gather_shapes, firsts, weights)
        ):

            @pl.when((chunk >= first) & (chunk < first + blocks * wide))
            def _(number=number, first=first, wide=wide, weight=weight):
                row = ((chunk - first) // wide) * lanes
                column = ((chunk - first) % wide) * width
                if number == 1:
                    column = column + jnp.where(column >= weights[2].shape[1], lanes, 0)
                source = weight.at[
                    pl.ds(pl.multiple_of(row, lanes), lanes),
                    pl.ds(pl.multiple_of(column, lanes), width),
                ]
                pltpu.make_async_copy(source, buf.at[slot, mine], loaded.at[slot]).start()

    def exchange(done, begun):
        def phase(chunk):
            for kind in done:
                link(kind, chunk).wait()
            for kind in begun:
                link(kind, chunk).start()

        return phase

    def send(chunk):
        slot = chunk % depth
        first = value_ref.at[pl.ds(0, lanes), pl.ds(0, width)]
        pltpu.make_async_copy(first, buf.at[slot, mine], loaded.at[slot]).wait()
        for kind in (0, 1, 2):
            link(kind, chunk).start()

    def store(chunk, kind):
        return pltpu.make_async_copy(
            (stage_h, stage_l)[kind].at[chunk % 2],
            (w_high, w_low)[kind].at[chunk],
            stored.at[kind, chunk % 2],
        )

    def product(left_h, left_l, right):
        return three((left_h[0], left_l[0]), (right[0][0], right[1][0]), 1, 0) + three(
            (left_h[1], left_l[1]), (right[0][1], right[1][1]), 1, 0
        )

    sequences, block_len = soft.shape[:2]

    def attention():
        shared_full = halves(shared_w[...])
        total = three(
            (mixed_h[0], mixed_l[0]), (shared_full[0][:, :half], shared_full[1][:, :half]), 1, 1
        ) + three(
            (mixed_h[1], mixed_l[1]), (shared_full[0][:, half:], shared_full[1][:, half:]), 1, 1
        )
        shared_pre[...] = total
        shared = total * jax.nn.sigmoid(total)
        queries = shared * affine[0:1] + affine[2:3]
        keys = shared * affine[1:2]
        for s in range(sequences):
            span = slice(s * block_len, (s + 1) * block_len)
            scores = contract(queries[span], keys[span], 1, 1, exact) * shared.shape[1] ** (-0.5)
            scores = jnp.where(key_valid[s] > 0.5, scores, masked_score)
            weight = jnp.exp(scores - jnp.max(scores, axis=1, keepdims=True))
            soft[s] = weight / jnp.sum(weight, axis=1, keepdims=True)

    def put(target_h, target_l, index, column, value):
        high, low = halves(value)
        target_h[(*index, slice(None), pl.ds(pl.multiple_of(column, lanes), lanes))] = high
        target_l[(*index, slice(None), pl.ds(pl.multiple_of(column, lanes), lanes))] = low

    def complete(chunk):
        slot = chunk % depth
        link(10, chunk).wait()

        @pl.when(chunk >= 2)
        def _():
            store(chunk - 2, 0).wait()
            store(chunk - 2, 1).wait()

        right = halves(buf[slot].reshape(2, half, width))
        stage_h[chunk % 2] = right[0]
        stage_l[chunk % 2] = right[1]
        store(chunk, 0).start()
        store(chunk, 1).start()

        def among(number):
            blocks, wide = gather_shapes[number]
            return (chunk >= firsts[number]) & (chunk < firsts[number] + blocks * wide)

        @pl.when(among(0))
        def _():
            total = product(normed_h, normed_l, right)
            value_pre[chunk] = total
            values = total * jax.nn.sigmoid(total)
            for s in range(sequences):
                span = slice(s * block_len, (s + 1) * block_len)
                attended[chunk, span] = contract(soft[s], values[span], 1, 0, exact)

        @pl.when(among(1))
        def _():
            tile = chunk - firsts[1]
            total = product(mixed_h, mixed_l, right)
            projected[tile] = total

            @pl.when((tile >= 4) & (tile < 12))
            def _():
                block = tile - 4
                gated = attended[block] * total * jax.nn.sigmoid(total)
                for j in range(2):
                    cut = gated[:, j * lanes : (j + 1) * lanes]
                    put(gated_h, gated_l, (j, block % 2), (block // 2) * lanes, cut)

        @pl.when(among(2))
        def _():
            j, tile = (chunk - firsts[2]) // 4, (chunk - firsts[2]) % 4
            total = product(gated_h.at[j], gated_l.at[j], right)

            @pl.when(j == 0)
            def _():
                cand_pre[tile] = projected[12 + tile] + total

            @pl.when(j == 1)
            def _():
                cand_pre[tile] = cand_pre[tile] + total

            @pl.when(chunk == firsts[3] - 1)
            def _():
                tiles = middle.shape[0]
                features = tiles * width
                total = 0.0
                for k in range(tiles):
                    cand = cand_pre[k]
                    cand = cand * jax.nn.sigmoid(cand)
                    value = masked[k] + jax.nn.sigmoid(projected[k]) * (cand - masked[k])
                    middle[k] = value
                    total = total + jnp.sum(value, axis=1, keepdims=True)
                centre = total / features
                total = 0.0
                for k in range(tiles):
                    shifted = middle[k] - centre
                    total = total + jnp.sum(shifted * shifted, axis=1, keepdims=True)
                scale = lax.rsqrt(total / features + norm_eps)
                for k in range(tiles):
                    value = (middle[k] - centre) * scale * gain_two[k]
                    for parity in range(2):
                        cut = value[:, parity * lanes : (parity + 1) * lanes]
                        put(two_h, two_l, (parity,), k * lanes, cut)
                    block_out[k] = jnp.zeros(block_out.shape[1:], jnp.float32)
                g_hidden[...] = jnp.zeros(g_hidden.shape, jnp.float32)

        @pl.when(among(3))
        def _():
            tile = chunk - firsts[3]
            total = product(two_h, two_l, right)
            g_wide[tile] = total
            hidden = total * jax.nn.sigmoid(total)
            for i in range(2):
                cut = hidden[:, i * lanes : (i + 1) * lanes]
                index = (2 * (tile % 2) + i, (tile // 2) % 2)
                put(hidden_h, hidden_l, index, (tile // 4) * lanes, cut)

        @pl.when(among(4))
        def _():
            j, tile = (chunk - firsts[4]) // 4, (chunk - firsts[4]) % 4
            block_out[tile] = block_out[tile] + product(hidden_h.at[j], hidden_l.at[j], right)
            grad = halves(g_out[tile])
            for parity in range(2):
                back = three(grad, (right[0][parity], right[1][parity]), 1, 1)
                g_hidden[j, parity] = g_hidden[j, parity] + back

    phases = (
        (0, load),
        (1, send),
        (1 + delay, exchange((0, 1, 2), (3, 4, 5, 6))),
        (1 + 2 * delay, exchange((3, 4, 5, 6), (7,))),
        (1 + 3 * delay, exchange((7,), (8,))),
        (1 + 4 * delay, exchange((8,), (9,))),
        (1 + 5 * delay, exchange((9,), (10,))),
        (1 + 6 * delay, complete),
    )

    def step(at, carry):
        for after, phase in phases[-2:0:-1]:

            @pl.when((at >= after) & (at < after + chunks))
            def _(after=after, phase=phase):
                phase(at - after)

        pl.when(at < chunks)(lambda: load(at))
        pl.when(at == 2)(attention)

        @pl.when(at >= phases[-1][0])
        def _():
            complete(at - phases[-1][0])

        return carry

    lax.fori_loop(0, chunks + phases[-1][0], step, 0)
    for chunk in (chunks - 2, chunks - 1):
        for kind in range(2):
            store(chunk, kind).wait()
    for k in range(middle.shape[0]):
        block_out[k] = (middle[k] + block_out[k]) * row_valid[...]
    for k in range(g_wide.shape[0]):
        for i in range(2):
            span = slice(i * lanes, (i + 1) * lanes)
            back = g_hidden[2 * (k % 2) + i, (k // 2) % 2, :, (k // 4) * lanes : (k // 4 + 1) * lanes]
            wide = g_wide[k, :, span]
            g_wide[k, :, span] = back * silu_slope(wide)


def call_forward(weights, operands, rows, sequences):
    width = 256
    _, chunks = chunk_table(gather_shapes)
    vmem, anywhere = pl.BlockSpec(memory_space=pltpu.VMEM), pl.BlockSpec(memory_space=pl.ANY)

    def f32(*shape):
        return jax.ShapeDtypeStruct(shape, jnp.float32)

    def b16(*shape):
        return jax.ShapeDtypeStruct(shape, jnp.bfloat16)

    half, block_len = 4 * lanes, rows // sequences
    shapes = [b16(chunks, 2, half, width)] * 2 + [
        f32(8, rows, width), f32(8, rows, width), f32(16, rows, width), f32(rows, lanes),
        f32(sequences, block_len, block_len), f32(4, rows, width), f32(4, rows, width), f32(4, rows, width),
        b16(2, rows, half), b16(2, rows, half), b16(2, 2, rows, half), b16(2, 2, rows, half),
        b16(4, 2, rows, half), b16(4, 2, rows, half), f32(16, rows, width),
    ]
    depth = 16
    return pl.pallas_call(
        forward_body,
        out_shape=shapes,
        in_specs=[anywhere] * len(weights) + [vmem] * len(operands),
        out_specs=[anywhere] * 2 + [vmem] * (len(shapes) - 2),
        scratch_shapes=[
            pltpu.VMEM((depth, 8, lanes, width), jnp.float32),
            pltpu.VMEM((2, 2, half, width), jnp.bfloat16),
            pltpu.VMEM((2, 2, half, width), jnp.bfloat16),
            pltpu.VMEM((4, 2, rows, half), jnp.float32),
            pltpu.SemaphoreType.DMA((depth,)),
            pltpu.SemaphoreType.DMA((11, depth)),
            pltpu.SemaphoreType.DMA((11, depth)),
            pltpu.SemaphoreType.DMA((2, 2)),
        ],
        compiler_params=pltpu.CompilerParams(
            collective_id=2, has_side_effects=True, vmem_limit_bytes=60 * 1024 * 1024
        ),
    )(*weights, *operands)


def backward_body(
    w_high, w_low, g_wide, value_pre, attended, projected, shared_pre, soft, cand_pre, middle, masked, g_out,
    gain_two, shared_w, affine, key_valid,
    g_projected, g_val, g_shared, g_mixed, g_normed, g_rest, gain_sum, affine_sum,
    buf_h, buf_l, g_two, g_gated, fetched,
):
    firsts, _ = chunk_table(gather_shapes)
    steps = 48
    tiles, rows, width = masked.shape
    half = 4 * lanes
    features = tiles * width
    sequences, block_len = soft.shape[:2]

    def fetch(step, kind):
        chunk = jnp.where(
            step < 16, firsts[3] + step, jnp.where(step < 24, step + 8, jnp.where(step < 40, step - 16, step - 40))
        )
        slot = step % 4
        return pltpu.make_async_copy(
            (w_high, w_low)[kind].at[chunk], (buf_h, buf_l)[kind].at[slot], fetched.at[kind, slot]
        )

    def both(step, call):
        for kind in range(2):
            getattr(fetch(step, kind), call)()

    for step in range(3):
        both(step, "start")

    def back(grad, slot, parity):
        return three(halves(grad), (buf_h[slot, parity], buf_l[slot, parity]), 1, 1)

    def norm_two_back():
        total = 0.0
        for k in range(tiles):
            total = total + jnp.sum(middle[k], axis=1, keepdims=True)
        centre = total / features
        total = 0.0
        for k in range(tiles):
            shifted = middle[k] - centre
            total = total + jnp.sum(shifted * shifted, axis=1, keepdims=True)
        scale = lax.rsqrt(total / features + norm_eps)

        def grad_of(k):
            span = slice(k * lanes, (k + 1) * lanes)
            return jnp.concatenate([g_two[0, :, span], g_two[1, :, span]], axis=1)

        plain, crossed = 0.0, 0.0
        for k in range(tiles):
            grad, hat = grad_of(k), (middle[k] - centre) * scale
            gain_sum[k] = jnp.sum(grad * hat, axis=0, keepdims=True)
            inner = grad * gain_two[k]
            plain = plain + jnp.sum(inner, axis=1, keepdims=True)
            crossed = crossed + jnp.sum(inner * hat, axis=1, keepdims=True)
        plain, crossed = plain / features, crossed / features
        for k in range(tiles):
            inner, hat = grad_of(k) * gain_two[k], (middle[k] - centre) * scale
            g_middle = g_out[k] + (inner - plain - hat * crossed) * scale
            update = jax.nn.sigmoid(projected[k])
            pre = cand_pre[k]
            gate = jax.nn.sigmoid(pre)
            g_rest[k] = g_middle * (1.0 - update)
            g_projected[k] = g_middle * (pre * gate - masked[k]) * update * (1.0 - update)
            g_projected[12 + k] = g_middle * update * (gate * (1.0 + pre * (1.0 - gate)))

    def attention_back():
        g_soft = [0.0] * sequences
        for m in range(8):
            span = slice((m // 2) * lanes, (m // 2 + 1) * lanes)
            grad = jnp.concatenate([g_gated[0, m % 2, :, span], g_gated[1, m % 2, :, span]], axis=1)
            pre = projected[4 + m]
            gate = jax.nn.sigmoid(pre)
            g_attended = grad * pre * gate
            g_projected[4 + m] = grad * attended[m] * (gate * (1.0 + pre * (1.0 - gate)))
            pre = value_pre[m]
            gate = jax.nn.sigmoid(pre)
            values, slope = pre * gate, gate * (1.0 + pre * (1.0 - gate))
            for s in range(sequences):
                part = slice(s * block_len, (s + 1) * block_len)
                own = halves(g_attended[part])
                g_soft[s] = g_soft[s] + three(own, halves(values[part]), 1, 1)
                g_val[m, part] = three(halves(soft[s]), own, 0, 0) * slope[part]
        pre = shared_pre[...]
        gate = jax.nn.sigmoid(pre)
        shared, slope = pre * gate, gate * (1.0 + pre * (1.0 - gate))
        score_scale = shared.shape[1] ** (-0.5)
        queries = shared * affine[0:1] + affine[2:3]
        keys = shared * affine[1:2]
        sums = [0.0, 0.0, 0.0]
        for s in range(sequences):
            part = slice(s * block_len, (s + 1) * block_len)
            weight = soft[s]
            g_scores = weight * (g_soft[s] - jnp.sum(g_soft[s] * weight, axis=1, keepdims=True))
            g_scores = jnp.where(key_valid[s] > 0.5, g_scores, 0.0) * score_scale
            g_queries = contract(g_scores, keys[part], 1, 0, exact)
            g_keys = contract(g_scores, queries[part], 0, 0, exact)
            g_shared[part] = (g_queries * affine[0:1] + g_keys * affine[1:2]) * slope[part]
            for number, term in enumerate((g_queries * shared[part], g_keys * shared[part], g_queries)):
                sums[number] = sums[number] + jnp.sum(term, axis=0, keepdims=True)
        for number in range(3):
            affine_sum[number : number + 1] = sums[number]
        own, full = halves(g_shared[...]), halves(shared_w[...])
        for parity in range(2):
            span = slice(parity * half, (parity + 1) * half)
            g_mixed[parity] = three(own, (full[0][:, span], full[1][:, span]), 1, 0)

    g_two[...] = jnp.zeros(g_two.shape, jnp.float32)
    g_gated[...] = jnp.zeros(g_gated.shape, jnp.float32)
    g_normed[...] = jnp.zeros(g_normed.shape, jnp.float32)

    def work(step, carry):
        slot = step % 4
        pl.when(step + 3 < steps)(lambda: both(step + 3, "start"))
        both(step, "wait")
        pl.when(step == 16)(norm_two_back)
        pl.when(step == 24)(attention_back)

        @pl.when(step < 16)
        def _():
            for parity in range(2):
                g_two[parity] = g_two[parity] + back(g_wide[step], slot, parity)

        @pl.when((step >= 16) & (step < 24))
        def _():
            j = (step - 16) // 4
            for parity in range(2):
                more = back(g_projected[12 + step % 4], slot, parity)
                g_gated[j, parity] = g_gated[j, parity] + more

        @pl.when((step >= 24) & (step < 40))
        def _():
            for parity in range(2):
                g_mixed[parity] = g_mixed[parity] + back(g_projected[step - 24], slot, parity)

        @pl.when(step >= 40)
        def _():
            for parity in range(2):
                g_normed[parity] = g_normed[parity] + back(g_val[step - 40], slot, parity)

        return carry

    lax.fori_loop(0, steps, work, 0)


def call_backward(w_high, w_low, *operands):
    masked = operands[8]
    tiles, rows, width = masked.shape
    half = 4 * lanes
    vmem, anywhere = pl.BlockSpec(memory_space=pltpu.VMEM), pl.BlockSpec(memory_space=pl.ANY)
    shapes = [
        (16, rows, width), (8, rows, width), (rows, lanes), (2, rows, half), (2, rows, half),
        (tiles, rows, width), (tiles, 1, width), (3, lanes),
    ]
    return pl.pallas_call(
        backward_body,
        out_shape=[jax.ShapeDtypeStruct(shape, jnp.float32) for shape in shapes],
        in_specs=[anywhere] * 2 + [vmem] * len(operands),
        out_specs=[vmem] * len(shapes),
        scratch_shapes=[
            pltpu.VMEM((4, 2, half, width), jnp.bfloat16),
            pltpu.VMEM((4, 2, half, width), jnp.bfloat16),
            pltpu.VMEM((2, rows, half), jnp.float32),
            pltpu.VMEM((2, 2, rows, half), jnp.float32),
            pltpu.SemaphoreType.DMA((2, 4)),
        ],
        compiler_params=pltpu.CompilerParams(vmem_limit_bytes=60 * 1024 * 1024),
    )(w_high, w_low, *operands)


def on_other(**coordinate):
    return dict(device_id=coordinate, device_id_type=pl.DeviceIdType.MESH)


def chunk_table(shapes):
    firsts, chunk = [], 0
    for blocks, wide in shapes:
        firsts.append(chunk)
        chunk += blocks * wide
    return firsts, chunk


def reduce_body(shapes, offsets, *refs):
    highs, refs = refs[: len(shapes)], refs[len(shapes) :]
    lows, refs = refs[: len(shapes)], refs[len(shapes) :]
    rights, refs = refs[: len(shapes)], refs[len(shapes) :]
    extra, out, away, keep, got, got_x, got_y, got_xy, got_yx, part = refs[:10]
    from_edge, from_inner, sent, came = refs[10:]
    firsts, chunks = chunk_table(shapes)
    depth, delay = away.shape[0], 2
    me, place = lax.axis_index("seq"), lax.axis_index("batch")
    core, along_x, along_y = me % 2, (me // 2) % 2, me // 4
    is_edge = (place == 0) | (place == 3)
    partner = jnp.where(place < 2, 1 - place, 5 - place)
    sibling, across_x, across_y = (
        {"seq": me + bit * (1 - 2 * own)} for bit, own in ((1, core), (2, along_x), (4, along_y))
    )

    barrier = pltpu.get_barrier_semaphore()
    for target in (sibling, across_x, across_y, {"batch": partner}):
        pl.semaphore_signal(barrier, inc=1, device_id=target, device_id_type=pl.DeviceIdType.MESH)

    @pl.when(jnp.logical_not(is_edge))
    def _():
        pl.semaphore_signal(
            barrier, inc=1, device_id={"batch": 3 - place}, device_id_type=pl.DeviceIdType.MESH
        )
        pl.semaphore_wait(barrier, 5)

    @pl.when(is_edge)
    def _():
        pl.semaphore_wait(barrier, 4)

    def copy(kind, slot, source, target, device):
        return pltpu.make_async_remote_copy(
            src_ref=source, dst_ref=target, send_sem=sent.at[kind, slot], recv_sem=came.at[kind, slot],
            device_id=device, device_id_type=pl.DeviceIdType.MESH,
        )

    def link(kind, chunk):
        slot = chunk % depth
        pairs = (
            lambda: (away.at[slot], got.at[slot], sibling),
            lambda: (keep.at[slot, :, 1 - along_x, 0], got_x.at[slot], across_x),
            lambda: (keep.at[slot, 1 - along_y, :, 1], got_y.at[slot], across_y),
            lambda: (got_x.at[slot, 1 - along_y], got_xy.at[slot], across_y),
            lambda: (got_y.at[slot, 1 - along_x], got_yx.at[slot], across_x),
            lambda: (part.at[slot], from_edge.at[slot], {"batch": partner}),
            lambda: (part.at[slot], from_inner.at[slot], {"batch": 3 - place}),
            lambda: (out.at[chunk], out.at[chunk], {"batch": partner}),
        )
        return copy(kind, slot, *pairs[kind]())

    def start(chunk):
        slot = chunk % depth
        to_sibling = link(0, chunk)

        for (blocks, wide), first, shift, high, low, right in zip(
            shapes, firsts, offsets, highs, lows, rights
        ):

            @pl.when((chunk >= first) & (chunk < first + blocks * wide))
            def _(first=first, wide=wide, shift=shift, high=high, low=low, right=right):
                block = (chunk - first) // wide
                other, rest = halves(right[shift + (chunk - first) % wide])

                def product(parity):
                    top, under = high[block, parity], low[block, parity]
                    total = turned(top, other) + (turned(under, other) + turned(top, rest))
                    return total.reshape(away.shape[1:])

                away[slot] = product(1 - core)
                to_sibling.start()
                keep[slot] = product(core)

        @pl.when(chunk == chunks)
        def _():
            away[slot] = extra[1 - core].reshape(away.shape[1:])
            to_sibling.start()
            keep[slot] = extra[core].reshape(away.shape[1:])

    def with_sibling(chunk):
        slot = chunk % depth
        to_sibling, first, second = (link(kind, chunk) for kind in (0, 1, 2))
        to_sibling.wait()
        keep[slot] = keep[slot] + got[slot]
        first.start()
        second.start()

    def with_neighbour(chunk):
        slot = chunk % depth
        first, second, third, fourth = (link(kind, chunk) for kind in (1, 2, 3, 4))
        first.wait()
        second.wait()
        got_x[slot] = got_x[slot] + keep[slot, :, along_x, 0]
        got_y[slot] = got_y[slot] + keep[slot, along_y, :, 1]
        third.start()
        fourth.start()

    def with_corner(chunk):
        slot = chunk % depth
        third, fourth, to_inner = (link(kind, chunk) for kind in (3, 4, 5))
        third.wait()
        fourth.wait()
        part[slot, 0] = got_x[slot, along_y] + got_xy[slot]
        part[slot, 1] = got_y[slot, along_x] + got_yx[slot]

        @pl.when(is_edge)
        def _():
            to_inner.start()

    def inner_sum(chunk):
        slot = chunk % depth
        to_inner, across = (link(kind, chunk) for kind in (5, 6))

        @pl.when(is_edge)
        def _():
            to_inner.wait_send()

        @pl.when(jnp.logical_not(is_edge))
        def _():
            to_inner.wait_recv()
            part[slot] = part[slot] + from_edge[slot]
            across.start()

    def total_sum(chunk):
        slot = chunk % depth
        across, to_edge = (link(kind, chunk) for kind in (6, 7))

        @pl.when(jnp.logical_not(is_edge))
        def _():
            across.wait()
            out[chunk] = (part[slot] + from_inner[slot]).reshape(out.shape[1:])
            to_edge.start()

    def finish(chunk):
        to_edge = link(7, chunk)

        @pl.when(is_edge)
        def _():
            to_edge.wait_recv()

        @pl.when(jnp.logical_not(is_edge))
        def _():
            to_edge.wait_send()

    phases = (start, with_sibling, with_neighbour, with_corner, inner_sum, total_sum, finish)

    def step(at, carry):
        for number in range(len(phases) - 1, -1, -1):
            chunk = at - number * delay

            @pl.when((chunk >= 0) & (chunk <= chunks))
            def _():
                phases[number](chunk)

        return carry

    lax.fori_loop(0, chunks + 1 + (len(phases) - 1) * delay, step, 0)


def reduce_grads(products, extra):
    shapes = tuple((item[0].shape[0], item[4]) for item in products)
    width = extra.shape[-1]
    _, chunks = chunk_table(shapes)
    depth, half = 8, lanes // 2
    vmem = pl.BlockSpec(memory_space=pltpu.VMEM)
    out = pl.pallas_call(
        functools.partial(reduce_body, shapes, tuple(item[3] for item in products)),
        out_shape=jax.ShapeDtypeStruct((chunks + 1, 2, half, width), jnp.float32),
        in_specs=[vmem] * (3 * len(products) + 1),
        out_specs=vmem,
        scratch_shapes=[pltpu.VMEM((depth, 2, 2, 2, half, width), jnp.float32)] * 3
        + [pltpu.VMEM((depth, 2, half, width), jnp.float32)] * 2
        + [pltpu.VMEM((depth, half, width), jnp.float32)] * 2
        + [pltpu.VMEM((depth, 2, half, width), jnp.float32)] * 3
        + [pltpu.SemaphoreType.DMA((8, depth))] * 2,
        compiler_params=pltpu.CompilerParams(
            collective_id=1, has_side_effects=True, vmem_limit_bytes=60 * 1024 * 1024
        ),
    )(
        *[item[0] for item in products],
        *[item[1] for item in products],
        *[item[2] for item in products],
        extra,
    )
    out = out.reshape(chunks + 1, lanes, width)
    grads = []
    for (blocks, wide), first in zip(shapes, chunk_table(shapes)[0]):
        piece = out[first : first + blocks * wide].reshape(blocks, wide, lanes, width)
        grads.append(piece.transpose(0, 2, 1, 3).reshape(blocks * lanes, wide * width))
    return grads, out[chunks]


def tree_sum(terms):
    while len(terms) > 1:
        terms = [a + b for a, b in zip(terms[::2], terms[1::2])] + (
            [terms[-1]] if len(terms) % 2 else []
        )
    return terms[0]


def filter_body(reverse, decay_ref, weight_ref, signal_ref, out_ref, end_ref):
    sequences, length = signal_ref.shape[:2]
    states = decay_ref.shape[0]
    for s in range(sequences):

        def step(t, held):
            at = length - 1 - t if reverse else t
            entry = signal_ref[s, at]
            held = tuple(decay_ref[n] * held[n] + entry for n in range(states))
            out_ref[s, at] = tree_sum([weight_ref[n] * held[n] for n in range(states)])
            return held

        zero = jnp.zeros(signal_ref.shape[2:], jnp.float32)
        held = lax.fori_loop(0, length, step, (zero,) * states, unroll=4)
        for n in range(states):
            end_ref[s, n] = held[n]


def carried_body(reverse, decay_ref, weight_ref, enter_ref, local_ref, out_ref):
    sequences, length = local_ref.shape[:2]
    states = decay_ref.shape[0]
    for s in range(sequences):

        def step(t, held):
            at = length - 1 - t if reverse else t
            held = tuple(decay_ref[n] * held[n] for n in range(states))
            out_ref[s, at] = local_ref[s, at] + tree_sum(list(held))
            return held

        start = tuple(weight_ref[n] * enter_ref[s, n] for n in range(states))
        lax.fori_loop(0, length, step, start, unroll=4)


def moments_body(decay_ref, enter_ref, signal_ref, grad_ref, direct_ref, slope_ref, last_ref):
    sequences, length = signal_ref.shape[:2]
    states = decay_ref.shape[0]
    group = min(8, states)
    zero = jnp.zeros(signal_ref.shape[2:], jnp.float32)
    for low in range(0, states, group):
        span = range(low, min(low + group, states))
        sums = ((zero,) * len(span), (zero,) * len(span))
        for s in range(sequences):

            def step(t, carry):
                held, slope, direct, sloped = carry
                entry, grad = signal_ref[s, t], grad_ref[s, t]
                slope = tuple(decay_ref[n] * d + h for n, d, h in zip(span, slope, held))
                held = tuple(decay_ref[n] * h + entry for n, h in zip(span, held))
                direct = tuple(q + grad * h for q, h in zip(direct, held))
                sloped = tuple(q + grad * d for q, d in zip(sloped, slope))
                return held, slope, direct, sloped

            start = (tuple(enter_ref[s, n] for n in span), (zero,) * len(span)) + sums
            _, slope, direct, sloped = lax.fori_loop(0, length, step, start, unroll=2)
            sums = (direct, sloped)
            for n, d in zip(span, slope):
                last_ref[s, n] = d
        for n, q, d in zip(span, *sums):
            direct_ref[n] = q
            slope_ref[n] = d


def call_kernel(body, shapes, *operands):
    return pl.pallas_call(
        body,
        out_shape=[jax.ShapeDtypeStruct(shape, jnp.float32) for shape in shapes],
        in_specs=[pl.BlockSpec(memory_space=pltpu.VMEM)] * len(operands),
        out_specs=[pl.BlockSpec(memory_space=pltpu.VMEM)] * len(shapes),
        compiler_params=pltpu.CompilerParams(vmem_limit_bytes=32 * 1024 * 1024),
    )(*operands)


def entering(ends, block_decay, backward):
    count, mine = lax.axis_size("seq"), lax.axis_index("seq")
    pieces = lax.all_gather(ends, "seq")
    if backward:
        mine = count - 1 - mine
    total = jnp.zeros_like(ends)
    for position in range(count - 1):
        piece = pieces[count - 1 - position if backward else position]
        total = jnp.where(position < mine, block_decay * total + piece, total)
    return total


def silu(value):
    return value * jax.nn.sigmoid(value)


def silu_slope(value):
    gate = jax.nn.sigmoid(value)
    return gate * (1.0 + value * (1.0 - gate))


def normalise(signal):
    centre = jnp.mean(signal, axis=-1, keepdims=True)
    shifted = signal - centre
    spread = jnp.mean(shifted * shifted, axis=-1, keepdims=True)
    scale = lax.rsqrt(spread + norm_eps)
    return shifted * scale, scale


def normalise_back(grad, gain, hat, scale):
    inner = grad * gain
    return (
        inner
        - jnp.mean(inner, axis=-1, keepdims=True)
        - hat * jnp.mean(inner * hat, axis=-1, keepdims=True)
    ) * scale


def times(left, right):
    return jnp.dot(left, right, precision=triple)


def times_back(left, right):
    return lax.dot_general(left, right, (((1,), (1,)), ((), ())), precision=triple)


def plain_layer(masked_in, normed, mix_pre, g_out, row_valid, key_valid, affine, gain_two, weights):
    value_full, mix_full, merge_full, widen_full, narrow_full = (gather_rows(w) for w in weights)
    rows, width = masked_in.shape
    sequences, _, block_len = key_valid.shape
    value_dim, shared_dim = value_full.shape[1], affine.shape[0]
    mixed = silu(mix_pre)
    value_pre = times(normed, value_full)
    values = silu(value_pre)
    projected = times(mixed, mix_full)
    second_cut = width + shared_dim
    third_cut = second_cut + value_dim
    update = jax.nn.sigmoid(projected[:, :width])
    shared_pre = projected[:, width:second_cut]
    reset_pre = projected[:, second_cut:third_cut]
    shared = silu(shared_pre)
    reset_gate = silu(reset_pre)
    queries = (shared * affine[:, 0] + affine[:, 2]).reshape(sequences, block_len, shared_dim)
    key_rows = (shared * affine[:, 1]).reshape(sequences, block_len, shared_dim)
    score_scale = shared_dim ** (-0.5)
    scores = jnp.einsum("cqz,ckz->cqk", queries, key_rows, precision=exact) * score_scale
    scores = jnp.where(key_valid > 0.5, scores, masked_score)
    soft = jax.nn.softmax(scores, axis=-1)
    values_cut = values.reshape(sequences, block_len, value_dim)
    attended = jnp.einsum("cqk,ckv->cqv", soft, values_cut, precision=triple)
    attended = attended.reshape(rows, value_dim)
    gated = attended * reset_gate
    cand_pre = projected[:, third_cut:] + times(gated, merge_full)
    candidate = silu(cand_pre)
    middle = masked_in + update * (candidate - masked_in)
    hat_two, scale_two = normalise(middle)
    normed_two = hat_two * gain_two
    wide_pre = times(normed_two, widen_full)
    hidden = silu(wide_pre)
    block_out = (middle + times(hidden, narrow_full)) * row_valid

    g_wide = times_back(g_out, narrow_full) * silu_slope(wide_pre)
    g_normed_two = times_back(g_wide, widen_full)
    gain_sum = jnp.sum(g_normed_two * hat_two, axis=0)
    g_middle = g_out + normalise_back(g_normed_two, gain_two, hat_two, scale_two)
    g_cand = g_middle * update * silu_slope(cand_pre)
    g_gated = times_back(g_cand, merge_full)
    g_attended = (g_gated * reset_gate).reshape(sequences, block_len, value_dim)
    g_soft = jnp.einsum("cqv,ckv->cqk", g_attended, values_cut, precision=triple)
    g_values = jnp.einsum("cqk,cqv->ckv", soft, g_attended, precision=triple)
    g_scores = soft * (g_soft - jnp.sum(g_soft * soft, axis=-1, keepdims=True))
    g_scores = jnp.where(key_valid > 0.5, g_scores, 0.0) * score_scale
    g_queries = jnp.einsum("cqk,ckz->cqz", g_scores, key_rows, precision=exact)
    g_keys = jnp.einsum("cqk,cqz->ckz", g_scores, queries, precision=exact)
    g_queries = g_queries.reshape(rows, shared_dim)
    g_keys = g_keys.reshape(rows, shared_dim)
    terms = (g_queries * shared, g_keys * shared, g_queries)
    affine_sum = jnp.stack([jnp.sum(term, axis=0) for term in terms])
    g_shared = (g_queries * affine[:, 0] + g_keys * affine[:, 1]) * silu_slope(shared_pre)
    g_update = g_middle * (candidate - masked_in) * update * (1.0 - update)
    g_reset = g_gated * attended * silu_slope(reset_pre)
    g_projected = jnp.concatenate([g_update, g_shared, g_reset, g_cand], axis=1)
    g_mixed = times_back(g_projected, mix_full)
    g_val = g_values.reshape(rows, value_dim) * silu_slope(value_pre)
    g_from_values = times_back(g_val, value_full)

    def total(packed):
        count = lax.axis_size("seq")
        features = packed.shape[1] // count

        def reduced(whole, tiled=True):
            part = lax.psum_scatter(whole, "seq", scatter_dimension=0, tiled=tiled)
            return lax.psum(part, "batch")

        pairs = (
            (normed, g_val),
            (mixed, g_projected),
            (gated, g_cand),
            (normed_two, g_wide),
            (hidden, g_out),
        )
        grads = tuple(reduced(product_grad(*pair)) for pair in pairs)
        blocks = packed.reshape(-1, count, features).transpose(1, 0, 2)
        return grads + (reduced(blocks, False),)

    return block_out, g_mixed, g_from_values, g_middle * (1.0 - update), gain_sum, affine_sum, total


def to_tiles(value):
    return value.reshape(value.shape[0], -1, 2 * lanes).transpose(1, 0, 2)


def from_tiles(value):
    return value.transpose(1, 0, 2).reshape(value.shape[1], -1)


def to_places(value):
    rows, columns = value.shape
    return value.reshape(rows, 4, 2, columns // 8).transpose(2, 0, 1, 3).reshape(2, rows, -1)


def from_places(value):
    _, rows, columns = value.shape
    return value.reshape(2, rows, 4, columns // 4).transpose(1, 2, 0, 3).reshape(rows, -1)


def plane_layer(
    masked_in, normed, mix_pre, g_out, row_valid, key_valid, affine, gain_two, weights, shared_full
):
    rows, width = masked_in.shape
    sequences = key_valid.shape[0]
    mixed = silu(mix_pre)
    normed_split, mixed_split = split(to_places(normed)), split(to_places(mixed))
    shared_w = shared_full.reshape(lanes, 4, 2, lanes).transpose(0, 2, 1, 3).reshape(lanes, width)
    affine_rows = affine.T
    valid = key_valid.astype(jnp.float32)
    masked, grad_tiles = to_tiles(masked_in), to_tiles(g_out)
    gain_tiles = to_tiles(gain_two)
    (
        w_high, w_low, value_pre, attended, projected, shared_pre, soft, cand_pre, middle, block_out,
        two_h, two_l, gated_h, gated_l, hidden_h, hidden_l, g_wide,
    ) = call_forward(
        weights,
        (*normed_split, *mixed_split, shared_w, affine_rows, valid, row_valid, masked, grad_tiles, gain_tiles),
        rows,
        sequences,
    )
    g_projected, g_val, g_shared, g_mixed, g_normed, g_rest, gain_sum, affine_sum = call_backward(
        w_high, w_low, g_wide, value_pre, attended, projected, shared_pre, soft, cand_pre, middle,
        masked, grad_tiles, gain_tiles, shared_w, affine_rows, valid,
    )

    def total(packed):
        blocks = packed.reshape(-1, 8, lanes).transpose(1, 0, 2)
        used = blocks.shape[1]
        blocks = jnp.pad(blocks, ((0, 0), (0, lanes - used), (0, 0)))
        last = product_grad(mixed, g_shared)
        extra = jnp.concatenate([last.reshape(8, lanes, lanes), blocks], axis=2)
        extra = extra.reshape(4, 2, lanes, -1).transpose(1, 0, 2, 3).reshape(2, 4 * lanes, -1)
        grads, rest = reduce_grads(
            (
                (hidden_h, hidden_l, grad_tiles, 0, 4),
                (two_h[None], two_l[None], g_wide, 0, 16),
                (gated_h, gated_l, g_projected, 12, 4),
                (mixed_split[0][None], mixed_split[1][None], g_projected, 0, 16),
                (normed_split[0][None], normed_split[1][None], g_val, 0, 8),
            ),
            extra,
        )
        narrow, widen, merge, mix, value = grads
        mix = jnp.concatenate([mix[:, :width], rest[:, :lanes], mix[:, width:]], axis=1)
        return value, mix, merge, widen, narrow, rest[:used, lanes:]

    return (
        from_tiles(block_out),
        from_places(g_mixed),
        from_places(g_normed),
        from_tiles(g_rest),
        gain_sum.reshape(width),
        affine_sum,
        total,
    )


def per_device(
    tokens,
    lengths,
    out_grad,
    first_gain,
    smooth_alpha,
    smooth_delta,
    smooth_beta,
    smooth_gamma,
    smooth_omega,
    value_weight,
    mix_weight,
    query_affine,
    merge_weight,
    second_gain,
    widen_weight,
    narrow_weight,
):
    sequences, block_len, width = tokens.shape
    count = lax.axis_size("seq")
    states = smooth_alpha.shape[1]
    own = first_gain.shape[0]
    own_shared = query_affine.shape[0]
    rows = sequences * block_len
    shared_dim = own_shared * count
    plane = count == 8 and lax.axis_size("batch") == 4

    affine_row = jnp.pad(query_affine.reshape(-1), (0, own - 3 * own_shared))
    packed = [
        smooth_alpha.T,
        smooth_delta.T,
        smooth_beta.T,
        smooth_gamma.T,
        jnp.stack([first_gain, smooth_omega, second_gain, affine_row]),
    ]
    if plane:
        packed.append(mix_weight[:, width : width + shared_dim].T)
    small = lax.all_gather(jnp.concatenate(packed, axis=0), "seq").transpose(1, 0, 2)

    tiles = (width // lanes, lanes)
    alpha_rate = jax.nn.sigmoid(small[:states].reshape(states, *tiles))
    damp_rate = jax.nn.sigmoid(small[states : 2 * states].reshape(states, *tiles))
    beta = small[2 * states : 3 * states].reshape(states, *tiles)
    gamma = small[3 * states : 4 * states].reshape(states, *tiles)
    gain_one = small[4 * states].reshape(1, width)
    omega = small[4 * states + 1].reshape(1, width)
    gain_two = small[4 * states + 2].reshape(1, width)
    affine = small[4 * states + 3, :, : 3 * own_shared].reshape(shared_dim, 3)
    out_scale = states ** (-0.5)
    decay = 1.0 - alpha_rate * damp_rate
    block_decay = jnp.exp(block_len * jnp.log1p(-alpha_rate * damp_rate))
    weight = alpha_rate * beta * gamma * out_scale

    offsets = lax.axis_index("seq") * block_len + lax.iota(jnp.int32, block_len)
    valid = (offsets[None, :] < lengths[:, None]).astype(jnp.float32)
    row_valid = valid.reshape(rows, 1)
    key_valid = valid.reshape(sequences, 1, block_len)

    masked_in = tokens.reshape(rows, width) * row_valid
    g_out = out_grad.reshape(rows, width) * row_valid
    hat_one, scale_one = normalise(masked_in)
    normed = hat_one * gain_one
    tiled = (sequences, block_len) + tiles
    ending = (sequences, states) + tiles
    signal = normed.reshape(tiled)
    local, ends = call_kernel(
        functools.partial(filter_body, False), [tiled, ending], decay, weight, signal
    )
    enter = entering(ends, block_decay, False)
    (smoothed,) = call_kernel(
        functools.partial(carried_body, False), [tiled], decay, weight, enter, local
    )
    mix_pre = smoothed.reshape(rows, width) + omega * normed

    weights = (value_weight, mix_weight, merge_weight, widen_weight, narrow_weight)
    operands = (masked_in, normed, mix_pre, g_out, row_valid, key_valid, affine, gain_two, weights)
    if plane:
        results = plane_layer(*operands, small[4 * states + 4 :])
    else:
        results = plain_layer(*operands)
    block_out, g_mixed, g_from_values, g_rest, second_gain_sum, affine_sum, total = results
    g_smooth = g_mixed * silu_slope(mix_pre)

    smooth_tiled = g_smooth.reshape(tiled)
    back_local, back_ends = call_kernel(
        functools.partial(filter_body, True), [tiled, ending], decay, weight, smooth_tiled
    )
    back_enter = entering(back_ends, block_decay, True)
    direct, slope, last = call_kernel(
        moments_body,
        [(states,) + tiles, (states,) + tiles, ending],
        decay,
        enter,
        signal,
        smooth_tiled,
    )
    (back_full,) = call_kernel(
        functools.partial(carried_body, True), [tiled], decay, weight, back_enter, back_local
    )
    slope = slope + decay * jnp.sum(back_enter * last, axis=0)
    decay_grad = weight * slope
    alpha_grad = (beta * gamma * out_scale * direct - damp_rate * decay_grad) * (
        alpha_rate * (1.0 - alpha_rate)
    )
    delta_grad = -alpha_rate * decay_grad * damp_rate * (1.0 - damp_rate)
    beta_grad = alpha_rate * gamma * out_scale * direct
    gamma_grad = alpha_rate * beta * out_scale * direct

    g_normed = g_from_values + g_smooth * omega + back_full.reshape(rows, width)
    tokens_grad = (g_rest + normalise_back(g_normed, gain_one, hat_one, scale_one)) * row_valid
    first_gain_sum = jnp.sum(g_normed * hat_one, axis=0)
    omega_sum = jnp.sum(g_smooth * normed, axis=0)
    affine_rows = jnp.pad(
        affine_sum.T.reshape(count, 3 * own_shared), ((0, 0), (0, own - 3 * own_shared))
    )
    small_rows = [
        alpha_grad.reshape(states, width),
        delta_grad.reshape(states, width),
        beta_grad.reshape(states, width),
        gamma_grad.reshape(states, width),
        jnp.stack([first_gain_sum, omega_sum, second_gain_sum, affine_rows.reshape(width)]),
    ]
    value_grad, mix_grad, merge_grad, widen_grad, narrow_grad, small_grad = total(
        jnp.concatenate(small_rows, axis=0)
    )

    return (
        block_out.reshape(tokens.shape),
        tokens_grad.reshape(tokens.shape),
        small_grad[4 * states],
        small_grad[:states].T,
        small_grad[states : 2 * states].T,
        small_grad[2 * states : 3 * states].T,
        small_grad[3 * states : 4 * states].T,
        small_grad[4 * states + 1],
        value_grad,
        mix_grad,
        small_grad[4 * states + 3, : 3 * own_shared].reshape(own_shared, 3),
        merge_grad,
        small_grad[4 * states + 2],
        widen_grad,
        narrow_grad,
    )


def solution(mesh):
    rows = P("batch", "seq", None)
    split = P("seq", None)
    in_specs = (
        (rows, P("batch"), rows, P("seq"))
        + (split,) * 4
        + (P("seq"),)
        + (split,) * 4
        + (P("seq"),)
        + (split,) * 2
    )
    out_specs = (
        (rows, rows, P("seq"))
        + (split,) * 4
        + (P("seq"),)
        + (split,) * 4
        + (P("seq"),)
        + (split,) * 2
    )
    return jax.shard_map(
        per_device, mesh=mesh, in_specs=in_specs, out_specs=out_specs, check_vma=False
    )
```

```python
import functools

import jax
import jax.numpy as jnp
from jax import lax
from jax.experimental import pallas as pl
from jax.experimental.pallas import tpu as pltpu
from jax.sharding import PartitionSpec as P

exact = lax.Precision.HIGHEST
triple = lax.Precision.HIGH
norm_eps = 1e-05
masked_score = -1000000000.0
lanes = 128


def gather_rows(shard):
    return lax.all_gather(shard, "seq", axis=0, tiled=True)


def product_grad(left, right):
    return lax.dot_general(left, right, (((0,), (0,)), ((), ())), precision=triple)


def halves(value):
    high = value.astype(jnp.bfloat16)
    return high, (value - high.astype(jnp.float32)).astype(jnp.bfloat16)


def contract(left, right, left_dim, right_dim, precision=None):
    return lax.dot_general(
        left, right, (((left_dim,), (right_dim,)), ((), ())),
        precision=precision, preferred_element_type=jnp.float32,
    )


def turned(left, right):
    return contract(left, right, 0, 0)


def three(left, right, left_dim, right_dim):
    (high, low), (other, rest) = left, right
    return contract(high, other, left_dim, right_dim) + (
        contract(low, other, left_dim, right_dim) + contract(high, rest, left_dim, right_dim)
    )


def place_of(device):
    return (device % 2) * 4 + device // 2


def tree_sum(terms):
    while len(terms) > 1:
        terms = [a + b for a, b in zip(terms[::2], terms[1::2])] + (
            [terms[-1]] if len(terms) % 2 else []
        )
    return terms[0]


def run_filter(reverse, s, decay_ref, weight_ref, signal_ref, out_ref, end_ref):
    length, states = signal_ref.shape[1], decay_ref.shape[0]

    def step(t, held):
        at = length - 1 - t if reverse else t
        entry = signal_ref[s, at]
        held = tuple(decay_ref[n] * held[n] + entry for n in range(states))
        out_ref[s, at] = tree_sum([weight_ref[n] * held[n] for n in range(states)])
        return held

    zero = jnp.zeros(signal_ref.shape[2:], jnp.float32)
    held = lax.fori_loop(0, length, step, (zero,) * states, unroll=4)
    for n in range(states):
        end_ref[s, n] = held[n]


def run_carried(reverse, s, decay_ref, weight_ref, enter_ref, local_ref, out_ref):
    length, states = local_ref.shape[1], decay_ref.shape[0]

    def step(t, held):
        at = length - 1 - t if reverse else t
        held = tuple(decay_ref[n] * held[n] for n in range(states))
        out_ref[s, at] = local_ref[s, at] + tree_sum(list(held))
        return held

    start = tuple(weight_ref[n] * enter_ref[s, n] for n in range(states))
    lax.fori_loop(0, length, step, start, unroll=4)


def run_moments(s, low, high, decay_ref, enter_ref, signal_ref, grad_ref, direct_ref, slope_ref, last_ref):
    length, span = signal_ref.shape[1], range(low, high)
    zero = jnp.zeros(signal_ref.shape[2:], jnp.float32)

    def step(t, carry):
        held, slope, direct, sloped = carry
        entry, grad = signal_ref[s, t], grad_ref[s, t]
        slope = tuple(decay_ref[n] * d + h for n, d, h in zip(span, slope, held))
        held = tuple(decay_ref[n] * h + entry for n, h in zip(span, held))
        direct = tuple(q + grad * h for q, h in zip(direct, held))
        sloped = tuple(q + grad * d for q, d in zip(sloped, slope))
        return held, slope, direct, sloped

    zeros = (zero,) * len(span)
    if s:
        sums = (tuple(direct_ref[n] for n in span), tuple(slope_ref[n] for n in span))
    else:
        sums = (zeros, zeros)
    start = (tuple(enter_ref[s, n] for n in span), zeros) + sums
    _, slope, direct, sloped = lax.fori_loop(0, length, step, start, unroll=2)
    for k, n in enumerate(span):
        last_ref[s, n], direct_ref[n], slope_ref[n] = slope[k], direct[k], sloped[k]


def filter_body(reverse, decay_ref, weight_ref, signal_ref, out_ref, end_ref):
    for s in range(signal_ref.shape[0]):
        run_filter(reverse, s, decay_ref, weight_ref, signal_ref, out_ref, end_ref)


def carried_body(reverse, decay_ref, weight_ref, enter_ref, local_ref, out_ref):
    for s in range(local_ref.shape[0]):
        run_carried(reverse, s, decay_ref, weight_ref, enter_ref, local_ref, out_ref)


def moments_body(decay_ref, enter_ref, signal_ref, grad_ref, *outs):
    states = decay_ref.shape[0]
    for low in range(0, states, 8):
        for s in range(signal_ref.shape[0]):
            run_moments(s, low, min(low + 8, states), decay_ref, enter_ref, signal_ref, grad_ref, *outs)


def run_entering(reverse, s, block_ref, ends_ref, me, enter_ref):
    count = ends_ref.shape[0]
    mine = count - 1 - me if reverse else me

    def one(n, carry):
        total = jnp.zeros(block_ref.shape[1:], jnp.float32)
        for position in range(count - 1):
            piece = ends_ref[count - 1 - position if reverse else position, s, n]
            total = jnp.where(position < mine, block_ref[n] * total + piece, total)
        enter_ref[s, n] = total
        return carry

    lax.fori_loop(0, block_ref.shape[0], one, 0)


def on_other(**coordinate):
    return dict(device_id=coordinate, device_id_type=pl.DeviceIdType.MESH)


def chunk_table(shapes):
    firsts, chunk = [], 0
    for blocks, wide in shapes:
        firsts.append(chunk)
        chunk += blocks * wide
    return firsts, chunk


def to_peers(source, target, sent, came):
    me = lax.axis_index("seq")
    for k in range(1, 8):
        yield pltpu.make_async_remote_copy(
            src_ref=source, dst_ref=target, send_sem=sent.at[k - 1], recv_sem=came.at[k - 1],
            **on_other(seq=(me // 4 + k // 4) % 2 * 4 + (me // 2 + k // 2) % 2 * 2 + (me + k) % 2),
        )


gather_shapes = ((1, 8), (1, 16), (2, 4), (1, 16), (4, 4))


def forward_body(
    value_ref, mix_ref, merge_ref, widen_ref, narrow_ref, packed, tokens, out_grad, row_valid, key_valid,
    w_high, w_low, value_pre, attended, projected, shared_pre, soft, cand_pre, middle, block_out,
    two_h, two_l, gated_h, gated_l, hidden_h, hidden_l, g_wide,
    normed_h, normed_l, mixed_h, mixed_l, masked, g_out, signal, enter, mix_pre, small, shared_w,
    buf, stage_h, stage_l, g_hidden, smoothed, ends, tables, loaded, sent, came, stored, near, sent_all, came_all,
):
    weights = (value_ref, mix_ref, merge_ref, widen_ref, narrow_ref)
    firsts, chunks = chunk_table(gather_shapes)
    depth, delay = buf.shape[0], 2
    width = buf.shape[-1]
    half = lanes * 4
    me, level = lax.axis_index("seq"), lax.axis_index("batch")
    core, along_x, along_y = me % 2, (me // 2) % 2, me // 4
    id_sibling = me + 1 - 2 * core
    id_x, id_y = me + 2 - 4 * along_x, me + 4 - 8 * along_y
    id_corner = id_x + 4 - 8 * along_y
    mine, at_x, at_y, at_corner = (place_of(device) for device in (me, id_x, id_y, id_corner))
    above, below = (level + 1) % 4, (level + 3) % 4
    quarter, eighth = lanes // 4, lanes // 8

    barrier = pltpu.get_barrier_semaphore()
    for other in range(1, 8):
        pl.semaphore_signal(barrier, inc=1, **on_other(seq=(me + other) % 8))
    for target in (above, below):
        pl.semaphore_signal(barrier, inc=1, **on_other(batch=target))
    pl.semaphore_wait(barrier, 9)

    def link(kind, chunk):
        slot = chunk % depth

        def rows(place, start, count):
            return buf.at[slot, place, pl.ds(pl.multiple_of(start, 8), count)]

        piece, target = (
            lambda: (buf.at[slot, mine], {"seq": id_x}),
            lambda: (buf.at[slot, mine], {"seq": id_y}),
            lambda: (buf.at[slot, mine], {"seq": id_sibling}),
            lambda: (rows(at_x, level * quarter, eighth), {"seq": id_y}),
            lambda: (rows(at_y, level * quarter + eighth, eighth), {"seq": id_x}),
            lambda: (buf.at[slot, at_x], {"seq": id_sibling}),
            lambda: (buf.at[slot, at_y], {"seq": id_sibling}),
            lambda: (rows(at_corner, level * quarter, quarter), {"batch": above}),
            lambda: (rows(at_corner, ((level + 3) % 4) * quarter, quarter), {"batch": above}),
            lambda: (rows(at_corner, ((level + 2) % 4) * quarter, quarter), {"batch": above}),
            lambda: (buf.at[slot, at_corner], {"seq": id_sibling}),
        )[kind]()
        return pltpu.make_async_remote_copy(
            src_ref=piece, dst_ref=piece, send_sem=sent.at[kind, slot], recv_sem=came.at[kind, slot],
            **on_other(**target),
        )

    def load(chunk):
        slot = chunk % depth
        for number, ((blocks, wide), first, weight) in enumerate(
            zip(gather_shapes, firsts, weights)
        ):

            @pl.when((chunk >= first) & (chunk < first + blocks * wide))
            def _(number=number, first=first, wide=wide, weight=weight):
                row = ((chunk - first) // wide) * lanes
                column = ((chunk - first) % wide) * width
                if number == 1:
                    column = column + jnp.where(column >= weights[2].shape[1], lanes, 0)
                source = weight.at[
                    pl.ds(pl.multiple_of(row, lanes), lanes),
                    pl.ds(pl.multiple_of(column, lanes), width),
                ]
                pltpu.make_async_copy(source, buf.at[slot, mine], loaded.at[slot]).start()

    def exchange(done, begun):
        def phase(chunk):
            for kind in done:
                link(kind, chunk).wait()
            for kind in begun:
                link(kind, chunk).start()

        return phase

    def send(chunk):
        slot = chunk % depth
        first = value_ref.at[pl.ds(0, lanes), pl.ds(0, width)]
        pltpu.make_async_copy(first, buf.at[slot, mine], loaded.at[slot]).wait()
        for kind in (0, 1, 2):
            link(kind, chunk).start()

    def store(chunk, kind):
        return pltpu.make_async_copy(
            (stage_h, stage_l)[kind].at[chunk % 2],
            (w_high, w_low)[kind].at[chunk],
            stored.at[kind, chunk % 2],
        )

    def product(left_h, left_l, right):
        return three((left_h[0], left_l[0]), (right[0][0], right[1][0]), 1, 0) + three(
            (left_h[1], left_l[1]), (right[0][1], right[1][1]), 1, 0
        )

    sequences, block_len = soft.shape[:2]
    states = tables.shape[1]
    decay, weight, block_decay = (tables.at[kind] for kind in range(3))
    features = tokens.shape[1]
    tiles = features // width

    def share(kind):
        if kind == 0:
            source = target = small.at[me]
        elif kind == 1:
            source = mix_ref.at[:, pl.ds(features, lanes)]
            target = shared_w.at[mine]
        else:
            source = target = ends.at[me]
        return list(to_peers(source, target, sent_all.at[kind], came_all.at[kind]))

    def own_shared():
        return pltpu.make_async_copy(mix_ref.at[:, pl.ds(features, lanes)], shared_w.at[mine], near)

    def row_of(number, k):
        return jnp.concatenate(
            [small[2 * k, number : number + 1], small[2 * k + 1, number : number + 1]], axis=1
        )

    def hand_out():
        small[me] = packed[...]
        for kind in (0, 1):
            for item in share(kind):
                item.start()
        own_shared().start()

    def norm_one():
        for kind in (0, 1):
            for item in share(kind):
                item.wait()
        own_shared().wait()
        for kind in range(3):
            for n in range(states):
                tables[kind, n] = small[:, kind * states + n]
        keep = row_valid[...]
        value = tokens[...] * keep
        centre = jnp.mean(value, axis=1, keepdims=True)
        shifted = value - centre
        scale = lax.rsqrt(jnp.mean(shifted * shifted, axis=1, keepdims=True) + norm_eps)
        gain = jnp.concatenate([row_of(3 * states, k) for k in range(tiles)], axis=1)
        normed = shifted * scale * gain
        for k in range(tiles):
            span = slice(k * width, (k + 1) * width)
            masked[k] = value[:, span]
            g_out[k] = out_grad[:, span] * keep
            for parity in range(2):
                start = k * width + parity * lanes
                put(normed_h, normed_l, (parity,), k * lanes, normed[:, start : start + lanes])
        for s in range(sequences):
            rows = normed[s * block_len : (s + 1) * block_len]
            signal[s] = rows.reshape(signal.shape[1:])

    def filter_one(s):
        run_filter(False, s, decay, weight, signal, smoothed, ends.at[me])
        if s == sequences - 1:
            for item in share(2):
                item.start()

    def carry_one(s):
        if s == 0:
            for item in share(2):
                item.wait()
        run_entering(False, s, block_decay, ends, me, enter)
        run_carried(False, s, decay, weight, enter, smoothed, smoothed)

    def mix_in():
        for s in range(sequences):
            span = slice(s * block_len, (s + 1) * block_len)
            skip = jnp.concatenate([row_of(3 * states + 1, k) for k in range(tiles)], axis=1)
            normed = signal[s].reshape(block_len, features)
            value = smoothed[s].reshape(block_len, features) + skip * normed
            mixed = value * jax.nn.sigmoid(value)
            for block in range(8):
                cut = slice(block * lanes, (block + 1) * lanes)
                to = (block % 2, span, slice(block // 2 * lanes, (block // 2 + 1) * lanes))
                mix_pre[to] = value[:, cut]
                mixed_h[to], mixed_l[to] = halves(mixed[:, cut])

    def attention():
        shared_full = halves(shared_w[...].reshape(2, half, lanes))
        total = product(mixed_h, mixed_l, shared_full)
        affine = tree_sum([small[k, 3 * states + 3 : 3 * states + 6] for k in range(8)])
        shared_pre[...] = total
        shared = total * jax.nn.sigmoid(total)
        queries = shared * affine[0:1] + affine[2:3]
        keys = shared * affine[1:2]
        for s in range(sequences):
            span = slice(s * block_len, (s + 1) * block_len)
            scores = contract(queries[span], keys[span], 1, 1, exact) * shared.shape[1] ** (-0.5)
            scores = jnp.where(key_valid[s] > 0.5, scores, masked_score)
            weight = jnp.exp(scores - jnp.max(scores, axis=1, keepdims=True))
            soft[s] = weight / jnp.sum(weight, axis=1, keepdims=True)

    def put(target_h, target_l, index, column, value):
        high, low = halves(value)
        target_h[(*index, slice(None), pl.ds(pl.multiple_of(column, lanes), lanes))] = high
        target_l[(*index, slice(None), pl.ds(pl.multiple_of(column, lanes), lanes))] = low

    def complete(chunk):
        slot = chunk % depth
        link(10, chunk).wait()

        @pl.when(chunk >= 2)
        def _():
            store(chunk - 2, 0).wait()
            store(chunk - 2, 1).wait()

        right = halves(buf[slot].reshape(2, half, width))
        stage_h[chunk % 2] = right[0]
        stage_l[chunk % 2] = right[1]
        store(chunk, 0).start()
        store(chunk, 1).start()

        def among(number):
            blocks, wide = gather_shapes[number]
            return (chunk >= firsts[number]) & (chunk < firsts[number] + blocks * wide)

        @pl.when(among(0))
        def _():
            total = product(normed_h, normed_l, right)
            value_pre[chunk] = total
            values = total * jax.nn.sigmoid(total)
            for s in range(sequences):
                span = slice(s * block_len, (s + 1) * block_len)
                attended[chunk, span] = contract(soft[s], values[span], 1, 0, exact)

        @pl.when(among(1))
        def _():
            tile = chunk - firsts[1]
            total = product(mixed_h, mixed_l, right)
            projected[tile] = total

            @pl.when((tile >= 4) & (tile < 12))
            def _():
                block = tile - 4
                gated = attended[block] * total * jax.nn.sigmoid(total)
                for j in range(2):
                    cut = gated[:, j * lanes : (j + 1) * lanes]
                    put(gated_h, gated_l, (j, block % 2), (block // 2) * lanes, cut)

        @pl.when(among(2))
        def _():
            j, tile = (chunk - firsts[2]) // 4, (chunk - firsts[2]) % 4
            total = product(gated_h.at[j], gated_l.at[j], right)

            @pl.when(j == 0)
            def _():
                cand_pre[tile] = projected[12 + tile] + total

            @pl.when(j == 1)
            def _():
                cand_pre[tile] = cand_pre[tile] + total

            @pl.when(chunk == firsts[3] - 1)
            def _():
                total = 0.0
                for k in range(tiles):
                    cand = cand_pre[k]
                    cand = cand * jax.nn.sigmoid(cand)
                    value = masked[k] + jax.nn.sigmoid(projected[k]) * (cand - masked[k])
                    middle[k] = value
                    total = total + jnp.sum(value, axis=1, keepdims=True)
                centre = total / features
                total = 0.0
                for k in range(tiles):
                    shifted = middle[k] - centre
                    total = total + jnp.sum(shifted * shifted, axis=1, keepdims=True)
                scale = lax.rsqrt(total / features + norm_eps)
                for k in range(tiles):
                    value = (middle[k] - centre) * scale * row_of(3 * states + 2, k)
                    for parity in range(2):
                        cut = value[:, parity * lanes : (parity + 1) * lanes]
                        put(two_h, two_l, (parity,), k * lanes, cut)
                block_out[...] = jnp.zeros(block_out.shape, jnp.float32)
                g_hidden[...] = jnp.zeros(g_hidden.shape, jnp.float32)

        @pl.when(among(3))
        def _():
            tile = chunk - firsts[3]
            total = product(two_h, two_l, right)
            g_wide[tile] = total
            hidden = total * jax.nn.sigmoid(total)
            for i in range(2):
                cut = hidden[:, i * lanes : (i + 1) * lanes]
                index = (2 * (tile % 2) + i, (tile // 2) % 2)
                put(hidden_h, hidden_l, index, (tile // 4) * lanes, cut)

        @pl.when(among(4))
        def _():
            j, tile = (chunk - firsts[4]) // 4, (chunk - firsts[4]) % 4
            to = (slice(None), pl.ds(pl.multiple_of(tile * width, width), width))
            block_out[to] = block_out[to] + product(hidden_h.at[j], hidden_l.at[j], right)
            grad = halves(g_out[tile])
            for parity in range(2):
                back = three(grad, (right[0][parity], right[1][parity]), 1, 1)
                g_hidden[j, parity] = g_hidden[j, parity] + back

    phases = (
        (0, load),
        (1, send),
        (1 + delay, exchange((0, 1, 2), (3, 4, 5, 6))),
        (1 + 2 * delay, exchange((3, 4, 5, 6), (7,))),
        (1 + 3 * delay, exchange((7,), (8,))),
        (1 + 4 * delay, exchange((8,), (9,))),
        (1 + 5 * delay, exchange((9,), (10,))),
        (1 + 6 * delay, complete),
    )

    def step(at, carry):
        for after, phase in phases[-2:0:-1]:

            @pl.when((at >= after) & (at < after + chunks))
            def _(after=after, phase=phase):
                phase(at - after)

        pl.when(at < chunks)(lambda: load(at))
        pl.when(at == 0)(hand_out)
        pl.when(at == 1)(norm_one)
        for s in range(sequences):
            pl.when(at == 2 + s)(functools.partial(filter_one, s))
            pl.when(at == 5 + s)(functools.partial(carry_one, s))
        pl.when(at == 8)(mix_in)
        pl.when(at == 9)(attention)

        @pl.when(at >= phases[-1][0])
        def _():
            complete(at - phases[-1][0])

        return carry

    lax.fori_loop(0, chunks + phases[-1][0], step, 0)
    for chunk in (chunks - 2, chunks - 1):
        for kind in range(2):
            store(chunk, kind).wait()
    for k in range(tiles):
        span = slice(k * width, (k + 1) * width)
        block_out[:, span] = (middle[k] + block_out[:, span]) * row_valid[...]
    for k in range(g_wide.shape[0]):
        for i in range(2):
            span = slice(i * lanes, (i + 1) * lanes)
            back = g_hidden[2 * (k % 2) + i, (k // 2) % 2, :, (k // 4) * lanes : (k // 4 + 1) * lanes]
            wide = g_wide[k, :, span]
            g_wide[k, :, span] = back * silu_slope(wide)


def f32(*shape):
    return jax.ShapeDtypeStruct(shape, jnp.float32)


def b16(*shape):
    return jax.ShapeDtypeStruct(shape, jnp.bfloat16)


def call_forward(weights, packed, tokens, out_grad, row_valid, key_valid, states):
    width, half = 2 * lanes, 4 * lanes
    rows, features = tokens.shape
    sequences = key_valid.shape[0]
    block_len = rows // sequences
    _, chunks = chunk_table(gather_shapes)
    vmem, anywhere = pl.BlockSpec(memory_space=pltpu.VMEM), pl.BlockSpec(memory_space=pl.ANY)
    line = (sequences, block_len, 8, lanes)
    shapes = [b16(chunks, 2, half, width)] * 2 + [
        f32(8, rows, width), f32(8, rows, width), f32(16, rows, width), f32(rows, lanes),
        f32(sequences, block_len, block_len), f32(4, rows, width), f32(4, rows, width), f32(rows, features),
        b16(2, rows, half), b16(2, rows, half), b16(2, 2, rows, half), b16(2, 2, rows, half),
        b16(4, 2, rows, half), b16(4, 2, rows, half), f32(16, rows, width),
        b16(2, rows, half), b16(2, rows, half), b16(2, rows, half), b16(2, rows, half),
        f32(4, rows, width), f32(4, rows, width), f32(*line), f32(sequences, states, 8, lanes),
        f32(2, rows, half), f32(8, *packed.shape), f32(8, lanes, lanes),
    ]
    depth = 16
    return pl.pallas_call(
        forward_body,
        out_shape=shapes,
        in_specs=[anywhere] * len(weights) + [vmem] * 5,
        out_specs=[anywhere] * 2 + [vmem] * (len(shapes) - 2),
        scratch_shapes=[
            pltpu.VMEM((depth, 8, lanes, width), jnp.float32),
            pltpu.VMEM((2, 2, half, width), jnp.bfloat16),
            pltpu.VMEM((2, 2, half, width), jnp.bfloat16),
            pltpu.VMEM((4, 2, rows, half), jnp.float32),
            pltpu.VMEM(line, jnp.float32),
            pltpu.VMEM((8, sequences, states, 8, lanes), jnp.float32),
            pltpu.VMEM((3, states, 8, lanes), jnp.float32),
            pltpu.SemaphoreType.DMA((depth,)),
            pltpu.SemaphoreType.DMA((11, depth)),
            pltpu.SemaphoreType.DMA((11, depth)),
            pltpu.SemaphoreType.DMA((2, 2)),
            pltpu.SemaphoreType.DMA,
            pltpu.SemaphoreType.DMA((3, 7)),
            pltpu.SemaphoreType.DMA((3, 7)),
        ],
        compiler_params=pltpu.CompilerParams(
            collective_id=2, has_side_effects=True, vmem_limit_bytes=62 * 1024 * 1024
        ),
    )(*weights, packed, tokens, out_grad, row_valid, key_valid)


reduce_shapes = ((4, 4), (1, 16), (2, 4), (1, 16), (1, 8))


def backward_body(
    w_high, w_low, value_src, projected_src, middle_src, g_wide, attended, shared_pre, soft, cand_pre,
    two_h, two_l, gated_h, gated_l, hidden_h, hidden_l, normed_h, normed_l, mixed_h, mixed_l,
    masked, g_out, signal, enter, mix_pre, small, shared_w, row_valid, key_valid,
    tokens_grad, narrow_grad, widen_grad, merge_grad, mix_grad, value_grad, small_grad,
    away, keep, got, got_x, got_y, got_xy, got_yx, part, from_edge, from_inner, done,
    value_pre, projected, middle, buf_h, buf_l, g_two, g_gated, g_mixed, g_normed, g_soft, g_shared,
    smooth, back, ends, back_enter, tables, direct, slope, last, small_sum,
    fetched, read, sent, came, written, sent_all, came_all,
):
    lefts = (
        (hidden_h, hidden_l), (two_h, two_l), (gated_h, gated_l), (mixed_h, mixed_l), (normed_h, normed_l)
    )
    rights = ((g_out, 0), (g_wide, 0), (projected, 12), (projected, 0), (value_pre, 0))
    grads = (narrow_grad, widen_grad, merge_grad, mix_grad, value_grad)
    firsts, chunks = chunk_table(reduce_shapes)
    gathered, _ = chunk_table(gather_shapes)
    delay = 2
    tiles, rows, width = masked.shape
    half, features = 4 * lanes, tiles * width
    sequences, block_len = soft.shape[:2]
    states = tables.shape[1]
    decay, weight, block_decay = (tables.at[kind] for kind in range(3))
    me, level = lax.axis_index("seq"), lax.axis_index("batch")
    core, along_x, along_y = me % 2, (me // 2) % 2, me // 4
    is_edge = (level == 0) | (level == 3)
    partner = jnp.where(level < 2, 1 - level, 5 - level)
    sibling, across_x, across_y = (
        {"seq": me + bit * (1 - 2 * own)} for bit, own in ((1, core), (2, along_x), (4, along_y))
    )

    copies_in = [
        pltpu.make_async_copy(source, target, read.at[number])
        for number, (source, target) in enumerate(
            ((middle_src, middle), (projected_src, projected), (value_src, value_pre))
        )
    ]
    for item in copies_in:
        item.start()

    barrier = pltpu.get_barrier_semaphore()
    for other in range(1, 8):
        pl.semaphore_signal(barrier, inc=1, **on_other(seq=(me + other) % 8))
    pl.semaphore_signal(barrier, inc=1, **on_other(batch=partner))

    @pl.when(jnp.logical_not(is_edge))
    def _():
        pl.semaphore_signal(barrier, inc=1, **on_other(batch=3 - level))
        pl.semaphore_wait(barrier, 9)

    @pl.when(is_edge)
    def _():
        pl.semaphore_wait(barrier, 8)

    def slot_in(ref, chunk):
        return chunk % ref.shape[0]

    def link(kind, chunk):
        def at(ref, *index):
            return ref.at[(slot_in(ref, chunk), *index)]

        source, target, device = (
            lambda: (at(away), at(got), sibling),
            lambda: (at(keep, slice(None), 1 - along_x, 0), at(got_x), across_x),
            lambda: (at(keep, 1 - along_y, slice(None), 1), at(got_y), across_y),
            lambda: (at(got_x, 1 - along_y), at(got_xy), across_y),
            lambda: (at(got_y, 1 - along_x), at(got_yx), across_x),
            lambda: (at(part), at(from_edge), {"batch": partner}),
            lambda: (at(part), at(from_inner), {"batch": 3 - level}),
        )[kind]()
        slot = chunk % sent.shape[1]
        return pltpu.make_async_remote_copy(
            src_ref=source, dst_ref=target, send_sem=sent.at[kind, slot], recv_sem=came.at[kind, slot],
            **on_other(**device),
        )

    def results(chunk, call):
        slot, at = slot_in(done, chunk), chunk % sent.shape[1]

        def pieces(number, source, target):
            yield lambda: pltpu.make_async_copy(source, target, written.at[number, at])
            yield lambda: pltpu.make_async_remote_copy(
                src_ref=source, dst_ref=target,
                send_sem=sent.at[7 + number, at], recv_sem=came.at[7 + number, at],
                **on_other(batch=partner),
            )

        for number, ((blocks, wide), first, grad) in enumerate(zip(reduce_shapes, firsts, grads)):

            @pl.when((chunk >= first) & (chunk < first + blocks * wide))
            def _(number=number, first=first, wide=wide, grad=grad):
                row = ((chunk - first) // wide) * lanes
                column = ((chunk - first) % wide) * width
                if number == 3:
                    column = column + jnp.where(column >= features, lanes, 0)
                target = grad.at[
                    pl.ds(pl.multiple_of(row, lanes), lanes),
                    pl.ds(pl.multiple_of(column, lanes), width),
                ]
                call(*pieces(0, done.at[slot], target))

        @pl.when(chunk == chunks)
        def _():
            target = mix_grad.at[:, pl.ds(features, lanes)]
            call(*pieces(0, done.at[slot, :, pl.ds(0, lanes)], target))
            call(*pieces(1, done.at[slot, :, pl.ds(lanes, lanes)], small_grad))

    def begin(chunk):
        slot, to = slot_in(away, chunk), slot_in(keep, chunk)
        for (blocks, wide), first, (high, low), (right, shift) in zip(
            reduce_shapes, firsts, lefts, rights
        ):

            @pl.when((chunk >= first) & (chunk < first + blocks * wide))
            def _(first=first, wide=wide, shift=shift, high=high, low=low, right=right):
                block = (chunk - first) // wide
                other, rest = halves(right[shift + (chunk - first) % wide])

                def product(parity):
                    top, under = (
                        (high[block, parity], low[block, parity])
                        if len(high.shape) == 4
                        else (high[parity], low[parity])
                    )
                    total = turned(top, other) + (turned(under, other) + turned(top, rest))
                    return total.reshape(away.shape[1:])

                away[slot] = product(1 - core)
                link(0, chunk).start()
                keep[to] = product(core)

        @pl.when(chunk == chunks)
        def _():
            right = halves(g_shared[...])

            def fill(ref, at, parity):
                total = three((mixed_h[parity], mixed_l[parity]), right, 0, 0)
                total = total.reshape(*away.shape[1:-1], lanes)
                sums = [small_sum[2 * q + parity].reshape(2, -1, lanes) for q in range(4)]
                sums = jnp.stack(sums, axis=0).reshape(total.shape)
                ref[at] = jnp.concatenate([total, sums], axis=-1)

            fill(away, slot, 1 - core)
            link(0, chunk).start()
            fill(keep, to, core)

    def with_sibling(chunk):
        slot = slot_in(keep, chunk)
        link(0, chunk).wait()
        keep[slot] = keep[slot] + got[slot_in(got, chunk)]
        link(1, chunk).start()
        link(2, chunk).start()

    def with_neighbour(chunk):
        slot = slot_in(got_x, chunk)
        link(1, chunk).wait()
        link(2, chunk).wait()
        from_slot = slot_in(keep, chunk)
        got_x[slot] = got_x[slot] + keep[from_slot, :, along_x, 0]
        got_y[slot] = got_y[slot] + keep[from_slot, along_y, :, 1]
        link(3, chunk).start()
        link(4, chunk).start()

    def with_corner(chunk):
        slot = slot_in(part, chunk)
        link(3, chunk).wait()
        link(4, chunk).wait()
        part[slot, 0] = got_x[slot, along_y] + got_xy[slot]
        part[slot, 1] = got_y[slot, along_x] + got_yx[slot]
        pl.when(is_edge)(lambda: link(5, chunk).start())

    def inner_sum(chunk):
        slot = slot_in(part, chunk)
        pl.when(is_edge)(lambda: link(5, chunk).wait_send())

        @pl.when(jnp.logical_not(is_edge))
        def _():
            link(5, chunk).wait_recv()
            part[slot] = part[slot] + from_edge[slot]
            link(6, chunk).start()

    def total_sum(chunk):
        slot = slot_in(part, chunk)

        @pl.when(jnp.logical_not(is_edge))
        def _():
            link(6, chunk).wait()
            done[slot] = (part[slot] + from_inner[slot]).reshape(done.shape[1:])

            def start(stay, go):
                stay().start()
                go().start()

            results(chunk, start)

    def finish(chunk):
        def receive(stay, go):
            go().wait_recv()

        def release(stay, go):
            stay().wait()
            go().wait_send()

        pl.when(is_edge)(lambda: results(chunk, receive))
        pl.when(jnp.logical_not(is_edge))(lambda: results(chunk, release))

    steps = 48

    def fetch(step, call):
        chunk = jnp.where(
            step < 16, gathered[3] + step, jnp.where(step < 24, step + 8, jnp.where(step < 40, step - 16, step - 40))
        )
        slot = slot_in(buf_h, step)
        for kind, (source, target) in enumerate(((w_high, buf_h), (w_low, buf_l))):
            item = pltpu.make_async_copy(source.at[chunk], target.at[slot], fetched.at[kind, slot])
            getattr(item, call)()

    def back_product(grad, step, parity):
        slot = slot_in(buf_h, step)
        return three(halves(grad), (buf_h[slot, parity], buf_l[slot, parity]), 1, 1)

    def row_of(number, k):
        return jnp.concatenate(
            [small[2 * k, number : number + 1], small[2 * k + 1, number : number + 1]], axis=1
        )

    def put_row(number, k, value):
        for i in range(2):
            small_sum[2 * k + i, number : number + 1] = value[:, i * lanes : (i + 1) * lanes]

    def statistics(ref):
        total = 0.0
        for k in range(tiles):
            total = total + jnp.sum(ref[k], axis=1, keepdims=True)
        centre = total / features
        total = 0.0
        for k in range(tiles):
            shifted = ref[k] - centre
            total = total + jnp.sum(shifted * shifted, axis=1, keepdims=True)
        return centre, lax.rsqrt(total / features + norm_eps)

    def norm_two_back():
        for item in copies_in:
            item.wait()
        centre, scale = statistics(middle)

        def grad_of(k):
            span = slice(k * lanes, (k + 1) * lanes)
            return jnp.concatenate([g_two[0, :, span], g_two[1, :, span]], axis=1)

        plain, crossed = 0.0, 0.0
        for k in range(tiles):
            grad, hat = grad_of(k), (middle[k] - centre) * scale
            put_row(2 * states + 2, k, jnp.sum(grad * hat, axis=0, keepdims=True))
            inner = grad * row_of(3 * states + 2, k)
            plain = plain + jnp.sum(inner, axis=1, keepdims=True)
            crossed = crossed + jnp.sum(inner * hat, axis=1, keepdims=True)
        plain, crossed = plain / features, crossed / features
        for k in range(tiles):
            inner, hat = grad_of(k) * row_of(3 * states + 2, k), (middle[k] - centre) * scale
            g_middle = g_out[k] + (inner - plain - hat * crossed) * scale
            update = jax.nn.sigmoid(projected[k])
            pre = cand_pre[k]
            gate = jax.nn.sigmoid(pre)
            middle[k] = g_middle * (1.0 - update)
            projected[k] = g_middle * (pre * gate - masked[k]) * update * (1.0 - update)
            projected[12 + k] = g_middle * update * (gate * (1.0 + pre * (1.0 - gate)))

    def attention_back(m):
        parity, start = m % 2, pl.multiple_of((m // 2) * lanes, lanes)
        grad = jnp.concatenate(
            [g_gated[0, parity, :, pl.ds(start, lanes)], g_gated[1, parity, :, pl.ds(start, lanes)]], axis=1
        )
        pre = projected[4 + m]
        gate = jax.nn.sigmoid(pre)
        g_attended = grad * pre * gate
        projected[4 + m] = grad * attended[m] * (gate * (1.0 + pre * (1.0 - gate)))
        pre = value_pre[m]
        gate = jax.nn.sigmoid(pre)
        values, bend = pre * gate, gate * (1.0 + pre * (1.0 - gate))
        g_values = []
        for s in range(sequences):
            span = slice(s * block_len, (s + 1) * block_len)
            own = halves(g_attended[span])
            g_soft[s] = g_soft[s] + three(own, halves(values[span]), 1, 1)
            g_values.append(three(halves(soft[s]), own, 0, 0) * bend[span])
        value_pre[m] = jnp.concatenate(g_values, axis=0)

    def scores_back():
        affine = tree_sum([small[k, 3 * states + 3 : 3 * states + 6] for k in range(8)])
        pre = shared_pre[...]
        gate = jax.nn.sigmoid(pre)
        shared, bend = pre * gate, gate * (1.0 + pre * (1.0 - gate))
        score_scale = shared.shape[1] ** (-0.5)
        queries = shared * affine[0:1] + affine[2:3]
        keys = shared * affine[1:2]
        sums = [0.0, 0.0, 0.0]
        for s in range(sequences):
            span = slice(s * block_len, (s + 1) * block_len)
            soft_weight, grad = soft[s], g_soft[s]
            g_scores = soft_weight * (grad - jnp.sum(grad * soft_weight, axis=1, keepdims=True))
            g_scores = jnp.where(key_valid[s] > 0.5, g_scores, 0.0) * score_scale
            g_queries = contract(g_scores, keys[span], 1, 0, exact)
            g_keys = contract(g_scores, queries[span], 0, 0, exact)
            g_shared[span] = (g_queries * affine[0:1] + g_keys * affine[1:2]) * bend[span]
            terms = (g_queries * shared[span], g_keys * shared[span], g_queries)
            for number, term in enumerate(terms):
                sums[number] = sums[number] + jnp.sum(term, axis=0, keepdims=True)
        for number in range(3):
            for k in range(8):
                row = 2 * states + 3 + number
                small_sum[k, row : row + 1] = sums[number]
        own, full = halves(g_shared[...]), halves(shared_w[...].reshape(2, half, lanes))
        for parity in range(2):
            g_mixed[parity] = three(own, (full[0][parity], full[1][parity]), 1, 1)

    def smooth_back():
        for kind in range(3):
            for n in range(states):
                tables[kind, n] = small[:, kind * states + n]
        for parity in range(2):
            pre = mix_pre[parity]
            g_mixed[parity] = g_mixed[parity] * silu_slope(pre)
        for s in range(sequences):
            span = slice(s * block_len, (s + 1) * block_len)
            blocks = [
                g_mixed[block % 2, span, block // 2 * lanes : (block // 2 + 1) * lanes]
                for block in range(8)
            ]
            smooth[s] = jnp.concatenate(blocks, axis=1).reshape(smooth.shape[1:])

    def share():
        return list(to_peers(ends.at[me], ends.at[me], sent_all, came_all))

    def filter_one(s):
        run_filter(True, s, decay, weight, smooth, back, ends.at[me])
        if s == sequences - 1:
            for item in share():
                item.start()

    def moments_one(s, low):
        run_moments(s, low, low + 8, decay, enter, signal, smooth, direct, slope, last)

    def carry_one(s):
        if s == 0:
            for item in share():
                item.wait()
        run_entering(True, s, block_decay, ends, me, back_enter)
        run_carried(True, s, decay, weight, back_enter, back, back)

    def norm_one_back():
        for n in range(states):
            total = slope[n]
            for s in range(sequences):
                total = total + decay[n] * back_enter[s, n] * last[s, n]
            small_sum[:, n] = direct[n]
            small_sum[:, states + n] = total
        centre, scale = statistics(masked)
        line = [back[s].reshape(block_len, features) for s in range(sequences)]
        line = jnp.concatenate(line, axis=0)

        def blocks(ref, k):
            span = slice(k * lanes, (k + 1) * lanes)
            return jnp.concatenate([ref[0, :, span], ref[1, :, span]], axis=1)

        plain, crossed = 0.0, 0.0
        for k in range(tiles):
            g_smooth, hat = blocks(g_mixed, k), (masked[k] - centre) * scale
            gain = row_of(3 * states, k)
            grad = blocks(g_normed, k) + g_smooth * row_of(3 * states + 1, k)
            grad = grad + line[:, k * width : (k + 1) * width]
            put_row(2 * states, k, jnp.sum(grad * hat, axis=0, keepdims=True))
            put_row(2 * states + 1, k, jnp.sum(g_smooth * (hat * gain), axis=0, keepdims=True))
            inner = grad * gain
            plain = plain + jnp.sum(inner, axis=1, keepdims=True)
            crossed = crossed + jnp.sum(inner * hat, axis=1, keepdims=True)
            tokens_grad[:, k * width : (k + 1) * width] = inner
        plain, crossed = plain / features, crossed / features
        for k in range(tiles):
            span = slice(k * width, (k + 1) * width)
            hat = (masked[k] - centre) * scale
            g_x = (tokens_grad[:, span] - plain - hat * crossed) * scale
            tokens_grad[:, span] = (middle[k] + g_x) * row_valid[...]

    g_two[...] = jnp.zeros(g_two.shape, jnp.float32)
    g_gated[...] = jnp.zeros(g_gated.shape, jnp.float32)
    g_normed[...] = jnp.zeros(g_normed.shape, jnp.float32)
    g_soft[...] = jnp.zeros(g_soft.shape, jnp.float32)
    small_sum[...] = jnp.zeros(small_sum.shape, jnp.float32)

    def work(at):
        @pl.when((at < 24) | ((at >= 32) & (at < 56)))
        def _():
            step = jnp.where(at < 24, at, at - 8)
            pl.when(step + 2 < steps)(lambda: fetch(step + 2, "start"))
            fetch(step, "wait")

            @pl.when(at < 16)
            def _():
                for parity in range(2):
                    g_two[parity] = g_two[parity] + back_product(g_wide[at], step, parity)

            pl.when(at == 16)(norm_two_back)

            @pl.when((at >= 16) & (at < 24))
            def _():
                j = (at - 16) // 4
                for parity in range(2):
                    more = back_product(projected[12 + at % 4], step, parity)
                    g_gated[j, parity] = g_gated[j, parity] + more

            pl.when(at == 32)(scores_back)

            @pl.when((at >= 32) & (at < 48))
            def _():
                for parity in range(2):
                    more = back_product(projected[at - 32], step, parity)
                    g_mixed[parity] = g_mixed[parity] + more

            @pl.when(at >= 48)
            def _():
                for parity in range(2):
                    more = back_product(value_pre[at - 48], step, parity)
                    g_normed[parity] = g_normed[parity] + more

        pl.when((at >= 24) & (at < 32))(lambda: attention_back(at - 24))
        pl.when(at == 48)(smooth_back)
        for s in range(sequences):
            pl.when(at == 49 + s)(functools.partial(filter_one, s))
            for low in range(0, states, 8):
                number = 51 + s * (states // 8) + low // 8
                pl.when(at == number)(functools.partial(moments_one, s, low))
            pl.when(at == 56 + s)(functools.partial(carry_one, s))
        pl.when(at == 59)(norm_one_back)

    phases = (begin, with_sibling, with_neighbour, with_corner, inner_sum, total_sum, finish)
    fetch(0, "start")
    fetch(1, "start")

    def step(at, carry):
        for number in range(len(phases) - 1, -1, -1):
            chunk = at - number * delay

            @pl.when((chunk >= 0) & (chunk <= chunks))
            def _(number=number, chunk=chunk):
                phases[number](chunk)

        work(at)
        return carry

    lax.fori_loop(0, chunks + 1 + (len(phases) - 1) * delay, step, 0)


def call_backward(operands, grad_shapes):
    g_wide, soft = operands[5], operands[8]
    signal, enter, small = operands[22], operands[23], operands[25]
    _, rows, width = g_wide.shape
    sequences, block_len = soft.shape[:2]
    states = enter.shape[1]
    half, piece, depth = 4 * lanes, lanes // 2, 8
    vmem, anywhere = pl.BlockSpec(memory_space=pltpu.VMEM), pl.BlockSpec(memory_space=pl.ANY)
    shapes = [f32(rows, 8 * lanes)] + [f32(*shape) for shape in grad_shapes] + [f32(lanes, lanes)]
    held = [
        (4, 2, 2, 2, piece, width), (6, 2, 2, 2, piece, width), (4, 2, 2, 2, piece, width),
        (depth, 2, piece, width), (depth, 2, piece, width), (depth, piece, width), (depth, piece, width),
        (depth, 2, piece, width), (depth, 2, piece, width), (depth, 2, piece, width), (depth, lanes, width),
        (8, rows, width), (16, rows, width), (4, rows, width),
    ]
    more = [
        (2, rows, half), (2, 2, rows, half), (2, rows, half), (2, rows, half), soft.shape, (rows, lanes),
        signal.shape, signal.shape, (8, *enter.shape), enter.shape, (3, states, 8, lanes),
        (states, 8, lanes), (states, 8, lanes), enter.shape, (8, lanes, lanes),
    ]
    return pl.pallas_call(
        backward_body,
        out_shape=shapes,
        in_specs=[anywhere] * 5 + [vmem] * (len(operands) - 5),
        out_specs=[vmem] + [anywhere] * (len(shapes) - 1),
        scratch_shapes=[pltpu.VMEM(shape, jnp.float32) for shape in held]
        + [pltpu.VMEM((3, 2, half, width), jnp.bfloat16)] * 2
        + [pltpu.VMEM(shape, jnp.float32) for shape in more]
        + [
            pltpu.SemaphoreType.DMA((2, 3)),
            pltpu.SemaphoreType.DMA((3,)),
            pltpu.SemaphoreType.DMA((9, depth)),
            pltpu.SemaphoreType.DMA((9, depth)),
            pltpu.SemaphoreType.DMA((2, depth)),
            pltpu.SemaphoreType.DMA((7,)),
            pltpu.SemaphoreType.DMA((7,)),
        ],
        compiler_params=pltpu.CompilerParams(
            collective_id=1, has_side_effects=True, vmem_limit_bytes=62 * 1024 * 1024
        ),
    )(*operands)


def call_kernel(body, shapes, *operands):
    return pl.pallas_call(
        body,
        out_shape=[jax.ShapeDtypeStruct(shape, jnp.float32) for shape in shapes],
        in_specs=[pl.BlockSpec(memory_space=pltpu.VMEM)] * len(operands),
        out_specs=[pl.BlockSpec(memory_space=pltpu.VMEM)] * len(shapes),
        compiler_params=pltpu.CompilerParams(vmem_limit_bytes=32 * 1024 * 1024),
    )(*operands)


def entering(ends, block_decay, backward):
    count, mine = lax.axis_size("seq"), lax.axis_index("seq")
    pieces = lax.all_gather(ends, "seq")
    if backward:
        mine = count - 1 - mine
    total = jnp.zeros_like(ends)
    for position in range(count - 1):
        piece = pieces[count - 1 - position if backward else position]
        total = jnp.where(position < mine, block_decay * total + piece, total)
    return total


def silu(value):
    return value * jax.nn.sigmoid(value)


def silu_slope(value):
    gate = jax.nn.sigmoid(value)
    return gate * (1.0 + value * (1.0 - gate))


def normalise(signal):
    centre = jnp.mean(signal, axis=-1, keepdims=True)
    shifted = signal - centre
    spread = jnp.mean(shifted * shifted, axis=-1, keepdims=True)
    scale = lax.rsqrt(spread + norm_eps)
    return shifted * scale, scale


def normalise_back(grad, gain, hat, scale):
    inner = grad * gain
    return (
        inner
        - jnp.mean(inner, axis=-1, keepdims=True)
        - hat * jnp.mean(inner * hat, axis=-1, keepdims=True)
    ) * scale


def times(left, right):
    return jnp.dot(left, right, precision=triple)


def times_back(left, right):
    return lax.dot_general(left, right, (((1,), (1,)), ((), ())), precision=triple)


def plain_layer(masked_in, normed, mix_pre, g_out, row_valid, key_valid, affine, gain_two, weights):
    value_full, mix_full, merge_full, widen_full, narrow_full = (gather_rows(w) for w in weights)
    rows, width = masked_in.shape
    sequences, _, block_len = key_valid.shape
    value_dim, shared_dim = value_full.shape[1], affine.shape[0]
    mixed = silu(mix_pre)
    value_pre = times(normed, value_full)
    values = silu(value_pre)
    projected = times(mixed, mix_full)
    second_cut = width + shared_dim
    third_cut = second_cut + value_dim
    update = jax.nn.sigmoid(projected[:, :width])
    shared_pre = projected[:, width:second_cut]
    reset_pre = projected[:, second_cut:third_cut]
    shared = silu(shared_pre)
    reset_gate = silu(reset_pre)
    queries = (shared * affine[:, 0] + affine[:, 2]).reshape(sequences, block_len, shared_dim)
    key_rows = (shared * affine[:, 1]).reshape(sequences, block_len, shared_dim)
    score_scale = shared_dim ** (-0.5)
    scores = jnp.einsum("cqz,ckz->cqk", queries, key_rows, precision=exact) * score_scale
    scores = jnp.where(key_valid > 0.5, scores, masked_score)
    soft = jax.nn.softmax(scores, axis=-1)
    values_cut = values.reshape(sequences, block_len, value_dim)
    attended = jnp.einsum("cqk,ckv->cqv", soft, values_cut, precision=triple)
    attended = attended.reshape(rows, value_dim)
    gated = attended * reset_gate
    cand_pre = projected[:, third_cut:] + times(gated, merge_full)
    candidate = silu(cand_pre)
    middle = masked_in + update * (candidate - masked_in)
    hat_two, scale_two = normalise(middle)
    normed_two = hat_two * gain_two
    wide_pre = times(normed_two, widen_full)
    hidden = silu(wide_pre)
    block_out = (middle + times(hidden, narrow_full)) * row_valid

    g_wide = times_back(g_out, narrow_full) * silu_slope(wide_pre)
    g_normed_two = times_back(g_wide, widen_full)
    gain_sum = jnp.sum(g_normed_two * hat_two, axis=0)
    g_middle = g_out + normalise_back(g_normed_two, gain_two, hat_two, scale_two)
    g_cand = g_middle * update * silu_slope(cand_pre)
    g_gated = times_back(g_cand, merge_full)
    g_attended = (g_gated * reset_gate).reshape(sequences, block_len, value_dim)
    g_soft = jnp.einsum("cqv,ckv->cqk", g_attended, values_cut, precision=triple)
    g_values = jnp.einsum("cqk,cqv->ckv", soft, g_attended, precision=triple)
    g_scores = soft * (g_soft - jnp.sum(g_soft * soft, axis=-1, keepdims=True))
    g_scores = jnp.where(key_valid > 0.5, g_scores, 0.0) * score_scale
    g_queries = jnp.einsum("cqk,ckz->cqz", g_scores, key_rows, precision=exact)
    g_keys = jnp.einsum("cqk,cqz->ckz", g_scores, queries, precision=exact)
    g_queries = g_queries.reshape(rows, shared_dim)
    g_keys = g_keys.reshape(rows, shared_dim)
    terms = (g_queries * shared, g_keys * shared, g_queries)
    affine_sum = jnp.stack([jnp.sum(term, axis=0) for term in terms])
    g_shared = (g_queries * affine[:, 0] + g_keys * affine[:, 1]) * silu_slope(shared_pre)
    g_update = g_middle * (candidate - masked_in) * update * (1.0 - update)
    g_reset = g_gated * attended * silu_slope(reset_pre)
    g_projected = jnp.concatenate([g_update, g_shared, g_reset, g_cand], axis=1)
    g_mixed = times_back(g_projected, mix_full)
    g_val = g_values.reshape(rows, value_dim) * silu_slope(value_pre)
    g_from_values = times_back(g_val, value_full)

    def total(packed):
        count = lax.axis_size("seq")
        features = packed.shape[1] // count

        def reduced(whole, tiled=True):
            part = lax.psum_scatter(whole, "seq", scatter_dimension=0, tiled=tiled)
            return lax.psum(part, "batch")

        pairs = (
            (normed, g_val),
            (mixed, g_projected),
            (gated, g_cand),
            (normed_two, g_wide),
            (hidden, g_out),
        )
        grads = tuple(reduced(product_grad(*pair)) for pair in pairs)
        blocks = packed.reshape(-1, count, features).transpose(1, 0, 2)
        return grads + (reduced(blocks, False),)

    return block_out, g_mixed, g_from_values, g_middle * (1.0 - update), gain_sum, affine_sum, total


def plane_layer(tokens, out_grad, valid, logits, rows_of, affine, weights):
    sequences, block_len, width = tokens.shape
    rows = sequences * block_len
    states, own = logits[0].shape
    device = lax.axis_index("seq")
    alpha, delta, beta, gamma = logits
    alpha_rate, damp_rate = jax.nn.sigmoid(alpha), jax.nn.sigmoid(delta)
    out_scale = states ** (-0.5)
    weight = alpha_rate * beta * gamma * out_scale
    block_decay = jnp.exp(block_len * jnp.log1p(-alpha_rate * damp_rate))
    spread = lax.dynamic_update_slice(
        jnp.zeros((3, own), jnp.float32), affine.T, (0, device * affine.shape[0])
    )
    packed = jnp.concatenate([1.0 - alpha_rate * damp_rate, weight, block_decay, rows_of, spread])
    packed = jnp.pad(packed, ((0, -packed.shape[0] % 8), (0, 0)))
    row_valid = valid.reshape(rows, 1)
    key_valid = valid.reshape(sequences, 1, block_len)
    (
        w_high, w_low, value_pre, attended, projected, shared_pre, soft, cand_pre, middle, block_out,
        two_h, two_l, gated_h, gated_l, hidden_h, hidden_l, g_wide,
        normed_h, normed_l, mixed_h, mixed_l, masked, g_out, signal, enter, mix_pre, small, shared_w,
    ) = call_forward(
        weights, packed, tokens.reshape(rows, width), out_grad.reshape(rows, width), row_valid, key_valid, states
    )
    value_weight, mix_weight, merge_weight, widen_weight, narrow_weight = weights
    tokens_grad, narrow, widen, merge, mix, value, sums = call_backward(
        (
            w_high, w_low, value_pre, projected, middle, g_wide, attended, shared_pre, soft, cand_pre,
            two_h, two_l, gated_h, gated_l, hidden_h, hidden_l, normed_h, normed_l, mixed_h, mixed_l,
            masked, g_out, signal, enter, mix_pre, small, shared_w, row_valid, key_valid,
        ),
        [w.shape for w in (narrow_weight, widen_weight, merge_weight, mix_weight, value_weight)],
    )
    direct, slope = sums[:states], sums[states : 2 * states]
    decay_grad = weight * slope
    alpha_grad = (beta * gamma * out_scale * direct - damp_rate * decay_grad) * (
        alpha_rate * (1.0 - alpha_rate)
    )
    delta_grad = -alpha_rate * decay_grad * damp_rate * (1.0 - damp_rate)
    beta_grad = alpha_rate * gamma * out_scale * direct
    gamma_grad = alpha_rate * beta * out_scale * direct
    affine_grad = lax.dynamic_slice(
        sums[2 * states + 3 : 2 * states + 6], (0, device * affine.shape[0]), affine.T.shape
    )
    return (
        block_out.reshape(tokens.shape),
        tokens_grad.reshape(tokens.shape),
        sums[2 * states],
        alpha_grad.T,
        delta_grad.T,
        beta_grad.T,
        gamma_grad.T,
        sums[2 * states + 1],
        value,
        mix,
        affine_grad.T,
        merge,
        sums[2 * states + 2],
        widen,
        narrow,
    )


def per_device(
    tokens,
    lengths,
    out_grad,
    first_gain,
    smooth_alpha,
    smooth_delta,
    smooth_beta,
    smooth_gamma,
    smooth_omega,
    value_weight,
    mix_weight,
    query_affine,
    merge_weight,
    second_gain,
    widen_weight,
    narrow_weight,
):
    sequences, block_len, width = tokens.shape
    count = lax.axis_size("seq")
    states = smooth_alpha.shape[1]
    own = first_gain.shape[0]
    own_shared = query_affine.shape[0]
    rows = sequences * block_len
    shared_dim = own_shared * count
    offsets = lax.axis_index("seq") * block_len + lax.iota(jnp.int32, block_len)
    valid = (offsets[None, :] < lengths[:, None]).astype(jnp.float32)
    weights = (value_weight, mix_weight, merge_weight, widen_weight, narrow_weight)
    if count == 8 and lax.axis_size("batch") == 4:
        logits = (smooth_alpha.T, smooth_delta.T, smooth_beta.T, smooth_gamma.T)
        rows_of = jnp.stack([first_gain, smooth_omega, second_gain])
        return plane_layer(tokens, out_grad, valid, logits, rows_of, query_affine, weights)

    affine_row = jnp.pad(query_affine.reshape(-1), (0, own - 3 * own_shared))
    packed = [
        smooth_alpha.T,
        smooth_delta.T,
        smooth_beta.T,
        smooth_gamma.T,
        jnp.stack([first_gain, smooth_omega, second_gain, affine_row]),
    ]
    small = lax.all_gather(jnp.concatenate(packed, axis=0), "seq").transpose(1, 0, 2)

    tiles = (width // lanes, lanes)
    alpha_rate = jax.nn.sigmoid(small[:states].reshape(states, *tiles))
    damp_rate = jax.nn.sigmoid(small[states : 2 * states].reshape(states, *tiles))
    beta = small[2 * states : 3 * states].reshape(states, *tiles)
    gamma = small[3 * states : 4 * states].reshape(states, *tiles)
    gain_one = small[4 * states].reshape(1, width)
    omega = small[4 * states + 1].reshape(1, width)
    gain_two = small[4 * states + 2].reshape(1, width)
    affine = small[4 * states + 3, :, : 3 * own_shared].reshape(shared_dim, 3)
    out_scale = states ** (-0.5)
    decay = 1.0 - alpha_rate * damp_rate
    block_decay = jnp.exp(block_len * jnp.log1p(-alpha_rate * damp_rate))
    weight = alpha_rate * beta * gamma * out_scale

    row_valid = valid.reshape(rows, 1)
    key_valid = valid.reshape(sequences, 1, block_len)

    masked_in = tokens.reshape(rows, width) * row_valid
    g_out = out_grad.reshape(rows, width) * row_valid
    hat_one, scale_one = normalise(masked_in)
    normed = hat_one * gain_one
    tiled = (sequences, block_len) + tiles
    ending = (sequences, states) + tiles
    signal = normed.reshape(tiled)
    local, ends = call_kernel(
        functools.partial(filter_body, False), [tiled, ending], decay, weight, signal
    )
    enter = entering(ends, block_decay, False)
    (smoothed,) = call_kernel(
        functools.partial(carried_body, False), [tiled], decay, weight, enter, local
    )
    mix_pre = smoothed.reshape(rows, width) + omega * normed

    results = plain_layer(
        masked_in, normed, mix_pre, g_out, row_valid, key_valid, affine, gain_two, weights
    )
    block_out, g_mixed, g_from_values, g_rest, second_gain_sum, affine_sum, total = results
    g_smooth = g_mixed * silu_slope(mix_pre)

    smooth_tiled = g_smooth.reshape(tiled)
    back_local, back_ends = call_kernel(
        functools.partial(filter_body, True), [tiled, ending], decay, weight, smooth_tiled
    )
    back_enter = entering(back_ends, block_decay, True)
    direct, slope, last = call_kernel(
        moments_body,
        [(states,) + tiles, (states,) + tiles, ending],
        decay,
        enter,
        signal,
        smooth_tiled,
    )
    (back_full,) = call_kernel(
        functools.partial(carried_body, True), [tiled], decay, weight, back_enter, back_local
    )
    slope = slope + decay * jnp.sum(back_enter * last, axis=0)
    decay_grad = weight * slope
    alpha_grad = (beta * gamma * out_scale * direct - damp_rate * decay_grad) * (
        alpha_rate * (1.0 - alpha_rate)
    )
    delta_grad = -alpha_rate * decay_grad * damp_rate * (1.0 - damp_rate)
    beta_grad = alpha_rate * gamma * out_scale * direct
    gamma_grad = alpha_rate * beta * out_scale * direct

    g_normed = g_from_values + g_smooth * omega + back_full.reshape(rows, width)
    tokens_grad = (g_rest + normalise_back(g_normed, gain_one, hat_one, scale_one)) * row_valid
    first_gain_sum = jnp.sum(g_normed * hat_one, axis=0)
    omega_sum = jnp.sum(g_smooth * normed, axis=0)
    affine_rows = jnp.pad(
        affine_sum.T.reshape(count, 3 * own_shared), ((0, 0), (0, own - 3 * own_shared))
    )
    small_rows = [
        alpha_grad.reshape(states, width),
        delta_grad.reshape(states, width),
        beta_grad.reshape(states, width),
        gamma_grad.reshape(states, width),
        jnp.stack([first_gain_sum, omega_sum, second_gain_sum, affine_rows.reshape(width)]),
    ]
    value_grad, mix_grad, merge_grad, widen_grad, narrow_grad, small_grad = total(
        jnp.concatenate(small_rows, axis=0)
    )

    return (
        block_out.reshape(tokens.shape),
        tokens_grad.reshape(tokens.shape),
        small_grad[4 * states],
        small_grad[:states].T,
        small_grad[states : 2 * states].T,
        small_grad[2 * states : 3 * states].T,
        small_grad[3 * states : 4 * states].T,
        small_grad[4 * states + 1],
        value_grad,
        mix_grad,
        small_grad[4 * states + 3, : 3 * own_shared].reshape(own_shared, 3),
        merge_grad,
        small_grad[4 * states + 2],
        widen_grad,
        narrow_grad,
    )


def solution(mesh):
    rows = P("batch", "seq", None)
    split = P("seq", None)
    in_specs = (
        (rows, P("batch"), rows, P("seq"))
        + (split,) * 4
        + (P("seq"),)
        + (split,) * 4
        + (P("seq"),)
        + (split,) * 2
    )
    out_specs = (
        (rows, rows, P("seq"))
        + (split,) * 4
        + (P("seq"),)
        + (split,) * 4
        + (P("seq"),)
        + (split,) * 2
    )
    return jax.shard_map(
        per_device, mesh=mesh, in_specs=in_specs, out_specs=out_specs, check_vma=False
    )
```

```python
import functools

import jax
import jax.numpy as jnp
from jax import lax
from jax.experimental import pallas as pl
from jax.experimental.pallas import tpu as pltpu
from jax.sharding import PartitionSpec as P

exact = lax.Precision.HIGHEST
triple = lax.Precision.HIGH
norm_eps = 1e-05
masked_score = -1000000000.0
lanes = 128


def gather_rows(shard):
    return lax.all_gather(shard, "seq", axis=0, tiled=True)


def product_grad(left, right):
    return lax.dot_general(left, right, (((0,), (0,)), ((), ())), precision=triple)


def halves(value):
    high = value.astype(jnp.bfloat16)
    return high, (value - high.astype(jnp.float32)).astype(jnp.bfloat16)


def contract(left, right, left_dim, right_dim, precision=None):
    return lax.dot_general(
        left, right, (((left_dim,), (right_dim,)), ((), ())),
        precision=precision, preferred_element_type=jnp.float32,
    )


def turned(left, right):
    return contract(left, right, 0, 0)


def three(left, right, left_dim, right_dim):
    (high, low), (other, rest) = left, right
    return contract(high, other, left_dim, right_dim) + (
        contract(low, other, left_dim, right_dim) + contract(high, rest, left_dim, right_dim)
    )


def place_of(device):
    return (device % 2) * 4 + device // 2


def tree_sum(terms):
    while len(terms) > 1:
        terms = [a + b for a, b in zip(terms[::2], terms[1::2])] + (
            [terms[-1]] if len(terms) % 2 else []
        )
    return terms[0]


def run_filter(reverse, s, decay_ref, weight_ref, signal_ref, out_ref, end_ref):
    length, states = signal_ref.shape[1], decay_ref.shape[0]

    def step(t, held):
        at = length - 1 - t if reverse else t
        entry = signal_ref[s, at]
        held = tuple(decay_ref[n] * held[n] + entry for n in range(states))
        out_ref[s, at] = tree_sum([weight_ref[n] * held[n] for n in range(states)])
        return held

    zero = jnp.zeros(signal_ref.shape[2:], jnp.float32)
    held = lax.fori_loop(0, length, step, (zero,) * states, unroll=4)
    for n in range(states):
        end_ref[s, n] = held[n]


def run_carried(reverse, s, decay_ref, weight_ref, enter_ref, local_ref, out_ref):
    length, states = local_ref.shape[1], decay_ref.shape[0]

    def step(t, held):
        at = length - 1 - t if reverse else t
        held = tuple(decay_ref[n] * held[n] for n in range(states))
        out_ref[s, at] = local_ref[s, at] + tree_sum(list(held))
        return held

    start = tuple(weight_ref[n] * enter_ref[s, n] for n in range(states))
    lax.fori_loop(0, length, step, start, unroll=4)


def run_moments(s, low, high, decay_ref, enter_ref, signal_ref, grad_ref, direct_ref, slope_ref, last_ref):
    length, span = signal_ref.shape[1], range(low, high)
    zero = jnp.zeros(signal_ref.shape[2:], jnp.float32)

    def step(t, carry):
        held, slope, direct, sloped = carry
        entry, grad = signal_ref[s, t], grad_ref[s, t]
        slope = tuple(decay_ref[n] * d + h for n, d, h in zip(span, slope, held))
        held = tuple(decay_ref[n] * h + entry for n, h in zip(span, held))
        direct = tuple(q + grad * h for q, h in zip(direct, held))
        sloped = tuple(q + grad * d for q, d in zip(sloped, slope))
        return held, slope, direct, sloped

    zeros = (zero,) * len(span)
    if s:
        sums = (tuple(direct_ref[n] for n in span), tuple(slope_ref[n] for n in span))
    else:
        sums = (zeros, zeros)
    start = (tuple(enter_ref[s, n] for n in span), zeros) + sums
    _, slope, direct, sloped = lax.fori_loop(0, length, step, start, unroll=2)
    for k, n in enumerate(span):
        last_ref[s, n], direct_ref[n], slope_ref[n] = slope[k], direct[k], sloped[k]


def filter_body(reverse, decay_ref, weight_ref, signal_ref, out_ref, end_ref):
    for s in range(signal_ref.shape[0]):
        run_filter(reverse, s, decay_ref, weight_ref, signal_ref, out_ref, end_ref)


def carried_body(reverse, decay_ref, weight_ref, enter_ref, local_ref, out_ref):
    for s in range(local_ref.shape[0]):
        run_carried(reverse, s, decay_ref, weight_ref, enter_ref, local_ref, out_ref)


def moments_body(decay_ref, enter_ref, signal_ref, grad_ref, *outs):
    states = decay_ref.shape[0]
    for low in range(0, states, 8):
        for s in range(signal_ref.shape[0]):
            run_moments(s, low, min(low + 8, states), decay_ref, enter_ref, signal_ref, grad_ref, *outs)


def run_entering(reverse, s, block_ref, ends_ref, me, enter_ref):
    count = ends_ref.shape[0]
    mine = count - 1 - me if reverse else me

    def one(n, carry):
        total = jnp.zeros(block_ref.shape[1:], jnp.float32)
        for position in range(count - 1):
            piece = ends_ref[count - 1 - position if reverse else position, s, n]
            total = jnp.where(position < mine, block_ref[n] * total + piece, total)
        enter_ref[s, n] = total
        return carry

    lax.fori_loop(0, block_ref.shape[0], one, 0)


def on_other(**coordinate):
    return dict(device_id=coordinate, device_id_type=pl.DeviceIdType.MESH)


def chunk_table(shapes):
    firsts, chunk = [], 0
    for blocks, wide in shapes:
        firsts.append(chunk)
        chunk += blocks * wide
    return firsts, chunk


def to_peers(source, target, sent, came):
    me = lax.axis_index("seq")
    for k in range(1, 8):
        yield pltpu.make_async_remote_copy(
            src_ref=source, dst_ref=target, send_sem=sent.at[k - 1], recv_sem=came.at[k - 1],
            **on_other(seq=(me // 4 + k // 4) % 2 * 4 + (me // 2 + k // 2) % 2 * 2 + (me + k) % 2),
        )


kept_count = 25
gather_shapes = ((1, 8), (1, 16), (2, 4), (1, 16), (4, 4))


def forward_body(
    value_ref, mix_ref, merge_ref, widen_ref, narrow_ref, packed, tokens, out_grad, row_valid, key_valid,
    block_out, w_high, w_low, *refs,
):
    kept, held, refs = refs[:kept_count], refs[kept_count : 2 * kept_count], refs[2 * kept_count :]
    (
        hidden_h, hidden_l, g_out, g_wide, two_h, two_l, gated_h, gated_l, mixed_h, mixed_l, normed_h, normed_l,
        value_pre, projected, middle, attended, shared_pre, soft, cand_pre, masked, signal, enter, mix_pre, small, shared_w,
    ) = held
    buf, stage_h, stage_l, g_hidden, smoothed, ends, tables = refs[:7]
    loaded, sent, came, stored, near, sent_all, came_all, saved = refs[7:]
    weights = (value_ref, mix_ref, merge_ref, widen_ref, narrow_ref)
    firsts, chunks = chunk_table(gather_shapes)
    depth, width = buf.shape[0], buf.shape[-1]
    half = lanes * 4
    me, level = lax.axis_index("seq"), lax.axis_index("batch")
    core, along_x, along_y = me % 2, (me // 2) % 2, me // 4
    id_sibling = me + 1 - 2 * core
    id_x, id_y = me + 2 - 4 * along_x, me + 4 - 8 * along_y
    id_corner = id_x + 4 - 8 * along_y
    mine, at_x, at_y, at_corner = (place_of(device) for device in (me, id_x, id_y, id_corner))
    above, below = (level + 1) % 4, (level + 3) % 4

    barrier = pltpu.get_barrier_semaphore()
    for other in range(1, 8):
        pl.semaphore_signal(barrier, inc=1, **on_other(seq=(me + other) % 8))
    for target in (above, below):
        pl.semaphore_signal(barrier, inc=1, **on_other(batch=target))
    pl.semaphore_wait(barrier, 9)

    names = ["x", "y", "sibling", "corner_x", "corner_y", "x_more", "y_more"]
    names += ["sibling_x", "sibling_y", "sibling_corner"]
    names += [f"ring{number}{of}" for of in ("", "_x", "_y") for number in range(3)]

    def link(name, chunk):
        slot = chunk % depth
        block = {"x": at_x, "y": at_y, "corner": at_corner}
        kind, _, of = name.partition("_")
        by_x, by_y, by_core, by_z = ({"seq": id_x}, {"seq": id_y}, {"seq": id_sibling}, {"batch": above})
        if kind == "sibling":
            piece, target = buf.at[slot, block[of] if of else mine], by_core
        elif kind == "corner":
            if of == "x":
                piece, target = buf.at[slot, at_x, level, pl.ds(0, 2)], by_y
            else:
                piece, target = buf.at[slot, at_y, level, pl.ds(2, 2)], by_x
        elif kind[:4] == "ring":
            quarter = (level + 4 - int(kind[4])) % 4
            if of:
                piece = buf.at[slot, block[of], quarter, 3 if of == "x" else 0]
            else:
                piece = buf.at[slot, at_corner, quarter]
            target = by_z
        else:
            target = by_x if kind == "x" else by_y
            if of == "more":
                piece = buf.at[slot, mine, level, 3 if kind == "x" else 0]
            elif of == "part":
                piece = buf.at[slot, mine, :, pl.ds(0 if kind == "x" else 1, 3)]
            else:
                piece = buf.at[slot, mine]
        number = names.index(name.removesuffix("_part"))
        return pltpu.make_async_remote_copy(
            src_ref=piece, dst_ref=piece, send_sem=sent.at[number, slot], recv_sem=came.at[number, slot],
            **on_other(**target),
        )

    def shares(chunk):
        return chunk % 3 != 2

    def own_load(weight, block, column, slot):
        source = weight.at[pl.ds(block * 4, 4), :, :, pl.ds(pl.multiple_of(column, lanes), width)]
        return pltpu.make_async_copy(source, buf.at[slot, mine], loaded.at[slot])

    def load(chunk):
        slot = chunk % depth
        for number, ((blocks, wide), first, weight) in enumerate(
            zip(gather_shapes, firsts, weights)
        ):

            @pl.when((chunk >= first) & (chunk < first + blocks * wide))
            def _(number=number, first=first, wide=wide, weight=weight):
                block = (chunk - first) // wide
                column = ((chunk - first) % wide) * width
                if number == 1:
                    column = column + jnp.where(column >= features, lanes, 0)
                own_load(weight, block, column, slot).start()

    def send(chunk):
        own_load(value_ref, 0, 0, chunk % depth).wait()
        both = shares(chunk)
        link("sibling", chunk).start()

        @pl.when(both)
        def _():
            for name in ("x_part", "y_part", "x_more", "y_more"):
                link(name, chunk).start()

        @pl.when(jnp.logical_not(both))
        def _():
            link("x", chunk).start()
            link("y", chunk).start()

    def relay(chunk):
        both = shares(chunk)
        link("sibling", chunk).wait()

        @pl.when(both)
        def _():
            for name in ("x_part", "y_part", "x_more", "y_more"):
                link(name, chunk).wait()
            link("ring0_x", chunk).start()
            link("ring0_y", chunk).start()

        @pl.when(jnp.logical_not(both))
        def _():
            link("x", chunk).wait()
            link("y", chunk).wait()

        link("corner_x", chunk).start()
        link("corner_y", chunk).start()

    def ring(number):
        def phase(chunk):
            if number:
                link(f"ring{number - 1}", chunk).wait()
            else:
                link("corner_x", chunk).wait()
                link("corner_y", chunk).wait()

            @pl.when(shares(chunk))
            def _():
                for of in "xy":
                    link(f"ring{number}_{of}", chunk).wait()
                    if number < 2:
                        link(f"ring{number + 1}_{of}", chunk).start()

            link(f"ring{number}", chunk).start()

        return phase

    def to_sibling(chunk):
        link("ring2", chunk).wait()
        for name in ("sibling_x", "sibling_y", "sibling_corner"):
            link(name, chunk).start()

    def store(chunk, kind):
        return pltpu.make_async_copy(
            (stage_h, stage_l)[kind].at[chunk % 2],
            (w_high, w_low)[kind].at[chunk],
            stored.at[kind, chunk % 2],
        )

    def product(left_h, left_l, right):
        return three((left_h[0], left_l[0]), (right[0][0], right[1][0]), 1, 0) + three(
            (left_h[1], left_l[1]), (right[0][1], right[1][1]), 1, 0
        )

    sequences, block_len = soft.shape[:2]
    states = tables.shape[1]
    decay, weight, block_decay = (tables.at[kind] for kind in range(3))
    features = tokens.shape[1]
    tiles = features // width

    def share(kind):
        if kind == 0:
            source = target = small.at[me]
        elif kind == 1:
            source = mix_ref.at[:, :, :, pl.ds(features, lanes)]
            target = shared_w.at[mine]
        else:
            source = target = ends.at[me]
        return list(to_peers(source, target, sent_all.at[kind], came_all.at[kind]))

    def own_shared():
        return pltpu.make_async_copy(
            mix_ref.at[:, :, :, pl.ds(features, lanes)], shared_w.at[mine], near
        )

    def row_of(number, k):
        return jnp.concatenate(
            [small[2 * k, number : number + 1], small[2 * k + 1, number : number + 1]], axis=1
        )

    def hand_out():
        small[me] = packed[...]
        for kind in (0, 1):
            for item in share(kind):
                item.start()
        own_shared().start()

    def norm_one():
        for kind in (0, 1):
            for item in share(kind):
                item.wait()
        own_shared().wait()
        for kind in range(3):
            for n in range(states):
                tables[kind, n] = small[:, kind * states + n]
        keep = row_valid[...]
        value = tokens[...] * keep
        centre = jnp.mean(value, axis=1, keepdims=True)
        shifted = value - centre
        scale = lax.rsqrt(jnp.mean(shifted * shifted, axis=1, keepdims=True) + norm_eps)
        gain = jnp.concatenate([row_of(3 * states, k) for k in range(tiles)], axis=1)
        normed = shifted * scale * gain
        for k in range(tiles):
            span = slice(k * width, (k + 1) * width)
            masked[k] = value[:, span]
            g_out[k] = out_grad[:, span] * keep
            for parity in range(2):
                start = k * width + parity * lanes
                put(normed_h, normed_l, (parity,), k * lanes, normed[:, start : start + lanes])
        for s in range(sequences):
            rows = normed[s * block_len : (s + 1) * block_len]
            signal[s] = rows.reshape(signal.shape[1:])

    def filter_one(s):
        run_filter(False, s, decay, weight, signal, smoothed, ends.at[me])
        if s == sequences - 1:
            for item in share(2):
                item.start()

    def carry_one(s):
        if s == 0:
            for item in share(2):
                item.wait()
        run_entering(False, s, block_decay, ends, me, enter)
        run_carried(False, s, decay, weight, enter, smoothed, smoothed)

    def mix_in():
        for s in range(sequences):
            span = slice(s * block_len, (s + 1) * block_len)
            skip = jnp.concatenate([row_of(3 * states + 1, k) for k in range(tiles)], axis=1)
            normed = signal[s].reshape(block_len, features)
            value = smoothed[s].reshape(block_len, features) + skip * normed
            mixed = value * jax.nn.sigmoid(value)
            for block in range(8):
                cut = slice(block * lanes, (block + 1) * lanes)
                to = (block % 2, span, slice(block // 2 * lanes, (block // 2 + 1) * lanes))
                mix_pre[to] = value[:, cut]
                mixed_h[to], mixed_l[to] = halves(mixed[:, cut])

    def attention():
        shared_full = halves(shared_w[...].reshape(2, half, lanes))
        total = product(mixed_h, mixed_l, shared_full)
        affine = tree_sum([small[k, 3 * states + 3 : 3 * states + 6] for k in range(8)])
        shared_pre[...] = total
        shared = total * jax.nn.sigmoid(total)
        queries = shared * affine[0:1] + affine[2:3]
        keys = shared * affine[1:2]
        for s in range(sequences):
            span = slice(s * block_len, (s + 1) * block_len)
            scores = contract(queries[span], keys[span], 1, 1, exact) * shared.shape[1] ** (-0.5)
            scores = jnp.where(key_valid[s] > 0.5, scores, masked_score)
            weight = jnp.exp(scores - jnp.max(scores, axis=1, keepdims=True))
            soft[s] = weight / jnp.sum(weight, axis=1, keepdims=True)

    def put(target_h, target_l, index, column, value):
        high, low = halves(value)
        target_h[(*index, slice(None), pl.ds(pl.multiple_of(column, lanes), lanes))] = high
        target_l[(*index, slice(None), pl.ds(pl.multiple_of(column, lanes), lanes))] = low

    def complete(chunk):
        slot = chunk % depth
        for name in ("sibling_x", "sibling_y", "sibling_corner"):
            link(name, chunk).wait()

        @pl.when(chunk >= 2)
        def _():
            store(chunk - 2, 0).wait()
            store(chunk - 2, 1).wait()

        right = halves(buf[slot].reshape(2, half, width))
        stage_h[chunk % 2] = right[0]
        stage_l[chunk % 2] = right[1]
        store(chunk, 0).start()
        store(chunk, 1).start()

        def among(number):
            blocks, wide = gather_shapes[number]
            return (chunk >= firsts[number]) & (chunk < firsts[number] + blocks * wide)

        @pl.when(among(0))
        def _():
            total = product(normed_h, normed_l, right)
            value_pre[chunk] = total
            values = total * jax.nn.sigmoid(total)
            for s in range(sequences):
                span = slice(s * block_len, (s + 1) * block_len)
                attended[chunk, span] = contract(soft[s], values[span], 1, 0, exact)

        @pl.when(among(1))
        def _():
            tile = chunk - firsts[1]
            total = product(mixed_h, mixed_l, right)
            projected[tile] = total

            @pl.when((tile >= 4) & (tile < 12))
            def _():
                block = tile - 4
                gated = attended[block] * total * jax.nn.sigmoid(total)
                for j in range(2):
                    cut = gated[:, j * lanes : (j + 1) * lanes]
                    put(gated_h, gated_l, (j, block % 2), (block // 2) * lanes, cut)

        @pl.when(among(2))
        def _():
            j, tile = (chunk - firsts[2]) // 4, (chunk - firsts[2]) % 4
            total = product(gated_h.at[j], gated_l.at[j], right)

            @pl.when(j == 0)
            def _():
                cand_pre[tile] = projected[12 + tile] + total

            @pl.when(j == 1)
            def _():
                cand_pre[tile] = cand_pre[tile] + total

            @pl.when(chunk == firsts[3] - 1)
            def _():
                total = 0.0
                for k in range(tiles):
                    cand = cand_pre[k]
                    cand = cand * jax.nn.sigmoid(cand)
                    value = masked[k] + jax.nn.sigmoid(projected[k]) * (cand - masked[k])
                    middle[k] = value
                    total = total + jnp.sum(value, axis=1, keepdims=True)
                centre = total / features
                total = 0.0
                for k in range(tiles):
                    shifted = middle[k] - centre
                    total = total + jnp.sum(shifted * shifted, axis=1, keepdims=True)
                scale = lax.rsqrt(total / features + norm_eps)
                for k in range(tiles):
                    value = (middle[k] - centre) * scale * row_of(3 * states + 2, k)
                    for parity in range(2):
                        cut = value[:, parity * lanes : (parity + 1) * lanes]
                        put(two_h, two_l, (parity,), k * lanes, cut)
                block_out[...] = jnp.zeros(block_out.shape, jnp.float32)
                g_hidden[...] = jnp.zeros(g_hidden.shape, jnp.float32)

        @pl.when(among(3))
        def _():
            tile = chunk - firsts[3]
            total = product(two_h, two_l, right)
            g_wide[tile] = total
            hidden = total * jax.nn.sigmoid(total)
            for i in range(2):
                cut = hidden[:, i * lanes : (i + 1) * lanes]
                index = (2 * (tile % 2) + i, (tile // 2) % 2)
                put(hidden_h, hidden_l, index, (tile // 4) * lanes, cut)

        @pl.when(among(4))
        def _():
            j, tile = (chunk - firsts[4]) // 4, (chunk - firsts[4]) % 4
            to = (slice(None), pl.ds(pl.multiple_of(tile * width, width), width))
            block_out[to] = block_out[to] + product(hidden_h.at[j], hidden_l.at[j], right)
            grad = halves(g_out[tile])
            for parity in range(2):
                back = three(grad, (right[0][parity], right[1][parity]), 1, 1)
                g_hidden[j, parity] = g_hidden[j, parity] + back

    def save(*numbers):
        return [
            pltpu.make_async_copy(held[number], kept[number], saved.at[number]) for number in numbers
        ]

    def begin_save(*numbers):
        for item in save(*numbers):
            item.start()

    phases = (
        (2, relay), (4, ring(0)), (6, ring(1)), (8, ring(2)), (10, to_sibling), (11, complete)
    )
    last, ahead = phases[-1][0], 1

    def step(at, carry):
        for after, phase in phases[-2::-1]:

            @pl.when((at >= after) & (at < after + chunks))
            def _(after=after, phase=phase):
                phase(at - after)

        @pl.when(at == 0)
        def _():
            for chunk in range(ahead):
                send(chunk)
            hand_out()

        pl.when((at >= 1) & (at + ahead - 1 < chunks))(lambda: send(at + ahead - 1))
        pl.when(at + ahead < chunks)(lambda: load(at + ahead))
        pl.when(at == 1)(norm_one)
        for s in range(sequences):
            pl.when(at == 2 + s)(functools.partial(filter_one, s))
            pl.when(at == 5 + s)(functools.partial(carry_one, s))
        pl.when(at == 7)(mix_in)
        pl.when(at == 8)(attention)
        pl.when(at == last)(lambda: begin_save(2, 8, 9, 10, 11, 16, 17, 19, 20, 21, 22, 23, 24))
        pl.when(at == last + firsts[3])(lambda: begin_save(4, 5, 6, 7, 12, 13, 14, 15, 18))
        pl.when(at == last + firsts[4])(lambda: begin_save(0, 1))

        @pl.when(at >= last)
        def _():
            complete(at - last)

        return carry

    for chunk in range(ahead):
        load(chunk)
    lax.fori_loop(0, chunks + last, step, 0)
    for chunk in (chunks - 2, chunks - 1):
        for kind in range(2):
            store(chunk, kind).wait()
    for k in range(tiles):
        span = slice(k * width, (k + 1) * width)
        block_out[:, span] = (middle[k] + block_out[:, span]) * row_valid[...]
    for k in range(g_wide.shape[0]):
        for i in range(2):
            span = slice(i * lanes, (i + 1) * lanes)
            back = g_hidden[2 * (k % 2) + i, (k // 2) % 2, :, (k // 4) * lanes : (k // 4 + 1) * lanes]
            wide = g_wide[k, :, span]
            g_wide[k, :, span] = back * silu_slope(wide)
    begin_save(3)
    for item in save(*range(kept_count)):
        item.wait()


def f32(*shape):
    return jax.ShapeDtypeStruct(shape, jnp.float32)


def b16(*shape):
    return jax.ShapeDtypeStruct(shape, jnp.bfloat16)


def call_forward(weights, packed, tokens, out_grad, row_valid, key_valid, states):
    width, half = 2 * lanes, 4 * lanes
    rows, features = tokens.shape
    sequences = key_valid.shape[0]
    block_len = rows // sequences
    _, chunks = chunk_table(gather_shapes)
    vmem, anywhere = pl.BlockSpec(memory_space=pltpu.VMEM), pl.BlockSpec(memory_space=pl.ANY)
    line = (sequences, block_len, 8, lanes)
    kept = [
        b16(4, 2, rows, half), b16(4, 2, rows, half), f32(4, rows, width), f32(16, rows, width),
        b16(2, rows, half), b16(2, rows, half), b16(2, 2, rows, half), b16(2, 2, rows, half),
        b16(2, rows, half), b16(2, rows, half), b16(2, rows, half), b16(2, rows, half),
        f32(8, rows, width), f32(16, rows, width), f32(4, rows, width), f32(8, rows, width), f32(rows, lanes),
        f32(sequences, block_len, block_len), f32(4, rows, width), f32(4, rows, width), f32(*line),
        f32(sequences, states, 8, lanes), f32(2, rows, half), f32(8, *packed.shape), f32(8, 4, 4, 8, lanes),
    ]
    shapes = [f32(rows, features)] + [b16(chunks, 2, half, width)] * 2 + kept
    depth, kinds = 16, 19
    return pl.pallas_call(
        forward_body,
        out_shape=shapes,
        in_specs=[anywhere] * len(weights) + [vmem] * 5,
        out_specs=[vmem] + [anywhere] * (len(shapes) - 1),
        scratch_shapes=[pltpu.VMEM(item.shape, item.dtype) for item in kept]
        + [
            pltpu.VMEM((depth, 8, 4, 4, 8, width), jnp.float32),
            pltpu.VMEM((2, 2, half, width), jnp.bfloat16),
            pltpu.VMEM((2, 2, half, width), jnp.bfloat16),
            pltpu.VMEM((4, 2, rows, half), jnp.float32),
            pltpu.VMEM(line, jnp.float32),
            pltpu.VMEM((8, sequences, states, 8, lanes), jnp.float32),
            pltpu.VMEM((3, states, 8, lanes), jnp.float32),
            pltpu.SemaphoreType.DMA((depth,)),
            pltpu.SemaphoreType.DMA((kinds, depth)),
            pltpu.SemaphoreType.DMA((kinds, depth)),
            pltpu.SemaphoreType.DMA((2, 2)),
            pltpu.SemaphoreType.DMA,
            pltpu.SemaphoreType.DMA((3, 7)),
            pltpu.SemaphoreType.DMA((3, 7)),
            pltpu.SemaphoreType.DMA((kept_count,)),
        ],
        compiler_params=pltpu.CompilerParams(
            collective_id=2, has_side_effects=True, vmem_limit_bytes=62 * 1024 * 1024
        ),
    )(*[w.reshape(-1, 4, 8, w.shape[1]) for w in weights], packed, tokens, out_grad, row_valid, key_valid)


reduce_shapes = ((4, 4), (1, 16), (2, 4), (1, 16), (1, 8))


def backward_body(
    row_valid, key_valid, w_high, w_low, *refs,
):
    kept, outs, refs = refs[:kept_count], refs[kept_count : kept_count + 7], refs[kept_count + 7 :]
    held, refs = refs[:kept_count], refs[kept_count:]
    (
        hidden_h, hidden_l, g_out, g_wide, two_h, two_l, gated_h, gated_l, mixed_h, mixed_l, normed_h, normed_l,
        value_pre, projected, middle, attended, shared_pre, soft, cand_pre, masked, signal, enter, mix_pre, small, shared_w,
    ) = held
    tokens_grad, narrow_grad, widen_grad, merge_grad, mix_grad, value_grad, small_grad = outs
    away, keep, got, got_x, got_y, got_xy, got_yx, part, from_edge, from_inner, done = refs[:11]
    buf_h, buf_l, g_two, g_gated, g_mixed, g_normed, g_soft, g_shared = refs[11:19]
    smooth, back, ends, back_enter, tables, direct, slope, last, small_sum = refs[19:28]
    fetched, read, sent, came, written, sent_all, came_all = refs[28:]
    lefts = (
        (hidden_h, hidden_l), (two_h, two_l), (gated_h, gated_l), (mixed_h, mixed_l), (normed_h, normed_l)
    )
    rights = ((g_out, 0), (g_wide, 0), (projected, 12), (projected, 0), (value_pre, 0))
    grads = (narrow_grad, widen_grad, merge_grad, mix_grad, value_grad)
    firsts, chunks = chunk_table(reduce_shapes)
    gathered, _ = chunk_table(gather_shapes)
    tiles, rows, width = masked.shape
    half, features = 4 * lanes, tiles * width
    sequences, block_len = soft.shape[:2]
    states = tables.shape[1]
    decay, weight, block_decay = (tables.at[kind] for kind in range(3))
    me, level = lax.axis_index("seq"), lax.axis_index("batch")
    core, along_x, along_y = me % 2, (me // 2) % 2, me // 4
    is_edge = (level == 0) | (level == 3)
    partner = jnp.where(level < 2, 1 - level, 5 - level)
    sibling, across_x, across_y = (
        {"seq": me + bit * (1 - 2 * own)} for bit, own in ((1, core), (2, along_x), (4, along_y))
    )

    copies_in = [
        pltpu.make_async_copy(source, target, read.at[number])
        for number, (source, target) in enumerate(zip(kept, held))
    ]
    for item in copies_in:
        item.start()

    barrier = pltpu.get_barrier_semaphore()
    for other in range(1, 8):
        pl.semaphore_signal(barrier, inc=1, **on_other(seq=(me + other) % 8))
    pl.semaphore_signal(barrier, inc=1, **on_other(batch=partner))

    @pl.when(jnp.logical_not(is_edge))
    def _():
        pl.semaphore_signal(barrier, inc=1, **on_other(batch=3 - level))
        pl.semaphore_wait(barrier, 9)

    @pl.when(is_edge)
    def _():
        pl.semaphore_wait(barrier, 8)

    def slot_in(ref, chunk):
        return chunk % ref.shape[0]

    def link(kind, chunk):
        def at(ref, *index):
            return ref.at[(slot_in(ref, chunk), *index)]

        source, target, device = (
            lambda: (at(away), at(got), sibling),
            lambda: (at(keep, slice(None), 1 - along_x, 0), at(got_x), across_x),
            lambda: (at(keep, 1 - along_y, slice(None), 1), at(got_y), across_y),
            lambda: (at(got_x, 1 - along_y), at(got_xy), across_y),
            lambda: (at(got_y, 1 - along_x), at(got_yx), across_x),
            lambda: (at(part), at(from_edge), {"batch": partner}),
            lambda: (at(part), at(from_inner), {"batch": 3 - level}),
        )[kind]()
        slot = chunk % sent.shape[1]
        return pltpu.make_async_remote_copy(
            src_ref=source, dst_ref=target, send_sem=sent.at[kind, slot], recv_sem=came.at[kind, slot],
            **on_other(**device),
        )

    def results(chunk, call):
        slot, at = slot_in(done, chunk), chunk % sent.shape[1]

        def pieces(number, source, target):
            yield lambda: pltpu.make_async_copy(source, target, written.at[number, at])
            yield lambda: pltpu.make_async_remote_copy(
                src_ref=source, dst_ref=target,
                send_sem=sent.at[7 + number, at], recv_sem=came.at[7 + number, at],
                **on_other(batch=partner),
            )

        for number, ((blocks, wide), first, grad) in enumerate(zip(reduce_shapes, firsts, grads)):

            @pl.when((chunk >= first) & (chunk < first + blocks * wide))
            def _(number=number, first=first, wide=wide, grad=grad):
                row = ((chunk - first) // wide) * lanes
                column = ((chunk - first) % wide) * width
                if number == 3:
                    column = column + jnp.where(column >= features, lanes, 0)
                target = grad.at[
                    pl.ds(pl.multiple_of(row, lanes), lanes),
                    pl.ds(pl.multiple_of(column, lanes), width),
                ]
                call(*pieces(0, done.at[slot], target))

        @pl.when(chunk == chunks)
        def _():
            target = mix_grad.at[:, pl.ds(features, lanes)]
            call(*pieces(0, done.at[slot, :, pl.ds(0, lanes)], target))
            call(*pieces(1, done.at[slot, :, pl.ds(lanes, lanes)], small_grad))

    def begin(chunk):
        slot, to = slot_in(away, chunk), slot_in(keep, chunk)
        for (blocks, wide), first, (high, low), (right, shift) in zip(
            reduce_shapes, firsts, lefts, rights
        ):

            @pl.when((chunk >= first) & (chunk < first + blocks * wide))
            def _(first=first, wide=wide, shift=shift, high=high, low=low, right=right):
                block = (chunk - first) // wide
                other, rest = halves(right[shift + (chunk - first) % wide])

                def product(parity):
                    top, under = (
                        (high[block, parity], low[block, parity])
                        if len(high.shape) == 4
                        else (high[parity], low[parity])
                    )
                    total = turned(top, other) + (turned(under, other) + turned(top, rest))
                    return total.reshape(away.shape[1:])

                away[slot] = product(1 - core)
                link(0, chunk).start()
                keep[to] = product(core)

        @pl.when(chunk == chunks)
        def _():
            right = halves(g_shared[...])

            def fill(ref, at, parity):
                total = three((mixed_h[parity], mixed_l[parity]), right, 0, 0)
                total = total.reshape(*away.shape[1:-1], lanes)
                sums = [small_sum[2 * q + parity].reshape(2, -1, lanes) for q in range(4)]
                sums = jnp.stack(sums, axis=0).reshape(total.shape)
                ref[at] = jnp.concatenate([total, sums], axis=-1)

            fill(away, slot, 1 - core)
            link(0, chunk).start()
            fill(keep, to, core)

    def with_sibling(chunk):
        slot = slot_in(keep, chunk)
        link(0, chunk).wait()
        keep[slot] = keep[slot] + got[slot_in(got, chunk)]
        link(1, chunk).start()
        link(2, chunk).start()

    def with_neighbour(chunk):
        slot = slot_in(got_x, chunk)
        link(1, chunk).wait()
        link(2, chunk).wait()
        from_slot = slot_in(keep, chunk)
        got_x[slot] = got_x[slot] + keep[from_slot, :, along_x, 0]
        got_y[slot] = got_y[slot] + keep[from_slot, along_y, :, 1]
        link(3, chunk).start()
        link(4, chunk).start()

    def with_corner(chunk):
        slot = slot_in(part, chunk)
        link(3, chunk).wait()
        link(4, chunk).wait()
        first, second = slot_in(got_x, chunk), slot_in(got_xy, chunk)
        part[slot, 0] = got_x[first, along_y] + got_xy[second]
        part[slot, 1] = got_y[first, along_x] + got_yx[second]
        pl.when(is_edge)(lambda: link(5, chunk).start())

    def inner_sum(chunk):
        slot = slot_in(part, chunk)
        pl.when(is_edge)(lambda: link(5, chunk).wait_send())

        @pl.when(jnp.logical_not(is_edge))
        def _():
            link(5, chunk).wait_recv()
            part[slot] = part[slot] + from_edge[slot]
            link(6, chunk).start()

    def total_sum(chunk):
        slot = slot_in(part, chunk)

        @pl.when(jnp.logical_not(is_edge))
        def _():
            link(6, chunk).wait()
            done[slot] = (part[slot] + from_inner[slot]).reshape(done.shape[1:])

            def start(stay, go):
                stay().start()
                go().start()

            results(chunk, start)

    def finish(chunk):
        def receive(stay, go):
            go().wait_recv()

        def release(stay, go):
            stay().wait()
            go().wait_send()

        pl.when(is_edge)(lambda: results(chunk, receive))
        pl.when(jnp.logical_not(is_edge))(lambda: results(chunk, release))

    steps = 48

    def fetch(step, call):
        chunk = jnp.where(
            step < 16, gathered[3] + step, jnp.where(step < 24, step + 8, jnp.where(step < 40, step - 16, step - 40))
        )
        slot = slot_in(buf_h, step)
        for kind, (source, target) in enumerate(((w_high, buf_h), (w_low, buf_l))):
            item = pltpu.make_async_copy(source.at[chunk], target.at[slot], fetched.at[kind, slot])
            getattr(item, call)()

    def back_product(grad, step, parity):
        slot = slot_in(buf_h, step)
        return three(halves(grad), (buf_h[slot, parity], buf_l[slot, parity]), 1, 1)

    def row_of(number, k):
        return jnp.concatenate(
            [small[2 * k, number : number + 1], small[2 * k + 1, number : number + 1]], axis=1
        )

    def put_row(number, k, value):
        for i in range(2):
            small_sum[2 * k + i, number : number + 1] = value[:, i * lanes : (i + 1) * lanes]

    def statistics(ref):
        total = 0.0
        for k in range(tiles):
            total = total + jnp.sum(ref[k], axis=1, keepdims=True)
        centre = total / features
        total = 0.0
        for k in range(tiles):
            shifted = ref[k] - centre
            total = total + jnp.sum(shifted * shifted, axis=1, keepdims=True)
        return centre, lax.rsqrt(total / features + norm_eps)

    def norm_two_back():
        centre, scale = statistics(middle)

        def grad_of(k):
            span = slice(k * lanes, (k + 1) * lanes)
            return jnp.concatenate([g_two[0, :, span], g_two[1, :, span]], axis=1)

        plain, crossed = 0.0, 0.0
        for k in range(tiles):
            grad, hat = grad_of(k), (middle[k] - centre) * scale
            put_row(2 * states + 2, k, jnp.sum(grad * hat, axis=0, keepdims=True))
            inner = grad * row_of(3 * states + 2, k)
            plain = plain + jnp.sum(inner, axis=1, keepdims=True)
            crossed = crossed + jnp.sum(inner * hat, axis=1, keepdims=True)
        plain, crossed = plain / features, crossed / features
        for k in range(tiles):
            inner, hat = grad_of(k) * row_of(3 * states + 2, k), (middle[k] - centre) * scale
            g_middle = g_out[k] + (inner - plain - hat * crossed) * scale
            update = jax.nn.sigmoid(projected[k])
            pre = cand_pre[k]
            gate = jax.nn.sigmoid(pre)
            middle[k] = g_middle * (1.0 - update)
            projected[k] = g_middle * (pre * gate - masked[k]) * update * (1.0 - update)
            projected[12 + k] = g_middle * update * (gate * (1.0 + pre * (1.0 - gate)))

    def attention_back(m):
        parity, start = m % 2, pl.multiple_of((m // 2) * lanes, lanes)
        grad = jnp.concatenate(
            [g_gated[0, parity, :, pl.ds(start, lanes)], g_gated[1, parity, :, pl.ds(start, lanes)]], axis=1
        )
        pre = projected[4 + m]
        gate = jax.nn.sigmoid(pre)
        g_attended = grad * pre * gate
        projected[4 + m] = grad * attended[m] * (gate * (1.0 + pre * (1.0 - gate)))
        pre = value_pre[m]
        gate = jax.nn.sigmoid(pre)
        values, bend = pre * gate, gate * (1.0 + pre * (1.0 - gate))
        g_values = []
        for s in range(sequences):
            span = slice(s * block_len, (s + 1) * block_len)
            own = halves(g_attended[span])
            g_soft[s] = g_soft[s] + three(own, halves(values[span]), 1, 1)
            g_values.append(three(halves(soft[s]), own, 0, 0) * bend[span])
        value_pre[m] = jnp.concatenate(g_values, axis=0)

    def scores_back():
        affine = tree_sum([small[k, 3 * states + 3 : 3 * states + 6] for k in range(8)])
        pre = shared_pre[...]
        gate = jax.nn.sigmoid(pre)
        shared, bend = pre * gate, gate * (1.0 + pre * (1.0 - gate))
        score_scale = shared.shape[1] ** (-0.5)
        queries = shared * affine[0:1] + affine[2:3]
        keys = shared * affine[1:2]
        sums = [0.0, 0.0, 0.0]
        for s in range(sequences):
            span = slice(s * block_len, (s + 1) * block_len)
            soft_weight, grad = soft[s], g_soft[s]
            g_scores = soft_weight * (grad - jnp.sum(grad * soft_weight, axis=1, keepdims=True))
            g_scores = jnp.where(key_valid[s] > 0.5, g_scores, 0.0) * score_scale
            g_queries = contract(g_scores, keys[span], 1, 0, exact)
            g_keys = contract(g_scores, queries[span], 0, 0, exact)
            g_shared[span] = (g_queries * affine[0:1] + g_keys * affine[1:2]) * bend[span]
            terms = (g_queries * shared[span], g_keys * shared[span], g_queries)
            for number, term in enumerate(terms):
                sums[number] = sums[number] + jnp.sum(term, axis=0, keepdims=True)
        for number in range(3):
            for k in range(8):
                row = 2 * states + 3 + number
                small_sum[k, row : row + 1] = sums[number]
        own, full = halves(g_shared[...]), halves(shared_w[...].reshape(2, half, lanes))
        for parity in range(2):
            g_mixed[parity] = three(own, (full[0][parity], full[1][parity]), 1, 1)

    def smooth_back():
        for kind in range(3):
            for n in range(states):
                tables[kind, n] = small[:, kind * states + n]
        for parity in range(2):
            pre = mix_pre[parity]
            g_mixed[parity] = g_mixed[parity] * silu_slope(pre)
        for s in range(sequences):
            span = slice(s * block_len, (s + 1) * block_len)
            blocks = [
                g_mixed[block % 2, span, block // 2 * lanes : (block // 2 + 1) * lanes]
                for block in range(8)
            ]
            smooth[s] = jnp.concatenate(blocks, axis=1).reshape(smooth.shape[1:])

    def share():
        return list(to_peers(ends.at[me], ends.at[me], sent_all, came_all))

    def filter_one(s):
        run_filter(True, s, decay, weight, smooth, back, ends.at[me])
        if s == sequences - 1:
            for item in share():
                item.start()

    def moments_one(s, low):
        run_moments(s, low, low + 8, decay, enter, signal, smooth, direct, slope, last)

    def carry_one(s):
        if s == 0:
            for item in share():
                item.wait()
        run_entering(True, s, block_decay, ends, me, back_enter)
        run_carried(True, s, decay, weight, back_enter, back, back)

    def norm_one_back():
        for n in range(states):
            total = slope[n]
            for s in range(sequences):
                total = total + decay[n] * back_enter[s, n] * last[s, n]
            small_sum[:, n] = direct[n]
            small_sum[:, states + n] = total
        centre, scale = statistics(masked)
        line = [back[s].reshape(block_len, features) for s in range(sequences)]
        line = jnp.concatenate(line, axis=0)

        def blocks(ref, k):
            span = slice(k * lanes, (k + 1) * lanes)
            return jnp.concatenate([ref[0, :, span], ref[1, :, span]], axis=1)

        plain, crossed = 0.0, 0.0
        for k in range(tiles):
            g_smooth, hat = blocks(g_mixed, k), (masked[k] - centre) * scale
            gain = row_of(3 * states, k)
            grad = blocks(g_normed, k) + g_smooth * row_of(3 * states + 1, k)
            grad = grad + line[:, k * width : (k + 1) * width]
            put_row(2 * states, k, jnp.sum(grad * hat, axis=0, keepdims=True))
            put_row(2 * states + 1, k, jnp.sum(g_smooth * (hat * gain), axis=0, keepdims=True))
            inner = grad * gain
            plain = plain + jnp.sum(inner, axis=1, keepdims=True)
            crossed = crossed + jnp.sum(inner * hat, axis=1, keepdims=True)
            tokens_grad[:, k * width : (k + 1) * width] = inner
        plain, crossed = plain / features, crossed / features
        for k in range(tiles):
            span = slice(k * width, (k + 1) * width)
            hat = (masked[k] - centre) * scale
            g_x = (tokens_grad[:, span] - plain - hat * crossed) * scale
            tokens_grad[:, span] = (middle[k] + g_x) * row_valid[...]

    g_two[...] = jnp.zeros(g_two.shape, jnp.float32)
    g_gated[...] = jnp.zeros(g_gated.shape, jnp.float32)
    g_normed[...] = jnp.zeros(g_normed.shape, jnp.float32)
    g_soft[...] = jnp.zeros(g_soft.shape, jnp.float32)
    small_sum[...] = jnp.zeros(small_sum.shape, jnp.float32)

    def work(at):
        @pl.when((at < 24) | ((at >= 32) & (at < 56)))
        def _():
            step = jnp.where(at < 24, at, at - 8)
            pl.when(step + 2 < steps)(lambda: fetch(step + 2, "start"))
            fetch(step, "wait")

            @pl.when(at < 16)
            def _():
                for parity in range(2):
                    g_two[parity] = g_two[parity] + back_product(g_wide[at], step, parity)

            pl.when(at == 16)(norm_two_back)

            @pl.when((at >= 16) & (at < 24))
            def _():
                j = (at - 16) // 4
                for parity in range(2):
                    more = back_product(projected[12 + at % 4], step, parity)
                    g_gated[j, parity] = g_gated[j, parity] + more

            pl.when(at == 32)(scores_back)

            @pl.when((at >= 32) & (at < 48))
            def _():
                for parity in range(2):
                    more = back_product(projected[at - 32], step, parity)
                    g_mixed[parity] = g_mixed[parity] + more

            @pl.when(at >= 48)
            def _():
                for parity in range(2):
                    more = back_product(value_pre[at - 48], step, parity)
                    g_normed[parity] = g_normed[parity] + more

        pl.when((at >= 24) & (at < 32))(lambda: attention_back(at - 24))
        pl.when(at == 48)(smooth_back)
        for s in range(sequences):
            pl.when(at == 49 + s)(functools.partial(filter_one, s))
            for low in range(0, states, 8):
                number = 51 + s * (states // 8) + low // 8
                pl.when(at == number)(functools.partial(moments_one, s, low))
            pl.when(at == 56 + s)(functools.partial(carry_one, s))
        pl.when(at == 59)(norm_one_back)

    phases = (
        (0, begin), (1, with_sibling), (3, with_neighbour), (5, with_corner), (7, inner_sum), (9, total_sum), (11, finish)
    )
    fetch(0, "start")
    fetch(1, "start")

    def arrive(first, end):
        for item in copies_in[first:end]:
            item.wait()

    arrive(0, 3)

    def step(at, carry):
        for after, phase in phases[::-1]:

            @pl.when((at >= after) & (at <= after + chunks))
            def _(after=after, phase=phase):
                phase(at - after)

        pl.when(at == 0)(lambda: arrive(3, 4))
        pl.when(at == 8)(lambda: arrive(4, kept_count))
        work(at)
        return carry

    lax.fori_loop(0, chunks + 1 + phases[-1][0], step, 0)


def call_backward(row_valid, key_valid, w_high, w_low, kept, grad_shapes):
    _, rows, width = kept[3].shape
    soft, signal, enter = kept[17], kept[20], kept[21]
    states = enter.shape[1]
    half, piece, depth = 4 * lanes, lanes // 2, 8
    vmem, anywhere = pl.BlockSpec(memory_space=pltpu.VMEM), pl.BlockSpec(memory_space=pl.ANY)
    shapes = [f32(rows, 8 * lanes)] + [f32(*shape) for shape in grad_shapes] + [f32(lanes, lanes)]
    held = [
        (4, 2, 2, 2, piece, width), (6, 2, 2, 2, piece, width), (4, 2, 2, 2, piece, width),
        (9, 2, piece, width), (9, 2, piece, width), (depth, piece, width), (depth, piece, width),
        (depth, 2, piece, width), (depth, 2, piece, width), (depth, 2, piece, width), (depth, lanes, width),
    ]
    more = [
        (2, rows, half), (2, 2, rows, half), (2, rows, half), (2, rows, half), soft.shape, (rows, lanes),
        signal.shape, signal.shape, (8, *enter.shape), enter.shape, (3, states, 8, lanes),
        (states, 8, lanes), (states, 8, lanes), enter.shape, (8, lanes, lanes),
    ]
    return pl.pallas_call(
        backward_body,
        out_shape=shapes,
        in_specs=[vmem] * 2 + [anywhere] * (2 + kept_count),
        out_specs=[vmem] + [anywhere] * (len(shapes) - 1),
        scratch_shapes=[pltpu.VMEM(item.shape, item.dtype) for item in kept]
        + [pltpu.VMEM(shape, jnp.float32) for shape in held]
        + [pltpu.VMEM((3, 2, half, width), jnp.bfloat16)] * 2
        + [pltpu.VMEM(shape, jnp.float32) for shape in more]
        + [
            pltpu.SemaphoreType.DMA((2, 3)),
            pltpu.SemaphoreType.DMA((kept_count,)),
            pltpu.SemaphoreType.DMA((9, depth)),
            pltpu.SemaphoreType.DMA((9, depth)),
            pltpu.SemaphoreType.DMA((2, depth)),
            pltpu.SemaphoreType.DMA((7,)),
            pltpu.SemaphoreType.DMA((7,)),
        ],
        compiler_params=pltpu.CompilerParams(
            collective_id=1, has_side_effects=True, vmem_limit_bytes=62 * 1024 * 1024
        ),
    )(row_valid, key_valid, w_high, w_low, *kept)


def call_kernel(body, shapes, *operands):
    return pl.pallas_call(
        body,
        out_shape=[jax.ShapeDtypeStruct(shape, jnp.float32) for shape in shapes],
        in_specs=[pl.BlockSpec(memory_space=pltpu.VMEM)] * len(operands),
        out_specs=[pl.BlockSpec(memory_space=pltpu.VMEM)] * len(shapes),
        compiler_params=pltpu.CompilerParams(vmem_limit_bytes=32 * 1024 * 1024),
    )(*operands)


def entering(ends, block_decay, backward):
    count, mine = lax.axis_size("seq"), lax.axis_index("seq")
    pieces = lax.all_gather(ends, "seq")
    if backward:
        mine = count - 1 - mine
    total = jnp.zeros_like(ends)
    for position in range(count - 1):
        piece = pieces[count - 1 - position if backward else position]
        total = jnp.where(position < mine, block_decay * total + piece, total)
    return total


def silu(value):
    return value * jax.nn.sigmoid(value)


def silu_slope(value):
    gate = jax.nn.sigmoid(value)
    return gate * (1.0 + value * (1.0 - gate))


def normalise(signal):
    centre = jnp.mean(signal, axis=-1, keepdims=True)
    shifted = signal - centre
    spread = jnp.mean(shifted * shifted, axis=-1, keepdims=True)
    scale = lax.rsqrt(spread + norm_eps)
    return shifted * scale, scale


def normalise_back(grad, gain, hat, scale):
    inner = grad * gain
    return (
        inner
        - jnp.mean(inner, axis=-1, keepdims=True)
        - hat * jnp.mean(inner * hat, axis=-1, keepdims=True)
    ) * scale


def times(left, right):
    return jnp.dot(left, right, precision=triple)


def times_back(left, right):
    return lax.dot_general(left, right, (((1,), (1,)), ((), ())), precision=triple)


def plain_layer(masked_in, normed, mix_pre, g_out, row_valid, key_valid, affine, gain_two, weights):
    value_full, mix_full, merge_full, widen_full, narrow_full = (gather_rows(w) for w in weights)
    rows, width = masked_in.shape
    sequences, _, block_len = key_valid.shape
    value_dim, shared_dim = value_full.shape[1], affine.shape[0]
    mixed = silu(mix_pre)
    value_pre = times(normed, value_full)
    values = silu(value_pre)
    projected = times(mixed, mix_full)
    second_cut = width + shared_dim
    third_cut = second_cut + value_dim
    update = jax.nn.sigmoid(projected[:, :width])
    shared_pre = projected[:, width:second_cut]
    reset_pre = projected[:, second_cut:third_cut]
    shared = silu(shared_pre)
    reset_gate = silu(reset_pre)
    queries = (shared * affine[:, 0] + affine[:, 2]).reshape(sequences, block_len, shared_dim)
    key_rows = (shared * affine[:, 1]).reshape(sequences, block_len, shared_dim)
    score_scale = shared_dim ** (-0.5)
    scores = jnp.einsum("cqz,ckz->cqk", queries, key_rows, precision=exact) * score_scale
    scores = jnp.where(key_valid > 0.5, scores, masked_score)
    soft = jax.nn.softmax(scores, axis=-1)
    values_cut = values.reshape(sequences, block_len, value_dim)
    attended = jnp.einsum("cqk,ckv->cqv", soft, values_cut, precision=triple)
    attended = attended.reshape(rows, value_dim)
    gated = attended * reset_gate
    cand_pre = projected[:, third_cut:] + times(gated, merge_full)
    candidate = silu(cand_pre)
    middle = masked_in + update * (candidate - masked_in)
    hat_two, scale_two = normalise(middle)
    normed_two = hat_two * gain_two
    wide_pre = times(normed_two, widen_full)
    hidden = silu(wide_pre)
    block_out = (middle + times(hidden, narrow_full)) * row_valid

    g_wide = times_back(g_out, narrow_full) * silu_slope(wide_pre)
    g_normed_two = times_back(g_wide, widen_full)
    gain_sum = jnp.sum(g_normed_two * hat_two, axis=0)
    g_middle = g_out + normalise_back(g_normed_two, gain_two, hat_two, scale_two)
    g_cand = g_middle * update * silu_slope(cand_pre)
    g_gated = times_back(g_cand, merge_full)
    g_attended = (g_gated * reset_gate).reshape(sequences, block_len, value_dim)
    g_soft = jnp.einsum("cqv,ckv->cqk", g_attended, values_cut, precision=triple)
    g_values = jnp.einsum("cqk,cqv->ckv", soft, g_attended, precision=triple)
    g_scores = soft * (g_soft - jnp.sum(g_soft * soft, axis=-1, keepdims=True))
    g_scores = jnp.where(key_valid > 0.5, g_scores, 0.0) * score_scale
    g_queries = jnp.einsum("cqk,ckz->cqz", g_scores, key_rows, precision=exact)
    g_keys = jnp.einsum("cqk,cqz->ckz", g_scores, queries, precision=exact)
    g_queries = g_queries.reshape(rows, shared_dim)
    g_keys = g_keys.reshape(rows, shared_dim)
    terms = (g_queries * shared, g_keys * shared, g_queries)
    affine_sum = jnp.stack([jnp.sum(term, axis=0) for term in terms])
    g_shared = (g_queries * affine[:, 0] + g_keys * affine[:, 1]) * silu_slope(shared_pre)
    g_update = g_middle * (candidate - masked_in) * update * (1.0 - update)
    g_reset = g_gated * attended * silu_slope(reset_pre)
    g_projected = jnp.concatenate([g_update, g_shared, g_reset, g_cand], axis=1)
    g_mixed = times_back(g_projected, mix_full)
    g_val = g_values.reshape(rows, value_dim) * silu_slope(value_pre)
    g_from_values = times_back(g_val, value_full)

    def total(packed):
        count = lax.axis_size("seq")
        features = packed.shape[1] // count

        def reduced(whole, tiled=True):
            part = lax.psum_scatter(whole, "seq", scatter_dimension=0, tiled=tiled)
            return lax.psum(part, "batch")

        pairs = (
            (normed, g_val),
            (mixed, g_projected),
            (gated, g_cand),
            (normed_two, g_wide),
            (hidden, g_out),
        )
        grads = tuple(reduced(product_grad(*pair)) for pair in pairs)
        blocks = packed.reshape(-1, count, features).transpose(1, 0, 2)
        return grads + (reduced(blocks, False),)

    return block_out, g_mixed, g_from_values, g_middle * (1.0 - update), gain_sum, affine_sum, total


def plane_layer(tokens, out_grad, valid, logits, rows_of, affine, weights):
    sequences, block_len, width = tokens.shape
    rows = sequences * block_len
    states, own = logits[0].shape
    device = lax.axis_index("seq")
    alpha, delta, beta, gamma = logits
    alpha_rate, damp_rate = jax.nn.sigmoid(alpha), jax.nn.sigmoid(delta)
    out_scale = states ** (-0.5)
    weight = alpha_rate * beta * gamma * out_scale
    block_decay = jnp.exp(block_len * jnp.log1p(-alpha_rate * damp_rate))
    spread = lax.dynamic_update_slice(
        jnp.zeros((3, own), jnp.float32), affine.T, (0, device * affine.shape[0])
    )
    packed = jnp.concatenate([1.0 - alpha_rate * damp_rate, weight, block_decay, rows_of, spread])
    packed = jnp.pad(packed, ((0, -packed.shape[0] % 8), (0, 0)))
    row_valid = valid.reshape(rows, 1)
    key_valid = valid.reshape(sequences, 1, block_len)
    block_out, w_high, w_low, *kept = call_forward(
        weights, packed, tokens.reshape(rows, width), out_grad.reshape(rows, width), row_valid, key_valid, states
    )
    value_weight, mix_weight, merge_weight, widen_weight, narrow_weight = weights
    tokens_grad, narrow, widen, merge, mix, value, sums = call_backward(
        row_valid,
        key_valid,
        w_high,
        w_low,
        kept,
        [w.shape for w in (narrow_weight, widen_weight, merge_weight, mix_weight, value_weight)],
    )
    direct, slope = sums[:states], sums[states : 2 * states]
    decay_grad = weight * slope
    alpha_grad = (beta * gamma * out_scale * direct - damp_rate * decay_grad) * (
        alpha_rate * (1.0 - alpha_rate)
    )
    delta_grad = -alpha_rate * decay_grad * damp_rate * (1.0 - damp_rate)
    beta_grad = alpha_rate * gamma * out_scale * direct
    gamma_grad = alpha_rate * beta * out_scale * direct
    affine_grad = lax.dynamic_slice(
        sums[2 * states + 3 : 2 * states + 6], (0, device * affine.shape[0]), affine.T.shape
    )
    return (
        block_out.reshape(tokens.shape),
        tokens_grad.reshape(tokens.shape),
        sums[2 * states],
        alpha_grad.T,
        delta_grad.T,
        beta_grad.T,
        gamma_grad.T,
        sums[2 * states + 1],
        value,
        mix,
        affine_grad.T,
        merge,
        sums[2 * states + 2],
        widen,
        narrow,
    )


def per_device(
    tokens,
    lengths,
    out_grad,
    first_gain,
    smooth_alpha,
    smooth_delta,
    smooth_beta,
    smooth_gamma,
    smooth_omega,
    value_weight,
    mix_weight,
    query_affine,
    merge_weight,
    second_gain,
    widen_weight,
    narrow_weight,
):
    sequences, block_len, width = tokens.shape
    count = lax.axis_size("seq")
    states = smooth_alpha.shape[1]
    own = first_gain.shape[0]
    own_shared = query_affine.shape[0]
    rows = sequences * block_len
    shared_dim = own_shared * count
    offsets = lax.axis_index("seq") * block_len + lax.iota(jnp.int32, block_len)
    valid = (offsets[None, :] < lengths[:, None]).astype(jnp.float32)
    weights = (value_weight, mix_weight, merge_weight, widen_weight, narrow_weight)
    if count == 8 and lax.axis_size("batch") == 4:
        logits = (smooth_alpha.T, smooth_delta.T, smooth_beta.T, smooth_gamma.T)
        rows_of = jnp.stack([first_gain, smooth_omega, second_gain])
        return plane_layer(tokens, out_grad, valid, logits, rows_of, query_affine, weights)

    affine_row = jnp.pad(query_affine.reshape(-1), (0, own - 3 * own_shared))
    packed = [
        smooth_alpha.T,
        smooth_delta.T,
        smooth_beta.T,
        smooth_gamma.T,
        jnp.stack([first_gain, smooth_omega, second_gain, affine_row]),
    ]
    small = lax.all_gather(jnp.concatenate(packed, axis=0), "seq").transpose(1, 0, 2)

    tiles = (width // lanes, lanes)
    alpha_rate = jax.nn.sigmoid(small[:states].reshape(states, *tiles))
    damp_rate = jax.nn.sigmoid(small[states : 2 * states].reshape(states, *tiles))
    beta = small[2 * states : 3 * states].reshape(states, *tiles)
    gamma = small[3 * states : 4 * states].reshape(states, *tiles)
    gain_one = small[4 * states].reshape(1, width)
    omega = small[4 * states + 1].reshape(1, width)
    gain_two = small[4 * states + 2].reshape(1, width)
    affine = small[4 * states + 3, :, : 3 * own_shared].reshape(shared_dim, 3)
    out_scale = states ** (-0.5)
    decay = 1.0 - alpha_rate * damp_rate
    block_decay = jnp.exp(block_len * jnp.log1p(-alpha_rate * damp_rate))
    weight = alpha_rate * beta * gamma * out_scale

    row_valid = valid.reshape(rows, 1)
    key_valid = valid.reshape(sequences, 1, block_len)

    masked_in = tokens.reshape(rows, width) * row_valid
    g_out = out_grad.reshape(rows, width) * row_valid
    hat_one, scale_one = normalise(masked_in)
    normed = hat_one * gain_one
    tiled = (sequences, block_len) + tiles
    ending = (sequences, states) + tiles
    signal = normed.reshape(tiled)
    local, ends = call_kernel(
        functools.partial(filter_body, False), [tiled, ending], decay, weight, signal
    )
    enter = entering(ends, block_decay, False)
    (smoothed,) = call_kernel(
        functools.partial(carried_body, False), [tiled], decay, weight, enter, local
    )
    mix_pre = smoothed.reshape(rows, width) + omega * normed

    results = plain_layer(
        masked_in, normed, mix_pre, g_out, row_valid, key_valid, affine, gain_two, weights
    )
    block_out, g_mixed, g_from_values, g_rest, second_gain_sum, affine_sum, total = results
    g_smooth = g_mixed * silu_slope(mix_pre)

    smooth_tiled = g_smooth.reshape(tiled)
    back_local, back_ends = call_kernel(
        functools.partial(filter_body, True), [tiled, ending], decay, weight, smooth_tiled
    )
    back_enter = entering(back_ends, block_decay, True)
    direct, slope, last = call_kernel(
        moments_body,
        [(states,) + tiles, (states,) + tiles, ending],
        decay,
        enter,
        signal,
        smooth_tiled,
    )
    (back_full,) = call_kernel(
        functools.partial(carried_body, True), [tiled], decay, weight, back_enter, back_local
    )
    slope = slope + decay * jnp.sum(back_enter * last, axis=0)
    decay_grad = weight * slope
    alpha_grad = (beta * gamma * out_scale * direct - damp_rate * decay_grad) * (
        alpha_rate * (1.0 - alpha_rate)
    )
    delta_grad = -alpha_rate * decay_grad * damp_rate * (1.0 - damp_rate)
    beta_grad = alpha_rate * gamma * out_scale * direct
    gamma_grad = alpha_rate * beta * out_scale * direct

    g_normed = g_from_values + g_smooth * omega + back_full.reshape(rows, width)
    tokens_grad = (g_rest + normalise_back(g_normed, gain_one, hat_one, scale_one)) * row_valid
    first_gain_sum = jnp.sum(g_normed * hat_one, axis=0)
    omega_sum = jnp.sum(g_smooth * normed, axis=0)
    affine_rows = jnp.pad(
        affine_sum.T.reshape(count, 3 * own_shared), ((0, 0), (0, own - 3 * own_shared))
    )
    small_rows = [
        alpha_grad.reshape(states, width),
        delta_grad.reshape(states, width),
        beta_grad.reshape(states, width),
        gamma_grad.reshape(states, width),
        jnp.stack([first_gain_sum, omega_sum, second_gain_sum, affine_rows.reshape(width)]),
    ]
    value_grad, mix_grad, merge_grad, widen_grad, narrow_grad, small_grad = total(
        jnp.concatenate(small_rows, axis=0)
    )

    return (
        block_out.reshape(tokens.shape),
        tokens_grad.reshape(tokens.shape),
        small_grad[4 * states],
        small_grad[:states].T,
        small_grad[states : 2 * states].T,
        small_grad[2 * states : 3 * states].T,
        small_grad[3 * states : 4 * states].T,
        small_grad[4 * states + 1],
        value_grad,
        mix_grad,
        small_grad[4 * states + 3, : 3 * own_shared].reshape(own_shared, 3),
        merge_grad,
        small_grad[4 * states + 2],
        widen_grad,
        narrow_grad,
    )


def solution(mesh):
    rows = P("batch", "seq", None)
    split = P("seq", None)
    in_specs = (
        (rows, P("batch"), rows, P("seq"))
        + (split,) * 4
        + (P("seq"),)
        + (split,) * 4
        + (P("seq"),)
        + (split,) * 2
    )
    out_specs = (
        (rows, rows, P("seq"))
        + (split,) * 4
        + (P("seq"),)
        + (split,) * 4
        + (P("seq"),)
        + (split,) * 2
    )
    return jax.shard_map(
        per_device, mesh=mesh, in_specs=in_specs, out_specs=out_specs, check_vma=False
    )
```

```python
import functools

import jax
import jax.numpy as jnp
from jax import lax
from jax.experimental import pallas as pl
from jax.experimental.pallas import tpu as pltpu
from jax.sharding import PartitionSpec as P

exact = lax.Precision.HIGHEST
triple = lax.Precision.HIGH
norm_eps = 1e-05
masked_score = -1000000000.0
lanes = 128


def gather_rows(shard):
    return lax.all_gather(shard, "seq", axis=0, tiled=True)


def product_grad(left, right):
    return lax.dot_general(left, right, (((0,), (0,)), ((), ())), precision=triple)


def halves(value):
    high = value.astype(jnp.bfloat16)
    return high, (value - high.astype(jnp.float32)).astype(jnp.bfloat16)


def contract(left, right, left_dim, right_dim, precision=None):
    return lax.dot_general(
        left, right, (((left_dim,), (right_dim,)), ((), ())),
        precision=precision, preferred_element_type=jnp.float32,
    )


def turned(left, right):
    return contract(left, right, 0, 0)


def three(left, right, left_dim, right_dim):
    (high, low), (other, rest) = left, right
    return contract(high, other, left_dim, right_dim) + (
        contract(low, other, left_dim, right_dim) + contract(high, rest, left_dim, right_dim)
    )


def place_of(device):
    return (device % 2) * 4 + device // 2


def tree_sum(terms):
    while len(terms) > 1:
        terms = [a + b for a, b in zip(terms[::2], terms[1::2])] + (
            [terms[-1]] if len(terms) % 2 else []
        )
    return terms[0]


def run_filter(reverse, s, decay_ref, weight_ref, signal_ref, out_ref, end_ref):
    length, states = signal_ref.shape[1], decay_ref.shape[0]

    def step(t, held):
        at = length - 1 - t if reverse else t
        entry = signal_ref[s, at]
        held = tuple(decay_ref[n] * held[n] + entry for n in range(states))
        out_ref[s, at] = tree_sum([weight_ref[n] * held[n] for n in range(states)])
        return held

    zero = jnp.zeros(signal_ref.shape[2:], jnp.float32)
    held = lax.fori_loop(0, length, step, (zero,) * states, unroll=4)
    for n in range(states):
        end_ref[s, n] = held[n]


def run_carried(reverse, s, decay_ref, weight_ref, enter_ref, local_ref, out_ref):
    length, states = local_ref.shape[1], decay_ref.shape[0]

    def step(t, held):
        at = length - 1 - t if reverse else t
        held = tuple(decay_ref[n] * held[n] for n in range(states))
        out_ref[s, at] = local_ref[s, at] + tree_sum(list(held))
        return held

    start = tuple(weight_ref[n] * enter_ref[s, n] for n in range(states))
    lax.fori_loop(0, length, step, start, unroll=4)


def run_moments(s, low, high, decay_ref, enter_ref, signal_ref, grad_ref, direct_ref, slope_ref, last_ref):
    length, span = signal_ref.shape[1], range(low, high)
    zero = jnp.zeros(signal_ref.shape[2:], jnp.float32)

    def step(t, carry):
        held, slope, direct, sloped = carry
        entry, grad = signal_ref[s, t], grad_ref[s, t]
        slope = tuple(decay_ref[n] * d + h for n, d, h in zip(span, slope, held))
        held = tuple(decay_ref[n] * h + entry for n, h in zip(span, held))
        direct = tuple(q + grad * h for q, h in zip(direct, held))
        sloped = tuple(q + grad * d for q, d in zip(sloped, slope))
        return held, slope, direct, sloped

    zeros = (zero,) * len(span)
    if s:
        sums = (tuple(direct_ref[n] for n in span), tuple(slope_ref[n] for n in span))
    else:
        sums = (zeros, zeros)
    start = (tuple(enter_ref[s, n] for n in span), zeros) + sums
    _, slope, direct, sloped = lax.fori_loop(0, length, step, start, unroll=2)
    for k, n in enumerate(span):
        last_ref[s, n], direct_ref[n], slope_ref[n] = slope[k], direct[k], sloped[k]


def filter_body(reverse, decay_ref, weight_ref, signal_ref, out_ref, end_ref):
    for s in range(signal_ref.shape[0]):
        run_filter(reverse, s, decay_ref, weight_ref, signal_ref, out_ref, end_ref)


def carried_body(reverse, decay_ref, weight_ref, enter_ref, local_ref, out_ref):
    for s in range(local_ref.shape[0]):
        run_carried(reverse, s, decay_ref, weight_ref, enter_ref, local_ref, out_ref)


def moments_body(decay_ref, enter_ref, signal_ref, grad_ref, *outs):
    states = decay_ref.shape[0]
    for low in range(0, states, 8):
        for s in range(signal_ref.shape[0]):
            run_moments(s, low, min(low + 8, states), decay_ref, enter_ref, signal_ref, grad_ref, *outs)


def on_other(**coordinate):
    return dict(device_id=coordinate, device_id_type=pl.DeviceIdType.MESH)


def chunk_table(shapes):
    firsts, chunk = [], 0
    for blocks, wide in shapes:
        firsts.append(chunk)
        chunk += blocks * wide
    return firsts, chunk


def others_of(me):
    core, along_x, along_y = me % 2, (me // 2) % 2, me // 4
    across_x = me + 2 - 4 * along_x
    return me + 1 - 2 * core, across_x, me + 4 - 8 * along_y, across_x + 4 - 8 * along_y


def state_exchange(reverse, block_ref, ends, chip_ends, halves_ref, enter_ref, sent, came):
    me = lax.axis_index("seq")
    core, chip = me % 2, me // 2
    sibling, *chips = others_of(me)
    first = 1 if reverse else 0
    _, sequences, states = ends.shape[:3]
    half = states // 2

    def copies(step):
        if step == 0:
            pairs = [(ends.at[core], sibling)]
        elif step == 1:
            pairs = [(chip_ends.at[chip], other) for other in chips]
        else:
            pairs = [(halves_ref.at[core], sibling)]
        for number, (piece, other) in enumerate(pairs):
            at = (0, 1, 4)[step] + number
            yield pltpu.make_async_remote_copy(
                src_ref=piece, dst_ref=piece, send_sem=sent.at[at], recv_sem=came.at[at], **on_other(seq=other)
            )

    def start(step):
        for item in copies(step):
            item.start()

    def wait(step):
        for item in copies(step):
            item.wait()

    def share_ends():
        start(0)

    def to_chips():
        wait(0)

        def one(i, carry):
            n = core * half + i
            for s in range(sequences):
                chip_ends[chip, s, i] = block_ref[n] * ends[first, s, n] + ends[1 - first, s, n]
            return carry

        lax.fori_loop(0, half, one, 0)
        start(1)

    def share_entering():
        wait(1)
        mine = 3 - chip if reverse else chip

        def one(i, carry):
            decay = block_ref[core * half + i]
            decay = decay * decay
            for s in range(sequences):
                total = jnp.zeros(block_ref.shape[1:], jnp.float32)
                for position in range(3):
                    piece = chip_ends[3 - position if reverse else position, s, i]
                    total = jnp.where(position < mine, decay * total + piece, total)
                halves_ref[core, s, i] = total
            return carry

        lax.fori_loop(0, half, one, 0)
        start(2)

    def enter():
        wait(2)

        def one(n, carry):
            for s in range(sequences):
                total = halves_ref[n // half, s, n % half]
                later = block_ref[n] * total + ends[first, s, n]
                enter_ref[s, n] = jnp.where(core == first, total, later)
            return carry

        lax.fori_loop(0, states, one, 0)

    return share_ends, to_chips, share_entering, enter


kept_count = 25
gather_shapes = ((1, 8), (1, 16), (2, 4), (1, 16), (4, 4))


def forward_body(
    value_ref, mix_ref, merge_ref, widen_ref, narrow_ref, packed, tokens, out_grad, row_valid, key_valid,
    block_out, w_high, w_low, *refs,
):
    kept, held, refs = refs[:kept_count], refs[kept_count : 2 * kept_count], refs[2 * kept_count :]
    (
        hidden_h, hidden_l, g_out, g_wide, two_h, two_l, gated_h, gated_l, mixed_h, mixed_l, normed_h, normed_l,
        value_pre, projected, middle, attended, shared_pre, soft, cand_pre, masked, signal, enter, mix_pre, small, shared_w,
    ) = held
    buf, stage_h, stage_l, g_hidden, smoothed, ends, chip_ends, halves_in, tables = refs[:9]
    loaded, sent, came, stored, near, sent_all, came_all, sent_state, came_state, saved = refs[9:]
    weights = (value_ref, mix_ref, merge_ref, widen_ref, narrow_ref)
    firsts, chunks = chunk_table(gather_shapes)
    depth, width = buf.shape[0], buf.shape[-1]
    half = lanes * 4
    me, level = lax.axis_index("seq"), lax.axis_index("batch")
    id_sibling, id_x, id_y, id_corner = others_of(me)
    mine, at_x, at_y, at_corner = (place_of(device) for device in (me, id_x, id_y, id_corner))
    above, below = (level + 1) % 4, (level + 3) % 4

    barrier = pltpu.get_barrier_semaphore()
    for other in (id_sibling, id_x, id_y, id_corner):
        pl.semaphore_signal(barrier, inc=1, **on_other(seq=other))
    for target in (above, below):
        pl.semaphore_signal(barrier, inc=1, **on_other(batch=target))
    pl.semaphore_wait(barrier, 6)

    names = ["x", "y", "sibling", "corner_x", "corner_y", "x_more", "y_more"]
    names += ["sibling_x", "sibling_y", "sibling_corner"]
    names += [f"ring{number}{of}" for of in ("", "_x", "_y") for number in range(3)]

    def link(name, chunk):
        slot = chunk % depth
        block = {"x": at_x, "y": at_y, "corner": at_corner}
        kind, _, of = name.partition("_")
        by_x, by_y, by_core, by_z = ({"seq": id_x}, {"seq": id_y}, {"seq": id_sibling}, {"batch": above})
        if kind == "sibling":
            piece, target = buf.at[slot, block[of] if of else mine], by_core
        elif kind == "corner":
            if of == "x":
                piece, target = buf.at[slot, at_x, level, pl.ds(0, 2)], by_y
            else:
                piece, target = buf.at[slot, at_y, level, pl.ds(2, 2)], by_x
        elif kind[:4] == "ring":
            quarter = (level + 4 - int(kind[4])) % 4
            if of:
                piece = buf.at[slot, block[of], quarter, 3 if of == "x" else 0]
            else:
                piece = buf.at[slot, at_corner, quarter]
            target = by_z
        else:
            target = by_x if kind == "x" else by_y
            if of == "more":
                piece = buf.at[slot, mine, level, 3 if kind == "x" else 0]
            elif of == "part":
                piece = buf.at[slot, mine, :, pl.ds(0 if kind == "x" else 1, 3)]
            else:
                piece = buf.at[slot, mine]
        number = names.index(name.removesuffix("_part"))
        return pltpu.make_async_remote_copy(
            src_ref=piece, dst_ref=piece, send_sem=sent.at[number, slot], recv_sem=came.at[number, slot],
            **on_other(**target),
        )

    def shares(chunk):
        return chunk % 3 != 2

    def own_load(weight, block, column, slot):
        source = weight.at[pl.ds(block * 4, 4), :, :, pl.ds(pl.multiple_of(column, lanes), width)]
        return pltpu.make_async_copy(source, buf.at[slot, mine], loaded.at[slot])

    def load(chunk):
        slot = chunk % depth
        for number, ((blocks, wide), first, weight) in enumerate(
            zip(gather_shapes, firsts, weights)
        ):

            @pl.when((chunk >= first) & (chunk < first + blocks * wide))
            def _(number=number, first=first, wide=wide, weight=weight):
                block = (chunk - first) // wide
                column = ((chunk - first) % wide) * width
                if number == 1:
                    column = column + jnp.where(column >= features, lanes, 0)
                own_load(weight, block, column, slot).start()

    def send(chunk):
        own_load(value_ref, 0, 0, chunk % depth).wait()
        both = shares(chunk)
        link("sibling", chunk).start()

        @pl.when(both)
        def _():
            for name in ("x_part", "y_part", "x_more", "y_more"):
                link(name, chunk).start()

        @pl.when(jnp.logical_not(both))
        def _():
            link("x", chunk).start()
            link("y", chunk).start()

    def relay(chunk):
        both = shares(chunk)
        link("sibling", chunk).wait()

        @pl.when(both)
        def _():
            for name in ("x_part", "y_part", "x_more", "y_more"):
                link(name, chunk).wait()
            link("ring0_x", chunk).start()
            link("ring0_y", chunk).start()

        @pl.when(jnp.logical_not(both))
        def _():
            link("x", chunk).wait()
            link("y", chunk).wait()

        link("corner_x", chunk).start()
        link("corner_y", chunk).start()

    def ring(number):
        def phase(chunk):
            if number:
                link(f"ring{number - 1}", chunk).wait()
            else:
                link("corner_x", chunk).wait()
                link("corner_y", chunk).wait()

            @pl.when(shares(chunk))
            def _():
                for of in "xy":
                    link(f"ring{number}_{of}", chunk).wait()
                    if number < 2:
                        link(f"ring{number + 1}_{of}", chunk).start()

            link(f"ring{number}", chunk).start()

        return phase

    def to_sibling(chunk):
        link("ring2", chunk).wait()
        for name in ("sibling_x", "sibling_y", "sibling_corner"):
            link(name, chunk).start()

    def store(chunk, kind):
        return pltpu.make_async_copy(
            (stage_h, stage_l)[kind].at[chunk % 2],
            (w_high, w_low)[kind].at[chunk],
            stored.at[kind, chunk % 2],
        )

    def product(left_h, left_l, right):
        return three((left_h[0], left_l[0]), (right[0][0], right[1][0]), 1, 0) + three(
            (left_h[1], left_l[1]), (right[0][1], right[1][1]), 1, 0
        )

    sequences, block_len = soft.shape[:2]
    states = tables.shape[1]
    decay, weight, block_decay = (tables.at[kind] for kind in range(3))
    features = tokens.shape[1]
    tiles = features // width

    share_ends, to_chips, share_entering, enter_states = state_exchange(
        False, block_decay, ends, chip_ends, halves_in, enter, sent_state, came_state
    )

    def share(kind, numbers):
        sources = (me,) * 4 + (id_x, id_y, id_corner)
        targets = (id_sibling, id_x, id_y, id_corner) + (id_sibling,) * 3
        for number in numbers:
            if kind == 0:
                piece = small.at[sources[number]]
            else:
                piece = shared_w.at[place_of(sources[number])]
            yield pltpu.make_async_remote_copy(
                src_ref=piece, dst_ref=piece, send_sem=sent_all.at[kind, number],
                recv_sem=came_all.at[kind, number], **on_other(seq=targets[number]),
            )

    def own_shared():
        return pltpu.make_async_copy(
            mix_ref.at[:, :, :, pl.ds(features, lanes)], shared_w.at[mine], near
        )

    def row_of(number, k):
        return jnp.concatenate(
            [small[2 * k, number : number + 1], small[2 * k + 1, number : number + 1]], axis=1
        )

    def hand_out():
        own_shared().start()
        small[me] = packed[...]
        for item in share(0, range(4)):
            item.start()
        own_shared().wait()
        for item in share(1, range(4)):
            item.start()

    def pass_on():
        for kind in (0, 1):
            for item in share(kind, range(4)):
                item.wait()
            for item in share(kind, range(4, 7)):
                item.start()

    def norm_one():
        for item in share(0, range(4, 7)):
            item.wait()
        for kind in range(3):
            for n in range(states):
                tables[kind, n] = small[:, kind * states + n]
        keep = row_valid[...]
        value = tokens[...] * keep
        centre = jnp.mean(value, axis=1, keepdims=True)
        shifted = value - centre
        scale = lax.rsqrt(jnp.mean(shifted * shifted, axis=1, keepdims=True) + norm_eps)
        gain = jnp.concatenate([row_of(3 * states, k) for k in range(tiles)], axis=1)
        normed = shifted * scale * gain
        for k in range(tiles):
            span = slice(k * width, (k + 1) * width)
            masked[k] = value[:, span]
            g_out[k] = out_grad[:, span] * keep
            for parity in range(2):
                start = k * width + parity * lanes
                put(normed_h, normed_l, (parity,), k * lanes, normed[:, start : start + lanes])
        for s in range(sequences):
            rows = normed[s * block_len : (s + 1) * block_len]
            signal[s] = rows.reshape(signal.shape[1:])

    def filter_one(s):
        run_filter(False, s, decay, weight, signal, smoothed, ends.at[me % 2])
        if s == sequences - 1:
            share_ends()

    def carry_one(s):
        if s == 0:
            enter_states()
        run_carried(False, s, decay, weight, enter, smoothed, smoothed)

    def mix_in():
        for s in range(sequences):
            span = slice(s * block_len, (s + 1) * block_len)
            skip = jnp.concatenate([row_of(3 * states + 1, k) for k in range(tiles)], axis=1)
            normed = signal[s].reshape(block_len, features)
            value = smoothed[s].reshape(block_len, features) + skip * normed
            mixed = value * jax.nn.sigmoid(value)
            for block in range(8):
                cut = slice(block * lanes, (block + 1) * lanes)
                to = (block % 2, span, slice(block // 2 * lanes, (block // 2 + 1) * lanes))
                mix_pre[to] = value[:, cut]
                mixed_h[to], mixed_l[to] = halves(mixed[:, cut])

    def attention():
        for item in share(1, range(4, 7)):
            item.wait()
        shared_full = halves(shared_w[...].reshape(2, half, lanes))
        total = product(mixed_h, mixed_l, shared_full)
        affine = tree_sum([small[k, 3 * states + 3 : 3 * states + 6] for k in range(8)])
        shared_pre[...] = total
        shared = total * jax.nn.sigmoid(total)
        queries = shared * affine[0:1] + affine[2:3]
        keys = shared * affine[1:2]
        for s in range(sequences):
            span = slice(s * block_len, (s + 1) * block_len)
            scores = contract(queries[span], keys[span], 1, 1, exact) * shared.shape[1] ** (-0.5)
            scores = jnp.where(key_valid[s] > 0.5, scores, masked_score)
            weight = jnp.exp(scores - jnp.max(scores, axis=1, keepdims=True))
            soft[s] = weight / jnp.sum(weight, axis=1, keepdims=True)

    def put(target_h, target_l, index, column, value):
        high, low = halves(value)
        target_h[(*index, slice(None), pl.ds(pl.multiple_of(column, lanes), lanes))] = high
        target_l[(*index, slice(None), pl.ds(pl.multiple_of(column, lanes), lanes))] = low

    def complete(chunk):
        slot = chunk % depth
        for name in ("sibling_x", "sibling_y", "sibling_corner"):
            link(name, chunk).wait()

        @pl.when(chunk >= 2)
        def _():
            store(chunk - 2, 0).wait()
            store(chunk - 2, 1).wait()

        right = halves(buf[slot].reshape(2, half, width))
        stage_h[chunk % 2] = right[0]
        stage_l[chunk % 2] = right[1]
        store(chunk, 0).start()
        store(chunk, 1).start()

        def among(number):
            blocks, wide = gather_shapes[number]
            return (chunk >= firsts[number]) & (chunk < firsts[number] + blocks * wide)

        @pl.when(among(0))
        def _():
            total = product(normed_h, normed_l, right)
            value_pre[chunk] = total
            values = total * jax.nn.sigmoid(total)
            for s in range(sequences):
                span = slice(s * block_len, (s + 1) * block_len)
                attended[chunk, span] = contract(soft[s], values[span], 1, 0, exact)

        @pl.when(among(1))
        def _():
            tile = chunk - firsts[1]
            total = product(mixed_h, mixed_l, right)
            projected[tile] = total

            @pl.when((tile >= 4) & (tile < 12))
            def _():
                block = tile - 4
                gated = attended[block] * total * jax.nn.sigmoid(total)
                for j in range(2):
                    cut = gated[:, j * lanes : (j + 1) * lanes]
                    put(gated_h, gated_l, (j, block % 2), (block // 2) * lanes, cut)

        @pl.when(among(2))
        def _():
            j, tile = (chunk - firsts[2]) // 4, (chunk - firsts[2]) % 4
            total = product(gated_h.at[j], gated_l.at[j], right)

            @pl.when(j == 0)
            def _():
                cand_pre[tile] = projected[12 + tile] + total

            @pl.when(j == 1)
            def _():
                cand_pre[tile] = cand_pre[tile] + total

            @pl.when(chunk == firsts[3] - 1)
            def _():
                total = 0.0
                for k in range(tiles):
                    cand = cand_pre[k]
                    cand = cand * jax.nn.sigmoid(cand)
                    value = masked[k] + jax.nn.sigmoid(projected[k]) * (cand - masked[k])
                    middle[k] = value
                    total = total + jnp.sum(value, axis=1, keepdims=True)
                centre = total / features
                total = 0.0
                for k in range(tiles):
                    shifted = middle[k] - centre
                    total = total + jnp.sum(shifted * shifted, axis=1, keepdims=True)
                scale = lax.rsqrt(total / features + norm_eps)
                for k in range(tiles):
                    value = (middle[k] - centre) * scale * row_of(3 * states + 2, k)
                    for parity in range(2):
                        cut = value[:, parity * lanes : (parity + 1) * lanes]
                        put(two_h, two_l, (parity,), k * lanes, cut)
                block_out[...] = jnp.zeros(block_out.shape, jnp.float32)
                g_hidden[...] = jnp.zeros(g_hidden.shape, jnp.float32)

        @pl.when(among(3))
        def _():
            tile = chunk - firsts[3]
            total = product(two_h, two_l, right)
            g_wide[tile] = total
            hidden = total * jax.nn.sigmoid(total)
            for i in range(2):
                cut = hidden[:, i * lanes : (i + 1) * lanes]
                index = (2 * (tile % 2) + i, (tile // 2) % 2)
                put(hidden_h, hidden_l, index, (tile // 4) * lanes, cut)

        @pl.when(among(4))
        def _():
            j, tile = (chunk - firsts[4]) // 4, (chunk - firsts[4]) % 4
            to = (slice(None), pl.ds(pl.multiple_of(tile * width, width), width))
            block_out[to] = block_out[to] + product(hidden_h.at[j], hidden_l.at[j], right)
            grad = halves(g_out[tile])
            for parity in range(2):
                back = three(grad, (right[0][parity], right[1][parity]), 1, 1)
                g_hidden[j, parity] = g_hidden[j, parity] + back

    def save(*numbers):
        return [
            pltpu.make_async_copy(held[number], kept[number], saved.at[number]) for number in numbers
        ]

    def begin_save(*numbers):
        for item in save(*numbers):
            item.start()

    phases = (
        (2, relay), (4, ring(0)), (6, ring(1)), (8, ring(2)), (10, to_sibling), (11, complete)
    )
    last, ahead = phases[-1][0], 1

    def step(at, carry):
        for after, phase in phases[-2::-1]:

            @pl.when((at >= after) & (at < after + chunks))
            def _(after=after, phase=phase):
                phase(at - after)

        @pl.when(at == 0)
        def _():
            for chunk in range(ahead):
                send(chunk)
            hand_out()

        pl.when((at >= 1) & (at + ahead - 1 < chunks))(lambda: send(at + ahead - 1))
        pl.when(at + ahead < chunks)(lambda: load(at + ahead))
        pl.when(at == 1)(pass_on)
        pl.when(at == 2)(norm_one)
        for s in range(sequences):
            pl.when(at == 3 + s)(functools.partial(filter_one, s))
            pl.when(at == 8 + s)(functools.partial(carry_one, s))
        pl.when(at == 5)(to_chips)
        pl.when(at == 7)(share_entering)

        @pl.when(at == 10)
        def _():
            mix_in()
            attention()

        pl.when(at == last)(lambda: begin_save(2, 8, 9, 10, 11, 16, 17, 19, 20, 21, 22, 23, 24))
        pl.when(at == last + firsts[3])(lambda: begin_save(4, 5, 6, 7, 12, 13, 14, 15, 18))
        pl.when(at == last + firsts[4])(lambda: begin_save(0, 1))

        @pl.when(at >= last)
        def _():
            complete(at - last)

        return carry

    for chunk in range(ahead):
        load(chunk)
    lax.fori_loop(0, chunks + last, step, 0)
    for chunk in (chunks - 2, chunks - 1):
        for kind in range(2):
            store(chunk, kind).wait()
    for k in range(tiles):
        span = slice(k * width, (k + 1) * width)
        block_out[:, span] = (middle[k] + block_out[:, span]) * row_valid[...]
    for k in range(g_wide.shape[0]):
        for i in range(2):
            span = slice(i * lanes, (i + 1) * lanes)
            back = g_hidden[2 * (k % 2) + i, (k // 2) % 2, :, (k // 4) * lanes : (k // 4 + 1) * lanes]
            wide = g_wide[k, :, span]
            g_wide[k, :, span] = back * silu_slope(wide)
    begin_save(3)
    for item in save(*range(kept_count)):
        item.wait()


def f32(*shape):
    return jax.ShapeDtypeStruct(shape, jnp.float32)


def b16(*shape):
    return jax.ShapeDtypeStruct(shape, jnp.bfloat16)


def call_forward(weights, packed, tokens, out_grad, row_valid, key_valid, states):
    width, half = 2 * lanes, 4 * lanes
    rows, features = tokens.shape
    sequences = key_valid.shape[0]
    block_len = rows // sequences
    _, chunks = chunk_table(gather_shapes)
    vmem, anywhere = pl.BlockSpec(memory_space=pltpu.VMEM), pl.BlockSpec(memory_space=pl.ANY)
    line = (sequences, block_len, 8, lanes)
    kept = [
        b16(4, 2, rows, half), b16(4, 2, rows, half), f32(4, rows, width), f32(16, rows, width),
        b16(2, rows, half), b16(2, rows, half), b16(2, 2, rows, half), b16(2, 2, rows, half),
        b16(2, rows, half), b16(2, rows, half), b16(2, rows, half), b16(2, rows, half),
        f32(8, rows, width), f32(16, rows, width), f32(4, rows, width), f32(8, rows, width), f32(rows, lanes),
        f32(sequences, block_len, block_len), f32(4, rows, width), f32(4, rows, width), f32(*line),
        f32(sequences, states, 8, lanes), f32(2, rows, half), f32(8, *packed.shape), f32(8, 4, 4, 8, lanes),
    ]
    shapes = [f32(rows, features)] + [b16(chunks, 2, half, width)] * 2 + kept
    depth, kinds = 16, 19
    return pl.pallas_call(
        forward_body,
        out_shape=shapes,
        in_specs=[anywhere] * len(weights) + [vmem] * 5,
        out_specs=[vmem] + [anywhere] * (len(shapes) - 1),
        scratch_shapes=[pltpu.VMEM(item.shape, item.dtype) for item in kept]
        + [
            pltpu.VMEM((depth, 8, 4, 4, 8, width), jnp.float32),
            pltpu.VMEM((2, 2, half, width), jnp.bfloat16),
            pltpu.VMEM((2, 2, half, width), jnp.bfloat16),
            pltpu.VMEM((4, 2, rows, half), jnp.float32),
            pltpu.VMEM(line, jnp.float32),
            pltpu.VMEM((2, sequences, states, 8, lanes), jnp.float32),
            pltpu.VMEM((4, sequences, states // 2, 8, lanes), jnp.float32),
            pltpu.VMEM((2, sequences, states // 2, 8, lanes), jnp.float32),
            pltpu.VMEM((3, states, 8, lanes), jnp.float32),
            pltpu.SemaphoreType.DMA((depth,)),
            pltpu.SemaphoreType.DMA((kinds, depth)),
            pltpu.SemaphoreType.DMA((kinds, depth)),
            pltpu.SemaphoreType.DMA((2, 2)),
            pltpu.SemaphoreType.DMA,
            pltpu.SemaphoreType.DMA((2, 7)),
            pltpu.SemaphoreType.DMA((2, 7)),
            pltpu.SemaphoreType.DMA((5,)),
            pltpu.SemaphoreType.DMA((5,)),
            pltpu.SemaphoreType.DMA((kept_count,)),
        ],
        compiler_params=pltpu.CompilerParams(
            collective_id=2, has_side_effects=True, vmem_limit_bytes=62 * 1024 * 1024
        ),
    )(*[w.reshape(-1, 4, 8, w.shape[1]) for w in weights], packed, tokens, out_grad, row_valid, key_valid)


reduce_shapes = ((4, 4), (1, 16), (2, 4), (1, 16), (1, 8))


def backward_body(
    row_valid, key_valid, w_high, w_low, *refs,
):
    kept, outs, refs = refs[:kept_count], refs[kept_count : kept_count + 7], refs[kept_count + 7 :]
    held, refs = refs[:kept_count], refs[kept_count:]
    (
        hidden_h, hidden_l, g_out, g_wide, two_h, two_l, gated_h, gated_l, mixed_h, mixed_l, normed_h, normed_l,
        value_pre, projected, middle, attended, shared_pre, soft, cand_pre, masked, signal, enter, mix_pre, small, shared_w,
    ) = held
    tokens_grad, narrow_grad, widen_grad, merge_grad, mix_grad, value_grad, small_grad = outs
    away, keep, got, got_x, got_y, got_xy, got_yx, part, from_edge, from_inner, done = refs[:11]
    buf_h, buf_l, g_two, g_gated, g_mixed, g_normed, g_soft, g_shared = refs[11:19]
    smooth, back, ends, chip_ends, halves_in, back_enter, tables, direct, slope, last, small_sum = refs[19:30]
    fetched, read, sent, came, written, sent_state, came_state = refs[30:]
    lefts = (
        (hidden_h, hidden_l), (two_h, two_l), (gated_h, gated_l), (mixed_h, mixed_l), (normed_h, normed_l)
    )
    rights = ((g_out, 0), (g_wide, 0), (projected, 12), (projected, 0), (value_pre, 0))
    grads = (narrow_grad, widen_grad, merge_grad, mix_grad, value_grad)
    firsts, chunks = chunk_table(reduce_shapes)
    gathered, _ = chunk_table(gather_shapes)
    tiles, rows, width = masked.shape
    half, features = 4 * lanes, tiles * width
    sequences, block_len = soft.shape[:2]
    states = tables.shape[1]
    decay, weight, block_decay = (tables.at[kind] for kind in range(3))
    me, level = lax.axis_index("seq"), lax.axis_index("batch")
    core, along_x, along_y = me % 2, (me // 2) % 2, me // 4
    is_edge = (level == 0) | (level == 3)
    partner = jnp.where(level < 2, 1 - level, 5 - level)
    near = others_of(me)
    sibling, across_x, across_y = ({"seq": other} for other in near[:3])

    copies_in = [
        pltpu.make_async_copy(source, target, read.at[number])
        for number, (source, target) in enumerate(zip(kept, held))
    ]
    for item in copies_in:
        item.start()

    barrier = pltpu.get_barrier_semaphore()
    for other in near:
        pl.semaphore_signal(barrier, inc=1, **on_other(seq=other))
    pl.semaphore_signal(barrier, inc=1, **on_other(batch=partner))

    @pl.when(jnp.logical_not(is_edge))
    def _():
        pl.semaphore_signal(barrier, inc=1, **on_other(batch=3 - level))
        pl.semaphore_wait(barrier, 6)

    @pl.when(is_edge)
    def _():
        pl.semaphore_wait(barrier, 5)

    def slot_in(ref, chunk):
        return chunk % ref.shape[0]

    def link(kind, chunk):
        def at(ref, *index):
            return ref.at[(slot_in(ref, chunk), *index)]

        source, target, device = (
            lambda: (at(away), at(got), sibling),
            lambda: (at(keep, slice(None), 1 - along_x, 0), at(got_x), across_x),
            lambda: (at(keep, 1 - along_y, slice(None), 1), at(got_y), across_y),
            lambda: (at(got_x, 1 - along_y), at(got_xy), across_y),
            lambda: (at(got_y, 1 - along_x), at(got_yx), across_x),
            lambda: (at(part), at(from_edge), {"batch": partner}),
            lambda: (at(part), at(from_inner), {"batch": 3 - level}),
        )[kind]()
        slot = chunk % sent.shape[1]
        return pltpu.make_async_remote_copy(
            src_ref=source, dst_ref=target, send_sem=sent.at[kind, slot], recv_sem=came.at[kind, slot],
            **on_other(**device),
        )

    def results(chunk, call):
        slot, at = slot_in(done, chunk), chunk % sent.shape[1]

        def pieces(number, source, target):
            yield lambda: pltpu.make_async_copy(source, target, written.at[number, at])
            yield lambda: pltpu.make_async_remote_copy(
                src_ref=source, dst_ref=target,
                send_sem=sent.at[7 + number, at], recv_sem=came.at[7 + number, at],
                **on_other(batch=partner),
            )

        for number, ((blocks, wide), first, grad) in enumerate(zip(reduce_shapes, firsts, grads)):

            @pl.when((chunk >= first) & (chunk < first + blocks * wide))
            def _(number=number, first=first, wide=wide, grad=grad):
                row = ((chunk - first) // wide) * lanes
                column = ((chunk - first) % wide) * width
                if number == 3:
                    column = column + jnp.where(column >= features, lanes, 0)
                target = grad.at[
                    pl.ds(pl.multiple_of(row, lanes), lanes),
                    pl.ds(pl.multiple_of(column, lanes), width),
                ]
                call(*pieces(0, done.at[slot], target))

        @pl.when(chunk == chunks)
        def _():
            target = mix_grad.at[:, pl.ds(features, lanes)]
            call(*pieces(0, done.at[slot, :, pl.ds(0, lanes)], target))
            call(*pieces(1, done.at[slot, :, pl.ds(lanes, lanes)], small_grad))

    def begin(chunk):
        slot, to = slot_in(away, chunk), slot_in(keep, chunk)
        for (blocks, wide), first, (high, low), (right, shift) in zip(
            reduce_shapes, firsts, lefts, rights
        ):

            @pl.when((chunk >= first) & (chunk < first + blocks * wide))
            def _(first=first, wide=wide, shift=shift, high=high, low=low, right=right):
                block = (chunk - first) // wide
                other, rest = halves(right[shift + (chunk - first) % wide])

                def product(parity):
                    top, under = (
                        (high[block, parity], low[block, parity])
                        if len(high.shape) == 4
                        else (high[parity], low[parity])
                    )
                    total = turned(top, other) + (turned(under, other) + turned(top, rest))
                    return total.reshape(away.shape[1:])

                away[slot] = product(1 - core)
                link(0, chunk).start()
                keep[to] = product(core)

        @pl.when(chunk == chunks)
        def _():
            right = halves(g_shared[...])

            def fill(ref, at, parity):
                total = three((mixed_h[parity], mixed_l[parity]), right, 0, 0)
                total = total.reshape(*away.shape[1:-1], lanes)
                sums = [small_sum[2 * q + parity].reshape(2, -1, lanes) for q in range(4)]
                sums = jnp.stack(sums, axis=0).reshape(total.shape)
                ref[at] = jnp.concatenate([total, sums], axis=-1)

            fill(away, slot, 1 - core)
            link(0, chunk).start()
            fill(keep, to, core)

    def with_sibling(chunk):
        slot = slot_in(keep, chunk)
        link(0, chunk).wait()
        keep[slot] = keep[slot] + got[slot_in(got, chunk)]
        link(1, chunk).start()
        link(2, chunk).start()

    def with_neighbour(chunk):
        slot = slot_in(got_x, chunk)
        link(1, chunk).wait()
        link(2, chunk).wait()
        from_slot = slot_in(keep, chunk)
        got_x[slot] = got_x[slot] + keep[from_slot, :, along_x, 0]
        got_y[slot] = got_y[slot] + keep[from_slot, along_y, :, 1]
        link(3, chunk).start()
        link(4, chunk).start()

    def with_corner(chunk):
        slot = slot_in(part, chunk)
        link(3, chunk).wait()
        link(4, chunk).wait()
        first, second = slot_in(got_x, chunk), slot_in(got_xy, chunk)
        part[slot, 0] = got_x[first, along_y] + got_xy[second]
        part[slot, 1] = got_y[first, along_x] + got_yx[second]
        pl.when(is_edge)(lambda: link(5, chunk).start())

    def inner_sum(chunk):
        slot = slot_in(part, chunk)
        pl.when(is_edge)(lambda: link(5, chunk).wait_send())

        @pl.when(jnp.logical_not(is_edge))
        def _():
            link(5, chunk).wait_recv()
            part[slot] = part[slot] + from_edge[slot]
            link(6, chunk).start()

    def total_sum(chunk):
        slot = slot_in(part, chunk)

        @pl.when(jnp.logical_not(is_edge))
        def _():
            link(6, chunk).wait()
            done[slot] = (part[slot] + from_inner[slot]).reshape(done.shape[1:])

            def start(stay, go):
                stay().start()
                go().start()

            results(chunk, start)

    def finish(chunk):
        def receive(stay, go):
            go().wait_recv()

        def release(stay, go):
            stay().wait()
            go().wait_send()

        pl.when(is_edge)(lambda: results(chunk, receive))
        pl.when(jnp.logical_not(is_edge))(lambda: results(chunk, release))

    steps = 48

    def fetch(step, call):
        chunk = jnp.where(
            step < 16, gathered[3] + step, jnp.where(step < 24, step + 8, jnp.where(step < 40, step - 16, step - 40))
        )
        slot = slot_in(buf_h, step)
        for kind, (source, target) in enumerate(((w_high, buf_h), (w_low, buf_l))):
            item = pltpu.make_async_copy(source.at[chunk], target.at[slot], fetched.at[kind, slot])
            getattr(item, call)()

    def back_product(grad, step, parity):
        slot = slot_in(buf_h, step)
        return three(halves(grad), (buf_h[slot, parity], buf_l[slot, parity]), 1, 1)

    def row_of(number, k):
        return jnp.concatenate(
            [small[2 * k, number : number + 1], small[2 * k + 1, number : number + 1]], axis=1
        )

    def put_row(number, k, value):
        for i in range(2):
            small_sum[2 * k + i, number : number + 1] = value[:, i * lanes : (i + 1) * lanes]

    def statistics(ref):
        total = 0.0
        for k in range(tiles):
            total = total + jnp.sum(ref[k], axis=1, keepdims=True)
        centre = total / features
        total = 0.0
        for k in range(tiles):
            shifted = ref[k] - centre
            total = total + jnp.sum(shifted * shifted, axis=1, keepdims=True)
        return centre, lax.rsqrt(total / features + norm_eps)

    def norm_two_back():
        centre, scale = statistics(middle)

        def grad_of(k):
            span = slice(k * lanes, (k + 1) * lanes)
            return jnp.concatenate([g_two[0, :, span], g_two[1, :, span]], axis=1)

        plain, crossed = 0.0, 0.0
        for k in range(tiles):
            grad, hat = grad_of(k), (middle[k] - centre) * scale
            put_row(2 * states + 2, k, jnp.sum(grad * hat, axis=0, keepdims=True))
            inner = grad * row_of(3 * states + 2, k)
            plain = plain + jnp.sum(inner, axis=1, keepdims=True)
            crossed = crossed + jnp.sum(inner * hat, axis=1, keepdims=True)
        plain, crossed = plain / features, crossed / features
        for k in range(tiles):
            inner, hat = grad_of(k) * row_of(3 * states + 2, k), (middle[k] - centre) * scale
            g_middle = g_out[k] + (inner - plain - hat * crossed) * scale
            update = jax.nn.sigmoid(projected[k])
            pre = cand_pre[k]
            gate = jax.nn.sigmoid(pre)
            middle[k] = g_middle * (1.0 - update)
            projected[k] = g_middle * (pre * gate - masked[k]) * update * (1.0 - update)
            projected[12 + k] = g_middle * update * (gate * (1.0 + pre * (1.0 - gate)))

    def attention_back(m):
        parity, start = m % 2, pl.multiple_of((m // 2) * lanes, lanes)
        grad = jnp.concatenate(
            [g_gated[0, parity, :, pl.ds(start, lanes)], g_gated[1, parity, :, pl.ds(start, lanes)]], axis=1
        )
        pre = projected[4 + m]
        gate = jax.nn.sigmoid(pre)
        g_attended = grad * pre * gate
        projected[4 + m] = grad * attended[m] * (gate * (1.0 + pre * (1.0 - gate)))
        pre = value_pre[m]
        gate = jax.nn.sigmoid(pre)
        values, bend = pre * gate, gate * (1.0 + pre * (1.0 - gate))
        g_values = []
        for s in range(sequences):
            span = slice(s * block_len, (s + 1) * block_len)
            own = halves(g_attended[span])
            g_soft[s] = g_soft[s] + three(own, halves(values[span]), 1, 1)
            g_values.append(three(halves(soft[s]), own, 0, 0) * bend[span])
        value_pre[m] = jnp.concatenate(g_values, axis=0)

    def scores_back():
        affine = tree_sum([small[k, 3 * states + 3 : 3 * states + 6] for k in range(8)])
        pre = shared_pre[...]
        gate = jax.nn.sigmoid(pre)
        shared, bend = pre * gate, gate * (1.0 + pre * (1.0 - gate))
        score_scale = shared.shape[1] ** (-0.5)
        queries = shared * affine[0:1] + affine[2:3]
        keys = shared * affine[1:2]
        sums = [0.0, 0.0, 0.0]
        for s in range(sequences):
            span = slice(s * block_len, (s + 1) * block_len)
            soft_weight, grad = soft[s], g_soft[s]
            g_scores = soft_weight * (grad - jnp.sum(grad * soft_weight, axis=1, keepdims=True))
            g_scores = jnp.where(key_valid[s] > 0.5, g_scores, 0.0) * score_scale
            g_queries = contract(g_scores, keys[span], 1, 0, exact)
            g_keys = contract(g_scores, queries[span], 0, 0, exact)
            g_shared[span] = (g_queries * affine[0:1] + g_keys * affine[1:2]) * bend[span]
            terms = (g_queries * shared[span], g_keys * shared[span], g_queries)
            for number, term in enumerate(terms):
                sums[number] = sums[number] + jnp.sum(term, axis=0, keepdims=True)
        for number in range(3):
            for k in range(8):
                row = 2 * states + 3 + number
                small_sum[k, row : row + 1] = sums[number]
        own, full = halves(g_shared[...]), halves(shared_w[...].reshape(2, half, lanes))
        for parity in range(2):
            g_mixed[parity] = three(own, (full[0][parity], full[1][parity]), 1, 1)

    def smooth_back():
        for kind in range(3):
            for n in range(states):
                tables[kind, n] = small[:, kind * states + n]
        for parity in range(2):
            pre = mix_pre[parity]
            g_mixed[parity] = g_mixed[parity] * silu_slope(pre)
        for s in range(sequences):
            span = slice(s * block_len, (s + 1) * block_len)
            blocks = [
                g_mixed[block % 2, span, block // 2 * lanes : (block // 2 + 1) * lanes]
                for block in range(8)
            ]
            smooth[s] = jnp.concatenate(blocks, axis=1).reshape(smooth.shape[1:])

    share_ends, to_chips, share_entering, enter_states = state_exchange(
        True, block_decay, ends, chip_ends, halves_in, back_enter, sent_state, came_state
    )

    def filter_one(s):
        run_filter(True, s, decay, weight, smooth, back, ends.at[core])
        if s == sequences - 1:
            share_ends()

    def moments_one(s, low):
        run_moments(s, low, low + 8, decay, enter, signal, smooth, direct, slope, last)

    def carry_one(s):
        if s == 0:
            enter_states()
        run_carried(True, s, decay, weight, back_enter, back, back)

    def norm_one_back():
        for n in range(states):
            total = slope[n]
            for s in range(sequences):
                total = total + decay[n] * back_enter[s, n] * last[s, n]
            small_sum[:, n] = direct[n]
            small_sum[:, states + n] = total
        centre, scale = statistics(masked)
        line = [back[s].reshape(block_len, features) for s in range(sequences)]
        line = jnp.concatenate(line, axis=0)

        def blocks(ref, k):
            span = slice(k * lanes, (k + 1) * lanes)
            return jnp.concatenate([ref[0, :, span], ref[1, :, span]], axis=1)

        plain, crossed = 0.0, 0.0
        for k in range(tiles):
            g_smooth, hat = blocks(g_mixed, k), (masked[k] - centre) * scale
            gain = row_of(3 * states, k)
            grad = blocks(g_normed, k) + g_smooth * row_of(3 * states + 1, k)
            grad = grad + line[:, k * width : (k + 1) * width]
            put_row(2 * states, k, jnp.sum(grad * hat, axis=0, keepdims=True))
            put_row(2 * states + 1, k, jnp.sum(g_smooth * (hat * gain), axis=0, keepdims=True))
            inner = grad * gain
            plain = plain + jnp.sum(inner, axis=1, keepdims=True)
            crossed = crossed + jnp.sum(inner * hat, axis=1, keepdims=True)
            tokens_grad[:, k * width : (k + 1) * width] = inner
        plain, crossed = plain / features, crossed / features
        for k in range(tiles):
            span = slice(k * width, (k + 1) * width)
            hat = (masked[k] - centre) * scale
            g_x = (tokens_grad[:, span] - plain - hat * crossed) * scale
            tokens_grad[:, span] = (middle[k] + g_x) * row_valid[...]

    g_two[...] = jnp.zeros(g_two.shape, jnp.float32)
    g_gated[...] = jnp.zeros(g_gated.shape, jnp.float32)
    g_normed[...] = jnp.zeros(g_normed.shape, jnp.float32)
    g_soft[...] = jnp.zeros(g_soft.shape, jnp.float32)
    small_sum[...] = jnp.zeros(small_sum.shape, jnp.float32)

    def work(at):
        @pl.when((at < 24) | ((at >= 32) & (at < 56)))
        def _():
            step = jnp.where(at < 24, at, at - 8)
            pl.when(step + 2 < steps)(lambda: fetch(step + 2, "start"))
            fetch(step, "wait")

            @pl.when(at < 16)
            def _():
                for parity in range(2):
                    g_two[parity] = g_two[parity] + back_product(g_wide[at], step, parity)

            pl.when(at == 16)(norm_two_back)

            @pl.when((at >= 16) & (at < 24))
            def _():
                j = (at - 16) // 4
                for parity in range(2):
                    more = back_product(projected[12 + at % 4], step, parity)
                    g_gated[j, parity] = g_gated[j, parity] + more

            pl.when(at == 32)(scores_back)

            @pl.when((at >= 32) & (at < 48))
            def _():
                for parity in range(2):
                    more = back_product(projected[at - 32], step, parity)
                    g_mixed[parity] = g_mixed[parity] + more

            @pl.when(at >= 48)
            def _():
                for parity in range(2):
                    more = back_product(value_pre[at - 48], step, parity)
                    g_normed[parity] = g_normed[parity] + more

        pl.when((at >= 24) & (at < 32))(lambda: attention_back(at - 24))
        pl.when(at == 48)(smooth_back)
        for s in range(sequences):
            pl.when(at == 49 + s)(functools.partial(filter_one, s))
            for low in range(0, states, 8):
                number = 51 + s * (states // 8) + low // 8
                pl.when(at == number)(functools.partial(moments_one, s, low))
            pl.when(at == 56 + s)(functools.partial(carry_one, s))
        pl.when(at == 52)(to_chips)
        pl.when(at == 54)(share_entering)
        pl.when(at == 59)(norm_one_back)

    phases = (
        (0, begin), (1, with_sibling), (3, with_neighbour), (5, with_corner), (7, inner_sum), (9, total_sum), (11, finish)
    )
    fetch(0, "start")
    fetch(1, "start")

    def arrive(first, end):
        for item in copies_in[first:end]:
            item.wait()

    arrive(0, 3)

    def step(at, carry):
        for after, phase in phases[::-1]:

            @pl.when((at >= after) & (at <= after + chunks))
            def _(after=after, phase=phase):
                phase(at - after)

        pl.when(at == 0)(lambda: arrive(3, 4))
        pl.when(at == 8)(lambda: arrive(4, kept_count))
        work(at)
        return carry

    lax.fori_loop(0, chunks + 1 + phases[-1][0], step, 0)


def call_backward(row_valid, key_valid, w_high, w_low, kept, grad_shapes):
    _, rows, width = kept[3].shape
    soft, signal, enter = kept[17], kept[20], kept[21]
    states = enter.shape[1]
    half, piece, depth = 4 * lanes, lanes // 2, 8
    vmem, anywhere = pl.BlockSpec(memory_space=pltpu.VMEM), pl.BlockSpec(memory_space=pl.ANY)
    shapes = [f32(rows, 8 * lanes)] + [f32(*shape) for shape in grad_shapes] + [f32(lanes, lanes)]
    held = [
        (4, 2, 2, 2, piece, width), (6, 2, 2, 2, piece, width), (4, 2, 2, 2, piece, width),
        (9, 2, piece, width), (9, 2, piece, width), (depth, piece, width), (depth, piece, width),
        (depth, 2, piece, width), (depth, 2, piece, width), (depth, 2, piece, width), (depth, lanes, width),
    ]
    more = [
        (2, rows, half), (2, 2, rows, half), (2, rows, half), (2, rows, half), soft.shape, (rows, lanes),
        signal.shape, signal.shape, (2, *enter.shape), (4, enter.shape[0], states // 2, 8, lanes),
        (2, enter.shape[0], states // 2, 8, lanes), enter.shape, (3, states, 8, lanes),
        (states, 8, lanes), (states, 8, lanes), enter.shape, (8, lanes, lanes),
    ]
    return pl.pallas_call(
        backward_body,
        out_shape=shapes,
        in_specs=[vmem] * 2 + [anywhere] * (2 + kept_count),
        out_specs=[vmem] + [anywhere] * (len(shapes) - 1),
        scratch_shapes=[pltpu.VMEM(item.shape, item.dtype) for item in kept]
        + [pltpu.VMEM(shape, jnp.float32) for shape in held]
        + [pltpu.VMEM((3, 2, half, width), jnp.bfloat16)] * 2
        + [pltpu.VMEM(shape, jnp.float32) for shape in more]
        + [
            pltpu.SemaphoreType.DMA((2, 3)),
            pltpu.SemaphoreType.DMA((kept_count,)),
            pltpu.SemaphoreType.DMA((9, depth)),
            pltpu.SemaphoreType.DMA((9, depth)),
            pltpu.SemaphoreType.DMA((2, depth)),
            pltpu.SemaphoreType.DMA((5,)),
            pltpu.SemaphoreType.DMA((5,)),
        ],
        compiler_params=pltpu.CompilerParams(
            collective_id=1, has_side_effects=True, vmem_limit_bytes=62 * 1024 * 1024
        ),
    )(row_valid, key_valid, w_high, w_low, *kept)


def call_kernel(body, shapes, *operands):
    return pl.pallas_call(
        body,
        out_shape=[jax.ShapeDtypeStruct(shape, jnp.float32) for shape in shapes],
        in_specs=[pl.BlockSpec(memory_space=pltpu.VMEM)] * len(operands),
        out_specs=[pl.BlockSpec(memory_space=pltpu.VMEM)] * len(shapes),
        compiler_params=pltpu.CompilerParams(vmem_limit_bytes=32 * 1024 * 1024),
    )(*operands)


def entering(ends, block_decay, backward):
    count, mine = lax.axis_size("seq"), lax.axis_index("seq")
    pieces = lax.all_gather(ends, "seq")
    if backward:
        mine = count - 1 - mine
    total = jnp.zeros_like(ends)
    for position in range(count - 1):
        piece = pieces[count - 1 - position if backward else position]
        total = jnp.where(position < mine, block_decay * total + piece, total)
    return total


def silu(value):
    return value * jax.nn.sigmoid(value)


def silu_slope(value):
    gate = jax.nn.sigmoid(value)
    return gate * (1.0 + value * (1.0 - gate))


def normalise(signal):
    centre = jnp.mean(signal, axis=-1, keepdims=True)
    shifted = signal - centre
    spread = jnp.mean(shifted * shifted, axis=-1, keepdims=True)
    scale = lax.rsqrt(spread + norm_eps)
    return shifted * scale, scale


def normalise_back(grad, gain, hat, scale):
    inner = grad * gain
    return (
        inner
        - jnp.mean(inner, axis=-1, keepdims=True)
        - hat * jnp.mean(inner * hat, axis=-1, keepdims=True)
    ) * scale


def times(left, right):
    return jnp.dot(left, right, precision=triple)


def times_back(left, right):
    return lax.dot_general(left, right, (((1,), (1,)), ((), ())), precision=triple)


def plain_layer(masked_in, normed, mix_pre, g_out, row_valid, key_valid, affine, gain_two, weights):
    value_full, mix_full, merge_full, widen_full, narrow_full = (gather_rows(w) for w in weights)
    rows, width = masked_in.shape
    sequences, _, block_len = key_valid.shape
    value_dim, shared_dim = value_full.shape[1], affine.shape[0]
    mixed = silu(mix_pre)
    value_pre = times(normed, value_full)
    values = silu(value_pre)
    projected = times(mixed, mix_full)
    second_cut = width + shared_dim
    third_cut = second_cut + value_dim
    update = jax.nn.sigmoid(projected[:, :width])
    shared_pre = projected[:, width:second_cut]
    reset_pre = projected[:, second_cut:third_cut]
    shared = silu(shared_pre)
    reset_gate = silu(reset_pre)
    queries = (shared * affine[:, 0] + affine[:, 2]).reshape(sequences, block_len, shared_dim)
    key_rows = (shared * affine[:, 1]).reshape(sequences, block_len, shared_dim)
    score_scale = shared_dim ** (-0.5)
    scores = jnp.einsum("cqz,ckz->cqk", queries, key_rows, precision=exact) * score_scale
    scores = jnp.where(key_valid > 0.5, scores, masked_score)
    soft = jax.nn.softmax(scores, axis=-1)
    values_cut = values.reshape(sequences, block_len, value_dim)
    attended = jnp.einsum("cqk,ckv->cqv", soft, values_cut, precision=triple)
    attended = attended.reshape(rows, value_dim)
    gated = attended * reset_gate
    cand_pre = projected[:, third_cut:] + times(gated, merge_full)
    candidate = silu(cand_pre)
    middle = masked_in + update * (candidate - masked_in)
    hat_two, scale_two = normalise(middle)
    normed_two = hat_two * gain_two
    wide_pre = times(normed_two, widen_full)
    hidden = silu(wide_pre)
    block_out = (middle + times(hidden, narrow_full)) * row_valid

    g_wide = times_back(g_out, narrow_full) * silu_slope(wide_pre)
    g_normed_two = times_back(g_wide, widen_full)
    gain_sum = jnp.sum(g_normed_two * hat_two, axis=0)
    g_middle = g_out + normalise_back(g_normed_two, gain_two, hat_two, scale_two)
    g_cand = g_middle * update * silu_slope(cand_pre)
    g_gated = times_back(g_cand, merge_full)
    g_attended = (g_gated * reset_gate).reshape(sequences, block_len, value_dim)
    g_soft = jnp.einsum("cqv,ckv->cqk", g_attended, values_cut, precision=triple)
    g_values = jnp.einsum("cqk,cqv->ckv", soft, g_attended, precision=triple)
    g_scores = soft * (g_soft - jnp.sum(g_soft * soft, axis=-1, keepdims=True))
    g_scores = jnp.where(key_valid > 0.5, g_scores, 0.0) * score_scale
    g_queries = jnp.einsum("cqk,ckz->cqz", g_scores, key_rows, precision=exact)
    g_keys = jnp.einsum("cqk,cqz->ckz", g_scores, queries, precision=exact)
    g_queries = g_queries.reshape(rows, shared_dim)
    g_keys = g_keys.reshape(rows, shared_dim)
    terms = (g_queries * shared, g_keys * shared, g_queries)
    affine_sum = jnp.stack([jnp.sum(term, axis=0) for term in terms])
    g_shared = (g_queries * affine[:, 0] + g_keys * affine[:, 1]) * silu_slope(shared_pre)
    g_update = g_middle * (candidate - masked_in) * update * (1.0 - update)
    g_reset = g_gated * attended * silu_slope(reset_pre)
    g_projected = jnp.concatenate([g_update, g_shared, g_reset, g_cand], axis=1)
    g_mixed = times_back(g_projected, mix_full)
    g_val = g_values.reshape(rows, value_dim) * silu_slope(value_pre)
    g_from_values = times_back(g_val, value_full)

    def total(packed):
        count = lax.axis_size("seq")
        features = packed.shape[1] // count

        def reduced(whole, tiled=True):
            part = lax.psum_scatter(whole, "seq", scatter_dimension=0, tiled=tiled)
            return lax.psum(part, "batch")

        pairs = (
            (normed, g_val),
            (mixed, g_projected),
            (gated, g_cand),
            (normed_two, g_wide),
            (hidden, g_out),
        )
        grads = tuple(reduced(product_grad(*pair)) for pair in pairs)
        blocks = packed.reshape(-1, count, features).transpose(1, 0, 2)
        return grads + (reduced(blocks, False),)

    return block_out, g_mixed, g_from_values, g_middle * (1.0 - update), gain_sum, affine_sum, total


def plane_layer(tokens, out_grad, valid, logits, rows_of, affine, weights):
    sequences, block_len, width = tokens.shape
    rows = sequences * block_len
    states, own = logits[0].shape
    device = lax.axis_index("seq")
    alpha, delta, beta, gamma = logits
    alpha_rate, damp_rate = jax.nn.sigmoid(alpha), jax.nn.sigmoid(delta)
    out_scale = states ** (-0.5)
    weight = alpha_rate * beta * gamma * out_scale
    block_decay = jnp.exp(block_len * jnp.log1p(-alpha_rate * damp_rate))
    spread = lax.dynamic_update_slice(
        jnp.zeros((3, own), jnp.float32), affine.T, (0, device * affine.shape[0])
    )
    packed = jnp.concatenate([1.0 - alpha_rate * damp_rate, weight, block_decay, rows_of, spread])
    packed = jnp.pad(packed, ((0, -packed.shape[0] % 8), (0, 0)))
    row_valid = valid.reshape(rows, 1)
    key_valid = valid.reshape(sequences, 1, block_len)
    block_out, w_high, w_low, *kept = call_forward(
        weights, packed, tokens.reshape(rows, width), out_grad.reshape(rows, width), row_valid, key_valid, states
    )
    value_weight, mix_weight, merge_weight, widen_weight, narrow_weight = weights
    tokens_grad, narrow, widen, merge, mix, value, sums = call_backward(
        row_valid,
        key_valid,
        w_high,
        w_low,
        kept,
        [w.shape for w in (narrow_weight, widen_weight, merge_weight, mix_weight, value_weight)],
    )
    direct, slope = sums[:states], sums[states : 2 * states]
    decay_grad = weight * slope
    alpha_grad = (beta * gamma * out_scale * direct - damp_rate * decay_grad) * (
        alpha_rate * (1.0 - alpha_rate)
    )
    delta_grad = -alpha_rate * decay_grad * damp_rate * (1.0 - damp_rate)
    beta_grad = alpha_rate * gamma * out_scale * direct
    gamma_grad = alpha_rate * beta * out_scale * direct
    affine_grad = lax.dynamic_slice(
        sums[2 * states + 3 : 2 * states + 6], (0, device * affine.shape[0]), affine.T.shape
    )
    return (
        block_out.reshape(tokens.shape),
        tokens_grad.reshape(tokens.shape),
        sums[2 * states],
        alpha_grad.T,
        delta_grad.T,
        beta_grad.T,
        gamma_grad.T,
        sums[2 * states + 1],
        value,
        mix,
        affine_grad.T,
        merge,
        sums[2 * states + 2],
        widen,
        narrow,
    )


def per_device(
    tokens,
    lengths,
    out_grad,
    first_gain,
    smooth_alpha,
    smooth_delta,
    smooth_beta,
    smooth_gamma,
    smooth_omega,
    value_weight,
    mix_weight,
    query_affine,
    merge_weight,
    second_gain,
    widen_weight,
    narrow_weight,
):
    sequences, block_len, width = tokens.shape
    count = lax.axis_size("seq")
    states = smooth_alpha.shape[1]
    own = first_gain.shape[0]
    own_shared = query_affine.shape[0]
    rows = sequences * block_len
    shared_dim = own_shared * count
    offsets = lax.axis_index("seq") * block_len + lax.iota(jnp.int32, block_len)
    valid = (offsets[None, :] < lengths[:, None]).astype(jnp.float32)
    weights = (value_weight, mix_weight, merge_weight, widen_weight, narrow_weight)
    if count == 8 and lax.axis_size("batch") == 4:
        logits = (smooth_alpha.T, smooth_delta.T, smooth_beta.T, smooth_gamma.T)
        rows_of = jnp.stack([first_gain, smooth_omega, second_gain])
        return plane_layer(tokens, out_grad, valid, logits, rows_of, query_affine, weights)

    affine_row = jnp.pad(query_affine.reshape(-1), (0, own - 3 * own_shared))
    packed = [
        smooth_alpha.T,
        smooth_delta.T,
        smooth_beta.T,
        smooth_gamma.T,
        jnp.stack([first_gain, smooth_omega, second_gain, affine_row]),
    ]
    small = lax.all_gather(jnp.concatenate(packed, axis=0), "seq").transpose(1, 0, 2)

    tiles = (width // lanes, lanes)
    alpha_rate = jax.nn.sigmoid(small[:states].reshape(states, *tiles))
    damp_rate = jax.nn.sigmoid(small[states : 2 * states].reshape(states, *tiles))
    beta = small[2 * states : 3 * states].reshape(states, *tiles)
    gamma = small[3 * states : 4 * states].reshape(states, *tiles)
    gain_one = small[4 * states].reshape(1, width)
    omega = small[4 * states + 1].reshape(1, width)
    gain_two = small[4 * states + 2].reshape(1, width)
    affine = small[4 * states + 3, :, : 3 * own_shared].reshape(shared_dim, 3)
    out_scale = states ** (-0.5)
    decay = 1.0 - alpha_rate * damp_rate
    block_decay = jnp.exp(block_len * jnp.log1p(-alpha_rate * damp_rate))
    weight = alpha_rate * beta * gamma * out_scale

    row_valid = valid.reshape(rows, 1)
    key_valid = valid.reshape(sequences, 1, block_len)

    masked_in = tokens.reshape(rows, width) * row_valid
    g_out = out_grad.reshape(rows, width) * row_valid
    hat_one, scale_one = normalise(masked_in)
    normed = hat_one * gain_one
    tiled = (sequences, block_len) + tiles
    ending = (sequences, states) + tiles
    signal = normed.reshape(tiled)
    local, ends = call_kernel(
        functools.partial(filter_body, False), [tiled, ending], decay, weight, signal
    )
    enter = entering(ends, block_decay, False)
    (smoothed,) = call_kernel(
        functools.partial(carried_body, False), [tiled], decay, weight, enter, local
    )
    mix_pre = smoothed.reshape(rows, width) + omega * normed

    results = plain_layer(
        masked_in, normed, mix_pre, g_out, row_valid, key_valid, affine, gain_two, weights
    )
    block_out, g_mixed, g_from_values, g_rest, second_gain_sum, affine_sum, total = results
    g_smooth = g_mixed * silu_slope(mix_pre)

    smooth_tiled = g_smooth.reshape(tiled)
    back_local, back_ends = call_kernel(
        functools.partial(filter_body, True), [tiled, ending], decay, weight, smooth_tiled
    )
    back_enter = entering(back_ends, block_decay, True)
    direct, slope, last = call_kernel(
        moments_body,
        [(states,) + tiles, (states,) + tiles, ending],
        decay,
        enter,
        signal,
        smooth_tiled,
    )
    (back_full,) = call_kernel(
        functools.partial(carried_body, True), [tiled], decay, weight, back_enter, back_local
    )
    slope = slope + decay * jnp.sum(back_enter * last, axis=0)
    decay_grad = weight * slope
    alpha_grad = (beta * gamma * out_scale * direct - damp_rate * decay_grad) * (
        alpha_rate * (1.0 - alpha_rate)
    )
    delta_grad = -alpha_rate * decay_grad * damp_rate * (1.0 - damp_rate)
    beta_grad = alpha_rate * gamma * out_scale * direct
    gamma_grad = alpha_rate * beta * out_scale * direct

    g_normed = g_from_values + g_smooth * omega + back_full.reshape(rows, width)
    tokens_grad = (g_rest + normalise_back(g_normed, gain_one, hat_one, scale_one)) * row_valid
    first_gain_sum = jnp.sum(g_normed * hat_one, axis=0)
    omega_sum = jnp.sum(g_smooth * normed, axis=0)
    affine_rows = jnp.pad(
        affine_sum.T.reshape(count, 3 * own_shared), ((0, 0), (0, own - 3 * own_shared))
    )
    small_rows = [
        alpha_grad.reshape(states, width),
        delta_grad.reshape(states, width),
        beta_grad.reshape(states, width),
        gamma_grad.reshape(states, width),
        jnp.stack([first_gain_sum, omega_sum, second_gain_sum, affine_rows.reshape(width)]),
    ]
    value_grad, mix_grad, merge_grad, widen_grad, narrow_grad, small_grad = total(
        jnp.concatenate(small_rows, axis=0)
    )

    return (
        block_out.reshape(tokens.shape),
        tokens_grad.reshape(tokens.shape),
        small_grad[4 * states],
        small_grad[:states].T,
        small_grad[states : 2 * states].T,
        small_grad[2 * states : 3 * states].T,
        small_grad[3 * states : 4 * states].T,
        small_grad[4 * states + 1],
        value_grad,
        mix_grad,
        small_grad[4 * states + 3, : 3 * own_shared].reshape(own_shared, 3),
        merge_grad,
        small_grad[4 * states + 2],
        widen_grad,
        narrow_grad,
    )


def solution(mesh):
    rows = P("batch", "seq", None)
    split = P("seq", None)
    in_specs = (
        (rows, P("batch"), rows, P("seq"))
        + (split,) * 4
        + (P("seq"),)
        + (split,) * 4
        + (P("seq"),)
        + (split,) * 2
    )
    out_specs = (
        (rows, rows, P("seq"))
        + (split,) * 4
        + (P("seq"),)
        + (split,) * 4
        + (P("seq"),)
        + (split,) * 2
    )
    return jax.shard_map(
        per_device, mesh=mesh, in_specs=in_specs, out_specs=out_specs, check_vma=False
    )
```

```python
import functools

import jax
import jax.numpy as jnp
from jax import lax
from jax.experimental import pallas as pl
from jax.experimental.pallas import tpu as pltpu
from jax.sharding import PartitionSpec as P

exact = lax.Precision.HIGHEST
triple = lax.Precision.HIGH
norm_eps = 1e-05
masked_score = -1000000000.0
lanes = 128


def gather_rows(shard):
    return lax.all_gather(shard, "seq", axis=0, tiled=True)


def product_grad(left, right):
    return lax.dot_general(left, right, (((0,), (0,)), ((), ())), precision=triple)


def halves(value):
    high = value.astype(jnp.bfloat16)
    return high, (value - high.astype(jnp.float32)).astype(jnp.bfloat16)


def contract(left, right, left_dim, right_dim, precision=None):
    return lax.dot_general(
        left, right, (((left_dim,), (right_dim,)), ((), ())),
        precision=precision, preferred_element_type=jnp.float32,
    )


def turned(left, right):
    return contract(left, right, 0, 0)


def three(left, right, left_dim, right_dim):
    (high, low), (other, rest) = left, right
    return contract(high, other, left_dim, right_dim) + (
        contract(low, other, left_dim, right_dim) + contract(high, rest, left_dim, right_dim)
    )


def place_of(device):
    return (device % 2) * 4 + device // 2


def tree_sum(terms):
    while len(terms) > 1:
        terms = [a + b for a, b in zip(terms[::2], terms[1::2])] + (
            [terms[-1]] if len(terms) % 2 else []
        )
    return terms[0]


def run_filter(reverse, s, decay_ref, weight_ref, signal_ref, out_ref, end_ref):
    length, states = signal_ref.shape[1], decay_ref.shape[0]

    def step(t, held):
        at = length - 1 - t if reverse else t
        entry = signal_ref[s, at]
        held = tuple(decay_ref[n] * held[n] + entry for n in range(states))
        out_ref[s, at] = tree_sum([weight_ref[n] * held[n] for n in range(states)])
        return held

    zero = jnp.zeros(signal_ref.shape[2:], jnp.float32)
    held = lax.fori_loop(0, length, step, (zero,) * states, unroll=4)
    for n in range(states):
        end_ref[s, n] = held[n]


def run_carried(reverse, s, decay_ref, weight_ref, enter_ref, local_ref, out_ref):
    length, states = local_ref.shape[1], decay_ref.shape[0]

    def step(t, held):
        at = length - 1 - t if reverse else t
        held = tuple(decay_ref[n] * held[n] for n in range(states))
        out_ref[s, at] = local_ref[s, at] + tree_sum(list(held))
        return held

    start = tuple(weight_ref[n] * enter_ref[s, n] for n in range(states))
    lax.fori_loop(0, length, step, start, unroll=4)


def run_moments(s, low, high, decay_ref, enter_ref, signal_ref, grad_ref, direct_ref, slope_ref, last_ref):
    length, span = signal_ref.shape[1], range(low, high)
    zero = jnp.zeros(signal_ref.shape[2:], jnp.float32)

    def step(t, carry):
        held, slope, direct, sloped = carry
        entry, grad = signal_ref[s, t], grad_ref[s, t]
        slope = tuple(decay_ref[n] * d + h for n, d, h in zip(span, slope, held))
        held = tuple(decay_ref[n] * h + entry for n, h in zip(span, held))
        direct = tuple(q + grad * h for q, h in zip(direct, held))
        sloped = tuple(q + grad * d for q, d in zip(sloped, slope))
        return held, slope, direct, sloped

    zeros = (zero,) * len(span)
    if s:
        sums = (tuple(direct_ref[n] for n in span), tuple(slope_ref[n] for n in span))
    else:
        sums = (zeros, zeros)
    start = (tuple(enter_ref[s, n] for n in span), zeros) + sums
    _, slope, direct, sloped = lax.fori_loop(0, length, step, start, unroll=2)
    for k, n in enumerate(span):
        last_ref[s, n], direct_ref[n], slope_ref[n] = slope[k], direct[k], sloped[k]


def filter_body(reverse, decay_ref, weight_ref, signal_ref, out_ref, end_ref):
    for s in range(signal_ref.shape[0]):
        run_filter(reverse, s, decay_ref, weight_ref, signal_ref, out_ref, end_ref)


def carried_body(reverse, decay_ref, weight_ref, enter_ref, local_ref, out_ref):
    for s in range(local_ref.shape[0]):
        run_carried(reverse, s, decay_ref, weight_ref, enter_ref, local_ref, out_ref)


def moments_body(decay_ref, enter_ref, signal_ref, grad_ref, *outs):
    states = decay_ref.shape[0]
    for low in range(0, states, 8):
        for s in range(signal_ref.shape[0]):
            run_moments(s, low, min(low + 8, states), decay_ref, enter_ref, signal_ref, grad_ref, *outs)


def on_other(**coordinate):
    return dict(device_id=coordinate, device_id_type=pl.DeviceIdType.MESH)


def chunk_table(shapes):
    firsts, chunk = [], 0
    for blocks, wide in shapes:
        firsts.append(chunk)
        chunk += blocks * wide
    return firsts, chunk


def others_of(me):
    core, along_x, along_y = me % 2, (me // 2) % 2, me // 4
    across_x = me + 2 - 4 * along_x
    return me + 1 - 2 * core, across_x, me + 4 - 8 * along_y, across_x + 4 - 8 * along_y


def state_exchange(reverse, block_ref, ends, chip_ends, halves_ref, enter_ref, sent, came):
    me = lax.axis_index("seq")
    core, chip = me % 2, me // 2
    sibling, *chips = others_of(me)
    first = 1 if reverse else 0
    _, sequences, states = ends.shape[:3]
    half = states // 2

    def copies(step):
        if step == 0:
            pairs = [(ends.at[core], sibling)]
        elif step == 1:
            pairs = [(chip_ends.at[chip], other) for other in chips]
        else:
            pairs = [(halves_ref.at[core], sibling)]
        for number, (piece, other) in enumerate(pairs):
            at = (0, 1, 4)[step] + number
            yield pltpu.make_async_remote_copy(
                src_ref=piece, dst_ref=piece, send_sem=sent.at[at], recv_sem=came.at[at], **on_other(seq=other)
            )

    def start(step):
        for item in copies(step):
            item.start()

    def wait(step):
        for item in copies(step):
            item.wait()

    def share_ends():
        start(0)

    def to_chips():
        wait(0)

        def one(i, carry):
            n = core * half + i
            for s in range(sequences):
                chip_ends[chip, s, i] = block_ref[n] * ends[first, s, n] + ends[1 - first, s, n]
            return carry

        lax.fori_loop(0, half, one, 0)
        start(1)

    def share_entering():
        wait(1)
        mine = 3 - chip if reverse else chip

        def one(i, carry):
            decay = block_ref[core * half + i]
            decay = decay * decay
            for s in range(sequences):
                total = jnp.zeros(block_ref.shape[1:], jnp.float32)
                for position in range(3):
                    piece = chip_ends[3 - position if reverse else position, s, i]
                    total = jnp.where(position < mine, decay * total + piece, total)
                halves_ref[core, s, i] = total
            return carry

        lax.fori_loop(0, half, one, 0)
        start(2)

    def enter():
        wait(2)

        def one(n, carry):
            for s in range(sequences):
                total = halves_ref[n // half, s, n % half]
                later = block_ref[n] * total + ends[first, s, n]
                enter_ref[s, n] = jnp.where(core == first, total, later)
            return carry

        lax.fori_loop(0, states, one, 0)

    return share_ends, to_chips, share_entering, enter


kept_count = 25
gather_shapes = ((1, 8), (1, 16), (2, 4), (1, 16), (4, 4))


def forward_body(
    value_ref, mix_ref, merge_ref, widen_ref, narrow_ref, packed, tokens, out_grad, row_valid, key_valid,
    block_out, w_high, w_low, *refs,
):
    kept, held, refs = refs[:kept_count], refs[kept_count : 2 * kept_count], refs[2 * kept_count :]
    (
        hidden_h, hidden_l, g_out, g_wide, two_h, two_l, gated_h, gated_l, mixed_h, mixed_l, normed_h, normed_l,
        value_pre, projected, middle, attended, shared_pre, soft, cand_pre, masked, signal, enter, mix_pre, small, shared_w,
    ) = held
    buf, stage_h, stage_l, g_hidden, smoothed, ends, chip_ends, halves_in, tables = refs[:9]
    loaded, sent, came, stored, near, sent_all, came_all, sent_state, came_state, saved = refs[9:]
    weights = (value_ref, mix_ref, merge_ref, widen_ref, narrow_ref)
    firsts, chunks = chunk_table(gather_shapes)
    depth, width = buf.shape[0], buf.shape[-1]
    half = lanes * 4
    me, level = lax.axis_index("seq"), lax.axis_index("batch")
    id_sibling, id_x, id_y, id_corner = others_of(me)
    mine, at_x, at_y, at_corner = (place_of(device) for device in (me, id_x, id_y, id_corner))
    above, below = (level + 1) % 4, (level + 3) % 4

    barrier = pltpu.get_barrier_semaphore()
    for other in (id_sibling, id_x, id_y, id_corner):
        pl.semaphore_signal(barrier, inc=1, **on_other(seq=other))
    for target in (above, below):
        pl.semaphore_signal(barrier, inc=1, **on_other(batch=target))
    pl.semaphore_wait(barrier, 6)

    names = ["x", "y", "sibling", "corner_x", "corner_y", "x_more", "y_more"]
    names += ["sibling_x", "sibling_y", "sibling_corner"]
    names += [f"ring{number}{of}" for of in ("", "_x", "_y") for number in range(3)]

    def link(name, chunk):
        slot = chunk % depth
        block = {"x": at_x, "y": at_y, "corner": at_corner}
        kind, _, of = name.partition("_")
        by_x, by_y, by_core, by_z = ({"seq": id_x}, {"seq": id_y}, {"seq": id_sibling}, {"batch": above})
        if kind == "sibling":
            piece, target = buf.at[slot, block[of] if of else mine], by_core
        elif kind == "corner":
            if of == "x":
                piece, target = buf.at[slot, at_x, level, pl.ds(0, 2)], by_y
            else:
                piece, target = buf.at[slot, at_y, level, pl.ds(2, 2)], by_x
        elif kind[:4] == "ring":
            quarter = (level + 4 - int(kind[4])) % 4
            if of:
                piece = buf.at[slot, block[of], quarter, 3 if of == "x" else 0]
            else:
                piece = buf.at[slot, at_corner, quarter]
            target = by_z
        else:
            target = by_x if kind == "x" else by_y
            if of == "more":
                piece = buf.at[slot, mine, level, 3 if kind == "x" else 0]
            elif of == "part":
                piece = buf.at[slot, mine, :, pl.ds(0 if kind == "x" else 1, 3)]
            else:
                piece = buf.at[slot, mine]
        number = names.index(name.removesuffix("_part"))
        return pltpu.make_async_remote_copy(
            src_ref=piece, dst_ref=piece, send_sem=sent.at[number, slot], recv_sem=came.at[number, slot],
            **on_other(**target),
        )

    def shares(chunk):
        return chunk % 3 != 2

    def own_load(weight, block, column, slot):
        source = weight.at[pl.ds(block * 4, 4), :, :, pl.ds(pl.multiple_of(column, lanes), width)]
        return pltpu.make_async_copy(source, buf.at[slot, mine], loaded.at[slot])

    def load(chunk):
        slot = chunk % depth
        for number, ((blocks, wide), first, weight) in enumerate(
            zip(gather_shapes, firsts, weights)
        ):

            @pl.when((chunk >= first) & (chunk < first + blocks * wide))
            def _(number=number, first=first, wide=wide, weight=weight):
                block = (chunk - first) // wide
                column = ((chunk - first) % wide) * width
                if number == 1:
                    column = column + jnp.where(column >= features, lanes, 0)
                own_load(weight, block, column, slot).start()

    def send(chunk):
        own_load(value_ref, 0, 0, chunk % depth).wait()
        both = shares(chunk)
        link("sibling", chunk).start()

        @pl.when(both)
        def _():
            for name in ("x_part", "y_part", "x_more", "y_more"):
                link(name, chunk).start()

        @pl.when(jnp.logical_not(both))
        def _():
            link("x", chunk).start()
            link("y", chunk).start()

    def relay(chunk):
        both = shares(chunk)
        link("sibling", chunk).wait()

        @pl.when(both)
        def _():
            for name in ("x_part", "y_part", "x_more", "y_more"):
                link(name, chunk).wait()
            link("ring0_x", chunk).start()
            link("ring0_y", chunk).start()

        @pl.when(jnp.logical_not(both))
        def _():
            link("x", chunk).wait()
            link("y", chunk).wait()

        link("corner_x", chunk).start()
        link("corner_y", chunk).start()

    def ring(number):
        def phase(chunk):
            if number:
                link(f"ring{number - 1}", chunk).wait()
            else:
                link("corner_x", chunk).wait()
                link("corner_y", chunk).wait()

            @pl.when(shares(chunk))
            def _():
                for of in "xy":
                    link(f"ring{number}_{of}", chunk).wait()
                    if number < 2:
                        link(f"ring{number + 1}_{of}", chunk).start()

            link(f"ring{number}", chunk).start()

        return phase

    def to_sibling(chunk):
        link("ring2", chunk).wait()
        for name in ("sibling_x", "sibling_y", "sibling_corner"):
            link(name, chunk).start()

    def store(chunk, kind):
        return pltpu.make_async_copy(
            (stage_h, stage_l)[kind].at[chunk % 2],
            (w_high, w_low)[kind].at[chunk],
            stored.at[kind, chunk % 2],
        )

    def product(left_h, left_l, right):
        return three((left_h[0], left_l[0]), (right[0][0], right[1][0]), 1, 0) + three(
            (left_h[1], left_l[1]), (right[0][1], right[1][1]), 1, 0
        )

    sequences, block_len = soft.shape[:2]
    states = tables.shape[1]
    decay, weight, block_decay = (tables.at[kind] for kind in range(3))
    features = tokens.shape[1]
    tiles = features // width

    share_ends, to_chips, share_entering, enter_states = state_exchange(
        False, block_decay, ends, chip_ends, halves_in, enter, sent_state, came_state
    )

    def share(kind, numbers):
        sources = (me,) * 4 + (id_x, id_y, id_corner)
        targets = (id_sibling, id_x, id_y, id_corner) + (id_sibling,) * 3
        for number in numbers:
            if kind == 0:
                piece = small.at[sources[number]]
            else:
                piece = shared_w.at[place_of(sources[number])]
            yield pltpu.make_async_remote_copy(
                src_ref=piece, dst_ref=piece, send_sem=sent_all.at[kind, number],
                recv_sem=came_all.at[kind, number], **on_other(seq=targets[number]),
            )

    def own_shared():
        return pltpu.make_async_copy(
            mix_ref.at[:, :, :, pl.ds(features, lanes)], shared_w.at[mine], near
        )

    def row_of(number, k):
        return jnp.concatenate(
            [small[2 * k, number : number + 1], small[2 * k + 1, number : number + 1]], axis=1
        )

    def hand_out():
        own_shared().start()
        small[me] = packed[...]
        for item in share(0, range(4)):
            item.start()
        own_shared().wait()
        for item in share(1, range(4)):
            item.start()

    def pass_on():
        for kind in (0, 1):
            for item in share(kind, range(4)):
                item.wait()
            for item in share(kind, range(4, 7)):
                item.start()

    def norm_one():
        for item in share(0, range(4, 7)):
            item.wait()
        for kind in range(3):
            for n in range(states):
                tables[kind, n] = small[:, kind * states + n]
        keep = row_valid[...]
        value = tokens[...] * keep
        centre = jnp.mean(value, axis=1, keepdims=True)
        shifted = value - centre
        scale = lax.rsqrt(jnp.mean(shifted * shifted, axis=1, keepdims=True) + norm_eps)
        gain = jnp.concatenate([row_of(3 * states, k) for k in range(tiles)], axis=1)
        normed = shifted * scale * gain
        for k in range(tiles):
            span = slice(k * width, (k + 1) * width)
            masked[k] = value[:, span]
            g_out[k] = out_grad[:, span] * keep
            for parity in range(2):
                start = k * width + parity * lanes
                put(normed_h, normed_l, (parity,), k * lanes, normed[:, start : start + lanes])
        for s in range(sequences):
            rows = normed[s * block_len : (s + 1) * block_len]
            signal[s] = rows.reshape(signal.shape[1:])

    def filter_one(s):
        run_filter(False, s, decay, weight, signal, smoothed, ends.at[me % 2])
        if s == sequences - 1:
            share_ends()

    def carry_one(s):
        if s == 0:
            enter_states()
        run_carried(False, s, decay, weight, enter, smoothed, smoothed)

    def mix_in():
        for s in range(sequences):
            span = slice(s * block_len, (s + 1) * block_len)
            skip = jnp.concatenate([row_of(3 * states + 1, k) for k in range(tiles)], axis=1)
            normed = signal[s].reshape(block_len, features)
            value = smoothed[s].reshape(block_len, features) + skip * normed
            mixed = value * jax.nn.sigmoid(value)
            for block in range(8):
                cut = slice(block * lanes, (block + 1) * lanes)
                to = (block % 2, span, slice(block // 2 * lanes, (block // 2 + 1) * lanes))
                mix_pre[to] = value[:, cut]
                mixed_h[to], mixed_l[to] = halves(mixed[:, cut])

    def attention():
        for item in share(1, range(4, 7)):
            item.wait()
        shared_full = halves(shared_w[...].reshape(2, half, lanes))
        total = product(mixed_h, mixed_l, shared_full)
        affine = tree_sum([small[k, 3 * states + 3 : 3 * states + 6] for k in range(8)])
        shared_pre[...] = total
        shared = total * jax.nn.sigmoid(total)
        queries = shared * affine[0:1] + affine[2:3]
        keys = shared * affine[1:2]
        for s in range(sequences):
            span = slice(s * block_len, (s + 1) * block_len)
            scores = contract(queries[span], keys[span], 1, 1, exact) * shared.shape[1] ** (-0.5)
            scores = jnp.where(key_valid[s] > 0.5, scores, masked_score)
            weight = jnp.exp(scores - jnp.max(scores, axis=1, keepdims=True))
            soft[s] = weight / jnp.sum(weight, axis=1, keepdims=True)

    def put(target_h, target_l, index, column, value):
        high, low = halves(value)
        target_h[(*index, slice(None), pl.ds(pl.multiple_of(column, lanes), lanes))] = high
        target_l[(*index, slice(None), pl.ds(pl.multiple_of(column, lanes), lanes))] = low

    def complete(chunk):
        slot = chunk % depth
        for name in ("sibling_x", "sibling_y", "sibling_corner"):
            link(name, chunk).wait()

        @pl.when(chunk >= 2)
        def _():
            store(chunk - 2, 0).wait()
            store(chunk - 2, 1).wait()

        right = halves(buf[slot].reshape(2, half, width))
        stage_h[chunk % 2] = right[0]
        stage_l[chunk % 2] = right[1]
        store(chunk, 0).start()
        store(chunk, 1).start()

        def among(number):
            blocks, wide = gather_shapes[number]
            return (chunk >= firsts[number]) & (chunk < firsts[number] + blocks * wide)

        @pl.when(among(0))
        def _():
            total = product(normed_h, normed_l, right)
            value_pre[chunk] = total
            values = total * jax.nn.sigmoid(total)
            for s in range(sequences):
                span = slice(s * block_len, (s + 1) * block_len)
                attended[chunk, span] = contract(soft[s], values[span], 1, 0, exact)

        @pl.when(among(1))
        def _():
            tile = chunk - firsts[1]
            total = product(mixed_h, mixed_l, right)
            projected[tile] = total

            @pl.when((tile >= 4) & (tile < 12))
            def _():
                block = tile - 4
                gated = attended[block] * total * jax.nn.sigmoid(total)
                for j in range(2):
                    cut = gated[:, j * lanes : (j + 1) * lanes]
                    put(gated_h, gated_l, (j, block % 2), (block // 2) * lanes, cut)

        @pl.when(among(2))
        def _():
            j, tile = (chunk - firsts[2]) // 4, (chunk - firsts[2]) % 4
            total = product(gated_h.at[j], gated_l.at[j], right)

            @pl.when(j == 0)
            def _():
                cand_pre[tile] = projected[12 + tile] + total

            @pl.when(j == 1)
            def _():
                cand_pre[tile] = cand_pre[tile] + total

            @pl.when(chunk == firsts[3] - 1)
            def _():
                total = 0.0
                for k in range(tiles):
                    cand = cand_pre[k]
                    cand = cand * jax.nn.sigmoid(cand)
                    value = masked[k] + jax.nn.sigmoid(projected[k]) * (cand - masked[k])
                    middle[k] = value
                    total = total + jnp.sum(value, axis=1, keepdims=True)
                centre = total / features
                total = 0.0
                for k in range(tiles):
                    shifted = middle[k] - centre
                    total = total + jnp.sum(shifted * shifted, axis=1, keepdims=True)
                scale = lax.rsqrt(total / features + norm_eps)
                for k in range(tiles):
                    value = (middle[k] - centre) * scale * row_of(3 * states + 2, k)
                    for parity in range(2):
                        cut = value[:, parity * lanes : (parity + 1) * lanes]
                        put(two_h, two_l, (parity,), k * lanes, cut)
                block_out[...] = jnp.zeros(block_out.shape, jnp.float32)
                g_hidden[...] = jnp.zeros(g_hidden.shape, jnp.float32)

        @pl.when(among(3))
        def _():
            tile = chunk - firsts[3]
            total = product(two_h, two_l, right)
            g_wide[tile] = total
            hidden = total * jax.nn.sigmoid(total)
            for i in range(2):
                cut = hidden[:, i * lanes : (i + 1) * lanes]
                index = (2 * (tile % 2) + i, (tile // 2) % 2)
                put(hidden_h, hidden_l, index, (tile // 4) * lanes, cut)

        @pl.when(among(4))
        def _():
            j, tile = (chunk - firsts[4]) // 4, (chunk - firsts[4]) % 4
            to = (slice(None), pl.ds(pl.multiple_of(tile * width, width), width))
            block_out[to] = block_out[to] + product(hidden_h.at[j], hidden_l.at[j], right)
            grad = halves(g_out[tile])
            for parity in range(2):
                back = three(grad, (right[0][parity], right[1][parity]), 1, 1)
                g_hidden[j, parity] = g_hidden[j, parity] + back

    def save(*numbers):
        return [
            pltpu.make_async_copy(held[number], kept[number], saved.at[number]) for number in numbers
        ]

    def begin_save(*numbers):
        for item in save(*numbers):
            item.start()

    phases = (
        (2, relay), (4, ring(0)), (6, ring(1)), (8, ring(2)), (10, to_sibling), (11, complete)
    )
    last, ahead = phases[-1][0], 1

    def step(at, carry):
        for after, phase in phases[-2::-1]:

            @pl.when((at >= after) & (at < after + chunks))
            def _(after=after, phase=phase):
                phase(at - after)

        @pl.when(at == 0)
        def _():
            for chunk in range(ahead):
                send(chunk)
            hand_out()

        pl.when((at >= 1) & (at + ahead - 1 < chunks))(lambda: send(at + ahead - 1))
        pl.when(at + ahead < chunks)(lambda: load(at + ahead))
        pl.when(at == 1)(pass_on)
        pl.when(at == 2)(norm_one)
        for s in range(sequences):
            pl.when(at == 3 + s)(functools.partial(filter_one, s))
            pl.when(at == 8 + s)(functools.partial(carry_one, s))
        pl.when(at == 5)(to_chips)
        pl.when(at == 7)(share_entering)

        @pl.when(at == 10)
        def _():
            mix_in()
            attention()

        pl.when(at == last)(lambda: begin_save(2, 8, 9, 10, 11, 16, 17, 19, 20, 21, 22, 23, 24))
        pl.when(at == last + firsts[3])(lambda: begin_save(4, 5, 6, 7, 12, 13, 14, 15, 18))
        pl.when(at == last + firsts[4])(lambda: begin_save(0, 1))

        @pl.when(at >= last)
        def _():
            complete(at - last)

        return carry

    for chunk in range(ahead):
        load(chunk)
    lax.fori_loop(0, chunks + last, step, 0)
    for chunk in (chunks - 2, chunks - 1):
        for kind in range(2):
            store(chunk, kind).wait()
    for k in range(tiles):
        span = slice(k * width, (k + 1) * width)
        block_out[:, span] = (middle[k] + block_out[:, span]) * row_valid[...]
    for k in range(g_wide.shape[0]):
        for i in range(2):
            span = slice(i * lanes, (i + 1) * lanes)
            back = g_hidden[2 * (k % 2) + i, (k // 2) % 2, :, (k // 4) * lanes : (k // 4 + 1) * lanes]
            wide = g_wide[k, :, span]
            g_wide[k, :, span] = back * silu_slope(wide)
    begin_save(3)
    for item in save(*range(kept_count)):
        item.wait()


def f32(*shape):
    return jax.ShapeDtypeStruct(shape, jnp.float32)


def b16(*shape):
    return jax.ShapeDtypeStruct(shape, jnp.bfloat16)


def call_forward(weights, packed, tokens, out_grad, row_valid, key_valid, states):
    width, half = 2 * lanes, 4 * lanes
    rows, features = tokens.shape
    sequences = key_valid.shape[0]
    block_len = rows // sequences
    _, chunks = chunk_table(gather_shapes)
    vmem, anywhere = pl.BlockSpec(memory_space=pltpu.VMEM), pl.BlockSpec(memory_space=pl.ANY)
    line = (sequences, block_len, 8, lanes)
    kept = [
        b16(4, 2, rows, half), b16(4, 2, rows, half), f32(4, rows, width), f32(16, rows, width),
        b16(2, rows, half), b16(2, rows, half), b16(2, 2, rows, half), b16(2, 2, rows, half),
        b16(2, rows, half), b16(2, rows, half), b16(2, rows, half), b16(2, rows, half),
        f32(8, rows, width), f32(16, rows, width), f32(4, rows, width), f32(8, rows, width), f32(rows, lanes),
        f32(sequences, block_len, block_len), f32(4, rows, width), f32(4, rows, width), f32(*line),
        f32(sequences, states, 8, lanes), f32(2, rows, half), f32(8, *packed.shape), f32(8, 4, 4, 8, lanes),
    ]
    shapes = [f32(rows, features)] + [b16(chunks, 2, half, width)] * 2 + kept
    depth, kinds = 16, 19
    return pl.pallas_call(
        forward_body,
        out_shape=shapes,
        in_specs=[anywhere] * len(weights) + [vmem] * 5,
        out_specs=[vmem] + [anywhere] * (len(shapes) - 1),
        scratch_shapes=[pltpu.VMEM(item.shape, item.dtype) for item in kept]
        + [
            pltpu.VMEM((depth, 8, 4, 4, 8, width), jnp.float32),
            pltpu.VMEM((2, 2, half, width), jnp.bfloat16),
            pltpu.VMEM((2, 2, half, width), jnp.bfloat16),
            pltpu.VMEM((4, 2, rows, half), jnp.float32),
            pltpu.VMEM(line, jnp.float32),
            pltpu.VMEM((2, sequences, states, 8, lanes), jnp.float32),
            pltpu.VMEM((4, sequences, states // 2, 8, lanes), jnp.float32),
            pltpu.VMEM((2, sequences, states // 2, 8, lanes), jnp.float32),
            pltpu.VMEM((3, states, 8, lanes), jnp.float32),
            pltpu.SemaphoreType.DMA((depth,)),
            pltpu.SemaphoreType.DMA((kinds, depth)),
            pltpu.SemaphoreType.DMA((kinds, depth)),
            pltpu.SemaphoreType.DMA((2, 2)),
            pltpu.SemaphoreType.DMA,
            pltpu.SemaphoreType.DMA((2, 7)),
            pltpu.SemaphoreType.DMA((2, 7)),
            pltpu.SemaphoreType.DMA((5,)),
            pltpu.SemaphoreType.DMA((5,)),
            pltpu.SemaphoreType.DMA((kept_count,)),
        ],
        compiler_params=pltpu.CompilerParams(
            collective_id=2, has_side_effects=True, vmem_limit_bytes=62 * 1024 * 1024
        ),
    )(*[w.reshape(-1, 4, 8, w.shape[1]) for w in weights], packed, tokens, out_grad, row_valid, key_valid)


reduce_shapes = ((4, 4), (1, 16), (2, 4), (1, 16), (1, 8))


def backward_body(
    row_valid, key_valid, w_high, w_low, *refs,
):
    kept, outs, refs = refs[:kept_count], refs[kept_count : kept_count + 7], refs[kept_count + 7 :]
    held, refs = refs[:kept_count], refs[kept_count:]
    (
        hidden_h, hidden_l, g_out, g_wide, two_h, two_l, gated_h, gated_l, mixed_h, mixed_l, normed_h, normed_l,
        value_pre, projected, middle, attended, shared_pre, soft, cand_pre, masked, signal, enter, mix_pre, small, shared_w,
    ) = held
    tokens_grad, narrow_grad, widen_grad, merge_grad, mix_grad, value_grad, small_grad = outs
    away, keep, got, got_x, got_y, got_xy, got_yx, part, from_edge, from_inner, done = refs[:11]
    ring, bend, straight, *refs = refs[11:]
    buf_h, buf_l, g_two, g_gated, g_mixed, g_normed, g_soft, g_shared = refs[:8]
    smooth, back, ends, chip_ends, halves_in, back_enter, tables, direct, slope, last, small_sum = refs[8:19]
    fetched, read, sent, came, written, sent_state, came_state = refs[19:]
    lefts = (
        (hidden_h, hidden_l), (two_h, two_l), (gated_h, gated_l), (mixed_h, mixed_l), (normed_h, normed_l)
    )
    rights = ((g_out, 0), (g_wide, 0), (projected, 12), (projected, 0), (value_pre, 0))
    grads = (narrow_grad, widen_grad, merge_grad, mix_grad, value_grad)
    firsts, chunks = chunk_table(reduce_shapes)
    gathered, _ = chunk_table(gather_shapes)
    tiles, rows, width = masked.shape
    half, features = 4 * lanes, tiles * width
    sequences, block_len = soft.shape[:2]
    states = tables.shape[1]
    decay, weight, block_decay = (tables.at[kind] for kind in range(3))
    me, level = lax.axis_index("seq"), lax.axis_index("batch")
    core, along_x, along_y = me % 2, (me // 2) % 2, me // 4
    is_edge = (level == 0) | (level == 3)
    partner = jnp.where(level < 2, 1 - level, 5 - level)
    near = others_of(me)
    sibling, across_x, across_y = ({"seq": other} for other in near[:3])

    copies_in = [
        pltpu.make_async_copy(source, target, read.at[number])
        for number, (source, target) in enumerate(zip(kept, held))
    ]
    for item in copies_in:
        item.start()

    barrier = pltpu.get_barrier_semaphore()
    for other in near:
        pl.semaphore_signal(barrier, inc=1, **on_other(seq=other))
    above = (level + 1) % 4
    for other in (above, (level + 3) % 4):
        pl.semaphore_signal(barrier, inc=1, **on_other(batch=other))
    pl.semaphore_wait(barrier, 6)

    def slot_in(ref, chunk):
        return chunk % ref.shape[0]

    def turns(chunk):
        return (chunk % 2 == 1) & (chunk < 45)

    def slot_of(chunk, plain, turning):
        number = chunk // 2
        return jnp.where(turns(chunk), plain + number % turning, chunk % plain)

    def turn_slot(chunk):
        return chunk // 2 % 6

    def keep_slot(chunk):
        return slot_of(chunk, 4, 6)

    def part_slot(chunk):
        return slot_of(chunk, 6, 4)

    def done_slot(chunk):
        return slot_of(chunk, 4, 4)

    def flag_slot(chunk):
        return slot_of(chunk, 8, 6)

    quarter, eighth = lanes // 4, lanes // 8

    def rows_of(ref, index, first, count):
        half_rows = ref.shape[-2]
        start = pl.multiple_of(first % half_rows, 8)
        return (*index, first // half_rows, pl.ds(start, count))

    def link(kind, chunk):
        def at(ref, *index):
            return ref.at[(slot_in(ref, chunk), *index)]

        to, turn = keep_slot(chunk), turn_slot(chunk)
        for_z, hold = part_slot(chunk), keep.at[to]
        source, target, device = (
            lambda: (at(away), at(got), sibling),
            lambda: (hold.at[:, 1 - along_x, 0], at(got_x), across_x),
            lambda: (hold.at[1 - along_y, :, 1], at(got_y), across_y),
            lambda: (at(got_x, 1 - along_y), at(got_xy), across_y),
            lambda: (at(got_y, 1 - along_x), at(got_yx), across_x),
            lambda: (part.at[for_z], from_edge.at[for_z], {"batch": partner}),
            lambda: (part.at[for_z], from_inner.at[for_z], {"batch": 3 - level}),
            None,
            None,
            lambda: (
                keep.at[rows_of(keep, (to, 1 - along_y, 1 - along_x), (level + 3) % 4 * quarter, quarter)],
                ring.at[0, turn], {"batch": above},
            ),
            lambda: (ring.at[0, turn], ring.at[1, turn], {"batch": above}),
            lambda: (ring.at[1, turn], ring.at[2, turn], {"batch": above}),
            lambda: (ring.at[2, turn, pl.ds(0, eighth)], bend.at[0, turn], across_x),
            lambda: (ring.at[2, turn, pl.ds(eighth, eighth)], bend.at[1, turn], across_y),
            lambda: (hold.at[along_y, 1 - along_x], straight.at[0, turn], across_x),
            lambda: (hold.at[1 - along_y, along_x], straight.at[1, turn], across_y),
        )[kind]()
        slot = flag_slot(chunk)
        return pltpu.make_async_remote_copy(
            src_ref=source, dst_ref=target, send_sem=sent.at[kind, slot], recv_sem=came.at[kind, slot],
            **on_other(**device),
        )

    def results(chunk, call):
        slot, at = done_slot(chunk), flag_slot(chunk)

        def pieces(number, source, target):
            yield lambda: pltpu.make_async_copy(source, target, written.at[number, at])
            yield lambda: pltpu.make_async_remote_copy(
                src_ref=source, dst_ref=target,
                send_sem=sent.at[7 + number, at], recv_sem=came.at[7 + number, at],
                **on_other(batch=partner),
            )

        for number, ((blocks, wide), first, grad) in enumerate(zip(reduce_shapes, firsts, grads)):

            @pl.when((chunk >= first) & (chunk < first + blocks * wide))
            def _(number=number, first=first, wide=wide, grad=grad):
                row = ((chunk - first) // wide) * lanes
                column = ((chunk - first) % wide) * width
                if number == 3:
                    column = column + jnp.where(column >= features, lanes, 0)
                target = grad.at[
                    pl.ds(pl.multiple_of(row, lanes), lanes),
                    pl.ds(pl.multiple_of(column, lanes), width),
                ]
                call(*pieces(0, done.at[slot], target))

        @pl.when(chunk == chunks)
        def _():
            target = mix_grad.at[:, pl.ds(features, lanes)]
            call(*pieces(0, done.at[slot, :, pl.ds(0, lanes)], target))
            call(*pieces(1, done.at[slot, :, pl.ds(lanes, lanes)], small_grad))

    def begin(chunk):
        slot, to = slot_in(away, chunk), keep_slot(chunk)
        for (blocks, wide), first, (high, low), (right, shift) in zip(
            reduce_shapes, firsts, lefts, rights
        ):

            @pl.when((chunk >= first) & (chunk < first + blocks * wide))
            def _(first=first, wide=wide, shift=shift, high=high, low=low, right=right):
                block = (chunk - first) // wide
                other, rest = halves(right[shift + (chunk - first) % wide])

                def product(parity):
                    top, under = (
                        (high[block, parity], low[block, parity])
                        if len(high.shape) == 4
                        else (high[parity], low[parity])
                    )
                    total = turned(top, other) + (turned(under, other) + turned(top, rest))
                    return total.reshape(away.shape[1:])

                away[slot] = product(1 - core)
                link(0, chunk).start()
                keep[to] = product(core)

        @pl.when(chunk == chunks)
        def _():
            right = halves(g_shared[...])

            def fill(ref, at, parity):
                total = three((mixed_h[parity], mixed_l[parity]), right, 0, 0)
                total = total.reshape(*away.shape[1:-1], lanes)
                sums = [small_sum[2 * q + parity].reshape(2, -1, lanes) for q in range(4)]
                sums = jnp.stack(sums, axis=0).reshape(total.shape)
                ref[at] = jnp.concatenate([total, sums], axis=-1)

            fill(away, slot, 1 - core)
            link(0, chunk).start()
            fill(keep, to, core)

    def with_sibling(chunk):
        slot = keep_slot(chunk)
        link(0, chunk).wait()
        keep[slot] = keep[slot] + got[slot_in(got, chunk)]
        turning = turns(chunk)
        pl.when(turning)(lambda: link(9, chunk).start())

        @pl.when(jnp.logical_not(turning))
        def _():
            link(1, chunk).start()
            link(2, chunk).start()

    def with_neighbour(chunk):
        slot, from_slot = slot_in(got_x, chunk), keep_slot(chunk)
        link(1, chunk).wait()
        link(2, chunk).wait()
        got_x[slot] = got_x[slot] + keep[from_slot, :, along_x, 0]
        got_y[slot] = got_y[slot] + keep[from_slot, along_y, :, 1]
        link(3, chunk).start()
        link(4, chunk).start()

    def to_edge_or_on(chunk):
        pl.when(is_edge)(lambda: link(5, chunk).start())

    def with_corner(chunk):
        slot = part_slot(chunk)
        link(3, chunk).wait()
        link(4, chunk).wait()
        first, second = slot_in(got_x, chunk), slot_in(got_xy, chunk)
        part[slot, 0] = got_x[first, along_y] + got_xy[second]
        part[slot, 1] = got_y[first, along_x] + got_yx[second]
        to_edge_or_on(chunk)

    def along_z(number):
        def phase(chunk):
            slot = turn_slot(chunk)
            link(9 + number, chunk).wait()
            place = (keep_slot(chunk), 1 - along_y, 1 - along_x)
            own = keep[rows_of(keep, place, (level + 2 - number) % 4 * quarter, quarter)]
            ring[number, slot] = ring[number, slot] + own
            if number < 2:
                link(10 + number, chunk).start()
            else:
                link(12, chunk).start()
                link(13, chunk).start()

        return phase

    def go_straight(chunk):
        slot, to = turn_slot(chunk), keep_slot(chunk)
        link(12, chunk).wait()
        link(13, chunk).wait()
        upper = rows_of(keep, (to, 1 - along_y, along_x), level * quarter, eighth)
        lower = rows_of(keep, (to, along_y, 1 - along_x), level * quarter + eighth, eighth)
        keep[upper] = keep[upper] + bend[0, slot]
        keep[lower] = keep[lower] + bend[1, slot]
        link(14, chunk).start()
        link(15, chunk).start()

    def with_both(chunk):
        slot, turn = part_slot(chunk), turn_slot(chunk)
        link(14, chunk).wait()
        link(15, chunk).wait()
        part[slot] = keep[keep_slot(chunk), along_y, along_x] + straight[0, turn] + straight[1, turn]
        to_edge_or_on(chunk)

    def inner_sum(chunk):
        slot = part_slot(chunk)
        pl.when(is_edge)(lambda: link(5, chunk).wait_send())

        @pl.when(jnp.logical_not(is_edge))
        def _():
            link(5, chunk).wait_recv()
            part[slot] = part[slot] + from_edge[slot]
            link(6, chunk).start()

    def total_sum(chunk):
        slot = part_slot(chunk)

        @pl.when(jnp.logical_not(is_edge))
        def _():
            link(6, chunk).wait()
            done[done_slot(chunk)] = (part[slot] + from_inner[slot]).reshape(done.shape[1:])

            def start(stay, go):
                stay().start()
                go().start()

            results(chunk, start)

    def finish(chunk):
        def receive(stay, go):
            go().wait_recv()

        def release(stay, go):
            stay().wait()
            go().wait_send()

        pl.when(is_edge)(lambda: results(chunk, receive))
        pl.when(jnp.logical_not(is_edge))(lambda: results(chunk, release))

    steps = 48

    def fetch(step, call):
        chunk = jnp.where(
            step < 16, gathered[3] + step, jnp.where(step < 24, step + 8, jnp.where(step < 40, step - 16, step - 40))
        )
        slot = slot_in(buf_h, step)
        for kind, (source, target) in enumerate(((w_high, buf_h), (w_low, buf_l))):
            item = pltpu.make_async_copy(source.at[chunk], target.at[slot], fetched.at[kind, slot])
            getattr(item, call)()

    def back_product(grad, step, parity):
        slot = slot_in(buf_h, step)
        return three(halves(grad), (buf_h[slot, parity], buf_l[slot, parity]), 1, 1)

    def row_of(number, k):
        return jnp.concatenate(
            [small[2 * k, number : number + 1], small[2 * k + 1, number : number + 1]], axis=1
        )

    def put_row(number, k, value):
        for i in range(2):
            small_sum[2 * k + i, number : number + 1] = value[:, i * lanes : (i + 1) * lanes]

    def statistics(ref):
        total = 0.0
        for k in range(tiles):
            total = total + jnp.sum(ref[k], axis=1, keepdims=True)
        centre = total / features
        total = 0.0
        for k in range(tiles):
            shifted = ref[k] - centre
            total = total + jnp.sum(shifted * shifted, axis=1, keepdims=True)
        return centre, lax.rsqrt(total / features + norm_eps)

    def norm_two_back():
        centre, scale = statistics(middle)

        def grad_of(k):
            span = slice(k * lanes, (k + 1) * lanes)
            return jnp.concatenate([g_two[0, :, span], g_two[1, :, span]], axis=1)

        plain, crossed = 0.0, 0.0
        for k in range(tiles):
            grad, hat = grad_of(k), (middle[k] - centre) * scale
            put_row(2 * states + 2, k, jnp.sum(grad * hat, axis=0, keepdims=True))
            inner = grad * row_of(3 * states + 2, k)
            plain = plain + jnp.sum(inner, axis=1, keepdims=True)
            crossed = crossed + jnp.sum(inner * hat, axis=1, keepdims=True)
        plain, crossed = plain / features, crossed / features
        for k in range(tiles):
            inner, hat = grad_of(k) * row_of(3 * states + 2, k), (middle[k] - centre) * scale
            g_middle = g_out[k] + (inner - plain - hat * crossed) * scale
            update = jax.nn.sigmoid(projected[k])
            pre = cand_pre[k]
            gate = jax.nn.sigmoid(pre)
            middle[k] = g_middle * (1.0 - update)
            projected[k] = g_middle * (pre * gate - masked[k]) * update * (1.0 - update)
            projected[12 + k] = g_middle * update * (gate * (1.0 + pre * (1.0 - gate)))

    def attention_back(m):
        parity, start = m % 2, pl.multiple_of((m // 2) * lanes, lanes)
        grad = jnp.concatenate(
            [g_gated[0, parity, :, pl.ds(start, lanes)], g_gated[1, parity, :, pl.ds(start, lanes)]], axis=1
        )
        pre = projected[4 + m]
        gate = jax.nn.sigmoid(pre)
        g_attended = grad * pre * gate
        projected[4 + m] = grad * attended[m] * (gate * (1.0 + pre * (1.0 - gate)))
        pre = value_pre[m]
        gate = jax.nn.sigmoid(pre)
        values, curve = pre * gate, gate * (1.0 + pre * (1.0 - gate))
        g_values = []
        for s in range(sequences):
            span = slice(s * block_len, (s + 1) * block_len)
            own = halves(g_attended[span])
            g_soft[s] = g_soft[s] + three(own, halves(values[span]), 1, 1)
            g_values.append(three(halves(soft[s]), own, 0, 0) * curve[span])
        value_pre[m] = jnp.concatenate(g_values, axis=0)

    def scores_back():
        affine = tree_sum([small[k, 3 * states + 3 : 3 * states + 6] for k in range(8)])
        pre = shared_pre[...]
        gate = jax.nn.sigmoid(pre)
        shared, curve = pre * gate, gate * (1.0 + pre * (1.0 - gate))
        score_scale = shared.shape[1] ** (-0.5)
        queries = shared * affine[0:1] + affine[2:3]
        keys = shared * affine[1:2]
        sums = [0.0, 0.0, 0.0]
        for s in range(sequences):
            span = slice(s * block_len, (s + 1) * block_len)
            soft_weight, grad = soft[s], g_soft[s]
            g_scores = soft_weight * (grad - jnp.sum(grad * soft_weight, axis=1, keepdims=True))
            g_scores = jnp.where(key_valid[s] > 0.5, g_scores, 0.0) * score_scale
            g_queries = contract(g_scores, keys[span], 1, 0, exact)
            g_keys = contract(g_scores, queries[span], 0, 0, exact)
            g_shared[span] = (g_queries * affine[0:1] + g_keys * affine[1:2]) * curve[span]
            terms = (g_queries * shared[span], g_keys * shared[span], g_queries)
            for number, term in enumerate(terms):
                sums[number] = sums[number] + jnp.sum(term, axis=0, keepdims=True)
        for number in range(3):
            for k in range(8):
                row = 2 * states + 3 + number
                small_sum[k, row : row + 1] = sums[number]
        own, full = halves(g_shared[...]), halves(shared_w[...].reshape(2, half, lanes))
        for parity in range(2):
            g_mixed[parity] = three(own, (full[0][parity], full[1][parity]), 1, 1)

    def smooth_back():
        for kind in range(3):
            for n in range(states):
                tables[kind, n] = small[:, kind * states + n]
        for parity in range(2):
            pre = mix_pre[parity]
            g_mixed[parity] = g_mixed[parity] * silu_slope(pre)
        for s in range(sequences):
            span = slice(s * block_len, (s + 1) * block_len)
            blocks = [
                g_mixed[block % 2, span, block // 2 * lanes : (block // 2 + 1) * lanes]
                for block in range(8)
            ]
            smooth[s] = jnp.concatenate(blocks, axis=1).reshape(smooth.shape[1:])

    share_ends, to_chips, share_entering, enter_states = state_exchange(
        True, block_decay, ends, chip_ends, halves_in, back_enter, sent_state, came_state
    )

    def filter_one(s):
        run_filter(True, s, decay, weight, smooth, back, ends.at[core])
        if s == sequences - 1:
            share_ends()

    def moments_one(s, low):
        run_moments(s, low, low + 8, decay, enter, signal, smooth, direct, slope, last)

    def carry_one(s):
        if s == 0:
            enter_states()
        run_carried(True, s, decay, weight, back_enter, back, back)

    def norm_one_back():
        for n in range(states):
            total = slope[n]
            for s in range(sequences):
                total = total + decay[n] * back_enter[s, n] * last[s, n]
            small_sum[:, n] = direct[n]
            small_sum[:, states + n] = total
        centre, scale = statistics(masked)
        line = [back[s].reshape(block_len, features) for s in range(sequences)]
        line = jnp.concatenate(line, axis=0)

        def blocks(ref, k):
            span = slice(k * lanes, (k + 1) * lanes)
            return jnp.concatenate([ref[0, :, span], ref[1, :, span]], axis=1)

        plain, crossed = 0.0, 0.0
        for k in range(tiles):
            g_smooth, hat = blocks(g_mixed, k), (masked[k] - centre) * scale
            gain = row_of(3 * states, k)
            grad = blocks(g_normed, k) + g_smooth * row_of(3 * states + 1, k)
            grad = grad + line[:, k * width : (k + 1) * width]
            put_row(2 * states, k, jnp.sum(grad * hat, axis=0, keepdims=True))
            put_row(2 * states + 1, k, jnp.sum(g_smooth * (hat * gain), axis=0, keepdims=True))
            inner = grad * gain
            plain = plain + jnp.sum(inner, axis=1, keepdims=True)
            crossed = crossed + jnp.sum(inner * hat, axis=1, keepdims=True)
            tokens_grad[:, k * width : (k + 1) * width] = inner
        plain, crossed = plain / features, crossed / features
        for k in range(tiles):
            span = slice(k * width, (k + 1) * width)
            hat = (masked[k] - centre) * scale
            g_x = (tokens_grad[:, span] - plain - hat * crossed) * scale
            tokens_grad[:, span] = (middle[k] + g_x) * row_valid[...]

    g_two[...] = jnp.zeros(g_two.shape, jnp.float32)
    g_gated[...] = jnp.zeros(g_gated.shape, jnp.float32)
    g_normed[...] = jnp.zeros(g_normed.shape, jnp.float32)
    g_soft[...] = jnp.zeros(g_soft.shape, jnp.float32)
    small_sum[...] = jnp.zeros(small_sum.shape, jnp.float32)

    def work(at):
        @pl.when((at < 24) | ((at >= 32) & (at < 56)))
        def _():
            step = jnp.where(at < 24, at, at - 8)
            pl.when(step + 2 < steps)(lambda: fetch(step + 2, "start"))
            fetch(step, "wait")

            @pl.when(at < 16)
            def _():
                for parity in range(2):
                    g_two[parity] = g_two[parity] + back_product(g_wide[at], step, parity)

            pl.when(at == 16)(norm_two_back)

            @pl.when((at >= 16) & (at < 24))
            def _():
                j = (at - 16) // 4
                for parity in range(2):
                    more = back_product(projected[12 + at % 4], step, parity)
                    g_gated[j, parity] = g_gated[j, parity] + more

            pl.when(at == 32)(scores_back)

            @pl.when((at >= 32) & (at < 48))
            def _():
                for parity in range(2):
                    more = back_product(projected[at - 32], step, parity)
                    g_mixed[parity] = g_mixed[parity] + more

            @pl.when(at >= 48)
            def _():
                for parity in range(2):
                    more = back_product(value_pre[at - 48], step, parity)
                    g_normed[parity] = g_normed[parity] + more

        pl.when((at >= 24) & (at < 32))(lambda: attention_back(at - 24))
        pl.when(at == 48)(smooth_back)
        for s in range(sequences):
            pl.when(at == 49 + s)(functools.partial(filter_one, s))
            for low in range(0, states, 8):
                number = 51 + s * (states // 8) + low // 8
                pl.when(at == number)(functools.partial(moments_one, s, low))
            pl.when(at == 56 + s)(functools.partial(carry_one, s))
        pl.when(at == 52)(to_chips)
        pl.when(at == 54)(share_entering)
        pl.when(at == 59)(norm_one_back)

    every, straight_on, turning = None, False, True
    phases = (
        (0, begin, every), (1, with_sibling, every),
        (3, with_neighbour, straight_on), (5, with_corner, straight_on), (7, inner_sum, straight_on),
        (9, total_sum, straight_on), (11, finish, straight_on),
        (3, along_z(0), turning), (5, along_z(1), turning), (7, along_z(2), turning), (9, go_straight, turning),
        (11, with_both, turning), (13, inner_sum, turning), (15, total_sum, turning), (17, finish, turning),
    )
    fetch(0, "start")
    fetch(1, "start")

    def arrive(first, end):
        for item in copies_in[first:end]:
            item.wait()

    arrive(0, 3)

    def step(at, carry):
        for after, phase, which in sorted(phases, key=lambda item: -item[0]):
            chunk = at - after
            wanted = (chunk >= 0) & (chunk <= chunks)
            if which is not None:
                wanted = wanted & (turns(chunk) == which)

            @pl.when(wanted)
            def _(chunk=chunk, phase=phase):
                phase(chunk)

        pl.when(at == 0)(lambda: arrive(3, 4))
        pl.when(at == 8)(lambda: arrive(4, kept_count))
        work(at)
        return carry

    lax.fori_loop(0, chunks + 1 + 11, step, 0)


def call_backward(row_valid, key_valid, w_high, w_low, kept, grad_shapes):
    _, rows, width = kept[3].shape
    soft, signal, enter = kept[17], kept[20], kept[21]
    states = enter.shape[1]
    half, piece = 4 * lanes, lanes // 2
    vmem, anywhere = pl.BlockSpec(memory_space=pltpu.VMEM), pl.BlockSpec(memory_space=pl.ANY)
    shapes = [f32(rows, 8 * lanes)] + [f32(*shape) for shape in grad_shapes] + [f32(lanes, lanes)]
    held = [
        (4, 2, 2, 2, piece, width), (10, 2, 2, 2, piece, width), (4, 2, 2, 2, piece, width),
        (6, 2, piece, width), (6, 2, piece, width), (6, piece, width), (6, piece, width),
        (10, 2, piece, width), (10, 2, piece, width), (10, 2, piece, width), (8, lanes, width),
        (3, 6, lanes // 4, width), (2, 6, lanes // 8, width), (2, 6, 2, piece, width),
    ]
    more = [
        (2, rows, half), (2, 2, rows, half), (2, rows, half), (2, rows, half), soft.shape, (rows, lanes),
        signal.shape, signal.shape, (2, *enter.shape), (4, enter.shape[0], states // 2, 8, lanes),
        (2, enter.shape[0], states // 2, 8, lanes), enter.shape, (3, states, 8, lanes),
        (states, 8, lanes), (states, 8, lanes), enter.shape, (8, lanes, lanes),
    ]
    return pl.pallas_call(
        backward_body,
        out_shape=shapes,
        in_specs=[vmem] * 2 + [anywhere] * (2 + kept_count),
        out_specs=[vmem] + [anywhere] * (len(shapes) - 1),
        scratch_shapes=[pltpu.VMEM(item.shape, item.dtype) for item in kept]
        + [pltpu.VMEM(shape, jnp.float32) for shape in held]
        + [pltpu.VMEM((3, 2, half, width), jnp.bfloat16)] * 2
        + [pltpu.VMEM(shape, jnp.float32) for shape in more]
        + [
            pltpu.SemaphoreType.DMA((2, 3)),
            pltpu.SemaphoreType.DMA((kept_count,)),
            pltpu.SemaphoreType.DMA((16, 14)),
            pltpu.SemaphoreType.DMA((16, 14)),
            pltpu.SemaphoreType.DMA((2, 14)),
            pltpu.SemaphoreType.DMA((5,)),
            pltpu.SemaphoreType.DMA((5,)),
        ],
        compiler_params=pltpu.CompilerParams(
            collective_id=1, has_side_effects=True, vmem_limit_bytes=62 * 1024 * 1024
        ),
    )(row_valid, key_valid, w_high, w_low, *kept)


def call_kernel(body, shapes, *operands):
    return pl.pallas_call(
        body,
        out_shape=[jax.ShapeDtypeStruct(shape, jnp.float32) for shape in shapes],
        in_specs=[pl.BlockSpec(memory_space=pltpu.VMEM)] * len(operands),
        out_specs=[pl.BlockSpec(memory_space=pltpu.VMEM)] * len(shapes),
        compiler_params=pltpu.CompilerParams(vmem_limit_bytes=32 * 1024 * 1024),
    )(*operands)


def entering(ends, block_decay, backward):
    count, mine = lax.axis_size("seq"), lax.axis_index("seq")
    pieces = lax.all_gather(ends, "seq")
    if backward:
        mine = count - 1 - mine
    total = jnp.zeros_like(ends)
    for position in range(count - 1):
        piece = pieces[count - 1 - position if backward else position]
        total = jnp.where(position < mine, block_decay * total + piece, total)
    return total


def silu(value):
    return value * jax.nn.sigmoid(value)


def silu_slope(value):
    gate = jax.nn.sigmoid(value)
    return gate * (1.0 + value * (1.0 - gate))


def normalise(signal):
    centre = jnp.mean(signal, axis=-1, keepdims=True)
    shifted = signal - centre
    spread = jnp.mean(shifted * shifted, axis=-1, keepdims=True)
    scale = lax.rsqrt(spread + norm_eps)
    return shifted * scale, scale


def normalise_back(grad, gain, hat, scale):
    inner = grad * gain
    return (
        inner
        - jnp.mean(inner, axis=-1, keepdims=True)
        - hat * jnp.mean(inner * hat, axis=-1, keepdims=True)
    ) * scale


def times(left, right):
    return jnp.dot(left, right, precision=triple)


def times_back(left, right):
    return lax.dot_general(left, right, (((1,), (1,)), ((), ())), precision=triple)


def plain_layer(masked_in, normed, mix_pre, g_out, row_valid, key_valid, affine, gain_two, weights):
    value_full, mix_full, merge_full, widen_full, narrow_full = (gather_rows(w) for w in weights)
    rows, width = masked_in.shape
    sequences, _, block_len = key_valid.shape
    value_dim, shared_dim = value_full.shape[1], affine.shape[0]
    mixed = silu(mix_pre)
    value_pre = times(normed, value_full)
    values = silu(value_pre)
    projected = times(mixed, mix_full)
    second_cut = width + shared_dim
    third_cut = second_cut + value_dim
    update = jax.nn.sigmoid(projected[:, :width])
    shared_pre = projected[:, width:second_cut]
    reset_pre = projected[:, second_cut:third_cut]
    shared = silu(shared_pre)
    reset_gate = silu(reset_pre)
    queries = (shared * affine[:, 0] + affine[:, 2]).reshape(sequences, block_len, shared_dim)
    key_rows = (shared * affine[:, 1]).reshape(sequences, block_len, shared_dim)
    score_scale = shared_dim ** (-0.5)
    scores = jnp.einsum("cqz,ckz->cqk", queries, key_rows, precision=exact) * score_scale
    scores = jnp.where(key_valid > 0.5, scores, masked_score)
    soft = jax.nn.softmax(scores, axis=-1)
    values_cut = values.reshape(sequences, block_len, value_dim)
    attended = jnp.einsum("cqk,ckv->cqv", soft, values_cut, precision=triple)
    attended = attended.reshape(rows, value_dim)
    gated = attended * reset_gate
    cand_pre = projected[:, third_cut:] + times(gated, merge_full)
    candidate = silu(cand_pre)
    middle = masked_in + update * (candidate - masked_in)
    hat_two, scale_two = normalise(middle)
    normed_two = hat_two * gain_two
    wide_pre = times(normed_two, widen_full)
    hidden = silu(wide_pre)
    block_out = (middle + times(hidden, narrow_full)) * row_valid

    g_wide = times_back(g_out, narrow_full) * silu_slope(wide_pre)
    g_normed_two = times_back(g_wide, widen_full)
    gain_sum = jnp.sum(g_normed_two * hat_two, axis=0)
    g_middle = g_out + normalise_back(g_normed_two, gain_two, hat_two, scale_two)
    g_cand = g_middle * update * silu_slope(cand_pre)
    g_gated = times_back(g_cand, merge_full)
    g_attended = (g_gated * reset_gate).reshape(sequences, block_len, value_dim)
    g_soft = jnp.einsum("cqv,ckv->cqk", g_attended, values_cut, precision=triple)
    g_values = jnp.einsum("cqk,cqv->ckv", soft, g_attended, precision=triple)
    g_scores = soft * (g_soft - jnp.sum(g_soft * soft, axis=-1, keepdims=True))
    g_scores = jnp.where(key_valid > 0.5, g_scores, 0.0) * score_scale
    g_queries = jnp.einsum("cqk,ckz->cqz", g_scores, key_rows, precision=exact)
    g_keys = jnp.einsum("cqk,cqz->ckz", g_scores, queries, precision=exact)
    g_queries = g_queries.reshape(rows, shared_dim)
    g_keys = g_keys.reshape(rows, shared_dim)
    terms = (g_queries * shared, g_keys * shared, g_queries)
    affine_sum = jnp.stack([jnp.sum(term, axis=0) for term in terms])
    g_shared = (g_queries * affine[:, 0] + g_keys * affine[:, 1]) * silu_slope(shared_pre)
    g_update = g_middle * (candidate - masked_in) * update * (1.0 - update)
    g_reset = g_gated * attended * silu_slope(reset_pre)
    g_projected = jnp.concatenate([g_update, g_shared, g_reset, g_cand], axis=1)
    g_mixed = times_back(g_projected, mix_full)
    g_val = g_values.reshape(rows, value_dim) * silu_slope(value_pre)
    g_from_values = times_back(g_val, value_full)

    def total(packed):
        count = lax.axis_size("seq")
        features = packed.shape[1] // count

        def reduced(whole, tiled=True):
            part = lax.psum_scatter(whole, "seq", scatter_dimension=0, tiled=tiled)
            return lax.psum(part, "batch")

        pairs = (
            (normed, g_val),
            (mixed, g_projected),
            (gated, g_cand),
            (normed_two, g_wide),
            (hidden, g_out),
        )
        grads = tuple(reduced(product_grad(*pair)) for pair in pairs)
        blocks = packed.reshape(-1, count, features).transpose(1, 0, 2)
        return grads + (reduced(blocks, False),)

    return block_out, g_mixed, g_from_values, g_middle * (1.0 - update), gain_sum, affine_sum, total


def plane_layer(tokens, out_grad, valid, logits, rows_of, affine, weights):
    sequences, block_len, width = tokens.shape
    rows = sequences * block_len
    states, own = logits[0].shape
    device = lax.axis_index("seq")
    alpha, delta, beta, gamma = logits
    alpha_rate, damp_rate = jax.nn.sigmoid(alpha), jax.nn.sigmoid(delta)
    out_scale = states ** (-0.5)
    weight = alpha_rate * beta * gamma * out_scale
    block_decay = jnp.exp(block_len * jnp.log1p(-alpha_rate * damp_rate))
    spread = lax.dynamic_update_slice(
        jnp.zeros((3, own), jnp.float32), affine.T, (0, device * affine.shape[0])
    )
    packed = jnp.concatenate([1.0 - alpha_rate * damp_rate, weight, block_decay, rows_of, spread])
    packed = jnp.pad(packed, ((0, -packed.shape[0] % 8), (0, 0)))
    row_valid = valid.reshape(rows, 1)
    key_valid = valid.reshape(sequences, 1, block_len)
    block_out, w_high, w_low, *kept = call_forward(
        weights, packed, tokens.reshape(rows, width), out_grad.reshape(rows, width), row_valid, key_valid, states
    )
    value_weight, mix_weight, merge_weight, widen_weight, narrow_weight = weights
    tokens_grad, narrow, widen, merge, mix, value, sums = call_backward(
        row_valid,
        key_valid,
        w_high,
        w_low,
        kept,
        [w.shape for w in (narrow_weight, widen_weight, merge_weight, mix_weight, value_weight)],
    )
    direct, slope = sums[:states], sums[states : 2 * states]
    decay_grad = weight * slope
    alpha_grad = (beta * gamma * out_scale * direct - damp_rate * decay_grad) * (
        alpha_rate * (1.0 - alpha_rate)
    )
    delta_grad = -alpha_rate * decay_grad * damp_rate * (1.0 - damp_rate)
    beta_grad = alpha_rate * gamma * out_scale * direct
    gamma_grad = alpha_rate * beta * out_scale * direct
    affine_grad = lax.dynamic_slice(
        sums[2 * states + 3 : 2 * states + 6], (0, device * affine.shape[0]), affine.T.shape
    )
    return (
        block_out.reshape(tokens.shape),
        tokens_grad.reshape(tokens.shape),
        sums[2 * states],
        alpha_grad.T,
        delta_grad.T,
        beta_grad.T,
        gamma_grad.T,
        sums[2 * states + 1],
        value,
        mix,
        affine_grad.T,
        merge,
        sums[2 * states + 2],
        widen,
        narrow,
    )


def per_device(
    tokens,
    lengths,
    out_grad,
    first_gain,
    smooth_alpha,
    smooth_delta,
    smooth_beta,
    smooth_gamma,
    smooth_omega,
    value_weight,
    mix_weight,
    query_affine,
    merge_weight,
    second_gain,
    widen_weight,
    narrow_weight,
):
    sequences, block_len, width = tokens.shape
    count = lax.axis_size("seq")
    states = smooth_alpha.shape[1]
    own = first_gain.shape[0]
    own_shared = query_affine.shape[0]
    rows = sequences * block_len
    shared_dim = own_shared * count
    offsets = lax.axis_index("seq") * block_len + lax.iota(jnp.int32, block_len)
    valid = (offsets[None, :] < lengths[:, None]).astype(jnp.float32)
    weights = (value_weight, mix_weight, merge_weight, widen_weight, narrow_weight)
    if count == 8 and lax.axis_size("batch") == 4:
        logits = (smooth_alpha.T, smooth_delta.T, smooth_beta.T, smooth_gamma.T)
        rows_of = jnp.stack([first_gain, smooth_omega, second_gain])
        return plane_layer(tokens, out_grad, valid, logits, rows_of, query_affine, weights)

    affine_row = jnp.pad(query_affine.reshape(-1), (0, own - 3 * own_shared))
    packed = [
        smooth_alpha.T,
        smooth_delta.T,
        smooth_beta.T,
        smooth_gamma.T,
        jnp.stack([first_gain, smooth_omega, second_gain, affine_row]),
    ]
    small = lax.all_gather(jnp.concatenate(packed, axis=0), "seq").transpose(1, 0, 2)

    tiles = (width // lanes, lanes)
    alpha_rate = jax.nn.sigmoid(small[:states].reshape(states, *tiles))
    damp_rate = jax.nn.sigmoid(small[states : 2 * states].reshape(states, *tiles))
    beta = small[2 * states : 3 * states].reshape(states, *tiles)
    gamma = small[3 * states : 4 * states].reshape(states, *tiles)
    gain_one = small[4 * states].reshape(1, width)
    omega = small[4 * states + 1].reshape(1, width)
    gain_two = small[4 * states + 2].reshape(1, width)
    affine = small[4 * states + 3, :, : 3 * own_shared].reshape(shared_dim, 3)
    out_scale = states ** (-0.5)
    decay = 1.0 - alpha_rate * damp_rate
    block_decay = jnp.exp(block_len * jnp.log1p(-alpha_rate * damp_rate))
    weight = alpha_rate * beta * gamma * out_scale

    row_valid = valid.reshape(rows, 1)
    key_valid = valid.reshape(sequences, 1, block_len)

    masked_in = tokens.reshape(rows, width) * row_valid
    g_out = out_grad.reshape(rows, width) * row_valid
    hat_one, scale_one = normalise(masked_in)
    normed = hat_one * gain_one
    tiled = (sequences, block_len) + tiles
    ending = (sequences, states) + tiles
    signal = normed.reshape(tiled)
    local, ends = call_kernel(
        functools.partial(filter_body, False), [tiled, ending], decay, weight, signal
    )
    enter = entering(ends, block_decay, False)
    (smoothed,) = call_kernel(
        functools.partial(carried_body, False), [tiled], decay, weight, enter, local
    )
    mix_pre = smoothed.reshape(rows, width) + omega * normed

    results = plain_layer(
        masked_in, normed, mix_pre, g_out, row_valid, key_valid, affine, gain_two, weights
    )
    block_out, g_mixed, g_from_values, g_rest, second_gain_sum, affine_sum, total = results
    g_smooth = g_mixed * silu_slope(mix_pre)

    smooth_tiled = g_smooth.reshape(tiled)
    back_local, back_ends = call_kernel(
        functools.partial(filter_body, True), [tiled, ending], decay, weight, smooth_tiled
    )
    back_enter = entering(back_ends, block_decay, True)
    direct, slope, last = call_kernel(
        moments_body,
        [(states,) + tiles, (states,) + tiles, ending],
        decay,
        enter,
        signal,
        smooth_tiled,
    )
    (back_full,) = call_kernel(
        functools.partial(carried_body, True), [tiled], decay, weight, back_enter, back_local
    )
    slope = slope + decay * jnp.sum(back_enter * last, axis=0)
    decay_grad = weight * slope
    alpha_grad = (beta * gamma * out_scale * direct - damp_rate * decay_grad) * (
        alpha_rate * (1.0 - alpha_rate)
    )
    delta_grad = -alpha_rate * decay_grad * damp_rate * (1.0 - damp_rate)
    beta_grad = alpha_rate * gamma * out_scale * direct
    gamma_grad = alpha_rate * beta * out_scale * direct

    g_normed = g_from_values + g_smooth * omega + back_full.reshape(rows, width)
    tokens_grad = (g_rest + normalise_back(g_normed, gain_one, hat_one, scale_one)) * row_valid
    first_gain_sum = jnp.sum(g_normed * hat_one, axis=0)
    omega_sum = jnp.sum(g_smooth * normed, axis=0)
    affine_rows = jnp.pad(
        affine_sum.T.reshape(count, 3 * own_shared), ((0, 0), (0, own - 3 * own_shared))
    )
    small_rows = [
        alpha_grad.reshape(states, width),
        delta_grad.reshape(states, width),
        beta_grad.reshape(states, width),
        gamma_grad.reshape(states, width),
        jnp.stack([first_gain_sum, omega_sum, second_gain_sum, affine_rows.reshape(width)]),
    ]
    value_grad, mix_grad, merge_grad, widen_grad, narrow_grad, small_grad = total(
        jnp.concatenate(small_rows, axis=0)
    )

    return (
        block_out.reshape(tokens.shape),
        tokens_grad.reshape(tokens.shape),
        small_grad[4 * states],
        small_grad[:states].T,
        small_grad[states : 2 * states].T,
        small_grad[2 * states : 3 * states].T,
        small_grad[3 * states : 4 * states].T,
        small_grad[4 * states + 1],
        value_grad,
        mix_grad,
        small_grad[4 * states + 3, : 3 * own_shared].reshape(own_shared, 3),
        merge_grad,
        small_grad[4 * states + 2],
        widen_grad,
        narrow_grad,
    )


def solution(mesh):
    rows = P("batch", "seq", None)
    split = P("seq", None)
    in_specs = (
        (rows, P("batch"), rows, P("seq"))
        + (split,) * 4
        + (P("seq"),)
        + (split,) * 4
        + (P("seq"),)
        + (split,) * 2
    )
    out_specs = (
        (rows, rows, P("seq"))
        + (split,) * 4
        + (P("seq"),)
        + (split,) * 4
        + (P("seq"),)
        + (split,) * 2
    )
    return jax.shard_map(
        per_device, mesh=mesh, in_specs=in_specs, out_specs=out_specs, check_vma=False
    )
```

```python
import functools

import jax
import jax.numpy as jnp
from jax import lax
from jax.experimental import pallas as pl
from jax.experimental.pallas import tpu as pltpu
from jax.sharding import PartitionSpec as P

exact = lax.Precision.HIGHEST
triple = lax.Precision.HIGH
norm_eps = 1e-05
masked_score = -1000000000.0
lanes = 128


def gather_rows(shard):
    return lax.all_gather(shard, "seq", axis=0, tiled=True)


def product_grad(left, right):
    return lax.dot_general(left, right, (((0,), (0,)), ((), ())), precision=triple)


def halves(value):
    high = value.astype(jnp.bfloat16)
    return high, (value - high.astype(jnp.float32)).astype(jnp.bfloat16)


def contract(left, right, left_dim, right_dim, precision=None):
    return lax.dot_general(
        left, right, (((left_dim,), (right_dim,)), ((), ())),
        precision=precision, preferred_element_type=jnp.float32,
    )


def turned(left, right):
    return contract(left, right, 0, 0)


def three(left, right, left_dim, right_dim):
    (high, low), (other, rest) = left, right
    return contract(high, other, left_dim, right_dim) + (
        contract(low, other, left_dim, right_dim) + contract(high, rest, left_dim, right_dim)
    )


def place_of(device):
    return (device % 2) * 4 + device // 2


def tree_sum(terms):
    while len(terms) > 1:
        terms = [a + b for a, b in zip(terms[::2], terms[1::2])] + (
            [terms[-1]] if len(terms) % 2 else []
        )
    return terms[0]


def run_filter(reverse, s, decay_ref, weight_ref, signal_ref, out_ref, end_ref):
    length, states = signal_ref.shape[1], decay_ref.shape[0]

    def step(t, held):
        at = length - 1 - t if reverse else t
        entry = signal_ref[s, at]
        held = tuple(decay_ref[n] * held[n] + entry for n in range(states))
        out_ref[s, at] = tree_sum([weight_ref[n] * held[n] for n in range(states)])
        return held

    zero = jnp.zeros(signal_ref.shape[2:], jnp.float32)
    held = lax.fori_loop(0, length, step, (zero,) * states, unroll=4)
    for n in range(states):
        end_ref[s, n] = held[n]


def run_carried(reverse, s, decay_ref, weight_ref, enter_ref, local_ref, out_ref):
    length, states = local_ref.shape[1], decay_ref.shape[0]

    def step(t, held):
        at = length - 1 - t if reverse else t
        held = tuple(decay_ref[n] * held[n] for n in range(states))
        out_ref[s, at] = local_ref[s, at] + tree_sum(list(held))
        return held

    start = tuple(weight_ref[n] * enter_ref[s, n] for n in range(states))
    lax.fori_loop(0, length, step, start, unroll=4)


def run_moments(s, low, high, decay_ref, enter_ref, signal_ref, grad_ref, direct_ref, slope_ref, last_ref):
    length, span = signal_ref.shape[1], range(low, high)
    zero = jnp.zeros(signal_ref.shape[2:], jnp.float32)

    def step(t, carry):
        held, slope, direct, sloped = carry
        entry, grad = signal_ref[s, t], grad_ref[s, t]
        slope = tuple(decay_ref[n] * d + h for n, d, h in zip(span, slope, held))
        held = tuple(decay_ref[n] * h + entry for n, h in zip(span, held))
        direct = tuple(q + grad * h for q, h in zip(direct, held))
        sloped = tuple(q + grad * d for q, d in zip(sloped, slope))
        return held, slope, direct, sloped

    zeros = (zero,) * len(span)
    if s:
        sums = (tuple(direct_ref[n] for n in span), tuple(slope_ref[n] for n in span))
    else:
        sums = (zeros, zeros)
    start = (tuple(enter_ref[s, n] for n in span), zeros) + sums
    _, slope, direct, sloped = lax.fori_loop(0, length, step, start, unroll=2)
    for k, n in enumerate(span):
        last_ref[s, n], direct_ref[n], slope_ref[n] = slope[k], direct[k], sloped[k]


def filter_body(reverse, decay_ref, weight_ref, signal_ref, out_ref, end_ref):
    for s in range(signal_ref.shape[0]):
        run_filter(reverse, s, decay_ref, weight_ref, signal_ref, out_ref, end_ref)


def carried_body(reverse, decay_ref, weight_ref, enter_ref, local_ref, out_ref):
    for s in range(local_ref.shape[0]):
        run_carried(reverse, s, decay_ref, weight_ref, enter_ref, local_ref, out_ref)


def moments_body(decay_ref, enter_ref, signal_ref, grad_ref, *outs):
    states = decay_ref.shape[0]
    for low in range(0, states, 8):
        for s in range(signal_ref.shape[0]):
            run_moments(s, low, min(low + 8, states), decay_ref, enter_ref, signal_ref, grad_ref, *outs)


def on_other(**coordinate):
    return dict(device_id=coordinate, device_id_type=pl.DeviceIdType.MESH)


def chunk_table(shapes):
    firsts, chunk = [], 0
    for blocks, wide in shapes:
        firsts.append(chunk)
        chunk += blocks * wide
    return firsts, chunk


def others_of(me):
    core, along_x, along_y = me % 2, (me // 2) % 2, me // 4
    across_x = me + 2 - 4 * along_x
    return me + 1 - 2 * core, across_x, me + 4 - 8 * along_y, across_x + 4 - 8 * along_y


def state_exchange(reverse, block_ref, ends, chip_ends, halves_ref, enter_ref, sent, came):
    me = lax.axis_index("seq")
    core, chip = me % 2, me // 2
    sibling, *chips = others_of(me)
    first = 1 if reverse else 0
    _, sequences, states = ends.shape[:3]
    half = states // 2

    def copies(step):
        if step == 0:
            pairs = [(ends.at[core], sibling)]
        elif step == 1:
            pairs = [(chip_ends.at[chip], other) for other in chips]
        else:
            pairs = [(halves_ref.at[core], sibling)]
        for number, (piece, other) in enumerate(pairs):
            at = (0, 1, 4)[step] + number
            yield pltpu.make_async_remote_copy(
                src_ref=piece, dst_ref=piece, send_sem=sent.at[at], recv_sem=came.at[at], **on_other(seq=other)
            )

    def start(step):
        for item in copies(step):
            item.start()

    def wait(step):
        for item in copies(step):
            item.wait()

    def share_ends():
        start(0)

    def to_chips():
        wait(0)

        def one(i, carry):
            n = core * half + i
            for s in range(sequences):
                chip_ends[chip, s, i] = block_ref[n] * ends[first, s, n] + ends[1 - first, s, n]
            return carry

        lax.fori_loop(0, half, one, 0)
        start(1)

    def share_entering():
        wait(1)
        mine = 3 - chip if reverse else chip

        def one(i, carry):
            decay = block_ref[core * half + i]
            decay = decay * decay
            for s in range(sequences):
                total = jnp.zeros(block_ref.shape[1:], jnp.float32)
                for position in range(3):
                    piece = chip_ends[3 - position if reverse else position, s, i]
                    total = jnp.where(position < mine, decay * total + piece, total)
                halves_ref[core, s, i] = total
            return carry

        lax.fori_loop(0, half, one, 0)
        start(2)

    def enter():
        wait(2)

        def one(n, carry):
            for s in range(sequences):
                total = halves_ref[n // half, s, n % half]
                later = block_ref[n] * total + ends[first, s, n]
                enter_ref[s, n] = jnp.where(core == first, total, later)
            return carry

        lax.fori_loop(0, states, one, 0)

    return share_ends, to_chips, share_entering, enter


kept_count = 25
gather_shapes = ((1, 8), (1, 16), (2, 4), (1, 16), (4, 4))


def forward_body(
    value_ref, mix_ref, merge_ref, widen_ref, narrow_ref, packed, tokens, out_grad, row_valid, key_valid,
    block_out, w_high, w_low, *refs,
):
    kept, held, refs = refs[:kept_count], refs[kept_count : 2 * kept_count], refs[2 * kept_count :]
    (
        hidden_h, hidden_l, g_out, g_wide, two_h, two_l, gated_h, gated_l, mixed_h, mixed_l, normed_h, normed_l,
        value_pre, projected, middle, attended, shared_pre, soft, cand_pre, masked, signal, enter, mix_pre, small, shared_w,
    ) = held
    buf, stage_h, stage_l, g_hidden, smoothed, ends, chip_ends, halves_in, tables = refs[:9]
    loaded, sent, came, stored, near, sent_all, came_all, sent_state, came_state, saved = refs[9:]
    weights = (value_ref, mix_ref, merge_ref, widen_ref, narrow_ref)
    firsts, chunks = chunk_table(gather_shapes)
    depth, width = buf.shape[0], buf.shape[-1]
    half = lanes * 4
    me, level = lax.axis_index("seq"), lax.axis_index("batch")
    id_sibling, id_x, id_y, id_corner = others_of(me)
    mine, at_x, at_y, at_corner = (place_of(device) for device in (me, id_x, id_y, id_corner))
    above, below = (level + 1) % 4, (level + 3) % 4

    barrier = pltpu.get_barrier_semaphore()
    for other in (id_sibling, id_x, id_y, id_corner):
        pl.semaphore_signal(barrier, inc=1, **on_other(seq=other))
    for target in (above, below):
        pl.semaphore_signal(barrier, inc=1, **on_other(batch=target))
    pl.semaphore_wait(barrier, 6)

    names = ["x", "y", "sibling", "corner_x", "corner_y", "x_more", "y_more"]
    names += ["sibling_x", "sibling_y", "sibling_corner"]
    names += [f"ring{number}{of}" for of in ("", "_x", "_y") for number in range(3)]

    def link(name, chunk):
        slot = chunk % depth
        block = {"x": at_x, "y": at_y, "corner": at_corner}
        kind, _, of = name.partition("_")
        by_x, by_y, by_core, by_z = ({"seq": id_x}, {"seq": id_y}, {"seq": id_sibling}, {"batch": above})
        if kind == "sibling":
            piece, target = buf.at[slot, block[of] if of else mine], by_core
        elif kind == "corner":
            if of == "x":
                piece, target = buf.at[slot, at_x, level, pl.ds(0, 2)], by_y
            else:
                piece, target = buf.at[slot, at_y, level, pl.ds(2, 2)], by_x
        elif kind[:4] == "ring":
            quarter = (level + 4 - int(kind[4])) % 4
            if of:
                piece = buf.at[slot, block[of], quarter, 3 if of == "x" else 0]
            else:
                piece = buf.at[slot, at_corner, quarter]
            target = by_z
        else:
            target = by_x if kind == "x" else by_y
            if of == "more":
                piece = buf.at[slot, mine, level, 3 if kind == "x" else 0]
            elif of == "part":
                piece = buf.at[slot, mine, :, pl.ds(0 if kind == "x" else 1, 3)]
            else:
                piece = buf.at[slot, mine]
        number = names.index(name.removesuffix("_part"))
        return pltpu.make_async_remote_copy(
            src_ref=piece, dst_ref=piece, send_sem=sent.at[number, slot], recv_sem=came.at[number, slot],
            **on_other(**target),
        )

    def shares(chunk):
        return (chunk % 3 != 2) & (chunk < 58)

    def own_load(weight, block, column, slot):
        source = weight.at[pl.ds(block * 4, 4), :, :, pl.ds(pl.multiple_of(column, lanes), width)]
        return pltpu.make_async_copy(source, buf.at[slot, mine], loaded.at[slot])

    def load(chunk):
        slot = chunk % depth
        for number, ((blocks, wide), first, weight) in enumerate(
            zip(gather_shapes, firsts, weights)
        ):

            @pl.when((chunk >= first) & (chunk < first + blocks * wide))
            def _(number=number, first=first, wide=wide, weight=weight):
                block = (chunk - first) // wide
                column = ((chunk - first) % wide) * width
                if number == 1:
                    column = column + jnp.where(column >= features, lanes, 0)
                own_load(weight, block, column, slot).start()

    def send(chunk):
        own_load(value_ref, 0, 0, chunk % depth).wait()
        both = shares(chunk)
        link("sibling", chunk).start()

        @pl.when(both)
        def _():
            for name in ("x_part", "y_part", "x_more", "y_more"):
                link(name, chunk).start()

        @pl.when(jnp.logical_not(both))
        def _():
            link("x", chunk).start()
            link("y", chunk).start()

    def relay(chunk):
        both = shares(chunk)
        link("sibling", chunk).wait()

        @pl.when(both)
        def _():
            for name in ("x_part", "y_part", "x_more", "y_more"):
                link(name, chunk).wait()
            link("ring0_x", chunk).start()
            link("ring0_y", chunk).start()

        @pl.when(jnp.logical_not(both))
        def _():
            link("x", chunk).wait()
            link("y", chunk).wait()

        link("corner_x", chunk).start()
        link("corner_y", chunk).start()

    def ring(number):
        def phase(chunk):
            if number:
                link(f"ring{number - 1}", chunk).wait()
            else:
                link("corner_x", chunk).wait()
                link("corner_y", chunk).wait()

            @pl.when(shares(chunk))
            def _():
                for of in "xy":
                    link(f"ring{number}_{of}", chunk).wait()
                    if number < 2:
                        link(f"ring{number + 1}_{of}", chunk).start()

            link(f"ring{number}", chunk).start()

        return phase

    def to_sibling(chunk):
        link("ring2", chunk).wait()
        for name in ("sibling_x", "sibling_y", "sibling_corner"):
            link(name, chunk).start()

    def store(chunk, kind):
        return pltpu.make_async_copy(
            (stage_h, stage_l)[kind].at[chunk % 2],
            (w_high, w_low)[kind].at[chunk],
            stored.at[kind, chunk % 2],
        )

    def product(left_h, left_l, right):
        return three((left_h[0], left_l[0]), (right[0][0], right[1][0]), 1, 0) + three(
            (left_h[1], left_l[1]), (right[0][1], right[1][1]), 1, 0
        )

    sequences, block_len = soft.shape[:2]
    states = tables.shape[1]
    decay, weight, block_decay = (tables.at[kind] for kind in range(3))
    features = tokens.shape[1]
    tiles = features // width

    share_ends, to_chips, share_entering, enter_states = state_exchange(
        False, block_decay, ends, chip_ends, halves_in, enter, sent_state, came_state
    )

    def share(kind, numbers):
        sources = (me,) * 4 + (id_x, id_y, id_corner)
        targets = (id_sibling, id_x, id_y, id_corner) + (id_sibling,) * 3
        for number in numbers:
            if kind == 0:
                piece = small.at[sources[number]]
            else:
                piece = shared_w.at[place_of(sources[number])]
            yield pltpu.make_async_remote_copy(
                src_ref=piece, dst_ref=piece, send_sem=sent_all.at[kind, number],
                recv_sem=came_all.at[kind, number], **on_other(seq=targets[number]),
            )

    def own_shared():
        return pltpu.make_async_copy(
            mix_ref.at[:, :, :, pl.ds(features, lanes)], shared_w.at[mine], near
        )

    def row_of(number, k):
        return jnp.concatenate(
            [small[2 * k, number : number + 1], small[2 * k + 1, number : number + 1]], axis=1
        )

    def hand_out():
        own_shared().start()
        small[me] = packed[...]
        for item in share(0, range(4)):
            item.start()
        own_shared().wait()
        for item in share(1, range(4)):
            item.start()

    def pass_on():
        for kind in (0, 1):
            for item in share(kind, range(4)):
                item.wait()
            for item in share(kind, range(4, 7)):
                item.start()

    def norm_one():
        for item in share(0, range(4, 7)):
            item.wait()
        for kind in range(3):
            for n in range(states):
                tables[kind, n] = small[:, kind * states + n]
        keep = row_valid[...]
        value = tokens[...] * keep
        centre = jnp.mean(value, axis=1, keepdims=True)
        shifted = value - centre
        scale = lax.rsqrt(jnp.mean(shifted * shifted, axis=1, keepdims=True) + norm_eps)
        gain = jnp.concatenate([row_of(3 * states, k) for k in range(tiles)], axis=1)
        normed = shifted * scale * gain
        for k in range(tiles):
            span = slice(k * width, (k + 1) * width)
            masked[k] = value[:, span]
            g_out[k] = out_grad[:, span] * keep
            for parity in range(2):
                start = k * width + parity * lanes
                put(normed_h, normed_l, (parity,), k * lanes, normed[:, start : start + lanes])
        for s in range(sequences):
            rows = normed[s * block_len : (s + 1) * block_len]
            signal[s] = rows.reshape(signal.shape[1:])

    def filter_one(s):
        run_filter(False, s, decay, weight, signal, smoothed, ends.at[me % 2])
        if s == sequences - 1:
            share_ends()

    def carry_one(s):
        if s == 0:
            enter_states()
        run_carried(False, s, decay, weight, enter, smoothed, smoothed)

    def mix_in():
        for s in range(sequences):
            span = slice(s * block_len, (s + 1) * block_len)
            skip = jnp.concatenate([row_of(3 * states + 1, k) for k in range(tiles)], axis=1)
            normed = signal[s].reshape(block_len, features)
            value = smoothed[s].reshape(block_len, features) + skip * normed
            mixed = value * jax.nn.sigmoid(value)
            for block in range(8):
                cut = slice(block * lanes, (block + 1) * lanes)
                to = (block % 2, span, slice(block // 2 * lanes, (block // 2 + 1) * lanes))
                mix_pre[to] = value[:, cut]
                mixed_h[to], mixed_l[to] = halves(mixed[:, cut])

    def attention():
        for item in share(1, range(4, 7)):
            item.wait()
        shared_full = halves(shared_w[...].reshape(2, half, lanes))
        total = product(mixed_h, mixed_l, shared_full)
        affine = tree_sum([small[k, 3 * states + 3 : 3 * states + 6] for k in range(8)])
        shared_pre[...] = total
        shared = total * jax.nn.sigmoid(total)
        queries = shared * affine[0:1] + affine[2:3]
        keys = shared * affine[1:2]
        for s in range(sequences):
            span = slice(s * block_len, (s + 1) * block_len)
            scores = contract(queries[span], keys[span], 1, 1, exact) * shared.shape[1] ** (-0.5)
            scores = jnp.where(key_valid[s] > 0.5, scores, masked_score)
            weight = jnp.exp(scores - jnp.max(scores, axis=1, keepdims=True))
            soft[s] = weight / jnp.sum(weight, axis=1, keepdims=True)

    def put(target_h, target_l, index, column, value):
        high, low = halves(value)
        target_h[(*index, slice(None), pl.ds(pl.multiple_of(column, lanes), lanes))] = high
        target_l[(*index, slice(None), pl.ds(pl.multiple_of(column, lanes), lanes))] = low

    def complete(chunk):
        slot = chunk % depth
        for name in ("sibling_x", "sibling_y", "sibling_corner"):
            link(name, chunk).wait()

        @pl.when(chunk >= 2)
        def _():
            store(chunk - 2, 0).wait()
            store(chunk - 2, 1).wait()

        right = halves(buf[slot].reshape(2, half, width))
        stage_h[chunk % 2] = right[0]
        stage_l[chunk % 2] = right[1]
        store(chunk, 0).start()
        store(chunk, 1).start()

        def among(number):
            blocks, wide = gather_shapes[number]
            return (chunk >= firsts[number]) & (chunk < firsts[number] + blocks * wide)

        @pl.when(among(0))
        def _():
            total = product(normed_h, normed_l, right)
            value_pre[chunk] = total
            values = total * jax.nn.sigmoid(total)
            for s in range(sequences):
                span = slice(s * block_len, (s + 1) * block_len)
                attended[chunk, span] = contract(soft[s], values[span], 1, 0, exact)

        @pl.when(among(1))
        def _():
            tile = chunk - firsts[1]
            total = product(mixed_h, mixed_l, right)
            projected[tile] = total

            @pl.when((tile >= 4) & (tile < 12))
            def _():
                block = tile - 4
                gated = attended[block] * total * jax.nn.sigmoid(total)
                for j in range(2):
                    cut = gated[:, j * lanes : (j + 1) * lanes]
                    put(gated_h, gated_l, (j, block % 2), (block // 2) * lanes, cut)

        @pl.when(among(2))
        def _():
            j, tile = (chunk - firsts[2]) // 4, (chunk - firsts[2]) % 4
            total = product(gated_h.at[j], gated_l.at[j], right)

            @pl.when(j == 0)
            def _():
                cand_pre[tile] = projected[12 + tile] + total

            @pl.when(j == 1)
            def _():
                cand_pre[tile] = cand_pre[tile] + total

            @pl.when(chunk == firsts[3] - 1)
            def _():
                total = 0.0
                for k in range(tiles):
                    cand = cand_pre[k]
                    cand = cand * jax.nn.sigmoid(cand)
                    value = masked[k] + jax.nn.sigmoid(projected[k]) * (cand - masked[k])
                    middle[k] = value
                    total = total + jnp.sum(value, axis=1, keepdims=True)
                centre = total / features
                total = 0.0
                for k in range(tiles):
                    shifted = middle[k] - centre
                    total = total + jnp.sum(shifted * shifted, axis=1, keepdims=True)
                scale = lax.rsqrt(total / features + norm_eps)
                for k in range(tiles):
                    value = (middle[k] - centre) * scale * row_of(3 * states + 2, k)
                    for parity in range(2):
                        cut = value[:, parity * lanes : (parity + 1) * lanes]
                        put(two_h, two_l, (parity,), k * lanes, cut)
                block_out[...] = jnp.zeros(block_out.shape, jnp.float32)
                g_hidden[...] = jnp.zeros(g_hidden.shape, jnp.float32)

        @pl.when(among(3))
        def _():
            tile = chunk - firsts[3]
            total = product(two_h, two_l, right)
            g_wide[tile] = total
            hidden = total * jax.nn.sigmoid(total)
            for i in range(2):
                cut = hidden[:, i * lanes : (i + 1) * lanes]
                index = (2 * (tile % 2) + i, (tile // 2) % 2)
                put(hidden_h, hidden_l, index, (tile // 4) * lanes, cut)

        @pl.when(among(4))
        def _():
            j, tile = (chunk - firsts[4]) // 4, (chunk - firsts[4]) % 4
            to = (slice(None), pl.ds(pl.multiple_of(tile * width, width), width))
            block_out[to] = block_out[to] + product(hidden_h.at[j], hidden_l.at[j], right)
            grad = halves(g_out[tile])
            for parity in range(2):
                back = three(grad, (right[0][parity], right[1][parity]), 1, 1)
                g_hidden[j, parity] = g_hidden[j, parity] + back

    def save(*numbers):
        return [
            pltpu.make_async_copy(held[number], kept[number], saved.at[number]) for number in numbers
        ]

    def begin_save(*numbers):
        for item in save(*numbers):
            item.start()

    phases = (
        (2, relay), (4, ring(0)), (6, ring(1)), (8, ring(2)), (10, to_sibling), (11, complete)
    )
    last, ahead = phases[-1][0], 1

    def step(at, carry):
        for after, phase in phases[-2::-1]:

            @pl.when((at >= after) & (at < after + chunks))
            def _(after=after, phase=phase):
                phase(at - after)

        @pl.when(at == 0)
        def _():
            for chunk in range(ahead):
                send(chunk)
            hand_out()

        pl.when((at >= 1) & (at + ahead - 1 < chunks))(lambda: send(at + ahead - 1))
        pl.when(at + ahead < chunks)(lambda: load(at + ahead))
        pl.when(at == 1)(pass_on)
        pl.when(at == 2)(norm_one)
        for s in range(sequences):
            pl.when(at == 3 + s)(functools.partial(filter_one, s))
            pl.when(at == 8 + s)(functools.partial(carry_one, s))
        pl.when(at == 5)(to_chips)
        pl.when(at == 7)(share_entering)

        @pl.when(at == 10)
        def _():
            mix_in()
            attention()

        pl.when(at == last)(lambda: begin_save(2, 8, 9, 10, 11, 16, 17, 19, 20, 21, 22, 23, 24))
        pl.when(at == last + firsts[3])(lambda: begin_save(4, 5, 6, 7, 12, 13, 14, 15, 18))
        pl.when(at == last + firsts[4])(lambda: begin_save(0, 1))

        @pl.when(at >= last)
        def _():
            complete(at - last)

        return carry

    for chunk in range(ahead):
        load(chunk)
    lax.fori_loop(0, chunks + last, step, 0)
    for chunk in (chunks - 2, chunks - 1):
        for kind in range(2):
            store(chunk, kind).wait()
    for k in range(tiles):
        span = slice(k * width, (k + 1) * width)
        block_out[:, span] = (middle[k] + block_out[:, span]) * row_valid[...]
    for k in range(g_wide.shape[0]):
        for i in range(2):
            span = slice(i * lanes, (i + 1) * lanes)
            back = g_hidden[2 * (k % 2) + i, (k // 2) % 2, :, (k // 4) * lanes : (k // 4 + 1) * lanes]
            wide = g_wide[k, :, span]
            g_wide[k, :, span] = back * silu_slope(wide)
    begin_save(3)
    for item in save(*range(kept_count)):
        item.wait()


def f32(*shape):
    return jax.ShapeDtypeStruct(shape, jnp.float32)


def b16(*shape):
    return jax.ShapeDtypeStruct(shape, jnp.bfloat16)


def call_forward(weights, packed, tokens, out_grad, row_valid, key_valid, states):
    width, half = 2 * lanes, 4 * lanes
    rows, features = tokens.shape
    sequences = key_valid.shape[0]
    block_len = rows // sequences
    _, chunks = chunk_table(gather_shapes)
    vmem, anywhere = pl.BlockSpec(memory_space=pltpu.VMEM), pl.BlockSpec(memory_space=pl.ANY)
    line = (sequences, block_len, 8, lanes)
    kept = [
        b16(4, 2, rows, half), b16(4, 2, rows, half), f32(4, rows, width), f32(16, rows, width),
        b16(2, rows, half), b16(2, rows, half), b16(2, 2, rows, half), b16(2, 2, rows, half),
        b16(2, rows, half), b16(2, rows, half), b16(2, rows, half), b16(2, rows, half),
        f32(8, rows, width), f32(16, rows, width), f32(4, rows, width), f32(8, rows, width), f32(rows, lanes),
        f32(sequences, block_len, block_len), f32(4, rows, width), f32(4, rows, width), f32(*line),
        f32(sequences, states, 8, lanes), f32(2, rows, half), f32(8, *packed.shape), f32(8, 4, 4, 8, lanes),
    ]
    shapes = [f32(rows, features)] + [b16(chunks, 2, half, width)] * 2 + kept
    depth, kinds = 16, 19
    return pl.pallas_call(
        forward_body,
        out_shape=shapes,
        in_specs=[anywhere] * len(weights) + [vmem] * 5,
        out_specs=[vmem] + [anywhere] * (len(shapes) - 1),
        scratch_shapes=[pltpu.VMEM(item.shape, item.dtype) for item in kept]
        + [
            pltpu.VMEM((depth, 8, 4, 4, 8, width), jnp.float32),
            pltpu.VMEM((2, 2, half, width), jnp.bfloat16),
            pltpu.VMEM((2, 2, half, width), jnp.bfloat16),
            pltpu.VMEM((4, 2, rows, half), jnp.float32),
            pltpu.VMEM(line, jnp.float32),
            pltpu.VMEM((2, sequences, states, 8, lanes), jnp.float32),
            pltpu.VMEM((4, sequences, states // 2, 8, lanes), jnp.float32),
            pltpu.VMEM((2, sequences, states // 2, 8, lanes), jnp.float32),
            pltpu.VMEM((3, states, 8, lanes), jnp.float32),
            pltpu.SemaphoreType.DMA((depth,)),
            pltpu.SemaphoreType.DMA((kinds, depth)),
            pltpu.SemaphoreType.DMA((kinds, depth)),
            pltpu.SemaphoreType.DMA((2, 2)),
            pltpu.SemaphoreType.DMA,
            pltpu.SemaphoreType.DMA((2, 7)),
            pltpu.SemaphoreType.DMA((2, 7)),
            pltpu.SemaphoreType.DMA((5,)),
            pltpu.SemaphoreType.DMA((5,)),
            pltpu.SemaphoreType.DMA((kept_count,)),
        ],
        compiler_params=pltpu.CompilerParams(
            collective_id=2, has_side_effects=True, vmem_limit_bytes=62 * 1024 * 1024
        ),
    )(*[w.reshape(-1, 4, 8, w.shape[1]) for w in weights], packed, tokens, out_grad, row_valid, key_valid)


reduce_shapes = ((4, 4), (1, 16), (2, 4), (1, 16), (1, 8))


def backward_body(
    row_valid, key_valid, w_high, w_low, *refs,
):
    kept, outs, refs = refs[:kept_count], refs[kept_count : kept_count + 7], refs[kept_count + 7 :]
    held, refs = refs[:kept_count], refs[kept_count:]
    (
        hidden_h, hidden_l, g_out, g_wide, two_h, two_l, gated_h, gated_l, mixed_h, mixed_l, normed_h, normed_l,
        value_pre, projected, middle, attended, shared_pre, soft, cand_pre, masked, signal, enter, mix_pre, small, shared_w,
    ) = held
    tokens_grad, narrow_grad, widen_grad, merge_grad, mix_grad, value_grad, small_grad = outs
    away, keep, got, got_x, got_y, got_xy, got_yx, part, from_edge, from_inner, done = refs[:11]
    ring, bend, straight, *refs = refs[11:]
    buf_h, buf_l, g_two, g_gated, g_mixed, g_normed, g_soft, g_shared = refs[:8]
    smooth, back, ends, chip_ends, halves_in, back_enter, tables, direct, slope, last, small_sum = refs[8:19]
    fetched, read, sent, came, written, sent_state, came_state = refs[19:]
    lefts = (
        (hidden_h, hidden_l), (two_h, two_l), (gated_h, gated_l), (mixed_h, mixed_l), (normed_h, normed_l)
    )
    rights = ((g_out, 0), (g_wide, 0), (projected, 12), (projected, 0), (value_pre, 0))
    grads = (narrow_grad, widen_grad, merge_grad, mix_grad, value_grad)
    firsts, chunks = chunk_table(reduce_shapes)
    gathered, _ = chunk_table(gather_shapes)
    tiles, rows, width = masked.shape
    half, features = 4 * lanes, tiles * width
    sequences, block_len = soft.shape[:2]
    states = tables.shape[1]
    decay, weight, block_decay = (tables.at[kind] for kind in range(3))
    me, level = lax.axis_index("seq"), lax.axis_index("batch")
    core, along_x, along_y = me % 2, (me // 2) % 2, me // 4
    is_edge = (level == 0) | (level == 3)
    partner = jnp.where(level < 2, 1 - level, 5 - level)
    near = others_of(me)
    sibling, across_x, across_y = ({"seq": other} for other in near[:3])

    copies_in = [
        pltpu.make_async_copy(source, target, read.at[number])
        for number, (source, target) in enumerate(zip(kept, held))
    ]
    for item in copies_in:
        item.start()

    barrier = pltpu.get_barrier_semaphore()
    for other in near:
        pl.semaphore_signal(barrier, inc=1, **on_other(seq=other))
    above = (level + 1) % 4
    for other in (above, (level + 3) % 4):
        pl.semaphore_signal(barrier, inc=1, **on_other(batch=other))
    pl.semaphore_wait(barrier, 6)

    def slot_in(ref, chunk):
        return chunk % ref.shape[0]

    def turns(chunk):
        return (chunk % 2 == 1) & (chunk < 49)

    def slot_of(chunk, plain, turning):
        number = chunk // 2
        return jnp.where(turns(chunk), plain + number % turning, chunk % plain)

    def turn_slot(chunk):
        return chunk // 2 % 6

    def keep_slot(chunk):
        return slot_of(chunk, 4, 6)

    def part_slot(chunk):
        return slot_of(chunk, 6, 4)

    def done_slot(chunk):
        return slot_of(chunk, 4, 4)

    def flag_slot(chunk):
        return slot_of(chunk, 8, 6)

    quarter, eighth = lanes // 4, lanes // 8

    def rows_of(ref, index, first, count):
        half_rows = ref.shape[-2]
        start = pl.multiple_of(first % half_rows, 8)
        return (*index, first // half_rows, pl.ds(start, count))

    def link(kind, chunk):
        def at(ref, *index):
            return ref.at[(slot_in(ref, chunk), *index)]

        to, turn = keep_slot(chunk), turn_slot(chunk)
        for_z, hold = part_slot(chunk), keep.at[to]
        source, target, device = (
            lambda: (at(away), at(got), sibling),
            lambda: (hold.at[:, 1 - along_x, 0], at(got_x), across_x),
            lambda: (hold.at[1 - along_y, :, 1], at(got_y), across_y),
            lambda: (at(got_x, 1 - along_y), at(got_xy), across_y),
            lambda: (at(got_y, 1 - along_x), at(got_yx), across_x),
            lambda: (part.at[for_z], from_edge.at[for_z], {"batch": partner}),
            lambda: (part.at[for_z], from_inner.at[for_z], {"batch": 3 - level}),
            None,
            None,
            lambda: (
                keep.at[rows_of(keep, (to, 1 - along_y, 1 - along_x), (level + 3) % 4 * quarter, quarter)],
                ring.at[0, turn], {"batch": above},
            ),
            lambda: (ring.at[0, turn], ring.at[1, turn], {"batch": above}),
            lambda: (ring.at[1, turn], ring.at[2, turn], {"batch": above}),
            lambda: (ring.at[2, turn, pl.ds(0, eighth)], bend.at[0, turn], across_x),
            lambda: (ring.at[2, turn, pl.ds(eighth, eighth)], bend.at[1, turn], across_y),
            lambda: (hold.at[along_y, 1 - along_x], straight.at[0, turn], across_x),
            lambda: (hold.at[1 - along_y, along_x], straight.at[1, turn], across_y),
        )[kind]()
        slot = flag_slot(chunk)
        return pltpu.make_async_remote_copy(
            src_ref=source, dst_ref=target, send_sem=sent.at[kind, slot], recv_sem=came.at[kind, slot],
            **on_other(**device),
        )

    def results(chunk, call):
        slot, at = done_slot(chunk), flag_slot(chunk)

        def pieces(number, source, target):
            yield lambda: pltpu.make_async_copy(source, target, written.at[number, at])
            yield lambda: pltpu.make_async_remote_copy(
                src_ref=source, dst_ref=target,
                send_sem=sent.at[7 + number, at], recv_sem=came.at[7 + number, at],
                **on_other(batch=partner),
            )

        for number, ((blocks, wide), first, grad) in enumerate(zip(reduce_shapes, firsts, grads)):

            @pl.when((chunk >= first) & (chunk < first + blocks * wide))
            def _(number=number, first=first, wide=wide, grad=grad):
                row = ((chunk - first) // wide) * lanes
                column = ((chunk - first) % wide) * width
                if number == 3:
                    column = column + jnp.where(column >= features, lanes, 0)
                target = grad.at[
                    pl.ds(pl.multiple_of(row, lanes), lanes),
                    pl.ds(pl.multiple_of(column, lanes), width),
                ]
                call(*pieces(0, done.at[slot], target))

        @pl.when(chunk == chunks)
        def _():
            target = mix_grad.at[:, pl.ds(features, lanes)]
            call(*pieces(0, done.at[slot, :, pl.ds(0, lanes)], target))
            call(*pieces(1, done.at[slot, :, pl.ds(lanes, lanes)], small_grad))

    def begin(chunk):
        slot, to = slot_in(away, chunk), keep_slot(chunk)
        for (blocks, wide), first, (high, low), (right, shift) in zip(
            reduce_shapes, firsts, lefts, rights
        ):

            @pl.when((chunk >= first) & (chunk < first + blocks * wide))
            def _(first=first, wide=wide, shift=shift, high=high, low=low, right=right):
                block = (chunk - first) // wide
                other, rest = halves(right[shift + (chunk - first) % wide])

                def product(parity):
                    top, under = (
                        (high[block, parity], low[block, parity])
                        if len(high.shape) == 4
                        else (high[parity], low[parity])
                    )
                    total = turned(top, other) + (turned(under, other) + turned(top, rest))
                    return total.reshape(away.shape[1:])

                away[slot] = product(1 - core)
                link(0, chunk).start()
                keep[to] = product(core)

        @pl.when(chunk == chunks)
        def _():
            right = halves(g_shared[...])

            def fill(ref, at, parity):
                total = three((mixed_h[parity], mixed_l[parity]), right, 0, 0)
                total = total.reshape(*away.shape[1:-1], lanes)
                sums = [small_sum[2 * q + parity].reshape(2, -1, lanes) for q in range(4)]
                sums = jnp.stack(sums, axis=0).reshape(total.shape)
                ref[at] = jnp.concatenate([total, sums], axis=-1)

            fill(away, slot, 1 - core)
            link(0, chunk).start()
            fill(keep, to, core)

    def with_sibling(chunk):
        slot = keep_slot(chunk)
        link(0, chunk).wait()
        keep[slot] = keep[slot] + got[slot_in(got, chunk)]
        turning = turns(chunk)
        pl.when(turning)(lambda: link(9, chunk).start())

        @pl.when(jnp.logical_not(turning))
        def _():
            link(1, chunk).start()
            link(2, chunk).start()

    def with_neighbour(chunk):
        slot, from_slot = slot_in(got_x, chunk), keep_slot(chunk)
        link(1, chunk).wait()
        link(2, chunk).wait()
        got_x[slot] = got_x[slot] + keep[from_slot, :, along_x, 0]
        got_y[slot] = got_y[slot] + keep[from_slot, along_y, :, 1]
        link(3, chunk).start()
        link(4, chunk).start()

    def to_edge_or_on(chunk):
        pl.when(is_edge)(lambda: link(5, chunk).start())

    def with_corner(chunk):
        slot = part_slot(chunk)
        link(3, chunk).wait()
        link(4, chunk).wait()
        first, second = slot_in(got_x, chunk), slot_in(got_xy, chunk)
        part[slot, 0] = got_x[first, along_y] + got_xy[second]
        part[slot, 1] = got_y[first, along_x] + got_yx[second]
        to_edge_or_on(chunk)

    def along_z(number):
        def phase(chunk):
            slot = turn_slot(chunk)
            link(9 + number, chunk).wait()
            place = (keep_slot(chunk), 1 - along_y, 1 - along_x)
            own = keep[rows_of(keep, place, (level + 2 - number) % 4 * quarter, quarter)]
            ring[number, slot] = ring[number, slot] + own
            if number < 2:
                link(10 + number, chunk).start()
            else:
                link(12, chunk).start()
                link(13, chunk).start()

        return phase

    def go_straight(chunk):
        slot, to = turn_slot(chunk), keep_slot(chunk)
        link(12, chunk).wait()
        link(13, chunk).wait()
        upper = rows_of(keep, (to, 1 - along_y, along_x), level * quarter, eighth)
        lower = rows_of(keep, (to, along_y, 1 - along_x), level * quarter + eighth, eighth)
        keep[upper] = keep[upper] + bend[0, slot]
        keep[lower] = keep[lower] + bend[1, slot]
        link(14, chunk).start()
        link(15, chunk).start()

    def with_both(chunk):
        slot, turn = part_slot(chunk), turn_slot(chunk)
        link(14, chunk).wait()
        link(15, chunk).wait()
        part[slot] = keep[keep_slot(chunk), along_y, along_x] + straight[0, turn] + straight[1, turn]
        to_edge_or_on(chunk)

    def inner_sum(chunk):
        slot = part_slot(chunk)
        pl.when(is_edge)(lambda: link(5, chunk).wait_send())

        @pl.when(jnp.logical_not(is_edge))
        def _():
            link(5, chunk).wait_recv()
            part[slot] = part[slot] + from_edge[slot]
            link(6, chunk).start()

    def total_sum(chunk):
        slot = part_slot(chunk)

        @pl.when(jnp.logical_not(is_edge))
        def _():
            link(6, chunk).wait()
            done[done_slot(chunk)] = (part[slot] + from_inner[slot]).reshape(done.shape[1:])

            def start(stay, go):
                stay().start()
                go().start()

            results(chunk, start)

    def finish(chunk):
        def receive(stay, go):
            go().wait_recv()

        def release(stay, go):
            stay().wait()
            go().wait_send()

        pl.when(is_edge)(lambda: results(chunk, receive))
        pl.when(jnp.logical_not(is_edge))(lambda: results(chunk, release))

    steps = 48

    def fetch(step, call):
        chunk = jnp.where(
            step < 16, gathered[3] + step, jnp.where(step < 24, step + 8, jnp.where(step < 40, step - 16, step - 40))
        )
        slot = slot_in(buf_h, step)
        for kind, (source, target) in enumerate(((w_high, buf_h), (w_low, buf_l))):
            item = pltpu.make_async_copy(source.at[chunk], target.at[slot], fetched.at[kind, slot])
            getattr(item, call)()

    def back_product(grad, step, parity):
        slot = slot_in(buf_h, step)
        return three(halves(grad), (buf_h[slot, parity], buf_l[slot, parity]), 1, 1)

    def row_of(number, k):
        return jnp.concatenate(
            [small[2 * k, number : number + 1], small[2 * k + 1, number : number + 1]], axis=1
        )

    def put_row(number, k, value):
        for i in range(2):
            small_sum[2 * k + i, number : number + 1] = value[:, i * lanes : (i + 1) * lanes]

    def statistics(ref):
        total = 0.0
        for k in range(tiles):
            total = total + jnp.sum(ref[k], axis=1, keepdims=True)
        centre = total / features
        total = 0.0
        for k in range(tiles):
            shifted = ref[k] - centre
            total = total + jnp.sum(shifted * shifted, axis=1, keepdims=True)
        return centre, lax.rsqrt(total / features + norm_eps)

    def norm_two_back():
        centre, scale = statistics(middle)

        def grad_of(k):
            span = slice(k * lanes, (k + 1) * lanes)
            return jnp.concatenate([g_two[0, :, span], g_two[1, :, span]], axis=1)

        plain, crossed = 0.0, 0.0
        for k in range(tiles):
            grad, hat = grad_of(k), (middle[k] - centre) * scale
            put_row(2 * states + 2, k, jnp.sum(grad * hat, axis=0, keepdims=True))
            inner = grad * row_of(3 * states + 2, k)
            plain = plain + jnp.sum(inner, axis=1, keepdims=True)
            crossed = crossed + jnp.sum(inner * hat, axis=1, keepdims=True)
        plain, crossed = plain / features, crossed / features
        for k in range(tiles):
            inner, hat = grad_of(k) * row_of(3 * states + 2, k), (middle[k] - centre) * scale
            g_middle = g_out[k] + (inner - plain - hat * crossed) * scale
            update = jax.nn.sigmoid(projected[k])
            pre = cand_pre[k]
            gate = jax.nn.sigmoid(pre)
            middle[k] = g_middle * (1.0 - update)
            projected[k] = g_middle * (pre * gate - masked[k]) * update * (1.0 - update)
            projected[12 + k] = g_middle * update * (gate * (1.0 + pre * (1.0 - gate)))

    def attention_back(m):
        parity, start = m % 2, pl.multiple_of((m // 2) * lanes, lanes)
        grad = jnp.concatenate(
            [g_gated[0, parity, :, pl.ds(start, lanes)], g_gated[1, parity, :, pl.ds(start, lanes)]], axis=1
        )
        pre = projected[4 + m]
        gate = jax.nn.sigmoid(pre)
        g_attended = grad * pre * gate
        projected[4 + m] = grad * attended[m] * (gate * (1.0 + pre * (1.0 - gate)))
        pre = value_pre[m]
        gate = jax.nn.sigmoid(pre)
        values, curve = pre * gate, gate * (1.0 + pre * (1.0 - gate))
        g_values = []
        for s in range(sequences):
            span = slice(s * block_len, (s + 1) * block_len)
            own = halves(g_attended[span])
            g_soft[s] = g_soft[s] + three(own, halves(values[span]), 1, 1)
            g_values.append(three(halves(soft[s]), own, 0, 0) * curve[span])
        value_pre[m] = jnp.concatenate(g_values, axis=0)

    def scores_back():
        affine = tree_sum([small[k, 3 * states + 3 : 3 * states + 6] for k in range(8)])
        pre = shared_pre[...]
        gate = jax.nn.sigmoid(pre)
        shared, curve = pre * gate, gate * (1.0 + pre * (1.0 - gate))
        score_scale = shared.shape[1] ** (-0.5)
        queries = shared * affine[0:1] + affine[2:3]
        keys = shared * affine[1:2]
        sums = [0.0, 0.0, 0.0]
        for s in range(sequences):
            span = slice(s * block_len, (s + 1) * block_len)
            soft_weight, grad = soft[s], g_soft[s]
            g_scores = soft_weight * (grad - jnp.sum(grad * soft_weight, axis=1, keepdims=True))
            g_scores = jnp.where(key_valid[s] > 0.5, g_scores, 0.0) * score_scale
            g_queries = contract(g_scores, keys[span], 1, 0, exact)
            g_keys = contract(g_scores, queries[span], 0, 0, exact)
            g_shared[span] = (g_queries * affine[0:1] + g_keys * affine[1:2]) * curve[span]
            terms = (g_queries * shared[span], g_keys * shared[span], g_queries)
            for number, term in enumerate(terms):
                sums[number] = sums[number] + jnp.sum(term, axis=0, keepdims=True)
        for number in range(3):
            for k in range(8):
                row = 2 * states + 3 + number
                small_sum[k, row : row + 1] = sums[number]
        own, full = halves(g_shared[...]), halves(shared_w[...].reshape(2, half, lanes))
        for parity in range(2):
            g_mixed[parity] = three(own, (full[0][parity], full[1][parity]), 1, 1)

    def smooth_back():
        for kind in range(3):
            for n in range(states):
                tables[kind, n] = small[:, kind * states + n]
        for parity in range(2):
            pre = mix_pre[parity]
            g_mixed[parity] = g_mixed[parity] * silu_slope(pre)
        for s in range(sequences):
            span = slice(s * block_len, (s + 1) * block_len)
            blocks = [
                g_mixed[block % 2, span, block // 2 * lanes : (block // 2 + 1) * lanes]
                for block in range(8)
            ]
            smooth[s] = jnp.concatenate(blocks, axis=1).reshape(smooth.shape[1:])

    share_ends, to_chips, share_entering, enter_states = state_exchange(
        True, block_decay, ends, chip_ends, halves_in, back_enter, sent_state, came_state
    )

    def filter_one(s):
        run_filter(True, s, decay, weight, smooth, back, ends.at[core])
        if s == sequences - 1:
            share_ends()

    def moments_one(s, low):
        run_moments(s, low, low + 8, decay, enter, signal, smooth, direct, slope, last)

    def carry_one(s):
        if s == 0:
            enter_states()
        run_carried(True, s, decay, weight, back_enter, back, back)

    def norm_one_back():
        for n in range(states):
            total = slope[n]
            for s in range(sequences):
                total = total + decay[n] * back_enter[s, n] * last[s, n]
            small_sum[:, n] = direct[n]
            small_sum[:, states + n] = total
        centre, scale = statistics(masked)
        line = [back[s].reshape(block_len, features) for s in range(sequences)]
        line = jnp.concatenate(line, axis=0)

        def blocks(ref, k):
            span = slice(k * lanes, (k + 1) * lanes)
            return jnp.concatenate([ref[0, :, span], ref[1, :, span]], axis=1)

        plain, crossed = 0.0, 0.0
        for k in range(tiles):
            g_smooth, hat = blocks(g_mixed, k), (masked[k] - centre) * scale
            gain = row_of(3 * states, k)
            grad = blocks(g_normed, k) + g_smooth * row_of(3 * states + 1, k)
            grad = grad + line[:, k * width : (k + 1) * width]
            put_row(2 * states, k, jnp.sum(grad * hat, axis=0, keepdims=True))
            put_row(2 * states + 1, k, jnp.sum(g_smooth * (hat * gain), axis=0, keepdims=True))
            inner = grad * gain
            plain = plain + jnp.sum(inner, axis=1, keepdims=True)
            crossed = crossed + jnp.sum(inner * hat, axis=1, keepdims=True)
            tokens_grad[:, k * width : (k + 1) * width] = inner
        plain, crossed = plain / features, crossed / features
        for k in range(tiles):
            span = slice(k * width, (k + 1) * width)
            hat = (masked[k] - centre) * scale
            g_x = (tokens_grad[:, span] - plain - hat * crossed) * scale
            tokens_grad[:, span] = (middle[k] + g_x) * row_valid[...]

    g_two[...] = jnp.zeros(g_two.shape, jnp.float32)
    g_gated[...] = jnp.zeros(g_gated.shape, jnp.float32)
    g_normed[...] = jnp.zeros(g_normed.shape, jnp.float32)
    g_soft[...] = jnp.zeros(g_soft.shape, jnp.float32)
    small_sum[...] = jnp.zeros(small_sum.shape, jnp.float32)

    def work(at):
        @pl.when((at < 24) | ((at >= 32) & (at < 56)))
        def _():
            step = jnp.where(at < 24, at, at - 8)
            pl.when(step + 2 < steps)(lambda: fetch(step + 2, "start"))
            fetch(step, "wait")

            @pl.when(at < 16)
            def _():
                for parity in range(2):
                    g_two[parity] = g_two[parity] + back_product(g_wide[at], step, parity)

            pl.when(at == 16)(norm_two_back)

            @pl.when((at >= 16) & (at < 24))
            def _():
                j = (at - 16) // 4
                for parity in range(2):
                    more = back_product(projected[12 + at % 4], step, parity)
                    g_gated[j, parity] = g_gated[j, parity] + more

            pl.when(at == 32)(scores_back)

            @pl.when((at >= 32) & (at < 48))
            def _():
                for parity in range(2):
                    more = back_product(projected[at - 32], step, parity)
                    g_mixed[parity] = g_mixed[parity] + more

            @pl.when(at >= 48)
            def _():
                for parity in range(2):
                    more = back_product(value_pre[at - 48], step, parity)
                    g_normed[parity] = g_normed[parity] + more

        pl.when((at >= 24) & (at < 32))(lambda: attention_back(at - 24))
        pl.when(at == 48)(smooth_back)
        for s in range(sequences):
            pl.when(at == 49 + s)(functools.partial(filter_one, s))
            for low in range(0, states, 8):
                number = 51 + s * (states // 8) + low // 8
                pl.when(at == number)(functools.partial(moments_one, s, low))
            pl.when(at == 56 + s)(functools.partial(carry_one, s))
        pl.when(at == 52)(to_chips)
        pl.when(at == 54)(share_entering)
        pl.when(at == 59)(norm_one_back)

    every, straight_on, turning = None, False, True
    phases = (
        (0, begin, every), (1, with_sibling, every),
        (3, with_neighbour, straight_on), (5, with_corner, straight_on), (7, inner_sum, straight_on),
        (9, total_sum, straight_on), (11, finish, straight_on),
        (3, along_z(0), turning), (5, along_z(1), turning), (7, along_z(2), turning), (9, go_straight, turning),
        (11, with_both, turning), (13, inner_sum, turning), (15, total_sum, turning), (17, finish, turning),
    )
    fetch(0, "start")
    fetch(1, "start")

    def arrive(first, end):
        for item in copies_in[first:end]:
            item.wait()

    arrive(0, 3)

    def step(at, carry):
        for after, phase, which in sorted(phases, key=lambda item: -item[0]):
            chunk = at - after
            wanted = (chunk >= 0) & (chunk <= chunks)
            if which is not None:
                wanted = wanted & (turns(chunk) == which)

            @pl.when(wanted)
            def _(chunk=chunk, phase=phase):
                phase(chunk)

        pl.when(at == 0)(lambda: arrive(3, 4))
        pl.when(at == 8)(lambda: arrive(4, kept_count))
        work(at)
        return carry

    lax.fori_loop(0, chunks + 1 + 11, step, 0)


def call_backward(row_valid, key_valid, w_high, w_low, kept, grad_shapes):
    _, rows, width = kept[3].shape
    soft, signal, enter = kept[17], kept[20], kept[21]
    states = enter.shape[1]
    half, piece = 4 * lanes, lanes // 2
    vmem, anywhere = pl.BlockSpec(memory_space=pltpu.VMEM), pl.BlockSpec(memory_space=pl.ANY)
    shapes = [f32(rows, 8 * lanes)] + [f32(*shape) for shape in grad_shapes] + [f32(lanes, lanes)]
    held = [
        (4, 2, 2, 2, piece, width), (10, 2, 2, 2, piece, width), (4, 2, 2, 2, piece, width),
        (6, 2, piece, width), (6, 2, piece, width), (6, piece, width), (6, piece, width),
        (10, 2, piece, width), (10, 2, piece, width), (10, 2, piece, width), (8, lanes, width),
        (3, 6, lanes // 4, width), (2, 6, lanes // 8, width), (2, 6, 2, piece, width),
    ]
    more = [
        (2, rows, half), (2, 2, rows, half), (2, rows, half), (2, rows, half), soft.shape, (rows, lanes),
        signal.shape, signal.shape, (2, *enter.shape), (4, enter.shape[0], states // 2, 8, lanes),
        (2, enter.shape[0], states // 2, 8, lanes), enter.shape, (3, states, 8, lanes),
        (states, 8, lanes), (states, 8, lanes), enter.shape, (8, lanes, lanes),
    ]
    return pl.pallas_call(
        backward_body,
        out_shape=shapes,
        in_specs=[vmem] * 2 + [anywhere] * (2 + kept_count),
        out_specs=[vmem] + [anywhere] * (len(shapes) - 1),
        scratch_shapes=[pltpu.VMEM(item.shape, item.dtype) for item in kept]
        + [pltpu.VMEM(shape, jnp.float32) for shape in held]
        + [pltpu.VMEM((3, 2, half, width), jnp.bfloat16)] * 2
        + [pltpu.VMEM(shape, jnp.float32) for shape in more]
        + [
            pltpu.SemaphoreType.DMA((2, 3)),
            pltpu.SemaphoreType.DMA((kept_count,)),
            pltpu.SemaphoreType.DMA((16, 14)),
            pltpu.SemaphoreType.DMA((16, 14)),
            pltpu.SemaphoreType.DMA((2, 14)),
            pltpu.SemaphoreType.DMA((5,)),
            pltpu.SemaphoreType.DMA((5,)),
        ],
        compiler_params=pltpu.CompilerParams(
            collective_id=1, has_side_effects=True, vmem_limit_bytes=62 * 1024 * 1024
        ),
    )(row_valid, key_valid, w_high, w_low, *kept)


def call_kernel(body, shapes, *operands):
    return pl.pallas_call(
        body,
        out_shape=[jax.ShapeDtypeStruct(shape, jnp.float32) for shape in shapes],
        in_specs=[pl.BlockSpec(memory_space=pltpu.VMEM)] * len(operands),
        out_specs=[pl.BlockSpec(memory_space=pltpu.VMEM)] * len(shapes),
        compiler_params=pltpu.CompilerParams(vmem_limit_bytes=32 * 1024 * 1024),
    )(*operands)


def entering(ends, block_decay, backward):
    count, mine = lax.axis_size("seq"), lax.axis_index("seq")
    pieces = lax.all_gather(ends, "seq")
    if backward:
        mine = count - 1 - mine
    total = jnp.zeros_like(ends)
    for position in range(count - 1):
        piece = pieces[count - 1 - position if backward else position]
        total = jnp.where(position < mine, block_decay * total + piece, total)
    return total


def silu(value):
    return value * jax.nn.sigmoid(value)


def silu_slope(value):
    gate = jax.nn.sigmoid(value)
    return gate * (1.0 + value * (1.0 - gate))


def normalise(signal):
    centre = jnp.mean(signal, axis=-1, keepdims=True)
    shifted = signal - centre
    spread = jnp.mean(shifted * shifted, axis=-1, keepdims=True)
    scale = lax.rsqrt(spread + norm_eps)
    return shifted * scale, scale


def normalise_back(grad, gain, hat, scale):
    inner = grad * gain
    return (
        inner
        - jnp.mean(inner, axis=-1, keepdims=True)
        - hat * jnp.mean(inner * hat, axis=-1, keepdims=True)
    ) * scale


def times(left, right):
    return jnp.dot(left, right, precision=triple)


def times_back(left, right):
    return lax.dot_general(left, right, (((1,), (1,)), ((), ())), precision=triple)


def plain_layer(masked_in, normed, mix_pre, g_out, row_valid, key_valid, affine, gain_two, weights):
    value_full, mix_full, merge_full, widen_full, narrow_full = (gather_rows(w) for w in weights)
    rows, width = masked_in.shape
    sequences, _, block_len = key_valid.shape
    value_dim, shared_dim = value_full.shape[1], affine.shape[0]
    mixed = silu(mix_pre)
    value_pre = times(normed, value_full)
    values = silu(value_pre)
    projected = times(mixed, mix_full)
    second_cut = width + shared_dim
    third_cut = second_cut + value_dim
    update = jax.nn.sigmoid(projected[:, :width])
    shared_pre = projected[:, width:second_cut]
    reset_pre = projected[:, second_cut:third_cut]
    shared = silu(shared_pre)
    reset_gate = silu(reset_pre)
    queries = (shared * affine[:, 0] + affine[:, 2]).reshape(sequences, block_len, shared_dim)
    key_rows = (shared * affine[:, 1]).reshape(sequences, block_len, shared_dim)
    score_scale = shared_dim ** (-0.5)
    scores = jnp.einsum("cqz,ckz->cqk", queries, key_rows, precision=exact) * score_scale
    scores = jnp.where(key_valid > 0.5, scores, masked_score)
    soft = jax.nn.softmax(scores, axis=-1)
    values_cut = values.reshape(sequences, block_len, value_dim)
    attended = jnp.einsum("cqk,ckv->cqv", soft, values_cut, precision=triple)
    attended = attended.reshape(rows, value_dim)
    gated = attended * reset_gate
    cand_pre = projected[:, third_cut:] + times(gated, merge_full)
    candidate = silu(cand_pre)
    middle = masked_in + update * (candidate - masked_in)
    hat_two, scale_two = normalise(middle)
    normed_two = hat_two * gain_two
    wide_pre = times(normed_two, widen_full)
    hidden = silu(wide_pre)
    block_out = (middle + times(hidden, narrow_full)) * row_valid

    g_wide = times_back(g_out, narrow_full) * silu_slope(wide_pre)
    g_normed_two = times_back(g_wide, widen_full)
    gain_sum = jnp.sum(g_normed_two * hat_two, axis=0)
    g_middle = g_out + normalise_back(g_normed_two, gain_two, hat_two, scale_two)
    g_cand = g_middle * update * silu_slope(cand_pre)
    g_gated = times_back(g_cand, merge_full)
    g_attended = (g_gated * reset_gate).reshape(sequences, block_len, value_dim)
    g_soft = jnp.einsum("cqv,ckv->cqk", g_attended, values_cut, precision=triple)
    g_values = jnp.einsum("cqk,cqv->ckv", soft, g_attended, precision=triple)
    g_scores = soft * (g_soft - jnp.sum(g_soft * soft, axis=-1, keepdims=True))
    g_scores = jnp.where(key_valid > 0.5, g_scores, 0.0) * score_scale
    g_queries = jnp.einsum("cqk,ckz->cqz", g_scores, key_rows, precision=exact)
    g_keys = jnp.einsum("cqk,cqz->ckz", g_scores, queries, precision=exact)
    g_queries = g_queries.reshape(rows, shared_dim)
    g_keys = g_keys.reshape(rows, shared_dim)
    terms = (g_queries * shared, g_keys * shared, g_queries)
    affine_sum = jnp.stack([jnp.sum(term, axis=0) for term in terms])
    g_shared = (g_queries * affine[:, 0] + g_keys * affine[:, 1]) * silu_slope(shared_pre)
    g_update = g_middle * (candidate - masked_in) * update * (1.0 - update)
    g_reset = g_gated * attended * silu_slope(reset_pre)
    g_projected = jnp.concatenate([g_update, g_shared, g_reset, g_cand], axis=1)
    g_mixed = times_back(g_projected, mix_full)
    g_val = g_values.reshape(rows, value_dim) * silu_slope(value_pre)
    g_from_values = times_back(g_val, value_full)

    def total(packed):
        count = lax.axis_size("seq")
        features = packed.shape[1] // count

        def reduced(whole, tiled=True):
            part = lax.psum_scatter(whole, "seq", scatter_dimension=0, tiled=tiled)
            return lax.psum(part, "batch")

        pairs = (
            (normed, g_val),
            (mixed, g_projected),
            (gated, g_cand),
            (normed_two, g_wide),
            (hidden, g_out),
        )
        grads = tuple(reduced(product_grad(*pair)) for pair in pairs)
        blocks = packed.reshape(-1, count, features).transpose(1, 0, 2)
        return grads + (reduced(blocks, False),)

    return block_out, g_mixed, g_from_values, g_middle * (1.0 - update), gain_sum, affine_sum, total


def plane_layer(tokens, out_grad, valid, logits, rows_of, affine, weights):
    sequences, block_len, width = tokens.shape
    rows = sequences * block_len
    states, own = logits[0].shape
    device = lax.axis_index("seq")
    alpha, delta, beta, gamma = logits
    alpha_rate, damp_rate = jax.nn.sigmoid(alpha), jax.nn.sigmoid(delta)
    out_scale = states ** (-0.5)
    weight = alpha_rate * beta * gamma * out_scale
    block_decay = jnp.exp(block_len * jnp.log1p(-alpha_rate * damp_rate))
    spread = lax.dynamic_update_slice(
        jnp.zeros((3, own), jnp.float32), affine.T, (0, device * affine.shape[0])
    )
    packed = jnp.concatenate([1.0 - alpha_rate * damp_rate, weight, block_decay, rows_of, spread])
    packed = jnp.pad(packed, ((0, -packed.shape[0] % 8), (0, 0)))
    row_valid = valid.reshape(rows, 1)
    key_valid = valid.reshape(sequences, 1, block_len)
    block_out, w_high, w_low, *kept = call_forward(
        weights, packed, tokens.reshape(rows, width), out_grad.reshape(rows, width), row_valid, key_valid, states
    )
    value_weight, mix_weight, merge_weight, widen_weight, narrow_weight = weights
    tokens_grad, narrow, widen, merge, mix, value, sums = call_backward(
        row_valid,
        key_valid,
        w_high,
        w_low,
        kept,
        [w.shape for w in (narrow_weight, widen_weight, merge_weight, mix_weight, value_weight)],
    )
    direct, slope = sums[:states], sums[states : 2 * states]
    decay_grad = weight * slope
    alpha_grad = (beta * gamma * out_scale * direct - damp_rate * decay_grad) * (
        alpha_rate * (1.0 - alpha_rate)
    )
    delta_grad = -alpha_rate * decay_grad * damp_rate * (1.0 - damp_rate)
    beta_grad = alpha_rate * gamma * out_scale * direct
    gamma_grad = alpha_rate * beta * out_scale * direct
    affine_grad = lax.dynamic_slice(
        sums[2 * states + 3 : 2 * states + 6], (0, device * affine.shape[0]), affine.T.shape
    )
    return (
        block_out.reshape(tokens.shape),
        tokens_grad.reshape(tokens.shape),
        sums[2 * states],
        alpha_grad.T,
        delta_grad.T,
        beta_grad.T,
        gamma_grad.T,
        sums[2 * states + 1],
        value,
        mix,
        affine_grad.T,
        merge,
        sums[2 * states + 2],
        widen,
        narrow,
    )


def per_device(
    tokens,
    lengths,
    out_grad,
    first_gain,
    smooth_alpha,
    smooth_delta,
    smooth_beta,
    smooth_gamma,
    smooth_omega,
    value_weight,
    mix_weight,
    query_affine,
    merge_weight,
    second_gain,
    widen_weight,
    narrow_weight,
):
    sequences, block_len, width = tokens.shape
    count = lax.axis_size("seq")
    states = smooth_alpha.shape[1]
    own = first_gain.shape[0]
    own_shared = query_affine.shape[0]
    rows = sequences * block_len
    shared_dim = own_shared * count
    offsets = lax.axis_index("seq") * block_len + lax.iota(jnp.int32, block_len)
    valid = (offsets[None, :] < lengths[:, None]).astype(jnp.float32)
    weights = (value_weight, mix_weight, merge_weight, widen_weight, narrow_weight)
    if count == 8 and lax.axis_size("batch") == 4:
        logits = (smooth_alpha.T, smooth_delta.T, smooth_beta.T, smooth_gamma.T)
        rows_of = jnp.stack([first_gain, smooth_omega, second_gain])
        return plane_layer(tokens, out_grad, valid, logits, rows_of, query_affine, weights)

    affine_row = jnp.pad(query_affine.reshape(-1), (0, own - 3 * own_shared))
    packed = [
        smooth_alpha.T,
        smooth_delta.T,
        smooth_beta.T,
        smooth_gamma.T,
        jnp.stack([first_gain, smooth_omega, second_gain, affine_row]),
    ]
    small = lax.all_gather(jnp.concatenate(packed, axis=0), "seq").transpose(1, 0, 2)

    tiles = (width // lanes, lanes)
    alpha_rate = jax.nn.sigmoid(small[:states].reshape(states, *tiles))
    damp_rate = jax.nn.sigmoid(small[states : 2 * states].reshape(states, *tiles))
    beta = small[2 * states : 3 * states].reshape(states, *tiles)
    gamma = small[3 * states : 4 * states].reshape(states, *tiles)
    gain_one = small[4 * states].reshape(1, width)
    omega = small[4 * states + 1].reshape(1, width)
    gain_two = small[4 * states + 2].reshape(1, width)
    affine = small[4 * states + 3, :, : 3 * own_shared].reshape(shared_dim, 3)
    out_scale = states ** (-0.5)
    decay = 1.0 - alpha_rate * damp_rate
    block_decay = jnp.exp(block_len * jnp.log1p(-alpha_rate * damp_rate))
    weight = alpha_rate * beta * gamma * out_scale

    row_valid = valid.reshape(rows, 1)
    key_valid = valid.reshape(sequences, 1, block_len)

    masked_in = tokens.reshape(rows, width) * row_valid
    g_out = out_grad.reshape(rows, width) * row_valid
    hat_one, scale_one = normalise(masked_in)
    normed = hat_one * gain_one
    tiled = (sequences, block_len) + tiles
    ending = (sequences, states) + tiles
    signal = normed.reshape(tiled)
    local, ends = call_kernel(
        functools.partial(filter_body, False), [tiled, ending], decay, weight, signal
    )
    enter = entering(ends, block_decay, False)
    (smoothed,) = call_kernel(
        functools.partial(carried_body, False), [tiled], decay, weight, enter, local
    )
    mix_pre = smoothed.reshape(rows, width) + omega * normed

    results = plain_layer(
        masked_in, normed, mix_pre, g_out, row_valid, key_valid, affine, gain_two, weights
    )
    block_out, g_mixed, g_from_values, g_rest, second_gain_sum, affine_sum, total = results
    g_smooth = g_mixed * silu_slope(mix_pre)

    smooth_tiled = g_smooth.reshape(tiled)
    back_local, back_ends = call_kernel(
        functools.partial(filter_body, True), [tiled, ending], decay, weight, smooth_tiled
    )
    back_enter = entering(back_ends, block_decay, True)
    direct, slope, last = call_kernel(
        moments_body,
        [(states,) + tiles, (states,) + tiles, ending],
        decay,
        enter,
        signal,
        smooth_tiled,
    )
    (back_full,) = call_kernel(
        functools.partial(carried_body, True), [tiled], decay, weight, back_enter, back_local
    )
    slope = slope + decay * jnp.sum(back_enter * last, axis=0)
    decay_grad = weight * slope
    alpha_grad = (beta * gamma * out_scale * direct - damp_rate * decay_grad) * (
        alpha_rate * (1.0 - alpha_rate)
    )
    delta_grad = -alpha_rate * decay_grad * damp_rate * (1.0 - damp_rate)
    beta_grad = alpha_rate * gamma * out_scale * direct
    gamma_grad = alpha_rate * beta * out_scale * direct

    g_normed = g_from_values + g_smooth * omega + back_full.reshape(rows, width)
    tokens_grad = (g_rest + normalise_back(g_normed, gain_one, hat_one, scale_one)) * row_valid
    first_gain_sum = jnp.sum(g_normed * hat_one, axis=0)
    omega_sum = jnp.sum(g_smooth * normed, axis=0)
    affine_rows = jnp.pad(
        affine_sum.T.reshape(count, 3 * own_shared), ((0, 0), (0, own - 3 * own_shared))
    )
    small_rows = [
        alpha_grad.reshape(states, width),
        delta_grad.reshape(states, width),
        beta_grad.reshape(states, width),
        gamma_grad.reshape(states, width),
        jnp.stack([first_gain_sum, omega_sum, second_gain_sum, affine_rows.reshape(width)]),
    ]
    value_grad, mix_grad, merge_grad, widen_grad, narrow_grad, small_grad = total(
        jnp.concatenate(small_rows, axis=0)
    )

    return (
        block_out.reshape(tokens.shape),
        tokens_grad.reshape(tokens.shape),
        small_grad[4 * states],
        small_grad[:states].T,
        small_grad[states : 2 * states].T,
        small_grad[2 * states : 3 * states].T,
        small_grad[3 * states : 4 * states].T,
        small_grad[4 * states + 1],
        value_grad,
        mix_grad,
        small_grad[4 * states + 3, : 3 * own_shared].reshape(own_shared, 3),
        merge_grad,
        small_grad[4 * states + 2],
        widen_grad,
        narrow_grad,
    )


def solution(mesh):
    rows = P("batch", "seq", None)
    split = P("seq", None)
    in_specs = (
        (rows, P("batch"), rows, P("seq"))
        + (split,) * 4
        + (P("seq"),)
        + (split,) * 4
        + (P("seq"),)
        + (split,) * 2
    )
    out_specs = (
        (rows, rows, P("seq"))
        + (split,) * 4
        + (P("seq"),)
        + (split,) * 4
        + (P("seq"),)
        + (split,) * 2
    )
    return jax.shard_map(
        per_device, mesh=mesh, in_specs=in_specs, out_specs=out_specs, check_vma=False
    )
```

```python
import functools

import jax
import jax.numpy as jnp
from jax import lax
from jax.experimental import pallas as pl
from jax.experimental.pallas import tpu as pltpu
from jax.sharding import PartitionSpec as P

exact = lax.Precision.HIGHEST
triple = lax.Precision.HIGH
norm_eps = 1e-05
masked_score = -1000000000.0
lanes = 128


def gather_rows(shard):
    return lax.all_gather(shard, "seq", axis=0, tiled=True)


def product_grad(left, right):
    return lax.dot_general(left, right, (((0,), (0,)), ((), ())), precision=triple)


def halves(value):
    high = value.astype(jnp.bfloat16)
    return high, (value - high.astype(jnp.float32)).astype(jnp.bfloat16)


def contract(left, right, left_dim, right_dim, precision=None):
    return lax.dot_general(
        left, right, (((left_dim,), (right_dim,)), ((), ())),
        precision=precision, preferred_element_type=jnp.float32,
    )


def turned(left, right):
    return contract(left, right, 0, 0)


def three(left, right, left_dim, right_dim):
    (high, low), (other, rest) = left, right
    return contract(high, other, left_dim, right_dim) + (
        contract(low, other, left_dim, right_dim) + contract(high, rest, left_dim, right_dim)
    )


def place_of(device):
    return (device % 2) * 4 + device // 2


def tree_sum(terms):
    while len(terms) > 1:
        terms = [a + b for a, b in zip(terms[::2], terms[1::2])] + (
            [terms[-1]] if len(terms) % 2 else []
        )
    return terms[0]


def run_filter(reverse, s, decay_ref, weight_ref, signal_ref, out_ref, end_ref):
    length, states = signal_ref.shape[1], decay_ref.shape[0]

    def step(t, held):
        at = length - 1 - t if reverse else t
        entry = signal_ref[s, at]
        held = tuple(decay_ref[n] * held[n] + entry for n in range(states))
        out_ref[s, at] = tree_sum([weight_ref[n] * held[n] for n in range(states)])
        return held

    zero = jnp.zeros(signal_ref.shape[2:], jnp.float32)
    held = lax.fori_loop(0, length, step, (zero,) * states, unroll=4)
    for n in range(states):
        end_ref[s, n] = held[n]


def run_carried(reverse, s, decay_ref, weight_ref, enter_ref, local_ref, out_ref):
    length, states = local_ref.shape[1], decay_ref.shape[0]

    def step(t, held):
        at = length - 1 - t if reverse else t
        held = tuple(decay_ref[n] * held[n] for n in range(states))
        out_ref[s, at] = local_ref[s, at] + tree_sum(list(held))
        return held

    start = tuple(weight_ref[n] * enter_ref[s, n] for n in range(states))
    lax.fori_loop(0, length, step, start, unroll=4)


def run_moments(s, low, high, decay_ref, enter_ref, signal_ref, grad_ref, direct_ref, slope_ref, last_ref):
    length, span = signal_ref.shape[1], range(low, high)
    zero = jnp.zeros(signal_ref.shape[2:], jnp.float32)

    def step(t, carry):
        held, slope, direct, sloped = carry
        entry, grad = signal_ref[s, t], grad_ref[s, t]
        slope = tuple(decay_ref[n] * d + h for n, d, h in zip(span, slope, held))
        held = tuple(decay_ref[n] * h + entry for n, h in zip(span, held))
        direct = tuple(q + grad * h for q, h in zip(direct, held))
        sloped = tuple(q + grad * d for q, d in zip(sloped, slope))
        return held, slope, direct, sloped

    zeros = (zero,) * len(span)
    if s:
        sums = (tuple(direct_ref[n] for n in span), tuple(slope_ref[n] for n in span))
    else:
        sums = (zeros, zeros)
    start = (tuple(enter_ref[s, n] for n in span), zeros) + sums
    _, slope, direct, sloped = lax.fori_loop(0, length, step, start, unroll=2)
    for k, n in enumerate(span):
        last_ref[s, n], direct_ref[n], slope_ref[n] = slope[k], direct[k], sloped[k]


def filter_body(reverse, decay_ref, weight_ref, signal_ref, out_ref, end_ref):
    for s in range(signal_ref.shape[0]):
        run_filter(reverse, s, decay_ref, weight_ref, signal_ref, out_ref, end_ref)


def carried_body(reverse, decay_ref, weight_ref, enter_ref, local_ref, out_ref):
    for s in range(local_ref.shape[0]):
        run_carried(reverse, s, decay_ref, weight_ref, enter_ref, local_ref, out_ref)


def moments_body(decay_ref, enter_ref, signal_ref, grad_ref, *outs):
    states = decay_ref.shape[0]
    for low in range(0, states, 8):
        for s in range(signal_ref.shape[0]):
            run_moments(s, low, min(low + 8, states), decay_ref, enter_ref, signal_ref, grad_ref, *outs)


def on_other(**coordinate):
    return dict(device_id=coordinate, device_id_type=pl.DeviceIdType.MESH)


def chunk_table(shapes):
    firsts, chunk = [], 0
    for blocks, wide in shapes:
        firsts.append(chunk)
        chunk += blocks * wide
    return firsts, chunk


def others_of(me):
    core, along_x, along_y = me % 2, (me // 2) % 2, me // 4
    across_x = me + 2 - 4 * along_x
    return me + 1 - 2 * core, across_x, me + 4 - 8 * along_y, across_x + 4 - 8 * along_y


def state_exchange(reverse, block_ref, ends, chip_ends, halves_ref, enter_ref, sent, came):
    me = lax.axis_index("seq")
    core, chip = me % 2, me // 2
    sibling, *chips = others_of(me)
    first = 1 if reverse else 0
    _, sequences, states = ends.shape[:3]
    half = states // 2

    def copies(step):
        if step == 0:
            pairs = [(ends.at[core], sibling)]
        elif step == 1:
            pairs = [(chip_ends.at[chip], other) for other in chips]
        else:
            pairs = [(halves_ref.at[core], sibling)]
        for number, (piece, other) in enumerate(pairs):
            at = (0, 1, 4)[step] + number
            yield pltpu.make_async_remote_copy(
                src_ref=piece, dst_ref=piece, send_sem=sent.at[at], recv_sem=came.at[at], **on_other(seq=other)
            )

    def start(step):
        for item in copies(step):
            item.start()

    def wait(step):
        for item in copies(step):
            item.wait()

    def share_ends():
        start(0)

    def to_chips():
        wait(0)

        def one(i, carry):
            n = core * half + i
            for s in range(sequences):
                chip_ends[chip, s, i] = block_ref[n] * ends[first, s, n] + ends[1 - first, s, n]
            return carry

        lax.fori_loop(0, half, one, 0)
        start(1)

    def share_entering():
        wait(1)
        mine = 3 - chip if reverse else chip

        def one(i, carry):
            decay = block_ref[core * half + i]
            decay = decay * decay
            for s in range(sequences):
                total = jnp.zeros(block_ref.shape[1:], jnp.float32)
                for position in range(3):
                    piece = chip_ends[3 - position if reverse else position, s, i]
                    total = jnp.where(position < mine, decay * total + piece, total)
                halves_ref[core, s, i] = total
            return carry

        lax.fori_loop(0, half, one, 0)
        start(2)

    def enter():
        wait(2)

        def one(n, carry):
            for s in range(sequences):
                total = halves_ref[n // half, s, n % half]
                later = block_ref[n] * total + ends[first, s, n]
                enter_ref[s, n] = jnp.where(core == first, total, later)
            return carry

        lax.fori_loop(0, states, one, 0)

    return share_ends, to_chips, share_entering, enter


kept_count = 25
gather_shapes = ((1, 8), (1, 16), (2, 4), (1, 16), (4, 4))


def forward_body(
    value_ref, mix_ref, merge_ref, widen_ref, narrow_ref, packed, tokens, out_grad, row_valid, key_valid,
    block_out, w_high, w_low, *refs,
):
    kept, held, refs = refs[:kept_count], refs[kept_count : 2 * kept_count], refs[2 * kept_count :]
    (
        hidden_h, hidden_l, g_out, g_wide, two_h, two_l, gated_h, gated_l, mixed_h, mixed_l, normed_h, normed_l,
        value_pre, projected, middle, attended, shared_pre, soft, cand_pre, masked, signal, enter, mix_pre, small, shared_w,
    ) = held
    buf, stage_h, stage_l, g_hidden, smoothed, ends, chip_ends, halves_in, tables = refs[:9]
    loaded, sent, came, stored, near, sent_all, came_all, sent_state, came_state, saved = refs[9:]
    weights = (value_ref, mix_ref, merge_ref, widen_ref, narrow_ref)
    firsts, chunks = chunk_table(gather_shapes)
    depth, width = buf.shape[0], buf.shape[-1]
    half = lanes * 4
    me, level = lax.axis_index("seq"), lax.axis_index("batch")
    id_sibling, id_x, id_y, id_corner = others_of(me)
    mine, at_x, at_y, at_corner = (place_of(device) for device in (me, id_x, id_y, id_corner))
    above, below = (level + 1) % 4, (level + 3) % 4

    barrier = pltpu.get_barrier_semaphore()
    for other in (id_sibling, id_x, id_y, id_corner):
        pl.semaphore_signal(barrier, inc=1, **on_other(seq=other))
    for target in (above, below):
        pl.semaphore_signal(barrier, inc=1, **on_other(batch=target))
    pl.semaphore_wait(barrier, 6)

    names = ["x", "y", "sibling", "corner_x", "corner_y", "x_more", "y_more"]
    names += ["sibling_x", "sibling_y", "sibling_corner"]
    names += [f"ring{number}{of}" for of in ("", "_x", "_y") for number in range(3)]

    def link(name, chunk):
        slot = chunk % depth
        block = {"x": at_x, "y": at_y, "corner": at_corner}
        kind, _, of = name.partition("_")
        by_x, by_y, by_core, by_z = ({"seq": id_x}, {"seq": id_y}, {"seq": id_sibling}, {"batch": above})
        if kind == "sibling":
            piece, target = buf.at[slot, block[of] if of else mine], by_core
        elif kind == "corner":
            if of == "x":
                piece, target = buf.at[slot, at_x, level, pl.ds(0, 2)], by_y
            else:
                piece, target = buf.at[slot, at_y, level, pl.ds(2, 2)], by_x
        elif kind[:4] == "ring":
            quarter = (level + 4 - int(kind[4])) % 4
            if of:
                piece = buf.at[slot, block[of], quarter, 3 if of == "x" else 0]
            else:
                piece = buf.at[slot, at_corner, quarter]
            target = by_z
        else:
            target = by_x if kind == "x" else by_y
            if of == "more":
                piece = buf.at[slot, mine, level, 3 if kind == "x" else 0]
            elif of == "part":
                piece = buf.at[slot, mine, :, pl.ds(0 if kind == "x" else 1, 3)]
            else:
                piece = buf.at[slot, mine]
        number = names.index(name.removesuffix("_part"))
        return pltpu.make_async_remote_copy(
            src_ref=piece, dst_ref=piece, send_sem=sent.at[number, slot], recv_sem=came.at[number, slot],
            **on_other(**target),
        )

    def shares(chunk):
        return (chunk % 3 != 2) & (chunk < 58)

    def own_load(weight, block, column, slot):
        source = weight.at[pl.ds(block * 4, 4), :, :, pl.ds(pl.multiple_of(column, lanes), width)]
        return pltpu.make_async_copy(source, buf.at[slot, mine], loaded.at[slot])

    def load(chunk):
        slot = chunk % depth
        for number, ((blocks, wide), first, weight) in enumerate(
            zip(gather_shapes, firsts, weights)
        ):

            @pl.when((chunk >= first) & (chunk < first + blocks * wide))
            def _(number=number, first=first, wide=wide, weight=weight):
                block = (chunk - first) // wide
                column = ((chunk - first) % wide) * width
                if number == 1:
                    column = column + jnp.where(column >= features, lanes, 0)
                own_load(weight, block, column, slot).start()

    def send(chunk):
        own_load(value_ref, 0, 0, chunk % depth).wait()
        both = shares(chunk)
        link("sibling", chunk).start()

        @pl.when(both)
        def _():
            for name in ("x_part", "y_part", "x_more", "y_more"):
                link(name, chunk).start()

        @pl.when(jnp.logical_not(both))
        def _():
            link("x", chunk).start()
            link("y", chunk).start()

    def relay(chunk):
        both = shares(chunk)
        link("sibling", chunk).wait()

        @pl.when(both)
        def _():
            for name in ("x_part", "y_part", "x_more", "y_more"):
                link(name, chunk).wait()
            link("ring0_x", chunk).start()
            link("ring0_y", chunk).start()

        @pl.when(jnp.logical_not(both))
        def _():
            link("x", chunk).wait()
            link("y", chunk).wait()

        link("corner_x", chunk).start()
        link("corner_y", chunk).start()

    def ring(number):
        def phase(chunk):
            if number:
                link(f"ring{number - 1}", chunk).wait()
            else:
                link("corner_x", chunk).wait()
                link("corner_y", chunk).wait()

            @pl.when(shares(chunk))
            def _():
                for of in "xy":
                    link(f"ring{number}_{of}", chunk).wait()
                    if number < 2:
                        link(f"ring{number + 1}_{of}", chunk).start()

            link(f"ring{number}", chunk).start()

        return phase

    def to_sibling(chunk):
        link("ring2", chunk).wait()
        for name in ("sibling_x", "sibling_y", "sibling_corner"):
            link(name, chunk).start()

    def store(chunk, kind):
        return pltpu.make_async_copy(
            (stage_h, stage_l)[kind].at[chunk % 2],
            (w_high, w_low)[kind].at[chunk],
            stored.at[kind, chunk % 2],
        )

    def product(left_h, left_l, right):
        return three((left_h[0], left_l[0]), (right[0][0], right[1][0]), 1, 0) + three(
            (left_h[1], left_l[1]), (right[0][1], right[1][1]), 1, 0
        )

    sequences, block_len = soft.shape[:2]
    states = tables.shape[1]
    decay, weight, block_decay = (tables.at[kind] for kind in range(3))
    features = tokens.shape[1]
    tiles = features // width

    share_ends, to_chips, share_entering, enter_states = state_exchange(
        False, block_decay, ends, chip_ends, halves_in, enter, sent_state, came_state
    )

    def share(kind, numbers):
        sources = (me,) * 4 + (id_x, id_y, id_corner)
        targets = (id_sibling, id_x, id_y, id_corner) + (id_sibling,) * 3
        for number in numbers:
            if kind == 0:
                piece = small.at[sources[number]]
            else:
                piece = shared_w.at[place_of(sources[number])]
            yield pltpu.make_async_remote_copy(
                src_ref=piece, dst_ref=piece, send_sem=sent_all.at[kind, number],
                recv_sem=came_all.at[kind, number], **on_other(seq=targets[number]),
            )

    def own_shared():
        return pltpu.make_async_copy(
            mix_ref.at[:, :, :, pl.ds(features, lanes)], shared_w.at[mine], near
        )

    def row_of(number, k):
        return jnp.concatenate(
            [small[2 * k, number : number + 1], small[2 * k + 1, number : number + 1]], axis=1
        )

    def hand_out():
        own_shared().start()
        small[me] = packed[...]
        for item in share(0, range(4)):
            item.start()
        own_shared().wait()
        for item in share(1, range(4)):
            item.start()

    def pass_on():
        for kind in (0, 1):
            for item in share(kind, range(4)):
                item.wait()
            for item in share(kind, range(4, 7)):
                item.start()

    def norm_one():
        for item in share(0, range(4, 7)):
            item.wait()
        for kind in range(3):
            for n in range(states):
                tables[kind, n] = small[:, kind * states + n]
        keep = row_valid[...]
        value = tokens[...] * keep
        centre = jnp.mean(value, axis=1, keepdims=True)
        shifted = value - centre
        scale = lax.rsqrt(jnp.mean(shifted * shifted, axis=1, keepdims=True) + norm_eps)
        gain = jnp.concatenate([row_of(3 * states, k) for k in range(tiles)], axis=1)
        normed = shifted * scale * gain
        for k in range(tiles):
            span = slice(k * width, (k + 1) * width)
            masked[k] = value[:, span]
            g_out[k] = out_grad[:, span] * keep
            for parity in range(2):
                start = k * width + parity * lanes
                put(normed_h, normed_l, (parity,), k * lanes, normed[:, start : start + lanes])
        for s in range(sequences):
            rows = normed[s * block_len : (s + 1) * block_len]
            signal[s] = rows.reshape(signal.shape[1:])

    def filter_one(s):
        run_filter(False, s, decay, weight, signal, smoothed, ends.at[me % 2])
        if s == sequences - 1:
            share_ends()

    def carry_one(s):
        if s == 0:
            enter_states()
        run_carried(False, s, decay, weight, enter, smoothed, smoothed)

    def mix_in():
        for s in range(sequences):
            span = slice(s * block_len, (s + 1) * block_len)
            skip = jnp.concatenate([row_of(3 * states + 1, k) for k in range(tiles)], axis=1)
            normed = signal[s].reshape(block_len, features)
            value = smoothed[s].reshape(block_len, features) + skip * normed
            mixed = value * jax.nn.sigmoid(value)
            for block in range(8):
                cut = slice(block * lanes, (block + 1) * lanes)
                to = (block % 2, span, slice(block // 2 * lanes, (block // 2 + 1) * lanes))
                mix_pre[to] = value[:, cut]
                mixed_h[to], mixed_l[to] = halves(mixed[:, cut])

    def attention():
        for item in share(1, range(4, 7)):
            item.wait()
        shared_full = halves(shared_w[...].reshape(2, half, lanes))
        total = product(mixed_h, mixed_l, shared_full)
        affine = tree_sum([small[k, 3 * states + 3 : 3 * states + 6] for k in range(8)])
        shared_pre[...] = total
        shared = total * jax.nn.sigmoid(total)
        queries = shared * affine[0:1] + affine[2:3]
        keys = shared * affine[1:2]
        for s in range(sequences):
            span = slice(s * block_len, (s + 1) * block_len)
            scores = contract(queries[span], keys[span], 1, 1, exact) * shared.shape[1] ** (-0.5)
            scores = jnp.where(key_valid[s] > 0.5, scores, masked_score)
            weight = jnp.exp(scores - jnp.max(scores, axis=1, keepdims=True))
            soft[s] = weight / jnp.sum(weight, axis=1, keepdims=True)

    def put(target_h, target_l, index, column, value):
        high, low = halves(value)
        target_h[(*index, slice(None), pl.ds(pl.multiple_of(column, lanes), lanes))] = high
        target_l[(*index, slice(None), pl.ds(pl.multiple_of(column, lanes), lanes))] = low

    def complete(chunk):
        slot = chunk % depth
        for name in ("sibling_x", "sibling_y", "sibling_corner"):
            link(name, chunk).wait()

        @pl.when(chunk >= 2)
        def _():
            store(chunk - 2, 0).wait()
            store(chunk - 2, 1).wait()

        right = halves(buf[slot].reshape(2, half, width))
        stage_h[chunk % 2] = right[0]
        stage_l[chunk % 2] = right[1]
        store(chunk, 0).start()
        store(chunk, 1).start()

        def among(number):
            blocks, wide = gather_shapes[number]
            return (chunk >= firsts[number]) & (chunk < firsts[number] + blocks * wide)

        @pl.when(among(0))
        def _():
            total = product(normed_h, normed_l, right)
            value_pre[chunk] = total
            values = total * jax.nn.sigmoid(total)
            for s in range(sequences):
                span = slice(s * block_len, (s + 1) * block_len)
                attended[chunk, span] = contract(soft[s], values[span], 1, 0, exact)

        @pl.when(among(1))
        def _():
            tile = chunk - firsts[1]
            total = product(mixed_h, mixed_l, right)
            projected[tile] = total

            @pl.when((tile >= 4) & (tile < 12))
            def _():
                block = tile - 4
                gated = attended[block] * total * jax.nn.sigmoid(total)
                for j in range(2):
                    cut = gated[:, j * lanes : (j + 1) * lanes]
                    put(gated_h, gated_l, (j, block % 2), (block // 2) * lanes, cut)

        @pl.when(among(2))
        def _():
            j, tile = (chunk - firsts[2]) // 4, (chunk - firsts[2]) % 4
            total = product(gated_h.at[j], gated_l.at[j], right)

            @pl.when(j == 0)
            def _():
                cand_pre[tile] = projected[12 + tile] + total

            @pl.when(j == 1)
            def _():
                cand_pre[tile] = cand_pre[tile] + total

            @pl.when(chunk == firsts[3] - 1)
            def _():
                total = 0.0
                for k in range(tiles):
                    cand = cand_pre[k]
                    cand = cand * jax.nn.sigmoid(cand)
                    value = masked[k] + jax.nn.sigmoid(projected[k]) * (cand - masked[k])
                    middle[k] = value
                    total = total + jnp.sum(value, axis=1, keepdims=True)
                centre = total / features
                total = 0.0
                for k in range(tiles):
                    shifted = middle[k] - centre
                    total = total + jnp.sum(shifted * shifted, axis=1, keepdims=True)
                scale = lax.rsqrt(total / features + norm_eps)
                for k in range(tiles):
                    value = (middle[k] - centre) * scale * row_of(3 * states + 2, k)
                    for parity in range(2):
                        cut = value[:, parity * lanes : (parity + 1) * lanes]
                        put(two_h, two_l, (parity,), k * lanes, cut)
                block_out[...] = jnp.zeros(block_out.shape, jnp.float32)
                g_hidden[...] = jnp.zeros(g_hidden.shape, jnp.float32)

        @pl.when(among(3))
        def _():
            tile = chunk - firsts[3]
            total = product(two_h, two_l, right)
            g_wide[tile] = total
            hidden = total * jax.nn.sigmoid(total)
            for i in range(2):
                cut = hidden[:, i * lanes : (i + 1) * lanes]
                index = (2 * (tile % 2) + i, (tile // 2) % 2)
                put(hidden_h, hidden_l, index, (tile // 4) * lanes, cut)

        @pl.when(among(4))
        def _():
            j, tile = (chunk - firsts[4]) // 4, (chunk - firsts[4]) % 4
            to = (slice(None), pl.ds(pl.multiple_of(tile * width, width), width))
            block_out[to] = block_out[to] + product(hidden_h.at[j], hidden_l.at[j], right)
            grad = halves(g_out[tile])
            for parity in range(2):
                back = three(grad, (right[0][parity], right[1][parity]), 1, 1)
                g_hidden[j, parity] = g_hidden[j, parity] + back

    def save(*numbers):
        return [
            pltpu.make_async_copy(held[number], kept[number], saved.at[number]) for number in numbers
        ]

    def begin_save(*numbers):
        for item in save(*numbers):
            item.start()

    phases = (
        (2, relay), (4, ring(0)), (6, ring(1)), (8, ring(2)), (10, to_sibling), (11, complete)
    )
    last, ahead = phases[-1][0], 2

    def step(at, carry):
        for after, phase in phases[-2::-1]:

            @pl.when((at >= after) & (at < after + chunks))
            def _(after=after, phase=phase):
                phase(at - after)

        @pl.when(at == 0)
        def _():
            for chunk in range(ahead):
                send(chunk)
            hand_out()

        pl.when((at >= 1) & (at + ahead - 1 < chunks))(lambda: send(at + ahead - 1))
        pl.when(at + ahead < chunks)(lambda: load(at + ahead))
        pl.when(at == 1)(pass_on)
        pl.when(at == 2)(norm_one)
        for s in range(sequences):
            pl.when(at == 3 + s)(functools.partial(filter_one, s))
            pl.when(at == 8 + s)(functools.partial(carry_one, s))
        pl.when(at == 5)(to_chips)
        pl.when(at == 7)(share_entering)

        @pl.when(at == 10)
        def _():
            mix_in()
            attention()

        pl.when(at == last)(lambda: begin_save(2, 8, 9, 10, 11, 16, 17, 19, 20, 21, 22, 23, 24))
        pl.when(at == last + firsts[3])(lambda: begin_save(4, 5, 6, 7, 12, 13, 14, 15, 18))
        pl.when(at == last + firsts[4])(lambda: begin_save(0, 1))

        @pl.when(at >= last)
        def _():
            complete(at - last)

        return carry

    for chunk in range(ahead):
        load(chunk)
    lax.fori_loop(0, chunks + last, step, 0)
    for chunk in (chunks - 2, chunks - 1):
        for kind in range(2):
            store(chunk, kind).wait()
    for k in range(tiles):
        span = slice(k * width, (k + 1) * width)
        block_out[:, span] = (middle[k] + block_out[:, span]) * row_valid[...]
    for k in range(g_wide.shape[0]):
        for i in range(2):
            span = slice(i * lanes, (i + 1) * lanes)
            back = g_hidden[2 * (k % 2) + i, (k // 2) % 2, :, (k // 4) * lanes : (k // 4 + 1) * lanes]
            wide = g_wide[k, :, span]
            g_wide[k, :, span] = back * silu_slope(wide)
    begin_save(3)
    for item in save(*range(kept_count)):
        item.wait()


def f32(*shape):
    return jax.ShapeDtypeStruct(shape, jnp.float32)


def b16(*shape):
    return jax.ShapeDtypeStruct(shape, jnp.bfloat16)


def call_forward(weights, packed, tokens, out_grad, row_valid, key_valid, states):
    width, half = 2 * lanes, 4 * lanes
    rows, features = tokens.shape
    sequences = key_valid.shape[0]
    block_len = rows // sequences
    _, chunks = chunk_table(gather_shapes)
    vmem, anywhere = pl.BlockSpec(memory_space=pltpu.VMEM), pl.BlockSpec(memory_space=pl.ANY)
    line = (sequences, block_len, 8, lanes)
    kept = [
        b16(4, 2, rows, half), b16(4, 2, rows, half), f32(4, rows, width), f32(16, rows, width),
        b16(2, rows, half), b16(2, rows, half), b16(2, 2, rows, half), b16(2, 2, rows, half),
        b16(2, rows, half), b16(2, rows, half), b16(2, rows, half), b16(2, rows, half),
        f32(8, rows, width), f32(16, rows, width), f32(4, rows, width), f32(8, rows, width), f32(rows, lanes),
        f32(sequences, block_len, block_len), f32(4, rows, width), f32(4, rows, width), f32(*line),
        f32(sequences, states, 8, lanes), f32(2, rows, half), f32(8, *packed.shape), f32(8, 4, 4, 8, lanes),
    ]
    shapes = [f32(rows, features)] + [b16(chunks, 2, half, width)] * 2 + kept
    depth, kinds = 16, 19
    return pl.pallas_call(
        forward_body,
        out_shape=shapes,
        in_specs=[anywhere] * len(weights) + [vmem] * 5,
        out_specs=[vmem] + [anywhere] * (len(shapes) - 1),
        scratch_shapes=[pltpu.VMEM(item.shape, item.dtype) for item in kept]
        + [
            pltpu.VMEM((depth, 8, 4, 4, 8, width), jnp.float32),
            pltpu.VMEM((2, 2, half, width), jnp.bfloat16),
            pltpu.VMEM((2, 2, half, width), jnp.bfloat16),
            pltpu.VMEM((4, 2, rows, half), jnp.float32),
            pltpu.VMEM(line, jnp.float32),
            pltpu.VMEM((2, sequences, states, 8, lanes), jnp.float32),
            pltpu.VMEM((4, sequences, states // 2, 8, lanes), jnp.float32),
            pltpu.VMEM((2, sequences, states // 2, 8, lanes), jnp.float32),
            pltpu.VMEM((3, states, 8, lanes), jnp.float32),
            pltpu.SemaphoreType.DMA((depth,)),
            pltpu.SemaphoreType.DMA((kinds, depth)),
            pltpu.SemaphoreType.DMA((kinds, depth)),
            pltpu.SemaphoreType.DMA((2, 2)),
            pltpu.SemaphoreType.DMA,
            pltpu.SemaphoreType.DMA((2, 7)),
            pltpu.SemaphoreType.DMA((2, 7)),
            pltpu.SemaphoreType.DMA((5,)),
            pltpu.SemaphoreType.DMA((5,)),
            pltpu.SemaphoreType.DMA((kept_count,)),
        ],
        compiler_params=pltpu.CompilerParams(
            collective_id=2, has_side_effects=True, vmem_limit_bytes=62 * 1024 * 1024
        ),
    )(*[w.reshape(-1, 4, 8, w.shape[1]) for w in weights], packed, tokens, out_grad, row_valid, key_valid)


reduce_shapes = ((4, 4), (1, 16), (2, 4), (1, 16), (1, 8))


def backward_body(
    row_valid, key_valid, w_high, w_low, *refs,
):
    kept, outs, refs = refs[:kept_count], refs[kept_count : kept_count + 7], refs[kept_count + 7 :]
    held, refs = refs[:kept_count], refs[kept_count:]
    (
        hidden_h, hidden_l, g_out, g_wide, two_h, two_l, gated_h, gated_l, mixed_h, mixed_l, normed_h, normed_l,
        value_pre, projected, middle, attended, shared_pre, soft, cand_pre, masked, signal, enter, mix_pre, small, shared_w,
    ) = held
    tokens_grad, narrow_grad, widen_grad, merge_grad, mix_grad, value_grad, small_grad = outs
    away, keep, got, got_x, got_y, got_xy, got_yx, part, from_edge, from_inner, done = refs[:11]
    ring, bend, straight, *refs = refs[11:]
    buf_h, buf_l, g_two, g_gated, g_mixed, g_normed, g_soft, g_shared = refs[:8]
    smooth, back, ends, chip_ends, halves_in, back_enter, tables, direct, slope, last, small_sum, stat = refs[8:20]
    fetched, read, sent, came, written, sent_state, came_state = refs[20:]
    lefts = (
        (hidden_h, hidden_l), (two_h, two_l), (gated_h, gated_l), (mixed_h, mixed_l), (normed_h, normed_l)
    )
    rights = ((g_out, 0), (g_wide, 0), (projected, 12), (projected, 0), (value_pre, 0))
    grads = (narrow_grad, widen_grad, merge_grad, mix_grad, value_grad)
    firsts, chunks = chunk_table(reduce_shapes)
    gathered, _ = chunk_table(gather_shapes)
    tiles, rows, width = masked.shape
    half, features = 4 * lanes, tiles * width
    sequences, block_len = soft.shape[:2]
    states = tables.shape[1]
    decay, weight, block_decay = (tables.at[kind] for kind in range(3))
    me, level = lax.axis_index("seq"), lax.axis_index("batch")
    core, along_x, along_y = me % 2, (me // 2) % 2, me // 4
    is_edge = (level == 0) | (level == 3)
    partner = jnp.where(level < 2, 1 - level, 5 - level)
    near = others_of(me)
    sibling, across_x, across_y = ({"seq": other} for other in near[:3])

    copies_in = [
        pltpu.make_async_copy(source, target, read.at[number])
        for number, (source, target) in enumerate(zip(kept, held))
    ]
    for item in copies_in:
        item.start()

    barrier = pltpu.get_barrier_semaphore()
    for other in near:
        pl.semaphore_signal(barrier, inc=1, **on_other(seq=other))
    above = (level + 1) % 4
    for other in (above, (level + 3) % 4):
        pl.semaphore_signal(barrier, inc=1, **on_other(batch=other))
    pl.semaphore_wait(barrier, 6)

    def slot_in(ref, chunk):
        return chunk % ref.shape[0]

    def turns(chunk):
        return (chunk % 2 == 1) & (chunk < 49)

    def slot_of(chunk, plain, turning):
        number = chunk // 2
        return jnp.where(turns(chunk), plain + number % turning, chunk % plain)

    def turn_slot(chunk):
        return chunk // 2 % 6

    def keep_slot(chunk):
        return slot_of(chunk, 4, 6)

    def part_slot(chunk):
        return slot_of(chunk, 6, 4)

    def done_slot(chunk):
        return slot_of(chunk, 4, 4)

    def flag_slot(chunk):
        return slot_of(chunk, 8, 6)

    quarter, eighth = lanes // 4, lanes // 8

    def rows_of(ref, index, first, count):
        half_rows = ref.shape[-2]
        start = pl.multiple_of(first % half_rows, 8)
        return (*index, first // half_rows, pl.ds(start, count))

    def link(kind, chunk):
        def at(ref, *index):
            return ref.at[(slot_in(ref, chunk), *index)]

        to, turn = keep_slot(chunk), turn_slot(chunk)
        for_z, hold = part_slot(chunk), keep.at[to]
        source, target, device = (
            lambda: (at(away), at(got), sibling),
            lambda: (hold.at[:, 1 - along_x, 0], at(got_x), across_x),
            lambda: (hold.at[1 - along_y, :, 1], at(got_y), across_y),
            lambda: (at(got_x, 1 - along_y), at(got_xy), across_y),
            lambda: (at(got_y, 1 - along_x), at(got_yx), across_x),
            lambda: (part.at[for_z], from_edge.at[for_z], {"batch": partner}),
            lambda: (part.at[for_z], from_inner.at[for_z], {"batch": 3 - level}),
            None,
            None,
            lambda: (
                keep.at[rows_of(keep, (to, 1 - along_y, 1 - along_x), (level + 3) % 4 * quarter, quarter)],
                ring.at[0, turn], {"batch": above},
            ),
            lambda: (ring.at[0, turn], ring.at[1, turn], {"batch": above}),
            lambda: (ring.at[1, turn], ring.at[2, turn], {"batch": above}),
            lambda: (ring.at[2, turn, pl.ds(0, eighth)], bend.at[0, turn], across_x),
            lambda: (ring.at[2, turn, pl.ds(eighth, eighth)], bend.at[1, turn], across_y),
            lambda: (hold.at[along_y, 1 - along_x], straight.at[0, turn], across_x),
            lambda: (hold.at[1 - along_y, along_x], straight.at[1, turn], across_y),
        )[kind]()
        slot = flag_slot(chunk)
        return pltpu.make_async_remote_copy(
            src_ref=source, dst_ref=target, send_sem=sent.at[kind, slot], recv_sem=came.at[kind, slot],
            **on_other(**device),
        )

    def results(chunk, call):
        slot, at = done_slot(chunk), flag_slot(chunk)

        def pieces(number, source, target):
            yield lambda: pltpu.make_async_copy(source, target, written.at[number, at])
            yield lambda: pltpu.make_async_remote_copy(
                src_ref=source, dst_ref=target,
                send_sem=sent.at[7 + number, at], recv_sem=came.at[7 + number, at],
                **on_other(batch=partner),
            )

        for number, ((blocks, wide), first, grad) in enumerate(zip(reduce_shapes, firsts, grads)):

            @pl.when((chunk >= first) & (chunk < first + blocks * wide))
            def _(number=number, first=first, wide=wide, grad=grad):
                row = ((chunk - first) // wide) * lanes
                column = ((chunk - first) % wide) * width
                if number == 3:
                    column = column + jnp.where(column >= features, lanes, 0)
                target = grad.at[
                    pl.ds(pl.multiple_of(row, lanes), lanes),
                    pl.ds(pl.multiple_of(column, lanes), width),
                ]
                call(*pieces(0, done.at[slot], target))

        @pl.when(chunk == chunks)
        def _():
            target = mix_grad.at[:, pl.ds(features, lanes)]
            call(*pieces(0, done.at[slot, :, pl.ds(0, lanes)], target))
            call(*pieces(1, done.at[slot, :, pl.ds(lanes, lanes)], small_grad))

    def begin(chunk):
        slot, to = slot_in(away, chunk), keep_slot(chunk)
        for (blocks, wide), first, (high, low), (right, shift) in zip(
            reduce_shapes, firsts, lefts, rights
        ):

            @pl.when((chunk >= first) & (chunk < first + blocks * wide))
            def _(first=first, wide=wide, shift=shift, high=high, low=low, right=right):
                block = (chunk - first) // wide
                other, rest = halves(right[shift + (chunk - first) % wide])

                def product(parity):
                    top, under = (
                        (high[block, parity], low[block, parity])
                        if len(high.shape) == 4
                        else (high[parity], low[parity])
                    )
                    total = turned(top, other) + (turned(under, other) + turned(top, rest))
                    return total.reshape(away.shape[1:])

                away[slot] = product(1 - core)
                link(0, chunk).start()
                keep[to] = product(core)

        @pl.when(chunk == chunks)
        def _():
            right = halves(g_shared[...])

            def fill(ref, at, parity):
                total = three((mixed_h[parity], mixed_l[parity]), right, 0, 0)
                total = total.reshape(*away.shape[1:-1], lanes)
                sums = [small_sum[2 * q + parity].reshape(2, -1, lanes) for q in range(4)]
                sums = jnp.stack(sums, axis=0).reshape(total.shape)
                ref[at] = jnp.concatenate([total, sums], axis=-1)

            fill(away, slot, 1 - core)
            link(0, chunk).start()
            fill(keep, to, core)

    def with_sibling(chunk):
        slot = keep_slot(chunk)
        link(0, chunk).wait()
        keep[slot] = keep[slot] + got[slot_in(got, chunk)]
        turning = turns(chunk)
        pl.when(turning)(lambda: link(9, chunk).start())

        @pl.when(jnp.logical_not(turning))
        def _():
            link(1, chunk).start()
            link(2, chunk).start()

    def with_neighbour(chunk):
        slot, from_slot = slot_in(got_x, chunk), keep_slot(chunk)
        link(1, chunk).wait()
        link(2, chunk).wait()
        got_x[slot] = got_x[slot] + keep[from_slot, :, along_x, 0]
        got_y[slot] = got_y[slot] + keep[from_slot, along_y, :, 1]
        link(3, chunk).start()
        link(4, chunk).start()

    def to_edge_or_on(chunk):
        pl.when(is_edge)(lambda: link(5, chunk).start())

    def with_corner(chunk):
        slot = part_slot(chunk)
        link(3, chunk).wait()
        link(4, chunk).wait()
        first, second = slot_in(got_x, chunk), slot_in(got_xy, chunk)
        part[slot, 0] = got_x[first, along_y] + got_xy[second]
        part[slot, 1] = got_y[first, along_x] + got_yx[second]
        to_edge_or_on(chunk)

    def along_z(number):
        def phase(chunk):
            slot = turn_slot(chunk)
            link(9 + number, chunk).wait()
            place = (keep_slot(chunk), 1 - along_y, 1 - along_x)
            own = keep[rows_of(keep, place, (level + 2 - number) % 4 * quarter, quarter)]
            ring[number, slot] = ring[number, slot] + own
            if number < 2:
                link(10 + number, chunk).start()
            else:
                link(12, chunk).start()
                link(13, chunk).start()

        return phase

    def go_straight(chunk):
        slot, to = turn_slot(chunk), keep_slot(chunk)
        link(12, chunk).wait()
        link(13, chunk).wait()
        upper = rows_of(keep, (to, 1 - along_y, along_x), level * quarter, eighth)
        lower = rows_of(keep, (to, along_y, 1 - along_x), level * quarter + eighth, eighth)
        keep[upper] = keep[upper] + bend[0, slot]
        keep[lower] = keep[lower] + bend[1, slot]
        link(14, chunk).start()
        link(15, chunk).start()

    def with_both(chunk):
        slot, turn = part_slot(chunk), turn_slot(chunk)
        link(14, chunk).wait()
        link(15, chunk).wait()
        part[slot] = keep[keep_slot(chunk), along_y, along_x] + straight[0, turn] + straight[1, turn]
        to_edge_or_on(chunk)

    def inner_sum(chunk):
        slot = part_slot(chunk)
        pl.when(is_edge)(lambda: link(5, chunk).wait_send())

        @pl.when(jnp.logical_not(is_edge))
        def _():
            link(5, chunk).wait_recv()
            part[slot] = part[slot] + from_edge[slot]
            link(6, chunk).start()

    def total_sum(chunk):
        slot = part_slot(chunk)

        @pl.when(jnp.logical_not(is_edge))
        def _():
            link(6, chunk).wait()
            done[done_slot(chunk)] = (part[slot] + from_inner[slot]).reshape(done.shape[1:])

            def start(stay, go):
                stay().start()
                go().start()

            results(chunk, start)

    def finish(chunk):
        def receive(stay, go):
            go().wait_recv()

        def release(stay, go):
            stay().wait()
            go().wait_send()

        pl.when(is_edge)(lambda: results(chunk, receive))
        pl.when(jnp.logical_not(is_edge))(lambda: results(chunk, release))

    steps = 48

    def fetch(step, call):
        chunk = jnp.where(
            step < 16, gathered[3] + step, jnp.where(step < 24, step + 8, jnp.where(step < 40, step - 16, step - 40))
        )
        slot = slot_in(buf_h, step)
        for kind, (source, target) in enumerate(((w_high, buf_h), (w_low, buf_l))):
            item = pltpu.make_async_copy(source.at[chunk], target.at[slot], fetched.at[kind, slot])
            getattr(item, call)()

    def back_product(grad, step, parity):
        slot = slot_in(buf_h, step)
        return three(halves(grad), (buf_h[slot, parity], buf_l[slot, parity]), 1, 1)

    def row_of(number, k):
        return jnp.concatenate(
            [small[2 * k, number : number + 1], small[2 * k + 1, number : number + 1]], axis=1
        )

    def put_row(number, k, value):
        for i in range(2):
            small_sum[2 * k + i, number : number + 1] = value[:, i * lanes : (i + 1) * lanes]

    def statistics(ref):
        total = 0.0
        for k in range(tiles):
            total = total + jnp.sum(ref[k], axis=1, keepdims=True)
        centre = total / features
        total = 0.0
        for k in range(tiles):
            shifted = ref[k] - centre
            total = total + jnp.sum(shifted * shifted, axis=1, keepdims=True)
        return centre, lax.rsqrt(total / features + norm_eps)

    def store_statistics(ref):
        for number, value in enumerate(statistics(ref)):
            stat[number] = jnp.broadcast_to(value, (rows, lanes))

    def store_means(plain, crossed):
        for number, value in enumerate((plain, crossed)):
            stat[2 + number] = jnp.broadcast_to(value / features, (rows, lanes))

    def stored(number):
        return stat[number, :, 0:1], stat[number + 1, :, 0:1]

    def grad_two(k):
        span = slice(k * lanes, (k + 1) * lanes)
        return jnp.concatenate([g_two[0, :, span], g_two[1, :, span]], axis=1)

    def norm_two_sums():
        centre, scale = stored(0)
        plain, crossed = 0.0, 0.0
        for k in range(tiles):
            grad, hat = grad_two(k), (middle[k] - centre) * scale
            put_row(2 * states + 2, k, jnp.sum(grad * hat, axis=0, keepdims=True))
            inner = grad * row_of(3 * states + 2, k)
            plain = plain + jnp.sum(inner, axis=1, keepdims=True)
            crossed = crossed + jnp.sum(inner * hat, axis=1, keepdims=True)
        store_means(plain, crossed)

    def norm_two_back():
        (centre, scale), (plain, crossed) = stored(0), stored(2)
        for k in range(tiles):
            inner, hat = grad_two(k) * row_of(3 * states + 2, k), (middle[k] - centre) * scale
            g_middle = g_out[k] + (inner - plain - hat * crossed) * scale
            update = jax.nn.sigmoid(projected[k])
            pre = cand_pre[k]
            gate = jax.nn.sigmoid(pre)
            middle[k] = g_middle * (1.0 - update)
            projected[k] = g_middle * (pre * gate - masked[k]) * update * (1.0 - update)
            projected[12 + k] = g_middle * update * (gate * (1.0 + pre * (1.0 - gate)))

    def attention_back(m):
        parity, start = m % 2, pl.multiple_of((m // 2) * lanes, lanes)
        grad = jnp.concatenate(
            [g_gated[0, parity, :, pl.ds(start, lanes)], g_gated[1, parity, :, pl.ds(start, lanes)]], axis=1
        )
        pre = projected[4 + m]
        gate = jax.nn.sigmoid(pre)
        g_attended = grad * pre * gate
        projected[4 + m] = grad * attended[m] * (gate * (1.0 + pre * (1.0 - gate)))
        pre = value_pre[m]
        gate = jax.nn.sigmoid(pre)
        values, curve = pre * gate, gate * (1.0 + pre * (1.0 - gate))
        g_values = []
        for s in range(sequences):
            span = slice(s * block_len, (s + 1) * block_len)
            own = halves(g_attended[span])
            g_soft[s] = g_soft[s] + three(own, halves(values[span]), 1, 1)
            g_values.append(three(halves(soft[s]), own, 0, 0) * curve[span])
        value_pre[m] = jnp.concatenate(g_values, axis=0)

    def scores_back():
        affine = tree_sum([small[k, 3 * states + 3 : 3 * states + 6] for k in range(8)])
        pre = shared_pre[...]
        gate = jax.nn.sigmoid(pre)
        shared, curve = pre * gate, gate * (1.0 + pre * (1.0 - gate))
        score_scale = shared.shape[1] ** (-0.5)
        queries = shared * affine[0:1] + affine[2:3]
        keys = shared * affine[1:2]
        sums = [0.0, 0.0, 0.0]
        for s in range(sequences):
            span = slice(s * block_len, (s + 1) * block_len)
            soft_weight, grad = soft[s], g_soft[s]
            g_scores = soft_weight * (grad - jnp.sum(grad * soft_weight, axis=1, keepdims=True))
            g_scores = jnp.where(key_valid[s] > 0.5, g_scores, 0.0) * score_scale
            g_queries = contract(g_scores, keys[span], 1, 0, exact)
            g_keys = contract(g_scores, queries[span], 0, 0, exact)
            g_shared[span] = (g_queries * affine[0:1] + g_keys * affine[1:2]) * curve[span]
            terms = (g_queries * shared[span], g_keys * shared[span], g_queries)
            for number, term in enumerate(terms):
                sums[number] = sums[number] + jnp.sum(term, axis=0, keepdims=True)
        for number in range(3):
            for k in range(8):
                row = 2 * states + 3 + number
                small_sum[k, row : row + 1] = sums[number]

    def shared_back():
        own, full = halves(g_shared[...]), halves(shared_w[...].reshape(2, half, lanes))
        for parity in range(2):
            g_mixed[parity] = three(own, (full[0][parity], full[1][parity]), 1, 1)

    def load_tables():
        for kind in range(3):
            for n in range(states):
                tables[kind, n] = small[:, kind * states + n]

    def smooth_back():
        for parity in range(2):
            pre = mix_pre[parity]
            g_mixed[parity] = g_mixed[parity] * silu_slope(pre)
        for s in range(sequences):
            span = slice(s * block_len, (s + 1) * block_len)
            blocks = [
                g_mixed[block % 2, span, block // 2 * lanes : (block // 2 + 1) * lanes]
                for block in range(8)
            ]
            smooth[s] = jnp.concatenate(blocks, axis=1).reshape(smooth.shape[1:])

    share_ends, to_chips, share_entering, enter_states = state_exchange(
        True, block_decay, ends, chip_ends, halves_in, back_enter, sent_state, came_state
    )

    def filter_one(s):
        run_filter(True, s, decay, weight, smooth, back, ends.at[core])
        if s == sequences - 1:
            share_ends()

    def moments_one(s, low):
        run_moments(s, low, low + 8, decay, enter, signal, smooth, direct, slope, last)

    def carry_one(s):
        run_carried(True, s, decay, weight, back_enter, back, back)

    def both_blocks(ref, k):
        span = slice(k * lanes, (k + 1) * lanes)
        return jnp.concatenate([ref[0, :, span], ref[1, :, span]], axis=1)

    def state_sums():
        for n in range(states):
            total = slope[n]
            for s in range(sequences):
                total = total + decay[n] * back_enter[s, n] * last[s, n]
            small_sum[:, n] = direct[n]
            small_sum[:, states + n] = total

    def norm_one_sums():
        centre, scale = stored(0)
        line = [back[s].reshape(block_len, features) for s in range(sequences)]
        line = jnp.concatenate(line, axis=0)
        plain, crossed = 0.0, 0.0
        for k in range(tiles):
            g_smooth, hat = both_blocks(g_mixed, k), (masked[k] - centre) * scale
            gain = row_of(3 * states, k)
            grad = both_blocks(g_normed, k) + g_smooth * row_of(3 * states + 1, k)
            grad = grad + line[:, k * width : (k + 1) * width]
            put_row(2 * states, k, jnp.sum(grad * hat, axis=0, keepdims=True))
            put_row(2 * states + 1, k, jnp.sum(g_smooth * (hat * gain), axis=0, keepdims=True))
            inner = grad * gain
            plain = plain + jnp.sum(inner, axis=1, keepdims=True)
            crossed = crossed + jnp.sum(inner * hat, axis=1, keepdims=True)
            tokens_grad[:, k * width : (k + 1) * width] = inner
        store_means(plain, crossed)

    def norm_one_back():
        (centre, scale), (plain, crossed) = stored(0), stored(2)
        for k in range(tiles):
            span = slice(k * width, (k + 1) * width)
            hat = (masked[k] - centre) * scale
            g_x = (tokens_grad[:, span] - plain - hat * crossed) * scale
            tokens_grad[:, span] = (middle[k] + g_x) * row_valid[...]

    g_two[...] = jnp.zeros(g_two.shape, jnp.float32)
    g_gated[...] = jnp.zeros(g_gated.shape, jnp.float32)
    g_normed[...] = jnp.zeros(g_normed.shape, jnp.float32)
    g_soft[...] = jnp.zeros(g_soft.shape, jnp.float32)
    small_sum[...] = jnp.zeros(small_sum.shape, jnp.float32)

    def work(at):
        merging, mixing, valuing = 18, 35, 51
        in_merge = (at >= merging) & (at < merging + 8)
        in_mix = (at >= mixing) & (at < mixing + 16)
        in_value = (at >= valuing) & (at < valuing + 8)
        pl.when(at == 14)(lambda: store_statistics(middle))
        pl.when(at == 16)(norm_two_sums)
        pl.when(at == 17)(norm_two_back)
        pl.when(at == 34)(scores_back)
        pl.when(at == 35)(shared_back)

        @pl.when((at < 16) | in_merge | in_mix | in_value)
        def _():
            step = jnp.where(at < 16, at, jnp.where(at < merging + 8, at - 2, at - 11))
            pl.when(step + 2 < steps)(lambda: fetch(step + 2, "start"))
            fetch(step, "wait")

            @pl.when(at < 16)
            def _():
                for parity in range(2):
                    g_two[parity] = g_two[parity] + back_product(g_wide[at], step, parity)

            @pl.when(in_merge)
            def _():
                j, tile = (at - merging) // 4, (at - merging) % 4
                for parity in range(2):
                    more = back_product(projected[12 + tile], step, parity)
                    g_gated[j, parity] = g_gated[j, parity] + more

            @pl.when(in_mix)
            def _():
                for parity in range(2):
                    more = back_product(projected[at - mixing], step, parity)
                    g_mixed[parity] = g_mixed[parity] + more

            @pl.when(in_value)
            def _():
                for parity in range(2):
                    more = back_product(value_pre[at - valuing], step, parity)
                    g_normed[parity] = g_normed[parity] + more

        pl.when((at >= 26) & (at < 34))(lambda: attention_back(at - 26))
        pl.when(at == 28)(load_tables)
        pl.when(at == 30)(lambda: store_statistics(masked))
        pl.when(at == 51)(smooth_back)
        for s in range(sequences):
            pl.when(at == 52 + s)(functools.partial(filter_one, s))
            for low in range(0, states, 8):
                number = 54 + s * (states // 8) + low // 8
                pl.when(at == number)(functools.partial(moments_one, s, low))
            pl.when(at == 60 + s)(functools.partial(carry_one, s))
        pl.when(at == 55)(to_chips)
        pl.when(at == 57)(share_entering)
        pl.when(at == 59)(enter_states)
        pl.when(at == 61)(state_sums)
        pl.when(at == 62)(norm_one_sums)
        pl.when(at == 63)(norm_one_back)

    every, straight_on, turning = None, False, True
    phases = (
        (0, begin, every), (1, with_sibling, every),
        (3, with_neighbour, straight_on), (5, with_corner, straight_on), (7, inner_sum, straight_on),
        (9, total_sum, straight_on), (11, finish, straight_on),
        (3, along_z(0), turning), (5, along_z(1), turning), (7, along_z(2), turning), (9, go_straight, turning),
        (11, with_both, turning), (13, inner_sum, turning), (15, total_sum, turning), (17, finish, turning),
    )
    fetch(0, "start")
    fetch(1, "start")

    def arrive(first, end):
        for item in copies_in[first:end]:
            item.wait()

    arrive(0, 3)

    def step(at, carry):
        for after, phase, which in sorted(phases, key=lambda item: -item[0]):
            chunk = at - after
            wanted = (chunk >= 0) & (chunk <= chunks)
            if which is not None:
                wanted = wanted & (turns(chunk) == which)

            @pl.when(wanted)
            def _(chunk=chunk, phase=phase):
                phase(chunk)

        pl.when(at == 0)(lambda: arrive(3, 4))
        pl.when(at == 8)(lambda: arrive(4, kept_count))
        work(at)
        return carry

    lax.fori_loop(0, chunks + 1 + 11, step, 0)


def call_backward(row_valid, key_valid, w_high, w_low, kept, grad_shapes):
    _, rows, width = kept[3].shape
    soft, signal, enter = kept[17], kept[20], kept[21]
    states = enter.shape[1]
    half, piece = 4 * lanes, lanes // 2
    vmem, anywhere = pl.BlockSpec(memory_space=pltpu.VMEM), pl.BlockSpec(memory_space=pl.ANY)
    shapes = [f32(rows, 8 * lanes)] + [f32(*shape) for shape in grad_shapes] + [f32(lanes, lanes)]
    held = [
        (4, 2, 2, 2, piece, width), (10, 2, 2, 2, piece, width), (4, 2, 2, 2, piece, width),
        (6, 2, piece, width), (6, 2, piece, width), (6, piece, width), (6, piece, width),
        (10, 2, piece, width), (10, 2, piece, width), (10, 2, piece, width), (8, lanes, width),
        (3, 6, lanes // 4, width), (2, 6, lanes // 8, width), (2, 6, 2, piece, width),
    ]
    more = [
        (2, rows, half), (2, 2, rows, half), (2, rows, half), (2, rows, half), soft.shape, (rows, lanes),
        signal.shape, signal.shape, (2, *enter.shape), (4, enter.shape[0], states // 2, 8, lanes),
        (2, enter.shape[0], states // 2, 8, lanes), enter.shape, (3, states, 8, lanes),
        (states, 8, lanes), (states, 8, lanes), enter.shape, (8, lanes, lanes), (4, rows, lanes),
    ]
    return pl.pallas_call(
        backward_body,
        out_shape=shapes,
        in_specs=[vmem] * 2 + [anywhere] * (2 + kept_count),
        out_specs=[vmem] + [anywhere] * (len(shapes) - 1),
        scratch_shapes=[pltpu.VMEM(item.shape, item.dtype) for item in kept]
        + [pltpu.VMEM(shape, jnp.float32) for shape in held]
        + [pltpu.VMEM((3, 2, half, width), jnp.bfloat16)] * 2
        + [pltpu.VMEM(shape, jnp.float32) for shape in more]
        + [
            pltpu.SemaphoreType.DMA((2, 3)),
            pltpu.SemaphoreType.DMA((kept_count,)),
            pltpu.SemaphoreType.DMA((16, 14)),
            pltpu.SemaphoreType.DMA((16, 14)),
            pltpu.SemaphoreType.DMA((2, 14)),
            pltpu.SemaphoreType.DMA((5,)),
            pltpu.SemaphoreType.DMA((5,)),
        ],
        compiler_params=pltpu.CompilerParams(
            collective_id=1, has_side_effects=True, vmem_limit_bytes=62 * 1024 * 1024
        ),
    )(row_valid, key_valid, w_high, w_low, *kept)


def call_kernel(body, shapes, *operands):
    return pl.pallas_call(
        body,
        out_shape=[jax.ShapeDtypeStruct(shape, jnp.float32) for shape in shapes],
        in_specs=[pl.BlockSpec(memory_space=pltpu.VMEM)] * len(operands),
        out_specs=[pl.BlockSpec(memory_space=pltpu.VMEM)] * len(shapes),
        compiler_params=pltpu.CompilerParams(vmem_limit_bytes=32 * 1024 * 1024),
    )(*operands)


def entering(ends, block_decay, backward):
    count, mine = lax.axis_size("seq"), lax.axis_index("seq")
    pieces = lax.all_gather(ends, "seq")
    if backward:
        mine = count - 1 - mine
    total = jnp.zeros_like(ends)
    for position in range(count - 1):
        piece = pieces[count - 1 - position if backward else position]
        total = jnp.where(position < mine, block_decay * total + piece, total)
    return total


def silu(value):
    return value * jax.nn.sigmoid(value)


def silu_slope(value):
    gate = jax.nn.sigmoid(value)
    return gate * (1.0 + value * (1.0 - gate))


def normalise(signal):
    centre = jnp.mean(signal, axis=-1, keepdims=True)
    shifted = signal - centre
    spread = jnp.mean(shifted * shifted, axis=-1, keepdims=True)
    scale = lax.rsqrt(spread + norm_eps)
    return shifted * scale, scale


def normalise_back(grad, gain, hat, scale):
    inner = grad * gain
    return (
        inner
        - jnp.mean(inner, axis=-1, keepdims=True)
        - hat * jnp.mean(inner * hat, axis=-1, keepdims=True)
    ) * scale


def times(left, right):
    return jnp.dot(left, right, precision=triple)


def times_back(left, right):
    return lax.dot_general(left, right, (((1,), (1,)), ((), ())), precision=triple)


def plain_layer(masked_in, normed, mix_pre, g_out, row_valid, key_valid, affine, gain_two, weights):
    value_full, mix_full, merge_full, widen_full, narrow_full = (gather_rows(w) for w in weights)
    rows, width = masked_in.shape
    sequences, _, block_len = key_valid.shape
    value_dim, shared_dim = value_full.shape[1], affine.shape[0]
    mixed = silu(mix_pre)
    value_pre = times(normed, value_full)
    values = silu(value_pre)
    projected = times(mixed, mix_full)
    second_cut = width + shared_dim
    third_cut = second_cut + value_dim
    update = jax.nn.sigmoid(projected[:, :width])
    shared_pre = projected[:, width:second_cut]
    reset_pre = projected[:, second_cut:third_cut]
    shared = silu(shared_pre)
    reset_gate = silu(reset_pre)
    queries = (shared * affine[:, 0] + affine[:, 2]).reshape(sequences, block_len, shared_dim)
    key_rows = (shared * affine[:, 1]).reshape(sequences, block_len, shared_dim)
    score_scale = shared_dim ** (-0.5)
    scores = jnp.einsum("cqz,ckz->cqk", queries, key_rows, precision=exact) * score_scale
    scores = jnp.where(key_valid > 0.5, scores, masked_score)
    soft = jax.nn.softmax(scores, axis=-1)
    values_cut = values.reshape(sequences, block_len, value_dim)
    attended = jnp.einsum("cqk,ckv->cqv", soft, values_cut, precision=triple)
    attended = attended.reshape(rows, value_dim)
    gated = attended * reset_gate
    cand_pre = projected[:, third_cut:] + times(gated, merge_full)
    candidate = silu(cand_pre)
    middle = masked_in + update * (candidate - masked_in)
    hat_two, scale_two = normalise(middle)
    normed_two = hat_two * gain_two
    wide_pre = times(normed_two, widen_full)
    hidden = silu(wide_pre)
    block_out = (middle + times(hidden, narrow_full)) * row_valid

    g_wide = times_back(g_out, narrow_full) * silu_slope(wide_pre)
    g_normed_two = times_back(g_wide, widen_full)
    gain_sum = jnp.sum(g_normed_two * hat_two, axis=0)
    g_middle = g_out + normalise_back(g_normed_two, gain_two, hat_two, scale_two)
    g_cand = g_middle * update * silu_slope(cand_pre)
    g_gated = times_back(g_cand, merge_full)
    g_attended = (g_gated * reset_gate).reshape(sequences, block_len, value_dim)
    g_soft = jnp.einsum("cqv,ckv->cqk", g_attended, values_cut, precision=triple)
    g_values = jnp.einsum("cqk,cqv->ckv", soft, g_attended, precision=triple)
    g_scores = soft * (g_soft - jnp.sum(g_soft * soft, axis=-1, keepdims=True))
    g_scores = jnp.where(key_valid > 0.5, g_scores, 0.0) * score_scale
    g_queries = jnp.einsum("cqk,ckz->cqz", g_scores, key_rows, precision=exact)
    g_keys = jnp.einsum("cqk,cqz->ckz", g_scores, queries, precision=exact)
    g_queries = g_queries.reshape(rows, shared_dim)
    g_keys = g_keys.reshape(rows, shared_dim)
    terms = (g_queries * shared, g_keys * shared, g_queries)
    affine_sum = jnp.stack([jnp.sum(term, axis=0) for term in terms])
    g_shared = (g_queries * affine[:, 0] + g_keys * affine[:, 1]) * silu_slope(shared_pre)
    g_update = g_middle * (candidate - masked_in) * update * (1.0 - update)
    g_reset = g_gated * attended * silu_slope(reset_pre)
    g_projected = jnp.concatenate([g_update, g_shared, g_reset, g_cand], axis=1)
    g_mixed = times_back(g_projected, mix_full)
    g_val = g_values.reshape(rows, value_dim) * silu_slope(value_pre)
    g_from_values = times_back(g_val, value_full)

    def total(packed):
        count = lax.axis_size("seq")
        features = packed.shape[1] // count

        def reduced(whole, tiled=True):
            part = lax.psum_scatter(whole, "seq", scatter_dimension=0, tiled=tiled)
            return lax.psum(part, "batch")

        pairs = (
            (normed, g_val),
            (mixed, g_projected),
            (gated, g_cand),
            (normed_two, g_wide),
            (hidden, g_out),
        )
        grads = tuple(reduced(product_grad(*pair)) for pair in pairs)
        blocks = packed.reshape(-1, count, features).transpose(1, 0, 2)
        return grads + (reduced(blocks, False),)

    return block_out, g_mixed, g_from_values, g_middle * (1.0 - update), gain_sum, affine_sum, total


def plane_layer(tokens, out_grad, valid, logits, rows_of, affine, weights):
    sequences, block_len, width = tokens.shape
    rows = sequences * block_len
    states, own = logits[0].shape
    device = lax.axis_index("seq")
    alpha, delta, beta, gamma = logits
    alpha_rate, damp_rate = jax.nn.sigmoid(alpha), jax.nn.sigmoid(delta)
    out_scale = states ** (-0.5)
    weight = alpha_rate * beta * gamma * out_scale
    block_decay = jnp.exp(block_len * jnp.log1p(-alpha_rate * damp_rate))
    spread = lax.dynamic_update_slice(
        jnp.zeros((3, own), jnp.float32), affine.T, (0, device * affine.shape[0])
    )
    packed = jnp.concatenate([1.0 - alpha_rate * damp_rate, weight, block_decay, rows_of, spread])
    packed = jnp.pad(packed, ((0, -packed.shape[0] % 8), (0, 0)))
    row_valid = valid.reshape(rows, 1)
    key_valid = valid.reshape(sequences, 1, block_len)
    block_out, w_high, w_low, *kept = call_forward(
        weights, packed, tokens.reshape(rows, width), out_grad.reshape(rows, width), row_valid, key_valid, states
    )
    value_weight, mix_weight, merge_weight, widen_weight, narrow_weight = weights
    tokens_grad, narrow, widen, merge, mix, value, sums = call_backward(
        row_valid,
        key_valid,
        w_high,
        w_low,
        kept,
        [w.shape for w in (narrow_weight, widen_weight, merge_weight, mix_weight, value_weight)],
    )
    direct, slope = sums[:states], sums[states : 2 * states]
    decay_grad = weight * slope
    alpha_grad = (beta * gamma * out_scale * direct - damp_rate * decay_grad) * (
        alpha_rate * (1.0 - alpha_rate)
    )
    delta_grad = -alpha_rate * decay_grad * damp_rate * (1.0 - damp_rate)
    beta_grad = alpha_rate * gamma * out_scale * direct
    gamma_grad = alpha_rate * beta * out_scale * direct
    affine_grad = lax.dynamic_slice(
        sums[2 * states + 3 : 2 * states + 6], (0, device * affine.shape[0]), affine.T.shape
    )
    return (
        block_out.reshape(tokens.shape),
        tokens_grad.reshape(tokens.shape),
        sums[2 * states],
        alpha_grad.T,
        delta_grad.T,
        beta_grad.T,
        gamma_grad.T,
        sums[2 * states + 1],
        value,
        mix,
        affine_grad.T,
        merge,
        sums[2 * states + 2],
        widen,
        narrow,
    )


def per_device(
    tokens,
    lengths,
    out_grad,
    first_gain,
    smooth_alpha,
    smooth_delta,
    smooth_beta,
    smooth_gamma,
    smooth_omega,
    value_weight,
    mix_weight,
    query_affine,
    merge_weight,
    second_gain,
    widen_weight,
    narrow_weight,
):
    sequences, block_len, width = tokens.shape
    count = lax.axis_size("seq")
    states = smooth_alpha.shape[1]
    own = first_gain.shape[0]
    own_shared = query_affine.shape[0]
    rows = sequences * block_len
    shared_dim = own_shared * count
    offsets = lax.axis_index("seq") * block_len + lax.iota(jnp.int32, block_len)
    valid = (offsets[None, :] < lengths[:, None]).astype(jnp.float32)
    weights = (value_weight, mix_weight, merge_weight, widen_weight, narrow_weight)
    if count == 8 and lax.axis_size("batch") == 4:
        logits = (smooth_alpha.T, smooth_delta.T, smooth_beta.T, smooth_gamma.T)
        rows_of = jnp.stack([first_gain, smooth_omega, second_gain])
        return plane_layer(tokens, out_grad, valid, logits, rows_of, query_affine, weights)

    affine_row = jnp.pad(query_affine.reshape(-1), (0, own - 3 * own_shared))
    packed = [
        smooth_alpha.T,
        smooth_delta.T,
        smooth_beta.T,
        smooth_gamma.T,
        jnp.stack([first_gain, smooth_omega, second_gain, affine_row]),
    ]
    small = lax.all_gather(jnp.concatenate(packed, axis=0), "seq").transpose(1, 0, 2)

    tiles = (width // lanes, lanes)
    alpha_rate = jax.nn.sigmoid(small[:states].reshape(states, *tiles))
    damp_rate = jax.nn.sigmoid(small[states : 2 * states].reshape(states, *tiles))
    beta = small[2 * states : 3 * states].reshape(states, *tiles)
    gamma = small[3 * states : 4 * states].reshape(states, *tiles)
    gain_one = small[4 * states].reshape(1, width)
    omega = small[4 * states + 1].reshape(1, width)
    gain_two = small[4 * states + 2].reshape(1, width)
    affine = small[4 * states + 3, :, : 3 * own_shared].reshape(shared_dim, 3)
    out_scale = states ** (-0.5)
    decay = 1.0 - alpha_rate * damp_rate
    block_decay = jnp.exp(block_len * jnp.log1p(-alpha_rate * damp_rate))
    weight = alpha_rate * beta * gamma * out_scale

    row_valid = valid.reshape(rows, 1)
    key_valid = valid.reshape(sequences, 1, block_len)

    masked_in = tokens.reshape(rows, width) * row_valid
    g_out = out_grad.reshape(rows, width) * row_valid
    hat_one, scale_one = normalise(masked_in)
    normed = hat_one * gain_one
    tiled = (sequences, block_len) + tiles
    ending = (sequences, states) + tiles
    signal = normed.reshape(tiled)
    local, ends = call_kernel(
        functools.partial(filter_body, False), [tiled, ending], decay, weight, signal
    )
    enter = entering(ends, block_decay, False)
    (smoothed,) = call_kernel(
        functools.partial(carried_body, False), [tiled], decay, weight, enter, local
    )
    mix_pre = smoothed.reshape(rows, width) + omega * normed

    results = plain_layer(
        masked_in, normed, mix_pre, g_out, row_valid, key_valid, affine, gain_two, weights
    )
    block_out, g_mixed, g_from_values, g_rest, second_gain_sum, affine_sum, total = results
    g_smooth = g_mixed * silu_slope(mix_pre)

    smooth_tiled = g_smooth.reshape(tiled)
    back_local, back_ends = call_kernel(
        functools.partial(filter_body, True), [tiled, ending], decay, weight, smooth_tiled
    )
    back_enter = entering(back_ends, block_decay, True)
    direct, slope, last = call_kernel(
        moments_body,
        [(states,) + tiles, (states,) + tiles, ending],
        decay,
        enter,
        signal,
        smooth_tiled,
    )
    (back_full,) = call_kernel(
        functools.partial(carried_body, True), [tiled], decay, weight, back_enter, back_local
    )
    slope = slope + decay * jnp.sum(back_enter * last, axis=0)
    decay_grad = weight * slope
    alpha_grad = (beta * gamma * out_scale * direct - damp_rate * decay_grad) * (
        alpha_rate * (1.0 - alpha_rate)
    )
    delta_grad = -alpha_rate * decay_grad * damp_rate * (1.0 - damp_rate)
    beta_grad = alpha_rate * gamma * out_scale * direct
    gamma_grad = alpha_rate * beta * out_scale * direct

    g_normed = g_from_values + g_smooth * omega + back_full.reshape(rows, width)
    tokens_grad = (g_rest + normalise_back(g_normed, gain_one, hat_one, scale_one)) * row_valid
    first_gain_sum = jnp.sum(g_normed * hat_one, axis=0)
    omega_sum = jnp.sum(g_smooth * normed, axis=0)
    affine_rows = jnp.pad(
        affine_sum.T.reshape(count, 3 * own_shared), ((0, 0), (0, own - 3 * own_shared))
    )
    small_rows = [
        alpha_grad.reshape(states, width),
        delta_grad.reshape(states, width),
        beta_grad.reshape(states, width),
        gamma_grad.reshape(states, width),
        jnp.stack([first_gain_sum, omega_sum, second_gain_sum, affine_rows.reshape(width)]),
    ]
    value_grad, mix_grad, merge_grad, widen_grad, narrow_grad, small_grad = total(
        jnp.concatenate(small_rows, axis=0)
    )

    return (
        block_out.reshape(tokens.shape),
        tokens_grad.reshape(tokens.shape),
        small_grad[4 * states],
        small_grad[:states].T,
        small_grad[states : 2 * states].T,
        small_grad[2 * states : 3 * states].T,
        small_grad[3 * states : 4 * states].T,
        small_grad[4 * states + 1],
        value_grad,
        mix_grad,
        small_grad[4 * states + 3, : 3 * own_shared].reshape(own_shared, 3),
        merge_grad,
        small_grad[4 * states + 2],
        widen_grad,
        narrow_grad,
    )


def solution(mesh):
    rows = P("batch", "seq", None)
    split = P("seq", None)
    in_specs = (
        (rows, P("batch"), rows, P("seq"))
        + (split,) * 4
        + (P("seq"),)
        + (split,) * 4
        + (P("seq"),)
        + (split,) * 2
    )
    out_specs = (
        (rows, rows, P("seq"))
        + (split,) * 4
        + (P("seq"),)
        + (split,) * 4
        + (P("seq"),)
        + (split,) * 2
    )
    return jax.shard_map(
        per_device, mesh=mesh, in_specs=in_specs, out_specs=out_specs, check_vma=False
    )
```
